32 devices in a mesh: row: 2 (over y), col: 16 (over z, x, core).
Axes of the slice: x: 2, y: 2, z: 4, core: 2. Of those that a mesh axis runs over, the one named last changes fastest.
Arguments:
- own_block: float32 [4, 64, 128, 128], P('row', 'col')
- neighbor_block: float32 [4, 4, 64, 128, 128], P(None, 'row', 'col'), may hold values from -0.1 to 0.1
- pattern: int32 [4, 64, 4], P('row', 'col'), may hold values 0 or 1
- capacity: float32 [4, 64, 128], P('row', 'col'), may hold values from 0.02 to 4
- initial: float32 [4, 64, 128], P('row', 'col'), may hold values from -4 to 4
- currents: float32 [2, 16, 16, 4, 512], P('row', 'col'), may hold values from -6 to 6
- slot_tile: int32 [2, 16, 16, 4], P('row', 'col'), may hold values from 0 to 8, as said below
Outputs:
- drops: float32 [4, 4, 64, 128], P(None, 'row', 'col')
The draws below stay inside these ranges and needn't reach their ends.
Inputs may be any that keep to these rules, and one draw needn't show every extreme that they name: `slot_tile`: empty slots hold 8. In every mesh row one destination column receives 4 live slots from every source column; other pairs hold 0 to 4 live slots, live ones first.
All inputs are finite; a program needn't handle non-finite values. No bound on the sum of `pattern` on one device may be relied on, other than what follows from the above.
Results may differ from the reference program's by a relative error of at most 0.0001.
Values sent between devices are 32-bit elements; how exact they have to be, the bound alone decides.
No kernel may reach another device: no remote copies, remote signals or barrier semaphores. Data moves between devices by JAX's collectives and lax.ppermute only.
A program may use at most 64 MiB of HBM per device.

```python
import math
import jax
import jax.numpy as jnp
from jax import lax

TILE = 128
TRD = 2
TCD = 4
CAP = 4
STEPS = 4
ITERS = 8
NTR = 4
NTC = 64
FRAMES = 512
N_ROW = 2
N_COL = 16


def draw_own_block(key, part):
    key_spread, key_middle = jax.random.split(key)
    spread = jax.random.uniform(key_spread, (NTR, NTC, TILE, TILE), jnp.float32, -0.1, 0.1)
    middle = jax.random.uniform(key_middle, (NTR, NTC, TILE), jnp.float32, 2.5, 6.0)
    identity = jnp.eye(TILE, dtype=jnp.float32)
    return spread * (1.0 - identity) + identity * middle[..., None]


def draw_slot_tile(key, part):
    key_count, key_busy, key_tiles = jax.random.split(key, 3)
    counts = jax.random.randint(key_count, (N_ROW, N_COL, N_COL), 0, CAP + 1)
    busiest = jax.random.randint(key_busy, (N_ROW,), 0, N_COL)
    is_busy = jnp.arange(N_COL)[None, None, :] == busiest[:, None, None]
    counts = jnp.where(is_busy, CAP, counts)
    targets = jax.random.randint(key_tiles, (N_ROW, N_COL, N_COL, CAP), 0, TRD * TCD)
    position = jnp.arange(CAP)[None, None, None, :]
    return jnp.where(position < counts[..., None], targets, TRD * TCD).astype(jnp.int32)


def set_ends(array, key, low, high):
    shape = array.shape
    index_at = [jax.random.randint(jax.random.fold_in(key, axis), (), 0, shape[axis]) for axis in range(len(shape))]
    array = array.at[tuple(index_at)].set(low)
    longest = shape.index(max(shape))
    index_at[longest] = (index_at[longest] + 1) % shape[longest]
    return array.at[tuple(index_at)].set(high)


def levels(rng, dims, cuts, smallest, top_value):
    def one(dim, shards_of):
        steps = jax.random.uniform(jax.random.fold_in(jax.random.fold_in(rng, 6), dim), (shards_of,), jnp.float32, smallest / len(cuts), top_value / len(cuts))
        return jnp.repeat(jnp.exp(steps), dims[dim] // shards_of).reshape((-1,) + (1,) * (len(dims) - dim - 1))

    loudness = one(*cuts[0])
    for cut in cuts[1:]:
        loudness = loudness * one(*cut)
    return loudness


def normal_values(rng, shape, width, limit, pieces=(), kind=jnp.bfloat16):
    factor_of = levels(rng, shape, pieces, -0.22, 0.18) if pieces else 1.0
    result = jax.random.normal(rng, shape, jnp.float32) * width * factor_of
    return jnp.minimum(jnp.maximum(result, -limit), limit).astype(kind)


def setup_inputs(seed: int = 0) -> dict:
    splits = jax.random.split(jax.random.key(seed), 8)
    return {
        "own_block": draw_own_block(jax.random.fold_in(splits[7], 71), 0),
        "neighbor_block": jnp.clip(jax.random.uniform(splits[1], (4, NTR, NTC, TILE, TILE), jnp.float32, -0.1, 0.1) * levels(splits[1], (4, NTR, NTC, TILE, TILE), ((1, 2), (2, 16)), -0.4, 0.0), -0.1, 0.1),
        "pattern": set_ends((jax.random.randint(splits[2], (NTR, NTC, 4), 0, 4) < 3).astype(jnp.int32), jax.random.fold_in(splits[2], 1), 0, 1),
        "capacity": jnp.clip(jnp.exp(math.log(4.0) - 5.2983174 * jax.random.uniform(splits[3], (NTR, NTC, TILE), jnp.float32) ** levels(splits[3], (NTR, NTC, TILE), ((0, 2), (1, 16)), -0.2, 0.2)), 0.02, 4.0),
        "initial": normal_values(splits[4], (NTR, NTC, TILE), 0.3, 4.0, ((0, 2), (1, 16)), jnp.float32),
        "currents": normal_values(splits[5], (N_ROW, N_COL, N_COL, CAP, FRAMES), 0.5, 6.0, ((0, 2), (1, 16)), jnp.float32),
        "slot_tile": draw_slot_tile(jax.random.fold_in(splits[7], 71), 0),
    }


spec_center = 6.4
spec_radius = 5.6


def couple(field, own_block, neighbor_block, pattern, capacity):
    padded = jnp.pad(field, ((1, 1), (1, 1), (0, 0)))
    upper_row = padded[:-2, 1:-1]
    lower_row = padded[2:, 1:-1]
    left_col = padded[1:-1, :-2]
    right_col = padded[1:-1, 2:]
    beside_all = jnp.stack([upper_row, lower_row, left_col, right_col])
    coupled = jnp.einsum("nijab,nijb->nija", neighbor_block, beside_all, precision=lax.Precision.HIGHEST)
    weights = jnp.moveaxis(pattern, 2, 0).astype(jnp.float32)[..., None]
    outside = jnp.sum(coupled * weights, axis=0)
    inside = jnp.einsum("ijab,ijb->ija", own_block, field, precision=lax.Precision.HIGHEST)
    return inside + outside + capacity * field


def sweeps(estimate, source, blocks):
    residue = source - couple(estimate, *blocks)
    search_dir = residue
    stride = 1.0 / spec_center
    for sweep in range(ITERS):
        if sweep == 0:
            search_dir = residue
            stride = 1.0 / spec_center
        else:
            if sweep == 1:
                momentum = 0.5 * (spec_radius * stride) ** 2
            else:
                momentum = (spec_radius * stride / 2.0) ** 2
            stride = 1.0 / (spec_center - momentum / stride)
            search_dir = residue + momentum * search_dir
        estimate = estimate + stride * search_dir
        if sweep + 1 < ITERS:
            residue = residue - stride * couple(search_dir, *blocks)
    return estimate


def reference(own_block, neighbor_block, pattern, capacity, initial, currents, slot_tile):
    tiles = TRD * TCD
    chooser = (slot_tile[..., None] == jnp.arange(tiles, dtype=jnp.int32)).astype(jnp.float32)
    injected = jnp.einsum("rsdkt,rsdkf->rdtf", chooser, currents, precision=lax.Precision.HIGHEST)
    injected = injected.reshape(N_ROW, N_COL, TRD, TCD, STEPS, TILE)
    injected = jnp.transpose(injected, (4, 0, 2, 1, 3, 5)).reshape(STEPS, NTR, NTC, TILE)
    blocks = (own_block, neighbor_block, pattern, capacity)
    voltage = initial
    frames = []
    for instant in range(STEPS):
        source = capacity * voltage + injected[instant]
        voltage = sweeps(voltage, source, blocks)
        frames.append(voltage)
    return jnp.stack(frames)
```

```python
import functools

import jax
import jax.numpy as jnp
from jax import lax
from jax.experimental import pallas as pl
from jax.experimental.pallas import tpu as pltpu
from jax.sharding import PartitionSpec as P

STEPS = 4
ITERS = 8

spec_center = 6.4
spec_radius = 5.6


def schedule():
    strides, momenta = [], []
    stride = 1.0 / spec_center
    for sweep in range(ITERS):
        if sweep == 0:
            momentum = 0.0
        else:
            if sweep == 1:
                momentum = 0.5 * (spec_radius * stride) ** 2
            else:
                momentum = (spec_radius * stride / 2.0) ** 2
            stride = 1.0 / (spec_center - momentum / stride)
        strides.append(stride)
        momenta.append(momentum)
    return strides, momenta


STRIDES, MOMENTA = schedule()


def swap_pairs(count, first):
    pairs = []
    for i in range(first, count - 1, 2):
        pairs += [(i, i + 1), (i + 1, i)]
    return pairs


def exchange(field):
    arrived = []
    for axis in ("row", "col"):
        count = lax.axis_size(axis)
        for first in (0, 1):
            pairs = swap_pairs(count, first)
            arrived.append(lax.ppermute(field, axis, pairs) if pairs else None)
    return arrived


def beside(field, halos, odd_row, odd_col, cols):
    tiles = field.shape[0]
    row_a, row_b, col_a, col_b = halos
    zero = jnp.zeros_like(field)
    row_a, row_b, col_a, col_b = [zero if h is None else h for h in (row_a, row_b, col_a, col_b)]
    above = jnp.where(odd_row, row_a, row_b)
    below = jnp.where(odd_row, row_b, row_a)
    west = jnp.where(odd_col, col_a, col_b)
    east = jnp.where(odd_col, col_b, col_a)
    up = jnp.concatenate([above[tiles - cols:], field[: tiles - cols]], axis=0)
    down = jnp.concatenate([field[cols:], below[:cols]], axis=0)
    column = lax.broadcasted_iota(jnp.int32, field.shape, 0) % cols
    rolled = jnp.concatenate([field[tiles - 1:], field[: tiles - 1]], axis=0)
    west_edge = jnp.concatenate([west[cols - 1:], west[: cols - 1]], axis=0)
    left = jnp.where(column == 0, west_edge, rolled)
    rolled = jnp.concatenate([field[1:], field[:1]], axis=0)
    east_edge = jnp.concatenate([east[tiles - cols + 1:], east[: tiles - cols + 1]], axis=0)
    right = jnp.where(column == cols - 1, east_edge, rolled)
    return up, down, left, right


def blocks_times(field, around, own_ref, nb_ref):
    tiles, width = field.shape
    chunk = 32
    lane = lax.broadcasted_iota(jnp.int32, (chunk, width), 1)
    sub = lax.broadcasted_iota(jnp.int32, (chunk, width), 0)
    outs = []
    for t in range(tiles):
        vecs = [f[t:t + 1] for f in around]
        mine = field[t:t + 1]
        spread = jnp.zeros((chunk, width), jnp.float32)
        for g in range(0, width, chunk):
            acc = own_ref[t, g:g + chunk, :] * mine
            for n, vec in enumerate(vecs):
                acc = acc + nb_ref[n, t, g:g + chunk, :] * vec
            total = jnp.sum(acc, axis=1, keepdims=True)
            spread = jnp.where(lane == sub + g, total, spread)
        outs.append(jnp.sum(spread, axis=0, keepdims=True))
    return jnp.concatenate(outs, axis=0)


def kernel(sweep, cols, present, flags, own_ref, nb_ref, weights, *refs):
    n_halo = sum(present)
    halo_refs, refs = refs[:n_halo], refs[n_halo:]
    halo_iter = iter(halo_refs)
    halos = [next(halo_iter)[...] if p else None for p in present]
    odd_row, odd_col = flags[0] == 1, flags[1] == 1
    field_ref, refs = refs[0], refs[1:]
    field = field_ref[...]
    around = beside(field, halos, odd_row, odd_col, cols)
    around = [f * weights[n] for n, f in enumerate(around)]
    product = blocks_times(field, around, own_ref, nb_ref)
    if sweep < 0:
        injected, search_out, residue_out, estimate_out = refs
        residue = injected[...] - product
        search_out[...] = residue
        residue_out[...] = residue
        estimate_out[...] = field + STRIDES[0] * residue
    else:
        capacity, residue_in, estimate_in = refs[:3]
        outs = refs[3:]
        residue = residue_in[...] - STRIDES[sweep] * (product + capacity[...] * field)
        search = residue + MOMENTA[sweep + 1] * field
        estimate = estimate_in[...] + STRIDES[sweep + 1] * search
        if sweep + 2 < ITERS:
            outs[0][...] = search
            outs[1][...] = residue
            outs[2][...] = estimate
        else:
            outs[0][...] = estimate


def shards(own_block, neighbor_block, pattern, capacity, initial, currents, slot_tile):
    tile_rows, tile_cols, width = initial.shape
    tiles = tile_rows * tile_cols
    n_col = lax.axis_size("col")
    slots = currents.shape[3]
    frames = currents.shape[4]
    flags = jnp.stack([lax.axis_index("row") % 2, lax.axis_index("col") % 2]).astype(jnp.int32)

    voltage = initial.reshape(tiles, width)
    halos = exchange(voltage)

    names = jnp.pad(slot_tile.astype(jnp.float32)[..., None, :],
                    ((0, 0), (0, 0), (0, 0), (0, 0), (0, frames - slots)))
    packed = jnp.concatenate([currents, names], axis=3)
    arrived = lax.all_to_all(packed, "col", split_axis=2, concat_axis=1, tiled=True)[0, :, 0]
    targets = arrived[:, slots, :slots]
    chooser = (targets[..., None] == jnp.arange(tiles, dtype=jnp.float32)).astype(jnp.float32)
    injected = jnp.einsum("skt,skf->tf", chooser, arrived[:, :slots], precision=lax.Precision.HIGHEST)
    injected = injected.reshape(tiles, STEPS, width)

    own = own_block.reshape(tiles, width, width)
    nb = neighbor_block.reshape(4, tiles, width, width)
    weights = jnp.broadcast_to(
        jnp.moveaxis(pattern.reshape(tiles, 4), 1, 0).astype(jnp.float32)[..., None], (4, tiles, width)
    )
    cap = capacity.reshape(tiles, width)
    shape = jax.ShapeDtypeStruct((tiles, width), jnp.float32)
    vmem = pl.BlockSpec(memory_space=pltpu.VMEM)
    smem = pl.BlockSpec(memory_space=pltpu.SMEM)

    def call(sweep, halos, *state):
        present = tuple(h is not None for h in halos)
        ins = (flags, own, nb, weights) + tuple(h for h in halos if h is not None) + state
        n_out = 1 if sweep + 2 == ITERS else 3
        out = pl.pallas_call(
            functools.partial(kernel, sweep, tile_cols, present),
            out_shape=(shape,) * n_out,
            in_specs=[smem] + [vmem] * (len(ins) - 1),
            out_specs=(vmem,) * n_out,
            compiler_params=pltpu.CompilerParams(vmem_limit_bytes=8 * 2**20),
            cost_estimate=pl.CostEstimate(flops=2 * 5 * tiles * width * width, bytes_accessed=5 * tiles * width * width * 4,
                                          transcendentals=0),
            name="couple",
        )(*ins)
        return out

    frames_out = []
    for instant in range(STEPS):
        if instant:
            halos = exchange(voltage)
        search, residue, estimate = call(-1, halos, voltage, injected[:, instant])
        for sweep in range(ITERS - 1):
            halos = exchange(search)
            out = call(sweep, halos, search, cap, residue, estimate)
            if sweep + 2 < ITERS:
                search, residue, estimate = out
            else:
                (voltage,) = out
        frames_out.append(voltage)
    return jnp.stack(frames_out).reshape(STEPS, tile_rows, tile_cols, width)


def solution(mesh):
    return jax.shard_map(
        shards,
        mesh=mesh,
        in_specs=(
            P("row", "col", None, None),
            P(None, "row", "col", None, None),
            P("row", "col", None),
            P("row", "col", None),
            P("row", "col", None),
            P("row", "col", None, None, None),
            P("row", "col", None, None),
        ),
        out_specs=P(None, "row", "col", None),
        check_vma=False,
    )
```

```python
import functools

import jax
import jax.numpy as jnp
from jax import lax
from jax.experimental import pallas as pl
from jax.experimental.pallas import tpu as pltpu
from jax.sharding import PartitionSpec as P

STEPS = 4
ITERS = 8

spec_center = 6.4
spec_radius = 5.6


def schedule():
    strides, momenta = [], []
    stride = 1.0 / spec_center
    for sweep in range(ITERS):
        if sweep == 0:
            momentum = 0.0
        else:
            if sweep == 1:
                momentum = 0.5 * (spec_radius * stride) ** 2
            else:
                momentum = (spec_radius * stride / 2.0) ** 2
            stride = 1.0 / (spec_center - momentum / stride)
        strides.append(stride)
        momenta.append(momentum)
    return strides, momenta


STRIDES, MOMENTA = schedule()


def swap_pairs(count, first):
    pairs = []
    for i in range(first, count - 1, 2):
        pairs += [(i, i + 1), (i + 1, i)]
    return pairs


def exchange(field):
    arrived = []
    for axis in ("row", "col"):
        count = lax.axis_size(axis)
        for first in (0, 1):
            pairs = swap_pairs(count, first)
            arrived.append(lax.ppermute(field, axis, pairs) if pairs else None)
    return arrived


def beside(field, halos, odd_row, odd_col, cols):
    tiles = field.shape[0]
    row_a, row_b, col_a, col_b = halos
    zero = jnp.zeros_like(field)
    row_a, row_b, col_a, col_b = [zero if h is None else h for h in (row_a, row_b, col_a, col_b)]
    above = jnp.where(odd_row, row_a, row_b)
    below = jnp.where(odd_row, row_b, row_a)
    west = jnp.where(odd_col, col_a, col_b)
    east = jnp.where(odd_col, col_b, col_a)
    up = jnp.concatenate([above[tiles - cols:], field[: tiles - cols]], axis=0)
    down = jnp.concatenate([field[cols:], below[:cols]], axis=0)
    column = lax.broadcasted_iota(jnp.int32, field.shape, 0) % cols
    rolled = jnp.concatenate([field[tiles - 1:], field[: tiles - 1]], axis=0)
    west_edge = jnp.concatenate([west[cols - 1:], west[: cols - 1]], axis=0)
    left = jnp.where(column == 0, west_edge, rolled)
    rolled = jnp.concatenate([field[1:], field[:1]], axis=0)
    east_edge = jnp.concatenate([east[tiles - cols + 1:], east[: tiles - cols + 1]], axis=0)
    right = jnp.where(column == cols - 1, east_edge, rolled)
    return up, down, left, right


def blocks_times(field, around, own_ref, nb_ref):
    tiles, width = field.shape
    chunk = 32
    lane = lax.broadcasted_iota(jnp.int32, (chunk, width), 1)
    sub = lax.broadcasted_iota(jnp.int32, (chunk, width), 0)
    outs = []
    for t in range(tiles):
        vecs = [f[t:t + 1] for f in around]
        mine = field[t:t + 1]
        spread = jnp.zeros((chunk, width), jnp.float32)
        for g in range(0, width, chunk):
            acc = own_ref[t, g:g + chunk, :] * mine
            for n, vec in enumerate(vecs):
                acc = acc + nb_ref[n, t, g:g + chunk, :] * vec
            total = jnp.sum(acc, axis=1, keepdims=True)
            spread = jnp.where(lane == sub + g, total, spread)
        outs.append(jnp.sum(spread, axis=0, keepdims=True))
    return jnp.concatenate(outs, axis=0)


def kernel(sweep, cols, present, flags, own_ref, nb_ref, weights, *refs):
    n_halo = sum(present)
    halo_refs, refs = refs[:n_halo], refs[n_halo:]
    halo_iter = iter(halo_refs)
    halos = [next(halo_iter)[...] if p else None for p in present]
    odd_row, odd_col = flags[0] == 1, flags[1] == 1
    field_ref, refs = refs[0], refs[1:]
    field = field_ref[...]
    around = beside(field, halos, odd_row, odd_col, cols)
    around = [f * weights[n] for n, f in enumerate(around)]
    product = blocks_times(field, around, own_ref, nb_ref)
    if sweep < 0:
        injected, search_out, residue_out, estimate_out = refs
        residue = injected[...] - product
        search_out[...] = residue
        residue_out[...] = residue
        estimate_out[...] = field + STRIDES[0] * residue
    else:
        capacity, residue_in, estimate_in = refs[:3]
        outs = refs[3:]
        residue = residue_in[...] - STRIDES[sweep] * (product + capacity[...] * field)
        search = residue + MOMENTA[sweep + 1] * field
        estimate = estimate_in[...] + STRIDES[sweep + 1] * search
        if sweep + 2 < ITERS:
            outs[0][...] = search
            outs[1][...] = residue
            outs[2][...] = estimate
        else:
            outs[0][...] = estimate


def collect(currents, slot_tile, tiles, width):
    slots, frames = currents.shape[3:]
    names = jnp.pad(slot_tile.astype(jnp.float32)[..., None, :],
                    ((0, 0), (0, 0), (0, 0), (0, 0), (0, frames - slots)))
    packed = jnp.concatenate([currents, names], axis=3)
    arrived = lax.all_to_all(packed, "col", split_axis=2, concat_axis=1, tiled=True)[0, :, 0]
    targets = arrived[:, slots, :slots]
    chooser = (targets[..., None] == jnp.arange(tiles, dtype=jnp.float32)).astype(jnp.float32)
    injected = jnp.einsum("skt,skf->tf", chooser, arrived[:, :slots], precision=lax.Precision.HIGHEST)
    return injected.reshape(tiles, STEPS, width)


def shards_general(own_block, neighbor_block, pattern, capacity, initial, currents, slot_tile):
    tile_rows, tile_cols, width = initial.shape
    tiles = tile_rows * tile_cols
    flags = jnp.stack([lax.axis_index("row") % 2, lax.axis_index("col") % 2]).astype(jnp.int32)

    voltage = initial.reshape(tiles, width)
    halos = exchange(voltage)

    injected = collect(currents, slot_tile, tiles, width)

    own = own_block.reshape(tiles, width, width)
    nb = neighbor_block.reshape(4, tiles, width, width)
    weights = jnp.broadcast_to(
        jnp.moveaxis(pattern.reshape(tiles, 4), 1, 0).astype(jnp.float32)[..., None], (4, tiles, width)
    )
    cap = capacity.reshape(tiles, width)
    shape = jax.ShapeDtypeStruct((tiles, width), jnp.float32)
    vmem = pl.BlockSpec(memory_space=pltpu.VMEM)
    smem = pl.BlockSpec(memory_space=pltpu.SMEM)

    def call(sweep, halos, *state):
        present = tuple(h is not None for h in halos)
        ins = (flags, own, nb, weights) + tuple(h for h in halos if h is not None) + state
        n_out = 1 if sweep + 2 == ITERS else 3
        out = pl.pallas_call(
            functools.partial(kernel, sweep, tile_cols, present),
            out_shape=(shape,) * n_out,
            in_specs=[smem] + [vmem] * (len(ins) - 1),
            out_specs=(vmem,) * n_out,
            compiler_params=pltpu.CompilerParams(vmem_limit_bytes=8 * 2**20),
            cost_estimate=pl.CostEstimate(flops=2 * 5 * tiles * width * width, bytes_accessed=5 * tiles * width * width * 4,
                                          transcendentals=0),
            name="couple",
        )(*ins)
        return out

    frames_out = []
    for instant in range(STEPS):
        if instant:
            halos = exchange(voltage)
        search, residue, estimate = call(-1, halos, voltage, injected[:, instant])
        for sweep in range(ITERS - 1):
            halos = exchange(search)
            out = call(sweep, halos, search, cap, residue, estimate)
            if sweep + 2 < ITERS:
                search, residue, estimate = out
            else:
                (voltage,) = out
        frames_out.append(voltage)
    return jnp.stack(frames_out).reshape(STEPS, tile_rows, tile_cols, width)


ROWS, HALF = 2, 2
OWN, SIDE_A, SIDE_B, INNER, OUTER, FACING = 0, 4, 8, 12, 16, 18


def ordered(x, row_dim, flip_row, flip_col, col_dim):
    x = jnp.where(flip_row, jnp.flip(x, row_dim), x)
    return jnp.where(flip_col, jnp.flip(x, col_dim), x)


def tile_terms(keep, recv, j, b):
    half, k = (keep, j) if j < ROWS else (recv, j - ROWS)
    terms = [(half, OWN + k * HALF + b, (j, b))]
    if j < ROWS:
        terms.append((half, INNER + k * HALF + b, (j + 1, b)))
        if k == 1:
            terms.append((half, OUTER + b, (j - 1, b)))
    else:
        terms.append((half, INNER + k * HALF + b, (j - 1, b)))
        if k == 0:
            terms.append((half, OUTER + b, (j + 1, b)))
    terms.append((half, (SIDE_A if b == 0 else SIDE_B) + k * HALF + b, (j, 1 - b)))
    return terms


def halo_term(keep, recv, j, b):
    half, k = (keep, j) if j < ROWS else (recv, j - ROWS)
    return half, (SIDE_B if b == 0 else SIDE_A) + k * HALF + b


def facing_term(keep, recv, beyond, j, b):
    if b == 0:
        return beyond, j
    return (keep, FACING + j) if j < ROWS else (recv, FACING + j - ROWS)


def matvec(terms, chunk=32):
    width = terms[0][2].shape[1]
    lane = lax.broadcasted_iota(jnp.int32, (chunk, width), 1)
    sub = lax.broadcasted_iota(jnp.int32, (chunk, width), 0)
    spread = jnp.zeros((chunk, width), jnp.float32)
    for g in range(0, width, chunk):
        acc = None
        for ref, index, vec in terms:
            part = ref[index, g:g + chunk, :] * vec
            acc = part if acc is None else acc + part
        total = jnp.sum(acc, axis=1, keepdims=True)
        spread = jnp.where(lane == sub + g, total, spread)
    return jnp.sum(spread, axis=0, keepdims=True)


TILES = [(j, b) for j in range(2 * ROWS) for b in range(HALF)]


def row_of(x, j, b):
    i = j * HALF + b
    return x[i:i + 1]


def inner_product(f, keep, recv):
    return jnp.concatenate(
        [matvec([(r, i, row_of(f, *at)) for r, i, at in tile_terms(keep, recv, j, b)]) for j, b in TILES], axis=0
    )


def messages(f, g):
    def column(x, b, rows):
        return [row_of(x, j, b) for j in rows]

    rows = range(2 * ROWS)
    to_a = jnp.concatenate(column(f, 1, rows[::-1]) + column(g, 1, rows[::-1]), axis=0)
    to_b = jnp.concatenate(column(f, 0, rows) + column(g, 0, rows), axis=0)
    return to_a, to_b


def ahead(first, sweep, f, q, residue, capacity, injected):
    if first:
        return injected - q
    return residue - STRIDES[sweep] * (q + capacity * f) + MOMENTA[sweep + 1] * f


def start_kernel(keep, recv, field, injected, msg_a, msg_b, q_out):
    f = field[...]
    q = inner_product(f, keep, recv)
    q_out[...] = q
    msg_a[...], msg_b[...] = messages(f, ahead(True, 0, f, q, None, None, injected[...]))


def pair_kernel(pair, last, keep, recv, beyond, capacity_ref, injected_ref, got_a, got_b, f_ref, q_ref, *refs):
    first = pair == 0
    capacity = capacity_ref[...]
    f, q = f_ref[...], q_ref[...]
    if not first:
        residue, estimate, refs = refs[0][...], refs[1][...], refs[2:]
    got = (got_b, got_a)
    sweep = 2 * pair - 1
    n = 2 * ROWS

    extra = []
    for j, b in TILES:
        r, i = halo_term(keep, recv, j, b)
        extra.append(matvec([(r, i, got[b][j:j + 1, :])]))
    product = q + jnp.concatenate(extra, axis=0)
    if first:
        residue = injected_ref[...] - product
        f2 = residue
        estimate = f + STRIDES[0] * f2
        scale = 1.0
    else:
        residue = residue - STRIDES[sweep] * (product + capacity * f)
        f2 = residue + MOMENTA[sweep + 1] * f
        estimate = estimate + STRIDES[sweep + 1] * f2
        scale = STRIDES[sweep]

    beside2 = {}
    for j, b in TILES:
        r, i = facing_term(keep, recv, beyond, j, b)
        beside2[j, b] = got[b][n + j:n + j + 1, :] - scale * matvec([(r, i, row_of(f, j, b))])

    outs = []
    for j, b in TILES:
        terms = [(r, i, row_of(f2, *at)) for r, i, at in tile_terms(keep, recv, j, b)]
        r, i = halo_term(keep, recv, j, b)
        outs.append(matvec(terms + [(r, i, beside2[j, b])]))
    sweep = 2 * pair
    residue = residue - STRIDES[sweep] * (jnp.concatenate(outs, axis=0) + capacity * f2)
    f3 = residue + MOMENTA[sweep + 1] * f2
    estimate = estimate + STRIDES[sweep + 1] * f3
    closing = sweep + 2 == ITERS
    if closing:
        f3 = estimate
    f_out, refs = refs[0], refs[1:]
    f_out[...] = f3
    if last:
        return
    q = inner_product(f3, keep, recv)
    q_out, msg_a, msg_b = refs[:3]
    q_out[...] = q
    msg_a[...], msg_b[...] = messages(f3, ahead(closing, sweep + 1, f3, q, residue, capacity, injected_ref[...]))
    if not closing:
        refs[3][...] = residue
        refs[4][...] = estimate


def shards_chain(own_block, neighbor_block, pattern, capacity, initial, currents, slot_tile):
    tile_rows, tile_cols, width = initial.shape
    n_col = lax.axis_size("col")
    row, col = lax.axis_index("row"), lax.axis_index("col")
    flip_row = row == 1
    flip_col = (row + col) % 2 == 1

    def trade_row(x):
        return lax.ppermute(x, "row", [(0, 1), (1, 0)])

    b_pairs = []
    for c in range(n_col - 1):
        r = (c + 1) % 2
        b_pairs += [(r * n_col + c, r * n_col + c + 1), (r * n_col + c + 1, r * n_col + c)]

    def trade_next(x):
        return lax.ppermute(x, ("row", "col"), b_pairs)

    def in_order(x):
        return ordered(x, 0, flip_row, flip_col, 1)

    def split(x):
        return x[:, :HALF], jnp.flip(x, (0, 1))[:, :HALF]

    flat = (ROWS * HALF, width, width)
    own = in_order(own_block)
    weighted = neighbor_block * jnp.moveaxis(pattern, 2, 0).astype(jnp.float32)[..., None, None]
    up, down, left, right = [weighted[d] for d in range(4)]
    up, down = jnp.where(flip_row, down, up), jnp.where(flip_row, up, down)
    side_b, side_a = jnp.where(flip_col, right, left), jnp.where(flip_col, left, right)
    up, down, side_b, side_a = [in_order(x) for x in (up, down, side_b, side_a)]
    own_k, own_s = split(own)
    up_k, down_s = split(up)
    down_k, up_s = split(down)
    b_k, a_s = split(side_b)
    a_k, b_s = split(side_a)
    keep = jnp.concatenate(
        [own_k.reshape(flat), a_k.reshape(flat), b_k.reshape(flat), down_k.reshape(flat), up_k[1], side_b[:, HALF]]
    )
    send = jnp.concatenate(
        [own_s.reshape(flat), a_s.reshape(flat), b_s.reshape(flat), up_s.reshape(flat), down_s[0],
         jnp.flip(side_a[:, HALF - 1], 0)]
    )
    recv = trade_row(send)

    injected = collect(currents, slot_tile, tile_rows * tile_cols, width)
    small = jnp.concatenate(
        [injected.reshape(tile_rows, tile_cols, STEPS * width), capacity, initial], axis=2
    )
    small_k, small_s = split(in_order(small))
    small = jnp.concatenate([small_k, trade_row(small_s)], axis=0).reshape(2 * ROWS * HALF, STEPS + 2, width)
    injected, cap, field = small[:, :STEPS], small[:, STEPS], small[:, STEPS + 1]
    beyond = trade_next(jnp.concatenate([keep[SIDE_B:SIDE_B + ROWS * HALF:HALF], recv[SIDE_B:SIDE_B + ROWS * HALF:HALF]]))

    tiles = 2 * ROWS * HALF
    shape = jax.ShapeDtypeStruct((tiles, width), jnp.float32)
    vmem = pl.BlockSpec(memory_space=pltpu.VMEM)

    def call(body, n_out, blocks, *ins):
        return pl.pallas_call(
            body,
            out_shape=(shape,) * n_out,
            in_specs=[vmem] * len(ins),
            out_specs=(vmem,) * n_out,
            compiler_params=pltpu.CompilerParams(vmem_limit_bytes=8 * 2**20),
            cost_estimate=pl.CostEstimate(flops=2 * blocks * width * width, bytes_accessed=blocks * width * width * 4,
                                          transcendentals=0),
            name="pair",
        )(*ins)

    msg_a, msg_b, q = call(start_kernel, 3, 28, keep, recv, field, injected[:, 0])
    frames = []
    for instant in range(STEPS):
        state = ()
        for pair in range(ITERS // 2):
            closing = pair + 1 == ITERS // 2
            last = closing and instant + 1 == STEPS
            got_b, got_a = trade_next(msg_b), trade_row(msg_a)
            feed = injected[:, min(instant + closing, STEPS - 1)]
            out = call(functools.partial(pair_kernel, pair, last), 1 if last else 4 if closing else 6, 80,
                       keep, recv, beyond, cap, feed, got_a, got_b, field, q, *state)
            field = out[0]
            if not last:
                q, msg_a, msg_b = out[1:4]
                state = tuple(out[4:])
        frames.append(field)

    done = jnp.stack(frames).reshape(STEPS, 2 * ROWS, HALF, width)
    got = trade_row(done[:, ROWS:])
    done = jnp.concatenate([done[:, :ROWS], jnp.flip(got, (1, 2))], axis=2)
    return ordered(done, 1, flip_row, flip_col, 2)


def solution(mesh):
    rows, cols = mesh.shape["row"], mesh.shape["col"]
    return jax.shard_map(
        shards_chain if rows == 2 and cols % 2 == 0 else shards_general,
        mesh=mesh,
        in_specs=(
            P("row", "col", None, None),
            P(None, "row", "col", None, None),
            P("row", "col", None),
            P("row", "col", None),
            P("row", "col", None),
            P("row", "col", None, None, None),
            P("row", "col", None, None),
        ),
        out_specs=P(None, "row", "col", None),
        check_vma=False,
    )
```

```python
import functools

import jax
import jax.numpy as jnp
from jax import lax
from jax.experimental import pallas as pl
from jax.experimental.pallas import tpu as pltpu
from jax.sharding import PartitionSpec as P

STEPS = 4
ITERS = 8

spec_center = 6.4
spec_radius = 5.6


def schedule():
    strides, momenta = [], []
    stride = 1.0 / spec_center
    for sweep in range(ITERS):
        if sweep == 0:
            momentum = 0.0
        else:
            if sweep == 1:
                momentum = 0.5 * (spec_radius * stride) ** 2
            else:
                momentum = (spec_radius * stride / 2.0) ** 2
            stride = 1.0 / (spec_center - momentum / stride)
        strides.append(stride)
        momenta.append(momentum)
    return strides, momenta


STRIDES, MOMENTA = schedule()


def swap_pairs(count, first):
    pairs = []
    for i in range(first, count - 1, 2):
        pairs += [(i, i + 1), (i + 1, i)]
    return pairs


def exchange(field):
    arrived = []
    for axis in ("row", "col"):
        count = lax.axis_size(axis)
        for first in (0, 1):
            pairs = swap_pairs(count, first)
            arrived.append(lax.ppermute(field, axis, pairs) if pairs else None)
    return arrived


def beside(field, halos, odd_row, odd_col, cols):
    tiles = field.shape[0]
    row_a, row_b, col_a, col_b = halos
    zero = jnp.zeros_like(field)
    row_a, row_b, col_a, col_b = [zero if h is None else h for h in (row_a, row_b, col_a, col_b)]
    above = jnp.where(odd_row, row_a, row_b)
    below = jnp.where(odd_row, row_b, row_a)
    west = jnp.where(odd_col, col_a, col_b)
    east = jnp.where(odd_col, col_b, col_a)
    up = jnp.concatenate([above[tiles - cols:], field[: tiles - cols]], axis=0)
    down = jnp.concatenate([field[cols:], below[:cols]], axis=0)
    column = lax.broadcasted_iota(jnp.int32, field.shape, 0) % cols
    rolled = jnp.concatenate([field[tiles - 1:], field[: tiles - 1]], axis=0)
    west_edge = jnp.concatenate([west[cols - 1:], west[: cols - 1]], axis=0)
    left = jnp.where(column == 0, west_edge, rolled)
    rolled = jnp.concatenate([field[1:], field[:1]], axis=0)
    east_edge = jnp.concatenate([east[tiles - cols + 1:], east[: tiles - cols + 1]], axis=0)
    right = jnp.where(column == cols - 1, east_edge, rolled)
    return up, down, left, right


def blocks_times(field, around, own_ref, nb_ref):
    tiles, width = field.shape
    chunk = 32
    lane = lax.broadcasted_iota(jnp.int32, (chunk, width), 1)
    sub = lax.broadcasted_iota(jnp.int32, (chunk, width), 0)
    outs = []
    for t in range(tiles):
        vecs = [f[t:t + 1] for f in around]
        mine = field[t:t + 1]
        spread = jnp.zeros((chunk, width), jnp.float32)
        for g in range(0, width, chunk):
            acc = own_ref[t, g:g + chunk, :] * mine
            for n, vec in enumerate(vecs):
                acc = acc + nb_ref[n, t, g:g + chunk, :] * vec
            total = jnp.sum(acc, axis=1, keepdims=True)
            spread = jnp.where(lane == sub + g, total, spread)
        outs.append(jnp.sum(spread, axis=0, keepdims=True))
    return jnp.concatenate(outs, axis=0)


def kernel(sweep, cols, present, flags, own_ref, nb_ref, weights, *refs):
    n_halo = sum(present)
    halo_refs, refs = refs[:n_halo], refs[n_halo:]
    halo_iter = iter(halo_refs)
    halos = [next(halo_iter)[...] if p else None for p in present]
    odd_row, odd_col = flags[0] == 1, flags[1] == 1
    field_ref, refs = refs[0], refs[1:]
    field = field_ref[...]
    around = beside(field, halos, odd_row, odd_col, cols)
    around = [f * weights[n] for n, f in enumerate(around)]
    product = blocks_times(field, around, own_ref, nb_ref)
    if sweep < 0:
        injected, search_out, residue_out, estimate_out = refs
        residue = injected[...] - product
        search_out[...] = residue
        residue_out[...] = residue
        estimate_out[...] = field + STRIDES[0] * residue
    else:
        capacity, residue_in, estimate_in = refs[:3]
        outs = refs[3:]
        residue = residue_in[...] - STRIDES[sweep] * (product + capacity[...] * field)
        search = residue + MOMENTA[sweep + 1] * field
        estimate = estimate_in[...] + STRIDES[sweep + 1] * search
        if sweep + 2 < ITERS:
            outs[0][...] = search
            outs[1][...] = residue
            outs[2][...] = estimate
        else:
            outs[0][...] = estimate


def collect(currents, slot_tile, tiles, width):
    slots, frames = currents.shape[3:]
    names = jnp.pad(slot_tile.astype(jnp.float32)[..., None, :],
                    ((0, 0), (0, 0), (0, 0), (0, 0), (0, frames - slots)))
    packed = jnp.concatenate([currents, names], axis=3)
    arrived = lax.all_to_all(packed, "col", split_axis=2, concat_axis=1, tiled=True)[0, :, 0]
    targets = arrived[:, slots, :slots]
    chooser = (targets[..., None] == jnp.arange(tiles, dtype=jnp.float32)).astype(jnp.float32)
    injected = jnp.einsum("skt,skf->tf", chooser, arrived[:, :slots], precision=lax.Precision.HIGHEST)
    return injected.reshape(tiles, STEPS, width)


def shards_general(own_block, neighbor_block, pattern, capacity, initial, currents, slot_tile):
    tile_rows, tile_cols, width = initial.shape
    tiles = tile_rows * tile_cols
    flags = jnp.stack([lax.axis_index("row") % 2, lax.axis_index("col") % 2]).astype(jnp.int32)

    voltage = initial.reshape(tiles, width)
    halos = exchange(voltage)

    injected = collect(currents, slot_tile, tiles, width)

    own = own_block.reshape(tiles, width, width)
    nb = neighbor_block.reshape(4, tiles, width, width)
    weights = jnp.broadcast_to(
        jnp.moveaxis(pattern.reshape(tiles, 4), 1, 0).astype(jnp.float32)[..., None], (4, tiles, width)
    )
    cap = capacity.reshape(tiles, width)
    shape = jax.ShapeDtypeStruct((tiles, width), jnp.float32)
    vmem = pl.BlockSpec(memory_space=pltpu.VMEM)
    smem = pl.BlockSpec(memory_space=pltpu.SMEM)

    def call(sweep, halos, *state):
        present = tuple(h is not None for h in halos)
        ins = (flags, own, nb, weights) + tuple(h for h in halos if h is not None) + state
        n_out = 1 if sweep + 2 == ITERS else 3
        out = pl.pallas_call(
            functools.partial(kernel, sweep, tile_cols, present),
            out_shape=(shape,) * n_out,
            in_specs=[smem] + [vmem] * (len(ins) - 1),
            out_specs=(vmem,) * n_out,
            compiler_params=pltpu.CompilerParams(vmem_limit_bytes=8 * 2**20),
            cost_estimate=pl.CostEstimate(flops=2 * 5 * tiles * width * width, bytes_accessed=5 * tiles * width * width * 4,
                                          transcendentals=0),
            name="couple",
        )(*ins)
        return out

    frames_out = []
    for instant in range(STEPS):
        if instant:
            halos = exchange(voltage)
        search, residue, estimate = call(-1, halos, voltage, injected[:, instant])
        for sweep in range(ITERS - 1):
            halos = exchange(search)
            out = call(sweep, halos, search, cap, residue, estimate)
            if sweep + 2 < ITERS:
                search, residue, estimate = out
            else:
                (voltage,) = out
        frames_out.append(voltage)
    return jnp.stack(frames_out).reshape(STEPS, tile_rows, tile_cols, width)


ROWS, HALF = 2, 2
N = 2 * ROWS
OWN, SIDE_A, SIDE_B, OUT_IN, IN_OUT, IN_IN, FACING, PACKED = 0, 4, 8, 12, 14, 16, 18, 20
TILES = [(j, b) for j in range(N) for b in range(HALF)]
ORIGIN = [(0, 0), (0, 1), (1, 1), (1, 0)]


def unit_device(unit, n_col):
    group, place = divmod(unit // 2, 4)
    x, row = ((0, 0), (1, 0), (1, 1), (0, 1))[place]
    return (row + group) % 2 * n_col + 4 * group + 2 * x + unit % 2


def deal_pairs(n_col, which):
    rounds = []
    for i in (0, 1):
        pairs = []
        for row in (0, 1):
            for col in range(n_col):
                k = row ^ i
                unit = 2 * col + k if which == 0 else 2 * col + (2 if k == 0 else -1)
                if 0 <= unit < 2 * n_col:
                    pairs.append((row * n_col + col, unit_device(unit, n_col)))
        rounds.append(pairs)
    return rounds


def pack_kernel(row_ref, pattern_ref, own_ref, nb_ref, send_0, send_1, facing_0, facing_1):
    y = row_ref[0]
    rows = (y, 1 - y)
    inward, outward = 1 - y, y
    cols = own_ref.shape[1]

    def coupling(direction, row, col):
        weight = pattern_ref[(row * cols + col) * 4 + direction].astype(jnp.float32)
        return nb_ref[direction, row, col] * weight

    for i, (send, facing) in enumerate(((send_0, facing_0), (send_1, facing_1))):
        k = (y + i) % 2
        at = [b + k * (cols - 1 - 2 * b) for b in range(HALF)]
        side_a, side_b = 3 - k, 2 + k
        for h in range(ROWS):
            for b in range(HALF):
                send[OWN + h * HALF + b] = own_ref[rows[h], at[b]]
                send[SIDE_A + h * HALF + b] = coupling(side_a, rows[h], at[b])
                send[SIDE_B + h * HALF + b] = coupling(side_b, rows[h], at[b])
            send[FACING + h] = coupling(2 + k, rows[h], HALF - k)
            facing[h] = coupling(3 - k, rows[h], (cols - 1) * (1 - k))
        for b in range(HALF):
            send[OUT_IN + b] = coupling(inward, rows[0], at[b])
            send[IN_OUT + b] = coupling(outward, rows[1], at[b])
            send[IN_IN + b] = coupling(inward, rows[1], at[b])


def tile_terms(halves, j, b):
    i, h = ORIGIN[j]
    half = halves[i]
    terms = [(half, OWN + h * HALF + b, (j, b))]
    if h == 0:
        terms.append((half, OUT_IN + b, ((1, 2)[i], b)))
    else:
        terms.append((half, IN_OUT + b, ((0, 3)[i], b)))
        terms.append((half, IN_IN + b, ((2, 1)[i], b)))
    terms.append((half, (SIDE_A if b == 0 else SIDE_B) + h * HALF + b, (j, 1 - b)))
    return terms


def halo_term(halves, j, b):
    i, h = ORIGIN[j]
    return halves[i], (SIDE_B if b == 0 else SIDE_A) + h * HALF + b


def facing_term(halves, beyond, j, b):
    i, h = ORIGIN[j]
    return (beyond[i], h) if b == 0 else (halves[i], FACING + h)


def matvec(terms, chunk=32):
    width = terms[0][2].shape[1]
    lane = lax.broadcasted_iota(jnp.int32, (chunk, width), 1)
    sub = lax.broadcasted_iota(jnp.int32, (chunk, width), 0)
    spread = jnp.zeros((chunk, width), jnp.float32)
    for g in range(0, width, chunk):
        acc = None
        for ref, index, vec in terms:
            part = ref[index, g:g + chunk, :] * vec
            acc = part if acc is None else acc + part
        total = jnp.sum(acc, axis=1, keepdims=True)
        spread = jnp.where(lane == sub + g, total, spread)
    return jnp.sum(spread, axis=0, keepdims=True)


def row_of(x, j, b):
    i = j * HALF + b
    return x[i:i + 1]


def inner_product(f, halves):
    return jnp.concatenate(
        [matvec([(r, i, row_of(f, *at)) for r, i, at in tile_terms(halves, j, b)]) for j, b in TILES], axis=0
    )


def messages(f, g):
    return [
        jnp.concatenate([row_of(x, j, b) for x in (f, g) for j in reversed(range(N))], axis=0) for b in (1, 0)
    ]


def ahead(first, sweep, f, q, residue, capacity, injected):
    if first:
        return injected - q
    return residue - STRIDES[sweep] * (q + capacity * f) + MOMENTA[sweep + 1] * f


def start_kernel(half_0, half_1, field, injected, msg_a, msg_b, q_out):
    f = field[...]
    q = inner_product(f, (half_0, half_1))
    q_out[...] = q
    msg_a[...], msg_b[...] = messages(f, ahead(True, 0, f, q, None, None, injected[...]))


def pair_kernel(pair, last, half_0, half_1, beyond_0, beyond_1, capacity_ref, injected_ref, got_a, got_b, f_ref, q_ref,
                *refs):
    halves, beyond = (half_0, half_1), (beyond_0, beyond_1)
    first = pair == 0
    capacity = capacity_ref[...]
    f, q = f_ref[...], q_ref[...]
    if not first:
        residue, estimate, refs = refs[0][...], refs[1][...], refs[2:]
    got = (got_b, got_a)
    sweep = 2 * pair - 1

    extra = []
    for j, b in TILES:
        r, i = halo_term(halves, j, b)
        extra.append(matvec([(r, i, got[b][j:j + 1, :])]))
    product = q + jnp.concatenate(extra, axis=0)
    if first:
        residue = injected_ref[...] - product
        f2 = residue
        estimate = f + STRIDES[0] * f2
        scale = 1.0
    else:
        residue = residue - STRIDES[sweep] * (product + capacity * f)
        f2 = residue + MOMENTA[sweep + 1] * f
        estimate = estimate + STRIDES[sweep + 1] * f2
        scale = STRIDES[sweep]

    beside2 = {}
    for j, b in TILES:
        r, i = facing_term(halves, beyond, j, b)
        beside2[j, b] = got[b][N + j:N + j + 1, :] - scale * matvec([(r, i, row_of(f, j, b))])

    outs = []
    for j, b in TILES:
        terms = [(r, i, row_of(f2, *at)) for r, i, at in tile_terms(halves, j, b)]
        r, i = halo_term(halves, j, b)
        outs.append(matvec(terms + [(r, i, beside2[j, b])]))
    sweep = 2 * pair
    residue = residue - STRIDES[sweep] * (jnp.concatenate(outs, axis=0) + capacity * f2)
    f3 = residue + MOMENTA[sweep + 1] * f2
    estimate = estimate + STRIDES[sweep + 1] * f3
    closing = sweep + 2 == ITERS
    if closing:
        f3 = estimate
    f_out, refs = refs[0], refs[1:]
    f_out[...] = f3
    if last:
        return
    q = inner_product(f3, halves)
    q_out, msg_a, msg_b = refs[:3]
    q_out[...] = q
    msg_a[...], msg_b[...] = messages(f3, ahead(closing, sweep + 1, f3, q, residue, capacity, injected_ref[...]))
    if not closing:
        refs[3][...] = residue
        refs[4][...] = estimate


def shards_chain(own_block, neighbor_block, pattern, capacity, initial, currents, slot_tile):
    tile_rows, tile_cols, width = initial.shape
    n_col = lax.axis_size("col")
    row = lax.axis_index("row")
    both = ("row", "col")
    deal = deal_pairs(n_col, 0)
    deal_b = deal_pairs(n_col, 1)
    a_pairs = [(c, c ^ 1) for c in range(n_col)]
    b_pairs = []
    for unit in range(1, 2 * n_col - 1, 2):
        one, two = unit_device(unit, n_col), unit_device(unit + 1, n_col)
        b_pairs += [(one, two), (two, one)]

    vmem = pl.BlockSpec(memory_space=pltpu.VMEM)
    smem = pl.BlockSpec(memory_space=pltpu.SMEM)
    limit = pltpu.CompilerParams(vmem_limit_bytes=16 * 2**20)
    packed = jax.ShapeDtypeStruct((PACKED, width, width), jnp.float32)
    facing = jax.ShapeDtypeStruct((ROWS, width, width), jnp.float32)
    send_0, send_1, facing_0, facing_1 = pl.pallas_call(
        pack_kernel,
        out_shape=(packed, packed, facing, facing),
        in_specs=[smem, smem, vmem, vmem],
        out_specs=(vmem,) * 4,
        compiler_params=limit,
        name="pack",
    )(row.astype(jnp.int32).reshape(1), pattern.reshape(-1), own_block, neighbor_block)
    half_0 = lax.ppermute(send_0, both, deal[0])
    half_1 = lax.ppermute(send_1, both, deal[1])
    beyond_0 = lax.ppermute(facing_0, both, deal_b[0])
    beyond_1 = lax.ppermute(facing_1, both, deal_b[1])

    injected = collect(currents, slot_tile, tile_rows * tile_cols, width)
    small = jnp.concatenate(
        [injected.reshape(tile_rows, tile_cols, STEPS * width), capacity, initial], axis=2
    )
    small = jnp.where(row == 1, jnp.flip(small, 0), small)
    unit_0, unit_1 = small[:, :HALF], jnp.flip(small, 1)[:, :HALF]
    got_0 = lax.ppermute(jnp.where(row == 1, unit_1, unit_0), both, deal[0])
    got_1 = lax.ppermute(jnp.where(row == 1, unit_0, unit_1), both, deal[1])
    small = jnp.concatenate([got_0, jnp.flip(got_1, 0)], axis=0).reshape(N * HALF, STEPS + 2, width)
    injected, cap, field = small[:, :STEPS], small[:, STEPS], small[:, STEPS + 1]

    shape = jax.ShapeDtypeStruct((N * HALF, width), jnp.float32)

    def call(body, n_out, blocks, *ins):
        return pl.pallas_call(
            body,
            out_shape=(shape,) * n_out,
            in_specs=[vmem] * len(ins),
            out_specs=(vmem,) * n_out,
            compiler_params=limit,
            cost_estimate=pl.CostEstimate(flops=2 * blocks * width * width, bytes_accessed=blocks * width * width * 4,
                                          transcendentals=0),
            name="pair",
        )(*ins)

    msg_a, msg_b, q = call(start_kernel, 3, 28, half_0, half_1, field, injected[:, 0])
    frames = []
    for instant in range(STEPS):
        state = ()
        for pair in range(ITERS // 2):
            closing = pair + 1 == ITERS // 2
            last = closing and instant + 1 == STEPS
            got_b = lax.ppermute(msg_b, both, b_pairs)
            got_a = lax.ppermute(msg_a, "col", a_pairs)
            feed = injected[:, min(instant + closing, STEPS - 1)]
            out = call(functools.partial(pair_kernel, pair, last), 1 if last else 4 if closing else 6, 80,
                       half_0, half_1, beyond_0, beyond_1, cap, feed, got_a, got_b, field, q, *state)
            field = out[0]
            if not last:
                q, msg_a, msg_b = out[1:4]
                state = tuple(out[4:])
        frames.append(field)

    done = jnp.stack(frames).reshape(STEPS, N, HALF, width)
    got_0 = lax.ppermute(done[:, :ROWS], both, [(b, a) for a, b in deal[0]])
    got_1 = lax.ppermute(jnp.flip(done[:, ROWS:], 1), both, [(b, a) for a, b in deal[1]])
    unit_0, unit_1 = jnp.where(row == 1, got_1, got_0), jnp.where(row == 1, got_0, got_1)
    done = jnp.concatenate([unit_0, jnp.flip(unit_1, 2)], axis=2)
    return jnp.where(row == 1, jnp.flip(done, 1), done)


def solution(mesh):
    rows, cols = mesh.shape["row"], mesh.shape["col"]
    return jax.shard_map(
        shards_chain if rows == 2 and cols % 4 == 0 else shards_general,
        mesh=mesh,
        in_specs=(
            P("row", "col", None, None),
            P(None, "row", "col", None, None),
            P("row", "col", None),
            P("row", "col", None),
            P("row", "col", None),
            P("row", "col", None, None, None),
            P("row", "col", None, None),
        ),
        out_specs=P(None, "row", "col", None),
        check_vma=False,
    )
```

```python
import functools

import jax
import jax.numpy as jnp
from jax import lax
from jax.experimental import pallas as pl
from jax.experimental.pallas import tpu as pltpu
from jax.sharding import PartitionSpec as P

STEPS = 4
ITERS = 8

spec_center = 6.4
spec_radius = 5.6


def schedule():
    strides, momenta = [], []
    stride = 1.0 / spec_center
    for sweep in range(ITERS):
        if sweep == 0:
            momentum = 0.0
        else:
            if sweep == 1:
                momentum = 0.5 * (spec_radius * stride) ** 2
            else:
                momentum = (spec_radius * stride / 2.0) ** 2
            stride = 1.0 / (spec_center - momentum / stride)
        strides.append(stride)
        momenta.append(momentum)
    return strides, momenta


STRIDES, MOMENTA = schedule()


def swap_pairs(count, first):
    pairs = []
    for i in range(first, count - 1, 2):
        pairs += [(i, i + 1), (i + 1, i)]
    return pairs


def exchange(field):
    arrived = []
    for axis in ("row", "col"):
        count = lax.axis_size(axis)
        for first in (0, 1):
            pairs = swap_pairs(count, first)
            arrived.append(lax.ppermute(field, axis, pairs) if pairs else None)
    return arrived


def beside(field, halos, odd_row, odd_col, cols):
    tiles = field.shape[0]
    row_a, row_b, col_a, col_b = halos
    zero = jnp.zeros_like(field)
    row_a, row_b, col_a, col_b = [zero if h is None else h for h in (row_a, row_b, col_a, col_b)]
    above = jnp.where(odd_row, row_a, row_b)
    below = jnp.where(odd_row, row_b, row_a)
    west = jnp.where(odd_col, col_a, col_b)
    east = jnp.where(odd_col, col_b, col_a)
    up = jnp.concatenate([above[tiles - cols:], field[: tiles - cols]], axis=0)
    down = jnp.concatenate([field[cols:], below[:cols]], axis=0)
    column = lax.broadcasted_iota(jnp.int32, field.shape, 0) % cols
    rolled = jnp.concatenate([field[tiles - 1:], field[: tiles - 1]], axis=0)
    west_edge = jnp.concatenate([west[cols - 1:], west[: cols - 1]], axis=0)
    left = jnp.where(column == 0, west_edge, rolled)
    rolled = jnp.concatenate([field[1:], field[:1]], axis=0)
    east_edge = jnp.concatenate([east[tiles - cols + 1:], east[: tiles - cols + 1]], axis=0)
    right = jnp.where(column == cols - 1, east_edge, rolled)
    return up, down, left, right


def blocks_times(field, around, own_ref, nb_ref):
    tiles, width = field.shape
    chunk = 32
    lane = lax.broadcasted_iota(jnp.int32, (chunk, width), 1)
    sub = lax.broadcasted_iota(jnp.int32, (chunk, width), 0)
    outs = []
    for t in range(tiles):
        vecs = [f[t:t + 1] for f in around]
        mine = field[t:t + 1]
        spread = jnp.zeros((chunk, width), jnp.float32)
        for g in range(0, width, chunk):
            acc = own_ref[t, g:g + chunk, :] * mine
            for n, vec in enumerate(vecs):
                acc = acc + nb_ref[n, t, g:g + chunk, :] * vec
            total = jnp.sum(acc, axis=1, keepdims=True)
            spread = jnp.where(lane == sub + g, total, spread)
        outs.append(jnp.sum(spread, axis=0, keepdims=True))
    return jnp.concatenate(outs, axis=0)


def kernel(sweep, cols, present, flags, own_ref, nb_ref, weights, *refs):
    n_halo = sum(present)
    halo_refs, refs = refs[:n_halo], refs[n_halo:]
    halo_iter = iter(halo_refs)
    halos = [next(halo_iter)[...] if p else None for p in present]
    odd_row, odd_col = flags[0] == 1, flags[1] == 1
    field_ref, refs = refs[0], refs[1:]
    field = field_ref[...]
    around = beside(field, halos, odd_row, odd_col, cols)
    around = [f * weights[n] for n, f in enumerate(around)]
    product = blocks_times(field, around, own_ref, nb_ref)
    if sweep < 0:
        injected, search_out, residue_out, estimate_out = refs
        residue = injected[...] - product
        search_out[...] = residue
        residue_out[...] = residue
        estimate_out[...] = field + STRIDES[0] * residue
    else:
        capacity, residue_in, estimate_in = refs[:3]
        outs = refs[3:]
        residue = residue_in[...] - STRIDES[sweep] * (product + capacity[...] * field)
        search = residue + MOMENTA[sweep + 1] * field
        estimate = estimate_in[...] + STRIDES[sweep + 1] * search
        if sweep + 2 < ITERS:
            outs[0][...] = search
            outs[1][...] = residue
            outs[2][...] = estimate
        else:
            outs[0][...] = estimate


def collect(currents, slot_tile, tiles, width):
    slots, frames = currents.shape[3:]
    names = jnp.pad(slot_tile.astype(jnp.float32)[..., None, :],
                    ((0, 0), (0, 0), (0, 0), (0, 0), (0, frames - slots)))
    packed = jnp.concatenate([currents, names], axis=3)
    arrived = lax.all_to_all(packed, "col", split_axis=2, concat_axis=1, tiled=True)[0, :, 0]
    targets = arrived[:, slots, :slots]
    chooser = (targets[..., None] == jnp.arange(tiles, dtype=jnp.float32)).astype(jnp.float32)
    injected = jnp.einsum("skt,skf->tf", chooser, arrived[:, :slots], precision=lax.Precision.HIGHEST)
    return injected.reshape(tiles, STEPS, width)


def shards_general(own_block, neighbor_block, pattern, capacity, initial, currents, slot_tile):
    tile_rows, tile_cols, width = initial.shape
    tiles = tile_rows * tile_cols
    flags = jnp.stack([lax.axis_index("row") % 2, lax.axis_index("col") % 2]).astype(jnp.int32)

    voltage = initial.reshape(tiles, width)
    halos = exchange(voltage)

    injected = collect(currents, slot_tile, tiles, width)

    own = own_block.reshape(tiles, width, width)
    nb = neighbor_block.reshape(4, tiles, width, width)
    weights = jnp.broadcast_to(
        jnp.moveaxis(pattern.reshape(tiles, 4), 1, 0).astype(jnp.float32)[..., None], (4, tiles, width)
    )
    cap = capacity.reshape(tiles, width)
    shape = jax.ShapeDtypeStruct((tiles, width), jnp.float32)
    vmem = pl.BlockSpec(memory_space=pltpu.VMEM)
    smem = pl.BlockSpec(memory_space=pltpu.SMEM)

    def call(sweep, halos, *state):
        present = tuple(h is not None for h in halos)
        ins = (flags, own, nb, weights) + tuple(h for h in halos if h is not None) + state
        n_out = 1 if sweep + 2 == ITERS else 3
        out = pl.pallas_call(
            functools.partial(kernel, sweep, tile_cols, present),
            out_shape=(shape,) * n_out,
            in_specs=[smem] + [vmem] * (len(ins) - 1),
            out_specs=(vmem,) * n_out,
            compiler_params=pltpu.CompilerParams(vmem_limit_bytes=8 * 2**20),
            cost_estimate=pl.CostEstimate(flops=2 * 5 * tiles * width * width, bytes_accessed=5 * tiles * width * width * 4,
                                          transcendentals=0),
            name="couple",
        )(*ins)
        return out

    frames_out = []
    for instant in range(STEPS):
        if instant:
            halos = exchange(voltage)
        search, residue, estimate = call(-1, halos, voltage, injected[:, instant])
        for sweep in range(ITERS - 1):
            halos = exchange(search)
            out = call(sweep, halos, search, cap, residue, estimate)
            if sweep + 2 < ITERS:
                search, residue, estimate = out
            else:
                (voltage,) = out
        frames_out.append(voltage)
    return jnp.stack(frames_out).reshape(STEPS, tile_rows, tile_cols, width)


ROWS, HALF = 2, 2
N = 2 * ROWS
OWN, SIDE_A, SIDE_B, OUT_IN, IN_OUT, IN_IN, FACING, PACKED = 0, 4, 8, 12, 14, 16, 18, 20
TILES = [(j, b) for j in range(N) for b in range(HALF)]
ORIGIN = [(0, 0), (0, 1), (1, 1), (1, 0)]


def unit_device(unit, n_col):
    group, place = divmod(unit // 2, 4)
    x, row = ((0, 0), (1, 0), (1, 1), (0, 1))[place]
    return (row + group) % 2 * n_col + 4 * group + 2 * x + unit % 2


def deal_pairs(n_col, which):
    rounds = []
    for i in (0, 1):
        pairs = []
        for row in (0, 1):
            for col in range(n_col):
                k = row ^ i
                unit = 2 * col + k if which == 0 else 2 * col + (2 if k == 0 else -1)
                if 0 <= unit < 2 * n_col:
                    pairs.append((row * n_col + col, unit_device(unit, n_col)))
        rounds.append(pairs)
    return rounds


def pack_kernel(n_col, place_ref, pattern_ref, own_ref, nb_ref, send_0, send_1, facing_0, facing_1):
    y, col = place_ref[0], place_ref[1]
    rows = (y, 1 - y)
    inward, outward = 1 - y, y
    cols = own_ref.shape[1]

    def coupling(direction, row, col):
        weight = pattern_ref[(row * cols + col) * 4 + direction].astype(jnp.float32)
        return nb_ref[direction, row, col] * weight

    for i, (send, facing) in enumerate(((send_0, facing_0), (send_1, facing_1))):
        k = (y + i) % 2
        at = [b + k * (cols - 1 - 2 * b) for b in range(HALF)]
        side_a, side_b = 3 - k, 2 + k
        inside = jnp.where(col == k * (n_col - 1), 0.0, 1.0)
        for h in range(ROWS):
            for b in range(HALF):
                send[OWN + h * HALF + b] = own_ref[rows[h], at[b]]
                send[SIDE_A + h * HALF + b] = coupling(side_a, rows[h], at[b])
                block = coupling(side_b, rows[h], at[b])
                send[SIDE_B + h * HALF + b] = block * inside if b == 0 else block
            send[FACING + h] = coupling(2 + k, rows[h], HALF - k)
            facing[h] = coupling(3 - k, rows[h], (cols - 1) * (1 - k))
        for b in range(HALF):
            send[OUT_IN + b] = coupling(inward, rows[0], at[b])
            send[IN_OUT + b] = coupling(outward, rows[1], at[b])
            send[IN_IN + b] = coupling(inward, rows[1], at[b])


def tile_terms(halves, j, b):
    i, h = ORIGIN[j]
    half = halves[i]
    terms = [(half, OWN + h * HALF + b, (j, b))]
    if h == 0:
        terms.append((half, OUT_IN + b, ((1, 2)[i], b)))
    else:
        terms.append((half, IN_OUT + b, ((0, 3)[i], b)))
        terms.append((half, IN_IN + b, ((2, 1)[i], b)))
    terms.append((half, (SIDE_A if b == 0 else SIDE_B) + h * HALF + b, (j, 1 - b)))
    return terms


def halo_term(halves, j, b):
    i, h = ORIGIN[j]
    return halves[i], (SIDE_B if b == 0 else SIDE_A) + h * HALF + b


def facing_term(halves, beyond, j, b):
    i, h = ORIGIN[j]
    return (beyond[i], h) if b == 0 else (halves[i], FACING + h)


def matvec(terms, chunk=32):
    width = terms[0][2].shape[1]
    lane = lax.broadcasted_iota(jnp.int32, (chunk, width), 1)
    sub = lax.broadcasted_iota(jnp.int32, (chunk, width), 0)
    spread = jnp.zeros((chunk, width), jnp.float32)
    for g in range(0, width, chunk):
        acc = None
        for ref, index, vec in terms:
            part = ref[index, g:g + chunk, :] * vec
            acc = part if acc is None else acc + part
        total = jnp.sum(acc, axis=1, keepdims=True)
        spread = jnp.where(lane == sub + g, total, spread)
    return jnp.sum(spread, axis=0, keepdims=True)


def row_of(x, j, b):
    i = j * HALF + b
    return x[i:i + 1]


def inner_product(f, halves):
    return jnp.concatenate(
        [matvec([(r, i, row_of(f, *at)) for r, i, at in tile_terms(halves, j, b)]) for j, b in TILES], axis=0
    )


def messages(f, g):
    return [
        jnp.concatenate([row_of(x, j, b) for x in (f, g) for j in reversed(range(N))], axis=0) for b in (1, 0)
    ]


def ahead(first, sweep, f, q, residue, capacity, injected):
    if first:
        return injected - q
    return residue - STRIDES[sweep] * (q + capacity * f) + MOMENTA[sweep + 1] * f


def start_kernel(half_0, half_1, field, injected, msg_a, msg_b, q_out):
    f = field[...]
    q = inner_product(f, (half_0, half_1))
    q_out[...] = q
    msg_a[...], msg_b[...] = messages(f, ahead(True, 0, f, q, None, None, injected[...]))


def pair_kernel(pair, last, half_0, half_1, beyond_0, beyond_1, capacity_ref, injected_ref, got_a, got_b, f_ref, q_ref,
                *refs):
    halves, beyond = (half_0, half_1), (beyond_0, beyond_1)
    first = pair == 0
    capacity = capacity_ref[...]
    f, q = f_ref[...], q_ref[...]
    if not first:
        residue, estimate, refs = refs[0][...], refs[1][...], refs[2:]
    got = (got_b, got_a)
    sweep = 2 * pair - 1

    extra = []
    for j, b in TILES:
        r, i = halo_term(halves, j, b)
        extra.append(matvec([(r, i, got[b][j:j + 1, :])]))
    product = q + jnp.concatenate(extra, axis=0)
    if first:
        residue = injected_ref[...] - product
        f2 = residue
        estimate = f + STRIDES[0] * f2
        scale = 1.0
    else:
        residue = residue - STRIDES[sweep] * (product + capacity * f)
        f2 = residue + MOMENTA[sweep + 1] * f
        estimate = estimate + STRIDES[sweep + 1] * f2
        scale = STRIDES[sweep]

    beside2 = {}
    for j, b in TILES:
        r, i = facing_term(halves, beyond, j, b)
        beside2[j, b] = got[b][N + j:N + j + 1, :] - scale * matvec([(r, i, row_of(f, j, b))])

    outs = []
    for j, b in TILES:
        terms = [(r, i, row_of(f2, *at)) for r, i, at in tile_terms(halves, j, b)]
        r, i = halo_term(halves, j, b)
        outs.append(matvec(terms + [(r, i, beside2[j, b])]))
    sweep = 2 * pair
    residue = residue - STRIDES[sweep] * (jnp.concatenate(outs, axis=0) + capacity * f2)
    f3 = residue + MOMENTA[sweep + 1] * f2
    estimate = estimate + STRIDES[sweep + 1] * f3
    closing = sweep + 2 == ITERS
    if closing:
        f3 = estimate
    f_out, refs = refs[0], refs[1:]
    f_out[...] = f3
    if last:
        return
    q = inner_product(f3, halves)
    q_out, msg_a, msg_b = refs[:3]
    q_out[...] = q
    msg_a[...], msg_b[...] = messages(f3, ahead(closing, sweep + 1, f3, q, residue, capacity, injected_ref[...]))
    if not closing:
        refs[3][...] = residue
        refs[4][...] = estimate


def shards_chain(own_block, neighbor_block, pattern, capacity, initial, currents, slot_tile):
    tile_rows, tile_cols, width = initial.shape
    n_col = lax.axis_size("col")
    row = lax.axis_index("row")
    both = ("row", "col")
    deal = deal_pairs(n_col, 0)
    deal_b = deal_pairs(n_col, 1)
    a_pairs = [(c, c ^ 1) for c in range(n_col)]
    b_pairs = [(unit_device(unit, n_col),) * 2 for unit in (0, 2 * n_col - 1)]
    for unit in range(1, 2 * n_col - 1, 2):
        one, two = unit_device(unit, n_col), unit_device(unit + 1, n_col)
        b_pairs += [(one, two), (two, one)]

    vmem = pl.BlockSpec(memory_space=pltpu.VMEM)
    smem = pl.BlockSpec(memory_space=pltpu.SMEM)
    limit = pltpu.CompilerParams(vmem_limit_bytes=16 * 2**20)
    packed = jax.ShapeDtypeStruct((PACKED, width, width), jnp.float32)
    facing = jax.ShapeDtypeStruct((ROWS, width, width), jnp.float32)
    send_0, send_1, facing_0, facing_1 = pl.pallas_call(
        functools.partial(pack_kernel, n_col),
        out_shape=(packed, packed, facing, facing),
        in_specs=[smem, smem, vmem, vmem],
        out_specs=(vmem,) * 4,
        compiler_params=limit,
        name="pack",
    )(jnp.stack([row, lax.axis_index("col")]).astype(jnp.int32), pattern.reshape(-1), own_block, neighbor_block)
    currents, slot_tile, facing_0, facing_1 = lax.optimization_barrier((currents, slot_tile, facing_0, facing_1))
    half_0 = lax.ppermute(send_0, both, deal[0])
    half_1 = lax.ppermute(send_1, both, deal[1])
    beyond_0 = lax.ppermute(facing_0, both, deal_b[0])
    beyond_1 = lax.ppermute(facing_1, both, deal_b[1])

    injected = collect(currents, slot_tile, tile_rows * tile_cols, width)
    small = jnp.concatenate(
        [injected.reshape(tile_rows, tile_cols, STEPS * width), capacity, initial], axis=2
    )
    small = jnp.where(row == 1, jnp.flip(small, 0), small)
    unit_0, unit_1 = small[:, :HALF], jnp.flip(small, 1)[:, :HALF]
    got_0 = lax.ppermute(jnp.where(row == 1, unit_1, unit_0), both, deal[0])
    got_1 = lax.ppermute(jnp.where(row == 1, unit_0, unit_1), both, deal[1])
    small = jnp.concatenate([got_0, jnp.flip(got_1, 0)], axis=0).reshape(N * HALF, STEPS + 2, width)
    injected, cap, field = small[:, :STEPS], small[:, STEPS], small[:, STEPS + 1]

    shape = jax.ShapeDtypeStruct((N * HALF, width), jnp.float32)

    def call(body, n_out, blocks, *ins):
        return pl.pallas_call(
            body,
            out_shape=(shape,) * n_out,
            in_specs=[vmem] * len(ins),
            out_specs=(vmem,) * n_out,
            compiler_params=limit,
            cost_estimate=pl.CostEstimate(flops=2 * blocks * width * width, bytes_accessed=blocks * width * width * 4,
                                          transcendentals=0),
            name="pair",
        )(*ins)

    msg_a, msg_b, q = call(start_kernel, 3, 28, half_0, half_1, field, injected[:, 0])
    frames = []
    for instant in range(STEPS):
        state = ()
        for pair in range(ITERS // 2):
            closing = pair + 1 == ITERS // 2
            last = closing and instant + 1 == STEPS
            got_b = lax.ppermute(msg_b, both, b_pairs)
            got_a = lax.ppermute(msg_a, "col", a_pairs)
            feed = injected[:, min(instant + closing, STEPS - 1)]
            out = call(functools.partial(pair_kernel, pair, last), 1 if last else 4 if closing else 6, 80,
                       half_0, half_1, beyond_0, beyond_1, cap, feed, got_a, got_b, field, q, *state)
            field = out[0]
            if not last:
                q, msg_a, msg_b = out[1:4]
                state = tuple(out[4:])
        frames.append(field)

    done = jnp.stack(frames).reshape(STEPS, N, HALF, width)
    got_0 = lax.ppermute(done[:, :ROWS], both, [(b, a) for a, b in deal[0]])
    got_1 = lax.ppermute(jnp.flip(done[:, ROWS:], 1), both, [(b, a) for a, b in deal[1]])
    unit_0, unit_1 = jnp.where(row == 1, got_1, got_0), jnp.where(row == 1, got_0, got_1)
    done = jnp.concatenate([unit_0, jnp.flip(unit_1, 2)], axis=2)
    return jnp.where(row == 1, jnp.flip(done, 1), done)


def solution(mesh):
    rows, cols = mesh.shape["row"], mesh.shape["col"]
    return jax.shard_map(
        shards_chain if rows == 2 and cols % 4 == 0 else shards_general,
        mesh=mesh,
        in_specs=(
            P("row", "col", None, None),
            P(None, "row", "col", None, None),
            P("row", "col", None),
            P("row", "col", None),
            P("row", "col", None),
            P("row", "col", None, None, None),
            P("row", "col", None, None),
        ),
        out_specs=P(None, "row", "col", None),
        check_vma=False,
    )
```

```python
import functools

import jax
import jax.numpy as jnp
from jax import lax
from jax.experimental import pallas as pl
from jax.experimental.pallas import tpu as pltpu
from jax.sharding import PartitionSpec as P

STEPS = 4
ITERS = 8

spec_center = 6.4
spec_radius = 5.6


def schedule():
    strides, momenta = [], []
    stride = 1.0 / spec_center
    for sweep in range(ITERS):
        if sweep == 0:
            momentum = 0.0
        else:
            if sweep == 1:
                momentum = 0.5 * (spec_radius * stride) ** 2
            else:
                momentum = (spec_radius * stride / 2.0) ** 2
            stride = 1.0 / (spec_center - momentum / stride)
        strides.append(stride)
        momenta.append(momentum)
    return strides, momenta


STRIDES, MOMENTA = schedule()


def swap_pairs(count, first):
    pairs = []
    for i in range(first, count - 1, 2):
        pairs += [(i, i + 1), (i + 1, i)]
    return pairs


def exchange(field):
    arrived = []
    for axis in ("row", "col"):
        count = lax.axis_size(axis)
        for first in (0, 1):
            pairs = swap_pairs(count, first)
            arrived.append(lax.ppermute(field, axis, pairs) if pairs else None)
    return arrived


def beside(field, halos, odd_row, odd_col, cols):
    tiles = field.shape[0]
    row_a, row_b, col_a, col_b = halos
    zero = jnp.zeros_like(field)
    row_a, row_b, col_a, col_b = [zero if h is None else h for h in (row_a, row_b, col_a, col_b)]
    above = jnp.where(odd_row, row_a, row_b)
    below = jnp.where(odd_row, row_b, row_a)
    west = jnp.where(odd_col, col_a, col_b)
    east = jnp.where(odd_col, col_b, col_a)
    up = jnp.concatenate([above[tiles - cols:], field[: tiles - cols]], axis=0)
    down = jnp.concatenate([field[cols:], below[:cols]], axis=0)
    column = lax.broadcasted_iota(jnp.int32, field.shape, 0) % cols
    rolled = jnp.concatenate([field[tiles - 1:], field[: tiles - 1]], axis=0)
    west_edge = jnp.concatenate([west[cols - 1:], west[: cols - 1]], axis=0)
    left = jnp.where(column == 0, west_edge, rolled)
    rolled = jnp.concatenate([field[1:], field[:1]], axis=0)
    east_edge = jnp.concatenate([east[tiles - cols + 1:], east[: tiles - cols + 1]], axis=0)
    right = jnp.where(column == cols - 1, east_edge, rolled)
    return up, down, left, right


def blocks_times(field, around, own_ref, nb_ref):
    tiles, width = field.shape
    chunk = 32
    lane = lax.broadcasted_iota(jnp.int32, (chunk, width), 1)
    sub = lax.broadcasted_iota(jnp.int32, (chunk, width), 0)
    outs = []
    for t in range(tiles):
        vecs = [f[t:t + 1] for f in around]
        mine = field[t:t + 1]
        spread = jnp.zeros((chunk, width), jnp.float32)
        for g in range(0, width, chunk):
            acc = own_ref[t, g:g + chunk, :] * mine
            for n, vec in enumerate(vecs):
                acc = acc + nb_ref[n, t, g:g + chunk, :] * vec
            total = jnp.sum(acc, axis=1, keepdims=True)
            spread = jnp.where(lane == sub + g, total, spread)
        outs.append(jnp.sum(spread, axis=0, keepdims=True))
    return jnp.concatenate(outs, axis=0)


def kernel(sweep, cols, present, flags, own_ref, nb_ref, weights, *refs):
    n_halo = sum(present)
    halo_refs, refs = refs[:n_halo], refs[n_halo:]
    halo_iter = iter(halo_refs)
    halos = [next(halo_iter)[...] if p else None for p in present]
    odd_row, odd_col = flags[0] == 1, flags[1] == 1
    field_ref, refs = refs[0], refs[1:]
    field = field_ref[...]
    around = beside(field, halos, odd_row, odd_col, cols)
    around = [f * weights[n] for n, f in enumerate(around)]
    product = blocks_times(field, around, own_ref, nb_ref)
    if sweep < 0:
        injected, search_out, residue_out, estimate_out = refs
        residue = injected[...] - product
        search_out[...] = residue
        residue_out[...] = residue
        estimate_out[...] = field + STRIDES[0] * residue
    else:
        capacity, residue_in, estimate_in = refs[:3]
        outs = refs[3:]
        residue = residue_in[...] - STRIDES[sweep] * (product + capacity[...] * field)
        search = residue + MOMENTA[sweep + 1] * field
        estimate = estimate_in[...] + STRIDES[sweep + 1] * search
        if sweep + 2 < ITERS:
            outs[0][...] = search
            outs[1][...] = residue
            outs[2][...] = estimate
        else:
            outs[0][...] = estimate


def collect(currents, slot_tile, tiles, width):
    slots, frames = currents.shape[3:]
    names = jnp.pad(slot_tile.astype(jnp.float32)[..., None, :],
                    ((0, 0), (0, 0), (0, 0), (0, 0), (0, frames - slots)))
    packed = jnp.concatenate([currents, names], axis=3)
    arrived = lax.all_to_all(packed, "col", split_axis=2, concat_axis=1, tiled=True)[0, :, 0]
    targets = arrived[:, slots, :slots]
    chooser = (targets[..., None] == jnp.arange(tiles, dtype=jnp.float32)).astype(jnp.float32)
    injected = jnp.einsum("skt,skf->tf", chooser, arrived[:, :slots], precision=lax.Precision.HIGHEST)
    return injected.reshape(tiles, STEPS, width)


def shards_general(own_block, neighbor_block, pattern, capacity, initial, currents, slot_tile):
    tile_rows, tile_cols, width = initial.shape
    tiles = tile_rows * tile_cols
    flags = jnp.stack([lax.axis_index("row") % 2, lax.axis_index("col") % 2]).astype(jnp.int32)

    voltage = initial.reshape(tiles, width)
    halos = exchange(voltage)

    injected = collect(currents, slot_tile, tiles, width)

    own = own_block.reshape(tiles, width, width)
    nb = neighbor_block.reshape(4, tiles, width, width)
    weights = jnp.broadcast_to(
        jnp.moveaxis(pattern.reshape(tiles, 4), 1, 0).astype(jnp.float32)[..., None], (4, tiles, width)
    )
    cap = capacity.reshape(tiles, width)
    shape = jax.ShapeDtypeStruct((tiles, width), jnp.float32)
    vmem = pl.BlockSpec(memory_space=pltpu.VMEM)
    smem = pl.BlockSpec(memory_space=pltpu.SMEM)

    def call(sweep, halos, *state):
        present = tuple(h is not None for h in halos)
        ins = (flags, own, nb, weights) + tuple(h for h in halos if h is not None) + state
        n_out = 1 if sweep + 2 == ITERS else 3
        out = pl.pallas_call(
            functools.partial(kernel, sweep, tile_cols, present),
            out_shape=(shape,) * n_out,
            in_specs=[smem] + [vmem] * (len(ins) - 1),
            out_specs=(vmem,) * n_out,
            compiler_params=pltpu.CompilerParams(vmem_limit_bytes=8 * 2**20),
            cost_estimate=pl.CostEstimate(flops=2 * 5 * tiles * width * width, bytes_accessed=5 * tiles * width * width * 4,
                                          transcendentals=0),
            name="couple",
        )(*ins)
        return out

    frames_out = []
    for instant in range(STEPS):
        if instant:
            halos = exchange(voltage)
        search, residue, estimate = call(-1, halos, voltage, injected[:, instant])
        for sweep in range(ITERS - 1):
            halos = exchange(search)
            out = call(sweep, halos, search, cap, residue, estimate)
            if sweep + 2 < ITERS:
                search, residue, estimate = out
            else:
                (voltage,) = out
        frames_out.append(voltage)
    return jnp.stack(frames_out).reshape(STEPS, tile_rows, tile_cols, width)


ROWS, HALF = 2, 2
N = 2 * ROWS
OWN, SIDE_A, SIDE_B, OUT_IN, IN_OUT, IN_IN, FACING, PACKED = 0, 4, 8, 12, 14, 16, 18, 20
TILES = [(j, b) for j in range(N) for b in range(HALF)]
ORIGIN = [(0, 0), (0, 1), (1, 1), (1, 0)]


def unit_device(unit, n_col):
    group, place = divmod(unit // 2, 4)
    x, row = ((0, 0), (1, 0), (1, 1), (0, 1))[place]
    return (row + group) % 2 * n_col + 4 * group + 2 * x + (unit + place) % 2


def deal_pairs(n_col, which):
    rounds = []
    for i in (0, 1):
        pairs = []
        for row in (0, 1):
            for col in range(n_col):
                k = row ^ i
                unit = 2 * col + k if which == 0 else 2 * col + (2 if k == 0 else -1)
                if 0 <= unit < 2 * n_col:
                    pairs.append((row * n_col + col, unit_device(unit, n_col)))
        rounds.append(pairs)
    return rounds


def pack_kernel(n_col, place_ref, pattern_ref, own_ref, nb_ref, send_0, send_1, facing_0, facing_1):
    y, col = place_ref[0], place_ref[1]
    rows = (y, 1 - y)
    inward, outward = 1 - y, y
    cols = own_ref.shape[1]

    def coupling(direction, row, col):
        weight = pattern_ref[(row * cols + col) * 4 + direction].astype(jnp.float32)
        return nb_ref[direction, row, col] * weight

    for i, (send, facing) in enumerate(((send_0, facing_0), (send_1, facing_1))):
        k = (y + i) % 2
        at = [b + k * (cols - 1 - 2 * b) for b in range(HALF)]
        side_a, side_b = 3 - k, 2 + k
        inside = jnp.where(col == k * (n_col - 1), 0.0, 1.0)
        for h in range(ROWS):
            for b in range(HALF):
                send[OWN + h * HALF + b] = own_ref[rows[h], at[b]]
                send[SIDE_A + h * HALF + b] = coupling(side_a, rows[h], at[b])
                block = coupling(side_b, rows[h], at[b])
                send[SIDE_B + h * HALF + b] = block * inside if b == 0 else block
            send[FACING + h] = coupling(2 + k, rows[h], HALF - k)
            facing[h] = coupling(3 - k, rows[h], (cols - 1) * (1 - k))
        for b in range(HALF):
            send[OUT_IN + b] = coupling(inward, rows[0], at[b])
            send[IN_OUT + b] = coupling(outward, rows[1], at[b])
            send[IN_IN + b] = coupling(inward, rows[1], at[b])


def tile_terms(halves, j, b):
    i, h = ORIGIN[j]
    half = halves[i]
    terms = [(half, OWN + h * HALF + b, (j, b))]
    if h == 0:
        terms.append((half, OUT_IN + b, ((1, 2)[i], b)))
    else:
        terms.append((half, IN_OUT + b, ((0, 3)[i], b)))
        terms.append((half, IN_IN + b, ((2, 1)[i], b)))
    terms.append((half, (SIDE_A if b == 0 else SIDE_B) + h * HALF + b, (j, 1 - b)))
    return terms


def halo_term(halves, j, b):
    i, h = ORIGIN[j]
    return halves[i], (SIDE_B if b == 0 else SIDE_A) + h * HALF + b


def facing_term(halves, beyond, j, b):
    i, h = ORIGIN[j]
    return (beyond[i], h) if b == 0 else (halves[i], FACING + h)


def matvec(terms, chunk=32):
    width = terms[0][2].shape[1]
    lane = lax.broadcasted_iota(jnp.int32, (chunk, width), 1)
    sub = lax.broadcasted_iota(jnp.int32, (chunk, width), 0)
    spread = jnp.zeros((chunk, width), jnp.float32)
    for g in range(0, width, chunk):
        acc = None
        for ref, index, vec in terms:
            part = ref[index, g:g + chunk, :] * vec
            acc = part if acc is None else acc + part
        total = jnp.sum(acc, axis=1, keepdims=True)
        spread = jnp.where(lane == sub + g, total, spread)
    return jnp.sum(spread, axis=0, keepdims=True)


def row_of(x, j, b):
    i = j * HALF + b
    return x[i:i + 1]


def inner_product(f, halves):
    return jnp.concatenate(
        [matvec([(r, i, row_of(f, *at)) for r, i, at in tile_terms(halves, j, b)]) for j, b in TILES], axis=0
    )


def messages(f, g):
    return [
        jnp.concatenate([row_of(x, j, b) for x in (f, g) for j in reversed(range(N))], axis=0) for b in (1, 0)
    ]


def ahead(first, sweep, f, q, residue, capacity, injected):
    if first:
        return injected - q
    return residue - STRIDES[sweep] * (q + capacity * f) + MOMENTA[sweep + 1] * f


def start_kernel(half_0, half_1, field, injected, msg_a, msg_b, q_out):
    f = field[...]
    q = inner_product(f, (half_0, half_1))
    q_out[...] = q
    msg_a[...], msg_b[...] = messages(f, ahead(True, 0, f, q, None, None, injected[...]))


def pair_kernel(pair, last, half_0, half_1, beyond_0, beyond_1, capacity_ref, injected_ref, got_b, got_a, f_ref, q_ref,
                *refs):
    halves, beyond = (half_0, half_1), (beyond_0, beyond_1)
    first = pair == 0
    capacity = capacity_ref[...]
    f, q = f_ref[...], q_ref[...]
    if not first:
        residue, estimate, refs = refs[0][...], refs[1][...], refs[2:]
    got = (got_b, got_a)
    sweep = 2 * pair - 1

    extra = []
    for j, b in TILES:
        r, i = halo_term(halves, j, b)
        extra.append(matvec([(r, i, got[b][j:j + 1, :])]))
    product = q + jnp.concatenate(extra, axis=0)
    if first:
        residue = injected_ref[...] - product
        f2 = residue
        estimate = f + STRIDES[0] * f2
        scale = 1.0
    else:
        residue = residue - STRIDES[sweep] * (product + capacity * f)
        f2 = residue + MOMENTA[sweep + 1] * f
        estimate = estimate + STRIDES[sweep + 1] * f2
        scale = STRIDES[sweep]

    beside2 = {}
    for j, b in TILES:
        r, i = facing_term(halves, beyond, j, b)
        beside2[j, b] = got[b][N + j:N + j + 1, :] - scale * matvec([(r, i, row_of(f, j, b))])

    outs = []
    for j, b in TILES:
        terms = [(r, i, row_of(f2, *at)) for r, i, at in tile_terms(halves, j, b)]
        r, i = halo_term(halves, j, b)
        outs.append(matvec(terms + [(r, i, beside2[j, b])]))
    sweep = 2 * pair
    residue = residue - STRIDES[sweep] * (jnp.concatenate(outs, axis=0) + capacity * f2)
    f3 = residue + MOMENTA[sweep + 1] * f2
    estimate = estimate + STRIDES[sweep + 1] * f3
    closing = sweep + 2 == ITERS
    if closing:
        f3 = estimate
    f_out, refs = refs[0], refs[1:]
    f_out[...] = f3
    if last:
        return
    q = inner_product(f3, halves)
    q_out, msg_a, msg_b = refs[:3]
    q_out[...] = q
    msg_a[...], msg_b[...] = messages(f3, ahead(closing, sweep + 1, f3, q, residue, capacity, injected_ref[...]))
    if not closing:
        refs[3][...] = residue
        refs[4][...] = estimate


def shards_chain(own_block, neighbor_block, pattern, capacity, initial, currents, slot_tile):
    tile_rows, tile_cols, width = initial.shape
    n_col = lax.axis_size("col")
    row = lax.axis_index("row")
    both = ("row", "col")
    deal = deal_pairs(n_col, 0)
    deal_b = deal_pairs(n_col, 1)
    a_pairs = [(c, c ^ 1) for c in range(n_col)]
    b_pairs = [(unit_device(unit, n_col),) * 2 for unit in (0, 2 * n_col - 1)]
    for unit in range(1, 2 * n_col - 1, 2):
        one, two = unit_device(unit, n_col), unit_device(unit + 1, n_col)
        b_pairs += [(one, two), (two, one)]

    vmem = pl.BlockSpec(memory_space=pltpu.VMEM)
    smem = pl.BlockSpec(memory_space=pltpu.SMEM)
    limit = pltpu.CompilerParams(vmem_limit_bytes=16 * 2**20)
    packed = jax.ShapeDtypeStruct((PACKED, width, width), jnp.float32)
    facing = jax.ShapeDtypeStruct((ROWS, width, width), jnp.float32)
    send_0, send_1, facing_0, facing_1 = pl.pallas_call(
        functools.partial(pack_kernel, n_col),
        out_shape=(packed, packed, facing, facing),
        in_specs=[smem, smem, vmem, vmem],
        out_specs=(vmem,) * 4,
        compiler_params=limit,
        name="pack",
    )(jnp.stack([row, lax.axis_index("col")]).astype(jnp.int32), pattern.reshape(-1), own_block, neighbor_block)
    half_0 = lax.ppermute(send_0, both, deal[0])
    half_1 = lax.ppermute(send_1, both, deal[1])
    beyond_0 = lax.ppermute(facing_0, both, deal_b[0])
    beyond_1 = lax.ppermute(facing_1, both, deal_b[1])

    def deal_small(currents, slot_tile, capacity, initial):
        injected = collect(currents, slot_tile, tile_rows * tile_cols, width)
        small = jnp.concatenate(
            [injected.reshape(tile_rows, tile_cols, STEPS * width), capacity, initial], axis=2
        )
        small = jnp.where(row == 1, jnp.flip(small, 0), small)
        unit_0, unit_1 = small[:, :HALF], jnp.flip(small, 1)[:, :HALF]
        got_0 = lax.ppermute(jnp.where(row == 1, unit_1, unit_0), both, deal[0])
        got_1 = lax.ppermute(jnp.where(row == 1, unit_0, unit_1), both, deal[1])
        return jnp.concatenate([got_0, jnp.flip(got_1, 0)], axis=0).reshape(N * HALF, STEPS + 2, width)

    small = lax.cond(
        row < lax.axis_size("row"),
        deal_small,
        lambda *_: jnp.zeros((N * HALF, STEPS + 2, width), jnp.float32),
        currents, slot_tile, capacity, initial,
    )
    injected, cap, field = small[:, :STEPS], small[:, STEPS], small[:, STEPS + 1]

    shape = jax.ShapeDtypeStruct((N * HALF, width), jnp.float32)

    def call(body, n_out, blocks, *ins):
        return pl.pallas_call(
            body,
            out_shape=(shape,) * n_out,
            in_specs=[vmem] * len(ins),
            out_specs=(vmem,) * n_out,
            compiler_params=limit,
            cost_estimate=pl.CostEstimate(flops=2 * blocks * width * width, bytes_accessed=blocks * width * width * 4,
                                          transcendentals=0),
            name="pair",
        )(*ins)

    msg_a, msg_b, q = call(start_kernel, 3, 28, half_0, half_1, field, injected[:, 0])
    frames = []
    for instant in range(STEPS):
        state = ()
        for pair in range(ITERS // 2):
            closing = pair + 1 == ITERS // 2
            last = closing and instant + 1 == STEPS
            got_b = lax.ppermute(msg_b, both, b_pairs)
            got_a = lax.ppermute(msg_a, "col", a_pairs)
            feed = injected[:, min(instant + closing, STEPS - 1)]
            out = call(functools.partial(pair_kernel, pair, last), 1 if last else 4 if closing else 6, 80,
                       half_0, half_1, beyond_0, beyond_1, cap, feed, got_b, got_a, field, q, *state)
            field = out[0]
            if not last:
                q, msg_a, msg_b = out[1:4]
                state = tuple(out[4:])
        frames.append(field)

    done = jnp.stack(frames).reshape(STEPS, N, HALF, width)
    got_0 = lax.ppermute(done[:, :ROWS], both, [(b, a) for a, b in deal[0]])
    got_1 = lax.ppermute(jnp.flip(done[:, ROWS:], 1), both, [(b, a) for a, b in deal[1]])
    unit_0, unit_1 = jnp.where(row == 1, got_1, got_0), jnp.where(row == 1, got_0, got_1)
    done = jnp.concatenate([unit_0, jnp.flip(unit_1, 2)], axis=2)
    return jnp.where(row == 1, jnp.flip(done, 1), done)


def solution(mesh):
    rows, cols = mesh.shape["row"], mesh.shape["col"]
    return jax.shard_map(
        shards_chain if rows == 2 and cols % 4 == 0 else shards_general,
        mesh=mesh,
        in_specs=(
            P("row", "col", None, None),
            P(None, "row", "col", None, None),
            P("row", "col", None),
            P("row", "col", None),
            P("row", "col", None),
            P("row", "col", None, None, None),
            P("row", "col", None, None),
        ),
        out_specs=P(None, "row", "col", None),
        check_vma=False,
    )
```

```python
import functools

import jax
import jax.numpy as jnp
from jax import lax
from jax.experimental import pallas as pl
from jax.experimental.pallas import tpu as pltpu
from jax.sharding import PartitionSpec as P

STEPS = 4
ITERS = 8

spec_center = 6.4
spec_radius = 5.6


def schedule():
    strides, momenta = [], []
    stride = 1.0 / spec_center
    for sweep in range(ITERS):
        if sweep == 0:
            momentum = 0.0
        else:
            if sweep == 1:
                momentum = 0.5 * (spec_radius * stride) ** 2
            else:
                momentum = (spec_radius * stride / 2.0) ** 2
            stride = 1.0 / (spec_center - momentum / stride)
        strides.append(stride)
        momenta.append(momentum)
    return strides, momenta


STRIDES, MOMENTA = schedule()


def swap_pairs(count, first):
    pairs = []
    for i in range(first, count - 1, 2):
        pairs += [(i, i + 1), (i + 1, i)]
    return pairs


def exchange(field):
    arrived = []
    for axis in ("row", "col"):
        count = lax.axis_size(axis)
        for first in (0, 1):
            pairs = swap_pairs(count, first)
            arrived.append(lax.ppermute(field, axis, pairs) if pairs else None)
    return arrived


def beside(field, halos, odd_row, odd_col, cols):
    tiles = field.shape[0]
    row_a, row_b, col_a, col_b = halos
    zero = jnp.zeros_like(field)
    row_a, row_b, col_a, col_b = [zero if h is None else h for h in (row_a, row_b, col_a, col_b)]
    above = jnp.where(odd_row, row_a, row_b)
    below = jnp.where(odd_row, row_b, row_a)
    west = jnp.where(odd_col, col_a, col_b)
    east = jnp.where(odd_col, col_b, col_a)
    up = jnp.concatenate([above[tiles - cols:], field[: tiles - cols]], axis=0)
    down = jnp.concatenate([field[cols:], below[:cols]], axis=0)
    column = lax.broadcasted_iota(jnp.int32, field.shape, 0) % cols
    rolled = jnp.concatenate([field[tiles - 1:], field[: tiles - 1]], axis=0)
    west_edge = jnp.concatenate([west[cols - 1:], west[: cols - 1]], axis=0)
    left = jnp.where(column == 0, west_edge, rolled)
    rolled = jnp.concatenate([field[1:], field[:1]], axis=0)
    east_edge = jnp.concatenate([east[tiles - cols + 1:], east[: tiles - cols + 1]], axis=0)
    right = jnp.where(column == cols - 1, east_edge, rolled)
    return up, down, left, right


def blocks_times(field, around, own_ref, nb_ref):
    tiles, width = field.shape
    chunk = 32
    lane = lax.broadcasted_iota(jnp.int32, (chunk, width), 1)
    sub = lax.broadcasted_iota(jnp.int32, (chunk, width), 0)
    outs = []
    for t in range(tiles):
        vecs = [f[t:t + 1] for f in around]
        mine = field[t:t + 1]
        spread = jnp.zeros((chunk, width), jnp.float32)
        for g in range(0, width, chunk):
            acc = own_ref[t, g:g + chunk, :] * mine
            for n, vec in enumerate(vecs):
                acc = acc + nb_ref[n, t, g:g + chunk, :] * vec
            total = jnp.sum(acc, axis=1, keepdims=True)
            spread = jnp.where(lane == sub + g, total, spread)
        outs.append(jnp.sum(spread, axis=0, keepdims=True))
    return jnp.concatenate(outs, axis=0)


def kernel(sweep, cols, present, flags, own_ref, nb_ref, weights, *refs):
    n_halo = sum(present)
    halo_refs, refs = refs[:n_halo], refs[n_halo:]
    halo_iter = iter(halo_refs)
    halos = [next(halo_iter)[...] if p else None for p in present]
    odd_row, odd_col = flags[0] == 1, flags[1] == 1
    field_ref, refs = refs[0], refs[1:]
    field = field_ref[...]
    around = beside(field, halos, odd_row, odd_col, cols)
    around = [f * weights[n] for n, f in enumerate(around)]
    product = blocks_times(field, around, own_ref, nb_ref)
    if sweep < 0:
        injected, search_out, residue_out, estimate_out = refs
        residue = injected[...] - product
        search_out[...] = residue
        residue_out[...] = residue
        estimate_out[...] = field + STRIDES[0] * residue
    else:
        capacity, residue_in, estimate_in = refs[:3]
        outs = refs[3:]
        residue = residue_in[...] - STRIDES[sweep] * (product + capacity[...] * field)
        search = residue + MOMENTA[sweep + 1] * field
        estimate = estimate_in[...] + STRIDES[sweep + 1] * search
        if sweep + 2 < ITERS:
            outs[0][...] = search
            outs[1][...] = residue
            outs[2][...] = estimate
        else:
            outs[0][...] = estimate


def collect(currents, slot_tile, tiles, width):
    slots, frames = currents.shape[3:]
    names = jnp.pad(slot_tile.astype(jnp.float32)[..., None, :],
                    ((0, 0), (0, 0), (0, 0), (0, 0), (0, frames - slots)))
    packed = jnp.concatenate([currents, names], axis=3)
    arrived = lax.all_to_all(packed, "col", split_axis=2, concat_axis=1, tiled=True)[0, :, 0]
    targets = arrived[:, slots, :slots]
    chooser = (targets[..., None] == jnp.arange(tiles, dtype=jnp.float32)).astype(jnp.float32)
    injected = jnp.einsum("skt,skf->tf", chooser, arrived[:, :slots], precision=lax.Precision.HIGHEST)
    return injected.reshape(tiles, STEPS, width)


def shards_general(own_block, neighbor_block, pattern, capacity, initial, currents, slot_tile):
    tile_rows, tile_cols, width = initial.shape
    tiles = tile_rows * tile_cols
    flags = jnp.stack([lax.axis_index("row") % 2, lax.axis_index("col") % 2]).astype(jnp.int32)

    voltage = initial.reshape(tiles, width)
    halos = exchange(voltage)

    injected = collect(currents, slot_tile, tiles, width)

    own = own_block.reshape(tiles, width, width)
    nb = neighbor_block.reshape(4, tiles, width, width)
    weights = jnp.broadcast_to(
        jnp.moveaxis(pattern.reshape(tiles, 4), 1, 0).astype(jnp.float32)[..., None], (4, tiles, width)
    )
    cap = capacity.reshape(tiles, width)
    shape = jax.ShapeDtypeStruct((tiles, width), jnp.float32)
    vmem = pl.BlockSpec(memory_space=pltpu.VMEM)
    smem = pl.BlockSpec(memory_space=pltpu.SMEM)

    def call(sweep, halos, *state):
        present = tuple(h is not None for h in halos)
        ins = (flags, own, nb, weights) + tuple(h for h in halos if h is not None) + state
        n_out = 1 if sweep + 2 == ITERS else 3
        out = pl.pallas_call(
            functools.partial(kernel, sweep, tile_cols, present),
            out_shape=(shape,) * n_out,
            in_specs=[smem] + [vmem] * (len(ins) - 1),
            out_specs=(vmem,) * n_out,
            compiler_params=pltpu.CompilerParams(vmem_limit_bytes=8 * 2**20),
            cost_estimate=pl.CostEstimate(flops=2 * 5 * tiles * width * width, bytes_accessed=5 * tiles * width * width * 4,
                                          transcendentals=0),
            name="couple",
        )(*ins)
        return out

    frames_out = []
    for instant in range(STEPS):
        if instant:
            halos = exchange(voltage)
        search, residue, estimate = call(-1, halos, voltage, injected[:, instant])
        for sweep in range(ITERS - 1):
            halos = exchange(search)
            out = call(sweep, halos, search, cap, residue, estimate)
            if sweep + 2 < ITERS:
                search, residue, estimate = out
            else:
                (voltage,) = out
        frames_out.append(voltage)
    return jnp.stack(frames_out).reshape(STEPS, tile_rows, tile_cols, width)


ROWS, HALF = 2, 2
N = 2 * ROWS
OWN, SIDE_A, SIDE_B, OUT_IN, IN_OUT, IN_IN, FACING, PACKED = 0, 4, 8, 12, 14, 16, 18, 20
TILES = [(j, b) for j in range(N) for b in range(HALF)]
ORIGIN = [(0, 0), (0, 1), (1, 1), (1, 0)]


def unit_device(unit, n_col):
    col = unit // 2
    return (unit + col) % 2, col


def pack_kernel(n_col, place_ref, pattern_ref, own_hbm, nb_hbm, keep, send, facing_0, facing_1, own_ref, nb_ref, sems):
    y, col = place_ref[0], place_ref[1]
    copies = [pltpu.make_async_copy(own_hbm, own_ref, sems.at[4])]
    copies += [pltpu.make_async_copy(nb_hbm.at[d], nb_ref.at[d], sems.at[d]) for d in (2, 3, 0, 1)]
    for copy in copies:
        copy.start()
    rows = (y, 1 - y)
    inward, outward = 1 - y, y
    cols = own_ref.shape[1]

    def coupling(direction, row, at_col):
        weight = pattern_ref[(row * cols + at_col) * 4 + direction].astype(jnp.float32)
        return nb_ref[direction, row, at_col] * weight

    halves = []
    for i, (half, facing) in enumerate(((keep, facing_0), (send, facing_1))):
        k = (y + col + i) % 2
        halves.append((half, facing, k, [b + k * (cols - 1 - 2 * b) for b in range(HALF)]))
    copies[0].wait()
    for half, facing, k, at in halves:
        for h in range(ROWS):
            for b in range(HALF):
                half[OWN + h * HALF + b] = own_ref[rows[h], at[b]]
    for copy in copies[1:3]:
        copy.wait()
    for half, facing, k, at in halves:
        inside = jnp.where(col == k * (n_col - 1), 0.0, 1.0)
        for h in range(ROWS):
            for b in range(HALF):
                half[SIDE_A + h * HALF + b] = coupling(3 - k, rows[h], at[b])
                block = coupling(2 + k, rows[h], at[b])
                if b == 0:
                    block = block * inside
                    facing[h] = block
                half[SIDE_B + h * HALF + b] = block
            half[FACING + h] = coupling(2 + k, rows[h], HALF - k)
    for copy in copies[3:]:
        copy.wait()
    for half, facing, k, at in halves:
        for b in range(HALF):
            half[OUT_IN + b] = coupling(inward, rows[0], at[b])
            half[IN_OUT + b] = coupling(outward, rows[1], at[b])
            half[IN_IN + b] = coupling(inward, rows[1], at[b])


def tile_terms(halves, j, b):
    i, h = ORIGIN[j]
    half = halves[i]
    terms = [(half, OWN + h * HALF + b, (j, b))]
    if h == 0:
        terms.append((half, OUT_IN + b, ((1, 2)[i], b)))
    else:
        terms.append((half, IN_OUT + b, ((0, 3)[i], b)))
        terms.append((half, IN_IN + b, ((2, 1)[i], b)))
    terms.append((half, (SIDE_A if b == 0 else SIDE_B) + h * HALF + b, (j, 1 - b)))
    return terms


def halo_term(halves, j, b):
    i, h = ORIGIN[j]
    return halves[i], (SIDE_B if b == 0 else SIDE_A) + h * HALF + b


def facing_term(halves, beyond, j, b):
    i, h = ORIGIN[j]
    return (beyond[i], h) if b == 0 else (halves[i], FACING + h)


def matvec(terms, chunk=32):
    width = terms[0][2].shape[1]
    lane = lax.broadcasted_iota(jnp.int32, (chunk, width), 1)
    sub = lax.broadcasted_iota(jnp.int32, (chunk, width), 0)
    spread = jnp.zeros((chunk, width), jnp.float32)
    for g in range(0, width, chunk):
        acc = None
        for ref, index, vec in terms:
            part = ref[index, g:g + chunk, :] * vec
            acc = part if acc is None else acc + part
        total = jnp.sum(acc, axis=1, keepdims=True)
        spread = jnp.where(lane == sub + g, total, spread)
    return jnp.sum(spread, axis=0, keepdims=True)


def row_of(x, j, b):
    i = j * HALF + b
    return x[i:i + 1]


def inner_product(f, halves):
    return jnp.concatenate(
        [matvec([(r, i, row_of(f, *at)) for r, i, at in tile_terms(halves, j, b)]) for j, b in TILES], axis=0
    )


def messages(f, g):
    return [
        jnp.concatenate([row_of(x, j, b) for x in (f, g) for j in order], axis=0)
        for b, order in ((1, range(N)[::-1]), (0, range(N)))
    ]


def ahead(first, sweep, f, q, residue, capacity, injected):
    if first:
        return injected - q
    return residue - STRIDES[sweep] * (q + capacity * f) + MOMENTA[sweep + 1] * f


def start_kernel(half_0, half_1, beyond_0, beyond_1, field, injected, msg_a, msg_b, q_out):
    f = field[...]
    q = inner_product(f, (half_0, half_1))
    q_out[...] = q
    msg_a[...], msg_b[...] = messages(f, ahead(True, 0, f, q, None, None, injected[...]))


def pair_kernel(pair, last, half_0, half_1, beyond_0, beyond_1, capacity_ref, injected_ref, got_a, got_b, f_ref, q_ref,
                *refs):
    halves, beyond = (half_0, half_1), (beyond_0, beyond_1)
    first = pair == 0
    capacity = capacity_ref[...]
    f, q = f_ref[...], q_ref[...]
    if not first:
        residue, estimate, refs = refs[0][...], refs[1][...], refs[2:]
    got = (got_b, got_a)
    sweep = 2 * pair - 1

    extra = []
    for j, b in TILES:
        r, i = halo_term(halves, j, b)
        extra.append(matvec([(r, i, got[b][j:j + 1, :])]))
    product = q + jnp.concatenate(extra, axis=0)
    if first:
        residue = injected_ref[...] - product
        f2 = residue
        estimate = f + STRIDES[0] * f2
        scale = 1.0
    else:
        residue = residue - STRIDES[sweep] * (product + capacity * f)
        f2 = residue + MOMENTA[sweep + 1] * f
        estimate = estimate + STRIDES[sweep + 1] * f2
        scale = STRIDES[sweep]

    beside2 = {}
    for j, b in TILES:
        r, i = facing_term(halves, beyond, j, b)
        beside2[j, b] = got[b][N + j:N + j + 1, :] - scale * matvec([(r, i, row_of(f, j, b))])

    outs = []
    for j, b in TILES:
        terms = [(r, i, row_of(f2, *at)) for r, i, at in tile_terms(halves, j, b)]
        r, i = halo_term(halves, j, b)
        outs.append(matvec(terms + [(r, i, beside2[j, b])]))
    sweep = 2 * pair
    residue = residue - STRIDES[sweep] * (jnp.concatenate(outs, axis=0) + capacity * f2)
    f3 = residue + MOMENTA[sweep + 1] * f2
    estimate = estimate + STRIDES[sweep + 1] * f3
    closing = sweep + 2 == ITERS
    if closing:
        f3 = estimate
    f_out, refs = refs[0], refs[1:]
    f_out[...] = f3
    if last:
        return
    q = inner_product(f3, halves)
    q_out, msg_a, msg_b = refs[:3]
    q_out[...] = q
    msg_a[...], msg_b[...] = messages(f3, ahead(closing, sweep + 1, f3, q, residue, capacity, injected_ref[...]))
    if not closing:
        refs[3][...] = residue
        refs[4][...] = estimate


def shards_chain(own_block, neighbor_block, pattern, capacity, initial, currents, slot_tile):
    tile_rows, tile_cols, width = initial.shape
    n_col = lax.axis_size("col")
    row, col = lax.axis_index("row"), lax.axis_index("col")
    both = ("row", "col")
    swap = [(0, 1), (1, 0)]
    b_pairs, b_cross = [], []
    for unit in range(1, 2 * n_col - 1, 2):
        ends = unit_device(unit, n_col), unit_device(unit + 1, n_col)
        for (r, c), (to_r, to_c) in (ends, ends[::-1]):
            b_pairs.append((r * n_col + c, to_r * n_col + to_c))
            b_cross.append(((1 - r) * n_col + c, to_r * n_col + to_c))
    parity = (row + col) % 2

    vmem = pl.BlockSpec(memory_space=pltpu.VMEM)
    smem = pl.BlockSpec(memory_space=pltpu.SMEM)
    hbm = pl.BlockSpec(memory_space=pltpu.HBM)
    limit = pltpu.CompilerParams(vmem_limit_bytes=16 * 2**20)
    packed = jax.ShapeDtypeStruct((PACKED, width, width), jnp.float32)
    facing = jax.ShapeDtypeStruct((ROWS, width, width), jnp.float32)
    half_0, send, facing_0, facing_1 = pl.pallas_call(
        functools.partial(pack_kernel, n_col),
        out_shape=(packed, packed, facing, facing),
        in_specs=[smem, smem, hbm, hbm],
        out_specs=(vmem,) * 4,
        scratch_shapes=[
            pltpu.VMEM(own_block.shape, jnp.float32),
            pltpu.VMEM(neighbor_block.shape, jnp.float32),
            pltpu.SemaphoreType.DMA((5,)),
        ],
        compiler_params=pltpu.CompilerParams(vmem_limit_bytes=48 * 2**20),
        name="pack",
    )(jnp.stack([row, col]).astype(jnp.int32), pattern.reshape(-1), own_block, neighbor_block)
    half_1 = lax.ppermute(send, "row", swap)
    beyond_0 = lax.ppermute(facing_0, both, b_pairs)
    beyond_1 = lax.ppermute(facing_1, both, b_cross)

    injected = collect(currents, slot_tile, tile_rows * tile_cols, width)
    small = jnp.concatenate(
        [injected.reshape(tile_rows, tile_cols, STEPS * width), capacity, initial], axis=2
    )
    small = jnp.where(row == 1, jnp.flip(small, 0), small)
    unit_0, unit_1 = small[:, :HALF], jnp.flip(small, 1)[:, :HALF]
    got = lax.ppermute(jnp.where(parity == 1, unit_0, unit_1), "row", swap)
    small = jnp.concatenate([jnp.where(parity == 1, unit_1, unit_0), jnp.flip(got, 0)], axis=0)
    small = small.reshape(N * HALF, STEPS + 2, width)
    injected, cap, field = small[:, :STEPS], small[:, STEPS], small[:, STEPS + 1]

    shape = jax.ShapeDtypeStruct((N * HALF, width), jnp.float32)

    def call(body, n_out, blocks, *ins):
        return pl.pallas_call(
            body,
            out_shape=(shape,) * n_out,
            in_specs=[vmem] * len(ins),
            out_specs=(vmem,) * n_out,
            compiler_params=limit,
            cost_estimate=pl.CostEstimate(flops=2 * blocks * width * width, bytes_accessed=blocks * width * width * 4,
                                          transcendentals=0),
            name="pair",
        )(*ins)

    msg_a, msg_b, q = call(start_kernel, 3, 28, half_0, half_1, beyond_0, beyond_1, field, injected[:, 0])
    frames = []
    for instant in range(STEPS):
        state = ()
        for pair in range(ITERS // 2):
            closing = pair + 1 == ITERS // 2
            last = closing and instant + 1 == STEPS
            got_b = lax.ppermute(msg_b, both, b_pairs)
            got_a = lax.ppermute(msg_a, "row", swap)
            feed = injected[:, min(instant + closing, STEPS - 1)]
            out = call(functools.partial(pair_kernel, pair, last), 1 if last else 4 if closing else 6, 80,
                       half_0, half_1, beyond_0, beyond_1, cap, feed, got_a, got_b, field, q, *state)
            field = out[0]
            if not last:
                q, msg_a, msg_b = out[1:4]
                state = tuple(out[4:])
        frames.append(field)

    done = jnp.stack(frames).reshape(STEPS, N, HALF, width)
    got = lax.ppermute(jnp.flip(done[:, ROWS:], 1), "row", swap)
    mine = done[:, :ROWS]
    unit_0, unit_1 = jnp.where(parity == 1, got, mine), jnp.where(parity == 1, mine, got)
    done = jnp.concatenate([unit_0, jnp.flip(unit_1, 2)], axis=2)
    return jnp.where(row == 1, jnp.flip(done, 1), done)


def solution(mesh):
    rows, cols = mesh.shape["row"], mesh.shape["col"]
    return jax.shard_map(
        shards_chain if rows == 2 else shards_general,
        mesh=mesh,
        in_specs=(
            P("row", "col", None, None),
            P(None, "row", "col", None, None),
            P("row", "col", None),
            P("row", "col", None),
            P("row", "col", None),
            P("row", "col", None, None, None),
            P("row", "col", None, None),
        ),
        out_specs=P(None, "row", "col", None),
        check_vma=False,
    )
```

```python
import functools

import jax
import jax.numpy as jnp
from jax import lax
from jax.experimental import pallas as pl
from jax.experimental.pallas import tpu as pltpu
from jax.sharding import PartitionSpec as P

STEPS = 4
ITERS = 8

spec_center = 6.4
spec_radius = 5.6


def schedule():
    strides, momenta = [], []
    stride = 1.0 / spec_center
    for sweep in range(ITERS):
        if sweep == 0:
            momentum = 0.0
        else:
            if sweep == 1:
                momentum = 0.5 * (spec_radius * stride) ** 2
            else:
                momentum = (spec_radius * stride / 2.0) ** 2
            stride = 1.0 / (spec_center - momentum / stride)
        strides.append(stride)
        momenta.append(momentum)
    return strides, momenta


STRIDES, MOMENTA = schedule()


def swap_pairs(count, first):
    pairs = []
    for i in range(first, count - 1, 2):
        pairs += [(i, i + 1), (i + 1, i)]
    return pairs


def exchange(field):
    arrived = []
    for axis in ("row", "col"):
        count = lax.axis_size(axis)
        for first in (0, 1):
            pairs = swap_pairs(count, first)
            arrived.append(lax.ppermute(field, axis, pairs) if pairs else None)
    return arrived


def beside(field, halos, odd_row, odd_col, cols):
    tiles = field.shape[0]
    row_a, row_b, col_a, col_b = halos
    zero = jnp.zeros_like(field)
    row_a, row_b, col_a, col_b = [zero if h is None else h for h in (row_a, row_b, col_a, col_b)]
    above = jnp.where(odd_row, row_a, row_b)
    below = jnp.where(odd_row, row_b, row_a)
    west = jnp.where(odd_col, col_a, col_b)
    east = jnp.where(odd_col, col_b, col_a)
    up = jnp.concatenate([above[tiles - cols:], field[: tiles - cols]], axis=0)
    down = jnp.concatenate([field[cols:], below[:cols]], axis=0)
    column = lax.broadcasted_iota(jnp.int32, field.shape, 0) % cols
    rolled = jnp.concatenate([field[tiles - 1:], field[: tiles - 1]], axis=0)
    west_edge = jnp.concatenate([west[cols - 1:], west[: cols - 1]], axis=0)
    left = jnp.where(column == 0, west_edge, rolled)
    rolled = jnp.concatenate([field[1:], field[:1]], axis=0)
    east_edge = jnp.concatenate([east[tiles - cols + 1:], east[: tiles - cols + 1]], axis=0)
    right = jnp.where(column == cols - 1, east_edge, rolled)
    return up, down, left, right


def blocks_times(field, around, own_ref, nb_ref):
    tiles, width = field.shape
    chunk = 32
    lane = lax.broadcasted_iota(jnp.int32, (chunk, width), 1)
    sub = lax.broadcasted_iota(jnp.int32, (chunk, width), 0)
    outs = []
    for t in range(tiles):
        vecs = [f[t:t + 1] for f in around]
        mine = field[t:t + 1]
        spread = jnp.zeros((chunk, width), jnp.float32)
        for g in range(0, width, chunk):
            acc = own_ref[t, g:g + chunk, :] * mine
            for n, vec in enumerate(vecs):
                acc = acc + nb_ref[n, t, g:g + chunk, :] * vec
            total = jnp.sum(acc, axis=1, keepdims=True)
            spread = jnp.where(lane == sub + g, total, spread)
        outs.append(jnp.sum(spread, axis=0, keepdims=True))
    return jnp.concatenate(outs, axis=0)


def kernel(sweep, cols, present, flags, own_ref, nb_ref, weights, *refs):
    n_halo = sum(present)
    halo_refs, refs = refs[:n_halo], refs[n_halo:]
    halo_iter = iter(halo_refs)
    halos = [next(halo_iter)[...] if p else None for p in present]
    odd_row, odd_col = flags[0] == 1, flags[1] == 1
    field_ref, refs = refs[0], refs[1:]
    field = field_ref[...]
    around = beside(field, halos, odd_row, odd_col, cols)
    around = [f * weights[n] for n, f in enumerate(around)]
    product = blocks_times(field, around, own_ref, nb_ref)
    if sweep < 0:
        injected, search_out, residue_out, estimate_out = refs
        residue = injected[...] - product
        search_out[...] = residue
        residue_out[...] = residue
        estimate_out[...] = field + STRIDES[0] * residue
    else:
        capacity, residue_in, estimate_in = refs[:3]
        outs = refs[3:]
        residue = residue_in[...] - STRIDES[sweep] * (product + capacity[...] * field)
        search = residue + MOMENTA[sweep + 1] * field
        estimate = estimate_in[...] + STRIDES[sweep + 1] * search
        if sweep + 2 < ITERS:
            outs[0][...] = search
            outs[1][...] = residue
            outs[2][...] = estimate
        else:
            outs[0][...] = estimate


def collect(currents, slot_tile, tiles, width):
    slots, frames = currents.shape[3:]
    names = jnp.pad(slot_tile.astype(jnp.float32)[..., None, :],
                    ((0, 0), (0, 0), (0, 0), (0, 0), (0, frames - slots)))
    packed = jnp.concatenate([currents, names], axis=3)
    arrived = lax.all_to_all(packed, "col", split_axis=2, concat_axis=1, tiled=True)[0, :, 0]
    targets = arrived[:, slots, :slots]
    chooser = (targets[..., None] == jnp.arange(tiles, dtype=jnp.float32)).astype(jnp.float32)
    injected = jnp.einsum("skt,skf->tf", chooser, arrived[:, :slots], precision=lax.Precision.HIGHEST)
    return injected.reshape(tiles, STEPS, width)


def shards_general(own_block, neighbor_block, pattern, capacity, initial, currents, slot_tile):
    tile_rows, tile_cols, width = initial.shape
    tiles = tile_rows * tile_cols
    flags = jnp.stack([lax.axis_index("row") % 2, lax.axis_index("col") % 2]).astype(jnp.int32)

    voltage = initial.reshape(tiles, width)
    halos = exchange(voltage)

    injected = collect(currents, slot_tile, tiles, width)

    own = own_block.reshape(tiles, width, width)
    nb = neighbor_block.reshape(4, tiles, width, width)
    weights = jnp.broadcast_to(
        jnp.moveaxis(pattern.reshape(tiles, 4), 1, 0).astype(jnp.float32)[..., None], (4, tiles, width)
    )
    cap = capacity.reshape(tiles, width)
    shape = jax.ShapeDtypeStruct((tiles, width), jnp.float32)
    vmem = pl.BlockSpec(memory_space=pltpu.VMEM)
    smem = pl.BlockSpec(memory_space=pltpu.SMEM)

    def call(sweep, halos, *state):
        present = tuple(h is not None for h in halos)
        ins = (flags, own, nb, weights) + tuple(h for h in halos if h is not None) + state
        n_out = 1 if sweep + 2 == ITERS else 3
        out = pl.pallas_call(
            functools.partial(kernel, sweep, tile_cols, present),
            out_shape=(shape,) * n_out,
            in_specs=[smem] + [vmem] * (len(ins) - 1),
            out_specs=(vmem,) * n_out,
            compiler_params=pltpu.CompilerParams(vmem_limit_bytes=8 * 2**20),
            cost_estimate=pl.CostEstimate(flops=2 * 5 * tiles * width * width, bytes_accessed=5 * tiles * width * width * 4,
                                          transcendentals=0),
            name="couple",
        )(*ins)
        return out

    frames_out = []
    for instant in range(STEPS):
        if instant:
            halos = exchange(voltage)
        search, residue, estimate = call(-1, halos, voltage, injected[:, instant])
        for sweep in range(ITERS - 1):
            halos = exchange(search)
            out = call(sweep, halos, search, cap, residue, estimate)
            if sweep + 2 < ITERS:
                search, residue, estimate = out
            else:
                (voltage,) = out
        frames_out.append(voltage)
    return jnp.stack(frames_out).reshape(STEPS, tile_rows, tile_cols, width)


ROWS, HALF = 2, 2
N = 2 * ROWS
OWN, SIDE_A, SIDE_B, OUT_IN, IN_OUT, IN_IN, FACING, PACKED = 0, 4, 8, 12, 14, 16, 18, 20
TILES = [(j, b) for j in range(N) for b in range(HALF)]
ORIGIN = [(0, 0), (0, 1), (1, 1), (1, 0)]
CAPACITY, INITIAL = STEPS, STEPS + 1


def unit_device(unit, n_col):
    col = unit // 2
    return (unit + col) % 2, col


def pack_kernel(n_col, place_ref, pattern_ref, own_hbm, nb_hbm, keep, send, facing_0, facing_1, own_ref, nb_ref, sems):
    y, col = place_ref[0], place_ref[1]
    copies = [pltpu.make_async_copy(own_hbm, own_ref, sems.at[4])]
    copies += [pltpu.make_async_copy(nb_hbm.at[d], nb_ref.at[d], sems.at[d]) for d in (2, 3, 0, 1)]
    for copy in copies:
        copy.start()
    rows = (y, 1 - y)
    inward, outward = 1 - y, y
    cols = own_ref.shape[1]

    def coupling(direction, row, at_col):
        weight = pattern_ref[row, at_col, direction].astype(jnp.float32)
        return nb_ref[direction, row, at_col] * weight

    halves = []
    for i, (half, facing) in enumerate(((keep, facing_0), (send, facing_1))):
        k = (y + col + i) % 2
        halves.append((half, facing, k, [b + k * (cols - 1 - 2 * b) for b in range(HALF)]))
    copies[0].wait()
    for half, facing, k, at in halves:
        for h in range(ROWS):
            for b in range(HALF):
                half[OWN + h * HALF + b] = own_ref[rows[h], at[b]]
    for copy in copies[1:3]:
        copy.wait()
    for half, facing, k, at in halves:
        inside = jnp.where(col == k * (n_col - 1), 0.0, 1.0)
        for h in range(ROWS):
            for b in range(HALF):
                half[SIDE_A + h * HALF + b] = coupling(3 - k, rows[h], at[b])
                block = coupling(2 + k, rows[h], at[b])
                if b == 0:
                    block = block * inside
                    facing[h] = block
                half[SIDE_B + h * HALF + b] = block
            half[FACING + h] = coupling(2 + k, rows[h], HALF - k)
    for copy in copies[3:]:
        copy.wait()
    for half, facing, k, at in halves:
        for b in range(HALF):
            half[OUT_IN + b] = coupling(inward, rows[0], at[b])
            half[IN_OUT + b] = coupling(outward, rows[1], at[b])
            half[IN_IN + b] = coupling(inward, rows[1], at[b])


def tile_terms(halves, j, b):
    i, h = ORIGIN[j]
    half = halves[i]
    terms = [(half, OWN + h * HALF + b, (j, b))]
    if h == 0:
        terms.append((half, OUT_IN + b, ((1, 2)[i], b)))
    else:
        terms.append((half, IN_OUT + b, ((0, 3)[i], b)))
        terms.append((half, IN_IN + b, ((2, 1)[i], b)))
    terms.append((half, (SIDE_A if b == 0 else SIDE_B) + h * HALF + b, (j, 1 - b)))
    return terms


def halo_term(halves, j, b):
    i, h = ORIGIN[j]
    return halves[i], (SIDE_B if b == 0 else SIDE_A) + h * HALF + b


def facing_term(halves, beyond, j, b):
    i, h = ORIGIN[j]
    return (beyond[i], h) if b == 0 else (halves[i], FACING + h)


def matvec(terms, chunk=32):
    width = terms[0][2].shape[1]
    lane = lax.broadcasted_iota(jnp.int32, (chunk, width), 1)
    sub = lax.broadcasted_iota(jnp.int32, (chunk, width), 0)
    spread = jnp.zeros((chunk, width), jnp.float32)
    for g in range(0, width, chunk):
        acc = None
        for ref, index, vec in terms:
            part = ref[index, g:g + chunk, :] * vec
            acc = part if acc is None else acc + part
        total = jnp.sum(acc, axis=1, keepdims=True)
        spread = jnp.where(lane == sub + g, total, spread)
    return jnp.sum(spread, axis=0, keepdims=True)


def row_of(x, j, b):
    i = j * HALF + b
    return x[i:i + 1]


def inner_product(f, halves):
    return jnp.concatenate(
        [matvec([(r, i, row_of(f, *at)) for r, i, at in tile_terms(halves, j, b)]) for j, b in TILES], axis=0
    )


def messages(f, g):
    return [
        jnp.concatenate([row_of(x, j, b) for x in (f, g) for j in order], axis=0)
        for b, order in ((1, range(N)[::-1]), (0, range(N)))
    ]


def ahead(first, sweep, f, q, residue, capacity, injected):
    if first:
        return injected - q
    return residue - STRIDES[sweep] * (q + capacity * f) + MOMENTA[sweep + 1] * f


def small_part(small, index):
    n = N * HALF
    return small[index * n:(index + 1) * n, :]


def start_kernel(half_0, half_1, small, msg_a, msg_b, q_out):
    f = small_part(small, INITIAL)
    q = inner_product(f, (half_0, half_1))
    q_out[...] = q
    msg_a[...], msg_b[...] = messages(f, ahead(True, 0, f, q, None, None, small_part(small, 0)))


def pair_kernel(instant, pair, last, half_0, half_1, beyond_0, beyond_1, small, got_a, got_b, q_ref, *refs):
    halves, beyond = (half_0, half_1), (beyond_0, beyond_1)
    first = pair == 0
    capacity = small_part(small, CAPACITY)
    q = q_ref[...]
    if first and instant == 0:
        f = small_part(small, INITIAL)
    else:
        f, refs = refs[0][...], refs[1:]
    if not first:
        residue, estimate, refs = refs[0][...], refs[1][...], refs[2:]
    got = (got_b, got_a)
    sweep = 2 * pair - 1

    extra = []
    for j, b in TILES:
        r, i = halo_term(halves, j, b)
        extra.append(matvec([(r, i, got[b][j:j + 1, :])]))
    product = q + jnp.concatenate(extra, axis=0)
    if first:
        residue = small_part(small, instant) - product
        f2 = residue
        estimate = f + STRIDES[0] * f2
        scale = 1.0
    else:
        residue = residue - STRIDES[sweep] * (product + capacity * f)
        f2 = residue + MOMENTA[sweep + 1] * f
        estimate = estimate + STRIDES[sweep + 1] * f2
        scale = STRIDES[sweep]

    beside2 = {}
    for j, b in TILES:
        r, i = facing_term(halves, beyond, j, b)
        beside2[j, b] = got[b][N + j:N + j + 1, :] - scale * matvec([(r, i, row_of(f, j, b))])

    outs = []
    for j, b in TILES:
        terms = [(r, i, row_of(f2, *at)) for r, i, at in tile_terms(halves, j, b)]
        r, i = halo_term(halves, j, b)
        outs.append(matvec(terms + [(r, i, beside2[j, b])]))
    sweep = 2 * pair
    residue = residue - STRIDES[sweep] * (jnp.concatenate(outs, axis=0) + capacity * f2)
    f3 = residue + MOMENTA[sweep + 1] * f2
    estimate = estimate + STRIDES[sweep + 1] * f3
    closing = sweep + 2 == ITERS
    if closing:
        f3 = estimate
    f_out, refs = refs[0], refs[1:]
    f_out[...] = f3
    if last:
        return
    q = inner_product(f3, halves)
    q_out, msg_a, msg_b = refs[:3]
    q_out[...] = q
    upcoming = small_part(small, instant + 1) if closing else None
    msg_a[...], msg_b[...] = messages(f3, ahead(closing, sweep + 1, f3, q, residue, capacity, upcoming))
    if not closing:
        refs[3][...] = residue
        refs[4][...] = estimate


def shards_chain(own_block, neighbor_block, pattern, capacity, initial, currents, slot_tile):
    tile_rows, tile_cols, width = initial.shape
    n_col = lax.axis_size("col")
    row, col = lax.axis_index("row"), lax.axis_index("col")
    both = ("row", "col")
    swap = [(0, 1), (1, 0)]
    b_pairs, b_cross = [], []
    for unit in range(1, 2 * n_col - 1, 2):
        ends = unit_device(unit, n_col), unit_device(unit + 1, n_col)
        for (r, c), (to_r, to_c) in (ends, ends[::-1]):
            b_pairs.append((r * n_col + c, to_r * n_col + to_c))
            b_cross.append(((1 - r) * n_col + c, to_r * n_col + to_c))
    parity = (row + col) % 2

    vmem = pl.BlockSpec(memory_space=pltpu.VMEM)
    smem = pl.BlockSpec(memory_space=pltpu.SMEM)
    hbm = pl.BlockSpec(memory_space=pltpu.HBM)
    limit = pltpu.CompilerParams(vmem_limit_bytes=16 * 2**20)
    packed = jax.ShapeDtypeStruct((PACKED, width, width), jnp.float32)
    facing = jax.ShapeDtypeStruct((ROWS, width, width), jnp.float32)
    half_0, send, facing_0, facing_1 = pl.pallas_call(
        functools.partial(pack_kernel, n_col),
        out_shape=(packed, packed, facing, facing),
        in_specs=[smem, smem, hbm, hbm],
        out_specs=(vmem,) * 4,
        scratch_shapes=[
            pltpu.VMEM(own_block.shape, jnp.float32),
            pltpu.VMEM(neighbor_block.shape, jnp.float32),
            pltpu.SemaphoreType.DMA((5,)),
        ],
        compiler_params=pltpu.CompilerParams(vmem_limit_bytes=48 * 2**20),
        name="pack",
    )(jnp.stack([row, col]).astype(jnp.int32), pattern,
      pltpu.with_memory_space_constraint(own_block, pltpu.HBM),
      pltpu.with_memory_space_constraint(neighbor_block, pltpu.HBM))
    half_1 = lax.ppermute(send, "row", swap)

    def beside(currents, slot_tile, capacity, initial, facing_0, facing_1):
        beyond_0 = lax.ppermute(facing_0, both, b_pairs)
        beyond_1 = lax.ppermute(facing_1, both, b_cross)
        injected = collect(currents, slot_tile, tile_rows * tile_cols, width)
        small = jnp.concatenate(
            [jnp.moveaxis(injected, 1, 0).reshape(STEPS, tile_rows, tile_cols, width), capacity[None], initial[None]]
        )
        small = jnp.where(row == 1, jnp.flip(small, 1), small)
        unit_0, unit_1 = small[:, :, :HALF], jnp.flip(small, 2)[:, :, :HALF]
        got = lax.ppermute(jnp.where(parity == 1, unit_0, unit_1), "row", swap)
        small = jnp.concatenate([jnp.where(parity == 1, unit_1, unit_0), jnp.flip(got, 1)], axis=1)
        return small.reshape((STEPS + 2) * N * HALF, width), beyond_0, beyond_1

    small, beyond_0, beyond_1 = lax.cond(
        row < lax.axis_size("row"),
        beside,
        lambda currents, slot_tile, capacity, initial, *blocks: (
            jnp.zeros(((STEPS + 2) * N * HALF, width), jnp.float32), *blocks
        ),
        currents, slot_tile, capacity, initial, facing_0, facing_1,
    )

    shape = jax.ShapeDtypeStruct((N * HALF, width), jnp.float32)

    def call(body, n_out, blocks, *ins):
        return pl.pallas_call(
            body,
            out_shape=(shape,) * n_out,
            in_specs=[vmem] * len(ins),
            out_specs=(vmem,) * n_out,
            compiler_params=limit,
            cost_estimate=pl.CostEstimate(flops=2 * blocks * width * width, bytes_accessed=blocks * width * width * 4,
                                          transcendentals=0),
            name="pair",
        )(*ins)

    msg_a, msg_b, q = call(start_kernel, 3, 28, half_0, half_1, small)
    frames = []
    state = ()
    for instant in range(STEPS):
        for pair in range(ITERS // 2):
            closing = pair + 1 == ITERS // 2
            last = closing and instant + 1 == STEPS
            got_b = lax.ppermute(msg_b, both, b_pairs)
            got_a = lax.ppermute(msg_a, "row", swap)
            out = call(functools.partial(pair_kernel, instant, pair, last), 1 if last else 4 if closing else 6, 80,
                       half_0, half_1, beyond_0, beyond_1, small, got_a, got_b, q, *state)
            if not last:
                q, msg_a, msg_b = out[1:4]
                state = (out[0], *out[4:])
        frames.append(out[0])

    done = jnp.stack(frames).reshape(STEPS, N, HALF, width)
    got = lax.ppermute(jnp.flip(done[:, ROWS:], 1), "row", swap)
    mine = done[:, :ROWS]
    unit_0, unit_1 = jnp.where(parity == 1, got, mine), jnp.where(parity == 1, mine, got)
    done = jnp.concatenate([unit_0, jnp.flip(unit_1, 2)], axis=2)
    return jnp.where(row == 1, jnp.flip(done, 1), done)


def solution(mesh):
    rows, cols = mesh.shape["row"], mesh.shape["col"]
    return jax.shard_map(
        shards_chain if rows == 2 else shards_general,
        mesh=mesh,
        in_specs=(
            P("row", "col", None, None),
            P(None, "row", "col", None, None),
            P("row", "col", None),
            P("row", "col", None),
            P("row", "col", None),
            P("row", "col", None, None, None),
            P("row", "col", None, None),
        ),
        out_specs=P(None, "row", "col", None),
        check_vma=False,
    )
```

```python
import functools

import jax
import jax.numpy as jnp
from jax import lax
from jax.experimental import pallas as pl
from jax.experimental.pallas import tpu as pltpu
from jax.sharding import PartitionSpec as P

STEPS = 4
ITERS = 8

spec_center = 6.4
spec_radius = 5.6


def schedule():
    strides, momenta = [], []
    stride = 1.0 / spec_center
    for sweep in range(ITERS):
        if sweep == 0:
            momentum = 0.0
        else:
            if sweep == 1:
                momentum = 0.5 * (spec_radius * stride) ** 2
            else:
                momentum = (spec_radius * stride / 2.0) ** 2
            stride = 1.0 / (spec_center - momentum / stride)
        strides.append(stride)
        momenta.append(momentum)
    return strides, momenta


STRIDES, MOMENTA = schedule()


def swap_pairs(count, first):
    pairs = []
    for i in range(first, count - 1, 2):
        pairs += [(i, i + 1), (i + 1, i)]
    return pairs


def exchange(field):
    arrived = []
    for axis in ("row", "col"):
        count = lax.axis_size(axis)
        for first in (0, 1):
            pairs = swap_pairs(count, first)
            arrived.append(lax.ppermute(field, axis, pairs) if pairs else None)
    return arrived


def beside(field, halos, odd_row, odd_col, cols):
    tiles = field.shape[0]
    row_a, row_b, col_a, col_b = halos
    zero = jnp.zeros_like(field)
    row_a, row_b, col_a, col_b = [zero if h is None else h for h in (row_a, row_b, col_a, col_b)]
    above = jnp.where(odd_row, row_a, row_b)
    below = jnp.where(odd_row, row_b, row_a)
    west = jnp.where(odd_col, col_a, col_b)
    east = jnp.where(odd_col, col_b, col_a)
    up = jnp.concatenate([above[tiles - cols:], field[: tiles - cols]], axis=0)
    down = jnp.concatenate([field[cols:], below[:cols]], axis=0)
    column = lax.broadcasted_iota(jnp.int32, field.shape, 0) % cols
    rolled = jnp.concatenate([field[tiles - 1:], field[: tiles - 1]], axis=0)
    west_edge = jnp.concatenate([west[cols - 1:], west[: cols - 1]], axis=0)
    left = jnp.where(column == 0, west_edge, rolled)
    rolled = jnp.concatenate([field[1:], field[:1]], axis=0)
    east_edge = jnp.concatenate([east[tiles - cols + 1:], east[: tiles - cols + 1]], axis=0)
    right = jnp.where(column == cols - 1, east_edge, rolled)
    return up, down, left, right


def blocks_times(field, around, own_ref, nb_ref):
    tiles, width = field.shape
    chunk = 32
    lane = lax.broadcasted_iota(jnp.int32, (chunk, width), 1)
    sub = lax.broadcasted_iota(jnp.int32, (chunk, width), 0)
    outs = []
    for t in range(tiles):
        vecs = [f[t:t + 1] for f in around]
        mine = field[t:t + 1]
        spread = jnp.zeros((chunk, width), jnp.float32)
        for g in range(0, width, chunk):
            acc = own_ref[t, g:g + chunk, :] * mine
            for n, vec in enumerate(vecs):
                acc = acc + nb_ref[n, t, g:g + chunk, :] * vec
            total = jnp.sum(acc, axis=1, keepdims=True)
            spread = jnp.where(lane == sub + g, total, spread)
        outs.append(jnp.sum(spread, axis=0, keepdims=True))
    return jnp.concatenate(outs, axis=0)


def kernel(sweep, cols, present, flags, own_ref, nb_ref, weights, *refs):
    n_halo = sum(present)
    halo_refs, refs = refs[:n_halo], refs[n_halo:]
    halo_iter = iter(halo_refs)
    halos = [next(halo_iter)[...] if p else None for p in present]
    odd_row, odd_col = flags[0] == 1, flags[1] == 1
    field_ref, refs = refs[0], refs[1:]
    field = field_ref[...]
    around = beside(field, halos, odd_row, odd_col, cols)
    around = [f * weights[n] for n, f in enumerate(around)]
    product = blocks_times(field, around, own_ref, nb_ref)
    if sweep < 0:
        injected, search_out, residue_out, estimate_out = refs
        residue = injected[...] - product
        search_out[...] = residue
        residue_out[...] = residue
        estimate_out[...] = field + STRIDES[0] * residue
    else:
        capacity, residue_in, estimate_in = refs[:3]
        outs = refs[3:]
        residue = residue_in[...] - STRIDES[sweep] * (product + capacity[...] * field)
        search = residue + MOMENTA[sweep + 1] * field
        estimate = estimate_in[...] + STRIDES[sweep + 1] * search
        if sweep + 2 < ITERS:
            outs[0][...] = search
            outs[1][...] = residue
            outs[2][...] = estimate
        else:
            outs[0][...] = estimate


def collect(currents, slot_tile, tiles, width):
    slots, frames = currents.shape[3:]
    names = jnp.pad(slot_tile.astype(jnp.float32)[..., None, :],
                    ((0, 0), (0, 0), (0, 0), (0, 0), (0, frames - slots)))
    packed = jnp.concatenate([currents, names], axis=3)
    arrived = lax.all_to_all(packed, "col", split_axis=2, concat_axis=1, tiled=True)[0, :, 0]
    targets = arrived[:, slots, :slots]
    chooser = (targets[..., None] == jnp.arange(tiles, dtype=jnp.float32)).astype(jnp.float32)
    injected = jnp.einsum("skt,skf->tf", chooser, arrived[:, :slots], precision=lax.Precision.HIGHEST)
    return injected.reshape(tiles, STEPS, width)


def shards_general(own_block, neighbor_block, pattern, capacity, initial, currents, slot_tile):
    tile_rows, tile_cols, width = initial.shape
    tiles = tile_rows * tile_cols
    flags = jnp.stack([lax.axis_index("row") % 2, lax.axis_index("col") % 2]).astype(jnp.int32)

    voltage = initial.reshape(tiles, width)
    halos = exchange(voltage)

    injected = collect(currents, slot_tile, tiles, width)

    own = own_block.reshape(tiles, width, width)
    nb = neighbor_block.reshape(4, tiles, width, width)
    weights = jnp.broadcast_to(
        jnp.moveaxis(pattern.reshape(tiles, 4), 1, 0).astype(jnp.float32)[..., None], (4, tiles, width)
    )
    cap = capacity.reshape(tiles, width)
    shape = jax.ShapeDtypeStruct((tiles, width), jnp.float32)
    vmem = pl.BlockSpec(memory_space=pltpu.VMEM)
    smem = pl.BlockSpec(memory_space=pltpu.SMEM)

    def call(sweep, halos, *state):
        present = tuple(h is not None for h in halos)
        ins = (flags, own, nb, weights) + tuple(h for h in halos if h is not None) + state
        n_out = 1 if sweep + 2 == ITERS else 3
        out = pl.pallas_call(
            functools.partial(kernel, sweep, tile_cols, present),
            out_shape=(shape,) * n_out,
            in_specs=[smem] + [vmem] * (len(ins) - 1),
            out_specs=(vmem,) * n_out,
            compiler_params=pltpu.CompilerParams(vmem_limit_bytes=8 * 2**20),
            cost_estimate=pl.CostEstimate(flops=2 * 5 * tiles * width * width, bytes_accessed=5 * tiles * width * width * 4,
                                          transcendentals=0),
            name="couple",
        )(*ins)
        return out

    frames_out = []
    for instant in range(STEPS):
        if instant:
            halos = exchange(voltage)
        search, residue, estimate = call(-1, halos, voltage, injected[:, instant])
        for sweep in range(ITERS - 1):
            halos = exchange(search)
            out = call(sweep, halos, search, cap, residue, estimate)
            if sweep + 2 < ITERS:
                search, residue, estimate = out
            else:
                (voltage,) = out
        frames_out.append(voltage)
    return jnp.stack(frames_out).reshape(STEPS, tile_rows, tile_cols, width)


ROWS, HALF = 2, 2
N = 2 * ROWS
OWN, SIDE_A, SIDE_B, OUT_IN, IN_OUT, IN_IN, FACING, PACKED = 0, 4, 8, 12, 14, 16, 18, 20
TILES = [(j, b) for j in range(N) for b in range(HALF)]
ORIGIN = [(0, 0), (0, 1), (1, 1), (1, 0)]
CAPACITY, INITIAL = STEPS, STEPS + 1
SPLIT = ((PACKED,), (OUT_IN, PACKED - OUT_IN))


def unit_device(unit, n_col):
    col = unit // 2
    return (unit + col) % 2, col


def half_tiles(y, col, n_col, cols, sent):
    k = (y + col + sent) % 2
    rows = (y, 1 - y)
    inward, outward = 1 - y, y
    at = [b + k * (cols - 1 - 2 * b) for b in range(HALF)]
    inside = jnp.where(col == k * (n_col - 1), 0.0, 1.0)
    tiles = [None] * PACKED
    for h in range(ROWS):
        for b in range(HALF):
            tiles[OWN + h * HALF + b] = (None, rows[h], at[b], None)
            tiles[SIDE_A + h * HALF + b] = (3 - k, rows[h], at[b], None)
            tiles[SIDE_B + h * HALF + b] = (2 + k, rows[h], at[b], inside if b == 0 else None)
        tiles[FACING + h] = (2 + k, rows[h], HALF - k, None)
    for b in range(HALF):
        tiles[OUT_IN + b] = (inward, rows[0], at[b], None)
        tiles[IN_OUT + b] = (outward, rows[1], at[b], None)
        tiles[IN_IN + b] = (inward, rows[1], at[b], None)
    return tiles


def pack_kernel(n_col, sent, first, count, place_ref, pattern_ref, own_hbm, nb_hbm, out, *rest):
    sems = rest[-1]
    tiles = half_tiles(place_ref[0], place_ref[1], n_col, own_hbm.shape[1], sent)
    copies = []
    for i in range(count):
        direction, row, at, _ = tiles[first + i]
        source = own_hbm.at[row, at] if direction is None else nb_hbm.at[direction, row, at]
        copies.append(pltpu.make_async_copy(source, out.at[i], sems.at[i]))
    for copy in copies:
        copy.start()
    for i in range(count):
        direction, row, at, weight = tiles[first + i]
        copies[i].wait()
        if direction is not None:
            scale = pattern_ref[row, at, direction].astype(jnp.float32)
            out[i] = out[i] * (scale if weight is None else scale * weight)
    if not sent:
        for h in range(ROWS):
            rest[0][h] = out[SIDE_B + h * HALF]


def block_of(refs, sizes, slot):
    for ref, size in zip(refs, sizes):
        if slot < size:
            return lambda g, n: ref[slot, g:g + n, :]
        slot -= size


def half_block(halves, i, slot):
    return block_of(halves[i], SPLIT[i], slot)


def tile_terms(halves, j, b):
    i, h = ORIGIN[j]
    terms = [(OWN + h * HALF + b, (j, b))]
    if h == 0:
        terms.append((OUT_IN + b, ((1, 2)[i], b)))
    else:
        terms.append((IN_OUT + b, ((0, 3)[i], b)))
        terms.append((IN_IN + b, ((2, 1)[i], b)))
    terms.append(((SIDE_A if b == 0 else SIDE_B) + h * HALF + b, (j, 1 - b)))
    return [(half_block(halves, i, slot), at) for slot, at in terms]


def halo_block(halves, j, b):
    i, h = ORIGIN[j]
    return half_block(halves, i, (SIDE_B if b == 0 else SIDE_A) + h * HALF + b)


def facing_block(halves, beyond_0, first_b, j, b):
    i, h = ORIGIN[j]
    if b == 1:
        return half_block(halves, i, FACING + h)
    if i == 0:
        return lambda g, n: beyond_0[h, g:g + n, :]
    start = 2 * N + h * first_b.shape[1]
    return lambda g, n: first_b[start + g:start + g + n, :]


def matvec(terms, chunk=32):
    width = terms[0][1].shape[1]
    lane = lax.broadcasted_iota(jnp.int32, (chunk, width), 1)
    sub = lax.broadcasted_iota(jnp.int32, (chunk, width), 0)
    spread = jnp.zeros((chunk, width), jnp.float32)
    for g in range(0, width, chunk):
        acc = None
        for block, vec in terms:
            part = block(g, chunk) * vec
            acc = part if acc is None else acc + part
        total = jnp.sum(acc, axis=1, keepdims=True)
        spread = jnp.where(lane == sub + g, total, spread)
    return jnp.sum(spread, axis=0, keepdims=True)


def row_of(x, j, b):
    i = j * HALF + b
    return x[i:i + 1]


def inner_product(f, halves):
    return jnp.concatenate(
        [matvec([(block, row_of(f, *at)) for block, at in tile_terms(halves, j, b)]) for j, b in TILES], axis=0
    )


def messages(f, g):
    return [
        jnp.concatenate([row_of(x, j, b) for x in (f, g) for j in order], axis=0)
        for b, order in ((1, range(N)[::-1]), (0, range(N)))
    ]


def ahead(first, sweep, f, q, residue, capacity, injected):
    if first:
        return injected - q
    return residue - STRIDES[sweep] * (q + capacity * f) + MOMENTA[sweep + 1] * f


def small_part(small, index):
    n = N * HALF
    return small[index * n:(index + 1) * n, :]


def start_kernel(keep, recv_0, recv_1, small, msg_a, msg_b, q_out):
    halves = ((keep,), (recv_0, recv_1))
    f = small_part(small, INITIAL)
    q = inner_product(f, halves)
    q_out[...] = q
    msg_a[...], to_b = messages(f, ahead(True, 0, f, q, None, None, small_part(small, 0)))
    msg_b[:2 * N, :] = to_b
    width = f.shape[1]
    for h in range(ROWS):
        start = 2 * N + h * width
        msg_b[start:start + width, :] = recv_0[SIDE_B + h * HALF]


def small_part(small, index):
    n = N * HALF
    return small[index * n:(index + 1) * n, :]


def beside_kernel(keep, recv_0, recv_1, beyond_0, first_b, got_a, f_ref, q_ref, response_out, q_out):
    halves = ((keep,), (recv_0, recv_1))
    f, q = f_ref[...], q_ref[...]
    response, total = [], []
    for j, b in TILES:
        response.append(matvec([(facing_block(halves, beyond_0, first_b, j, b), row_of(f, j, b))]))
        mine = row_of(q, j, b)
        if b == 1:
            mine = mine + matvec([(halo_block(halves, j, b), got_a[j:j + 1, :])])
        total.append(mine)
    response_out[...] = jnp.concatenate(response, axis=0)
    q_out[...] = jnp.concatenate(total, axis=0)


def pair_kernel(instant, pair, last, keep, recv_0, recv_1, small, got_a, got_b, response_ref, q_ref, f_ref, *refs):
    halves = ((keep,), (recv_0, recv_1))
    first = pair == 0
    capacity = small_part(small, CAPACITY)
    f, q, response = f_ref[...], q_ref[...], response_ref[...]
    if not first:
        residue, estimate, refs = refs[0][...], refs[1][...], refs[2:]
    got = (got_b, got_a)
    sweep = 2 * pair - 1

    product = []
    for j, b in TILES:
        mine = row_of(q, j, b)
        if b == 0:
            mine = mine + matvec([(halo_block(halves, j, b), got_b[j:j + 1, :])])
        product.append(mine)
    product = jnp.concatenate(product, axis=0)
    if first:
        residue = small_part(small, instant) - product
        f2 = residue
        estimate = f + STRIDES[0] * f2
        scale = 1.0
    else:
        residue = residue - STRIDES[sweep] * (product + capacity * f)
        f2 = residue + MOMENTA[sweep + 1] * f
        estimate = estimate + STRIDES[sweep + 1] * f2
        scale = STRIDES[sweep]

    outs = []
    for j, b in TILES:
        beside = got[b][N + j:N + j + 1, :] - scale * row_of(response, j, b)
        terms = [(block, row_of(f2, *at)) for block, at in tile_terms(halves, j, b)]
        outs.append(matvec(terms + [(halo_block(halves, j, b), beside)]))
    sweep = 2 * pair
    residue = residue - STRIDES[sweep] * (jnp.concatenate(outs, axis=0) + capacity * f2)
    f3 = residue + MOMENTA[sweep + 1] * f2
    estimate = estimate + STRIDES[sweep + 1] * f3
    closing = sweep + 2 == ITERS
    if closing:
        f3 = estimate
    f_out, refs = refs[0], refs[1:]
    f_out[...] = f3
    if last:
        return
    q = inner_product(f3, halves)
    q_out, msg_a, msg_b = refs[:3]
    q_out[...] = q
    upcoming = small_part(small, instant + 1) if closing else None
    msg_a[...], msg_b[...] = messages(f3, ahead(closing, sweep + 1, f3, q, residue, capacity, upcoming))
    if not closing:
        refs[3][...] = residue
        refs[4][...] = estimate


def shards_chain(own_block, neighbor_block, pattern, capacity, initial, currents, slot_tile):
    tile_rows, tile_cols, width = initial.shape
    n_col = lax.axis_size("col")
    row, col = lax.axis_index("row"), lax.axis_index("col")
    both = ("row", "col")
    swap = [(0, 1), (1, 0)]
    b_pairs = []
    for unit in range(1, 2 * n_col - 1, 2):
        ends = [r * n_col + c for r, c in (unit_device(unit, n_col), unit_device(unit + 1, n_col))]
        b_pairs += [tuple(ends), tuple(ends[::-1])]
    parity = (row + col) % 2

    vmem = pl.BlockSpec(memory_space=pltpu.VMEM)
    smem = pl.BlockSpec(memory_space=pltpu.SMEM)
    hbm = pl.BlockSpec(memory_space=pltpu.HBM)
    limit = pltpu.CompilerParams(vmem_limit_bytes=16 * 2**20)
    place = jnp.stack([row, col]).astype(jnp.int32)
    blocks = [pltpu.with_memory_space_constraint(x, pltpu.HBM) for x in (own_block, neighbor_block)]

    def pack(sent, first, count, extra=()):
        return pl.pallas_call(
            functools.partial(pack_kernel, n_col, sent, first, count),
            out_shape=[jax.ShapeDtypeStruct((n, width, width), jnp.float32) for n in (count, *extra)],
            in_specs=[smem, smem, hbm, hbm],
            out_specs=[vmem] * (1 + len(extra)),
            scratch_shapes=[pltpu.SemaphoreType.DMA((count,))],
            compiler_params=limit,
            name="pack",
        )(place, pattern, *blocks)

    recv = []
    for first, count in ((0, SPLIT[1][0]), SPLIT[1]):
        (send,) = pack(1, first, count)
        recv.append(lax.ppermute(send, "row", swap))
    keep, facing_0 = pack(0, 0, PACKED, (ROWS,))

    def beside(currents, slot_tile, capacity, initial, facing_0):
        beyond_0 = lax.ppermute(facing_0, both, b_pairs)
        injected = collect(currents, slot_tile, tile_rows * tile_cols, width)
        small = jnp.concatenate(
            [jnp.moveaxis(injected, 1, 0).reshape(STEPS, tile_rows, tile_cols, width), capacity[None], initial[None]]
        )
        small = jnp.where(row == 1, jnp.flip(small, 1), small)
        unit_0, unit_1 = small[:, :, :HALF], jnp.flip(small, 2)[:, :, :HALF]
        got = lax.ppermute(jnp.where(parity == 1, unit_0, unit_1), "row", swap)
        small = jnp.concatenate([jnp.where(parity == 1, unit_1, unit_0), jnp.flip(got, 1)], axis=1)
        return small.reshape((STEPS + 2) * N * HALF, width), beyond_0

    small, beyond_0 = lax.cond(
        row < lax.axis_size("row"),
        beside,
        lambda currents, slot_tile, capacity, initial, facing_0: (
            jnp.zeros(((STEPS + 2) * N * HALF, width), jnp.float32), facing_0
        ),
        currents, slot_tile, capacity, initial, facing_0,
    )

    shape = jax.ShapeDtypeStruct((N * HALF, width), jnp.float32)
    halves = (keep, *recv)

    def call(body, outs, blocks, *ins):
        return pl.pallas_call(
            body,
            out_shape=outs,
            in_specs=[vmem] * len(ins),
            out_specs=(vmem,) * len(outs),
            compiler_params=limit,
            cost_estimate=pl.CostEstimate(flops=2 * blocks * width * width, bytes_accessed=blocks * width * width * 4,
                                          transcendentals=0),
            name="pair",
        )(*ins)

    first_shape = jax.ShapeDtypeStruct((2 * N + ROWS * width, width), jnp.float32)
    msg_a, msg_b, q = call(start_kernel, (shape, first_shape, shape), 28, *halves, small)
    field, first_b = small[INITIAL * N * HALF:(INITIAL + 1) * N * HALF], None
    frames = []
    state = ()
    for instant in range(STEPS):
        for pair in range(ITERS // 2):
            closing = pair + 1 == ITERS // 2
            last = closing and instant + 1 == STEPS
            got_b = lax.ppermute(msg_b, both, b_pairs)
            got_a = lax.ppermute(msg_a, "row", swap)
            if first_b is None:
                first_b = got_b
            response, q = call(beside_kernel, (shape,) * 2, 12, *halves, beyond_0, first_b, got_a, field, q)
            out = call(functools.partial(pair_kernel, instant, pair, last), (shape,) * (1 if last else 4 if closing else 6),
                       68, *halves, small, got_a, got_b, response, q, field, *state)
            field = out[0]
            if not last:
                q, msg_a, msg_b = out[1:4]
                state = out[4:]
        frames.append(field)

    done = jnp.stack(frames).reshape(STEPS, N, HALF, width)
    got = lax.ppermute(jnp.flip(done[:, ROWS:], 1), "row", swap)
    mine = done[:, :ROWS]
    unit_0, unit_1 = jnp.where(parity == 1, got, mine), jnp.where(parity == 1, mine, got)
    done = jnp.concatenate([unit_0, jnp.flip(unit_1, 2)], axis=2)
    return jnp.where(row == 1, jnp.flip(done, 1), done)


def solution(mesh):
    rows, cols = mesh.shape["row"], mesh.shape["col"]
    return jax.shard_map(
        shards_chain if rows == 2 else shards_general,
        mesh=mesh,
        in_specs=(
            P("row", "col", None, None),
            P(None, "row", "col", None, None),
            P("row", "col", None),
            P("row", "col", None),
            P("row", "col", None),
            P("row", "col", None, None, None),
            P("row", "col", None, None),
        ),
        out_specs=P(None, "row", "col", None),
        check_vma=False,
    )
```

```python
import functools

import jax
import jax.numpy as jnp
from jax import lax
from jax.experimental import pallas as pl
from jax.experimental.pallas import tpu as pltpu
from jax.sharding import PartitionSpec as P

STEPS = 4
ITERS = 8

spec_center = 6.4
spec_radius = 5.6


def schedule():
    strides, momenta = [], []
    stride = 1.0 / spec_center
    for sweep in range(ITERS):
        if sweep == 0:
            momentum = 0.0
        else:
            if sweep == 1:
                momentum = 0.5 * (spec_radius * stride) ** 2
            else:
                momentum = (spec_radius * stride / 2.0) ** 2
            stride = 1.0 / (spec_center - momentum / stride)
        strides.append(stride)
        momenta.append(momentum)
    return strides, momenta


STRIDES, MOMENTA = schedule()


def swap_pairs(count, first):
    pairs = []
    for i in range(first, count - 1, 2):
        pairs += [(i, i + 1), (i + 1, i)]
    return pairs


def exchange(field):
    arrived = []
    for axis in ("row", "col"):
        count = lax.axis_size(axis)
        for first in (0, 1):
            pairs = swap_pairs(count, first)
            arrived.append(lax.ppermute(field, axis, pairs) if pairs else None)
    return arrived


def beside(field, halos, odd_row, odd_col, cols):
    tiles = field.shape[0]
    row_a, row_b, col_a, col_b = halos
    zero = jnp.zeros_like(field)
    row_a, row_b, col_a, col_b = [zero if h is None else h for h in (row_a, row_b, col_a, col_b)]
    above = jnp.where(odd_row, row_a, row_b)
    below = jnp.where(odd_row, row_b, row_a)
    west = jnp.where(odd_col, col_a, col_b)
    east = jnp.where(odd_col, col_b, col_a)
    up = jnp.concatenate([above[tiles - cols:], field[: tiles - cols]], axis=0)
    down = jnp.concatenate([field[cols:], below[:cols]], axis=0)
    column = lax.broadcasted_iota(jnp.int32, field.shape, 0) % cols
    rolled = jnp.concatenate([field[tiles - 1:], field[: tiles - 1]], axis=0)
    west_edge = jnp.concatenate([west[cols - 1:], west[: cols - 1]], axis=0)
    left = jnp.where(column == 0, west_edge, rolled)
    rolled = jnp.concatenate([field[1:], field[:1]], axis=0)
    east_edge = jnp.concatenate([east[tiles - cols + 1:], east[: tiles - cols + 1]], axis=0)
    right = jnp.where(column == cols - 1, east_edge, rolled)
    return up, down, left, right


def blocks_times(field, around, own_ref, nb_ref):
    tiles, width = field.shape
    chunk = 32
    lane = lax.broadcasted_iota(jnp.int32, (chunk, width), 1)
    sub = lax.broadcasted_iota(jnp.int32, (chunk, width), 0)
    outs = []
    for t in range(tiles):
        vecs = [f[t:t + 1] for f in around]
        mine = field[t:t + 1]
        spread = jnp.zeros((chunk, width), jnp.float32)
        for g in range(0, width, chunk):
            acc = own_ref[t, g:g + chunk, :] * mine
            for n, vec in enumerate(vecs):
                acc = acc + nb_ref[n, t, g:g + chunk, :] * vec
            total = jnp.sum(acc, axis=1, keepdims=True)
            spread = jnp.where(lane == sub + g, total, spread)
        outs.append(jnp.sum(spread, axis=0, keepdims=True))
    return jnp.concatenate(outs, axis=0)


def kernel(sweep, cols, present, flags, own_ref, nb_ref, weights, *refs):
    n_halo = sum(present)
    halo_refs, refs = refs[:n_halo], refs[n_halo:]
    halo_iter = iter(halo_refs)
    halos = [next(halo_iter)[...] if p else None for p in present]
    odd_row, odd_col = flags[0] == 1, flags[1] == 1
    field_ref, refs = refs[0], refs[1:]
    field = field_ref[...]
    around = beside(field, halos, odd_row, odd_col, cols)
    around = [f * weights[n] for n, f in enumerate(around)]
    product = blocks_times(field, around, own_ref, nb_ref)
    if sweep < 0:
        injected, search_out, residue_out, estimate_out = refs
        residue = injected[...] - product
        search_out[...] = residue
        residue_out[...] = residue
        estimate_out[...] = field + STRIDES[0] * residue
    else:
        capacity, residue_in, estimate_in = refs[:3]
        outs = refs[3:]
        residue = residue_in[...] - STRIDES[sweep] * (product + capacity[...] * field)
        search = residue + MOMENTA[sweep + 1] * field
        estimate = estimate_in[...] + STRIDES[sweep + 1] * search
        if sweep + 2 < ITERS:
            outs[0][...] = search
            outs[1][...] = residue
            outs[2][...] = estimate
        else:
            outs[0][...] = estimate


def collect(currents, slot_tile, tiles, width):
    slots, frames = currents.shape[3:]
    names = jnp.pad(slot_tile.astype(jnp.float32)[..., None, :],
                    ((0, 0), (0, 0), (0, 0), (0, 0), (0, frames - slots)))
    packed = jnp.concatenate([currents, names], axis=3)
    arrived = lax.all_to_all(packed, "col", split_axis=2, concat_axis=1, tiled=True)[0, :, 0]
    targets = arrived[:, slots, :slots]
    chooser = (targets[..., None] == jnp.arange(tiles, dtype=jnp.float32)).astype(jnp.float32)
    injected = jnp.einsum("skt,skf->tf", chooser, arrived[:, :slots], precision=lax.Precision.HIGHEST)
    return injected.reshape(tiles, STEPS, width)


def shards_general(own_block, neighbor_block, pattern, capacity, initial, currents, slot_tile):
    tile_rows, tile_cols, width = initial.shape
    tiles = tile_rows * tile_cols
    flags = jnp.stack([lax.axis_index("row") % 2, lax.axis_index("col") % 2]).astype(jnp.int32)

    voltage = initial.reshape(tiles, width)
    halos = exchange(voltage)

    injected = collect(currents, slot_tile, tiles, width)

    own = own_block.reshape(tiles, width, width)
    nb = neighbor_block.reshape(4, tiles, width, width)
    weights = jnp.broadcast_to(
        jnp.moveaxis(pattern.reshape(tiles, 4), 1, 0).astype(jnp.float32)[..., None], (4, tiles, width)
    )
    cap = capacity.reshape(tiles, width)
    shape = jax.ShapeDtypeStruct((tiles, width), jnp.float32)
    vmem = pl.BlockSpec(memory_space=pltpu.VMEM)
    smem = pl.BlockSpec(memory_space=pltpu.SMEM)

    def call(sweep, halos, *state):
        present = tuple(h is not None for h in halos)
        ins = (flags, own, nb, weights) + tuple(h for h in halos if h is not None) + state
        n_out = 1 if sweep + 2 == ITERS else 3
        out = pl.pallas_call(
            functools.partial(kernel, sweep, tile_cols, present),
            out_shape=(shape,) * n_out,
            in_specs=[smem] + [vmem] * (len(ins) - 1),
            out_specs=(vmem,) * n_out,
            compiler_params=pltpu.CompilerParams(vmem_limit_bytes=8 * 2**20),
            cost_estimate=pl.CostEstimate(flops=2 * 5 * tiles * width * width, bytes_accessed=5 * tiles * width * width * 4,
                                          transcendentals=0),
            name="couple",
        )(*ins)
        return out

    frames_out = []
    for instant in range(STEPS):
        if instant:
            halos = exchange(voltage)
        search, residue, estimate = call(-1, halos, voltage, injected[:, instant])
        for sweep in range(ITERS - 1):
            halos = exchange(search)
            out = call(sweep, halos, search, cap, residue, estimate)
            if sweep + 2 < ITERS:
                search, residue, estimate = out
            else:
                (voltage,) = out
        frames_out.append(voltage)
    return jnp.stack(frames_out).reshape(STEPS, tile_rows, tile_cols, width)


ROWS, HALF = 2, 2
N = 2 * ROWS
OWN, SIDE_A, SIDE_B, OUT_IN, IN_OUT, IN_IN, FACING, PACKED = 0, 4, 8, 12, 14, 16, 18, 20
TILES = [(j, b) for j in range(N) for b in range(HALF)]
ORIGIN = [(0, 0), (0, 1), (1, 1), (1, 0)]
CAPACITY, INITIAL = STEPS, STEPS + 1
SPLIT = ((PACKED,), (OUT_IN, PACKED - OUT_IN))


def unit_device(unit, n_col):
    col = unit // 2
    return (unit + col) % 2, col


def half_tiles(y, col, n_col, cols, sent):
    k = (y + col + sent) % 2
    rows = (y, 1 - y)
    inward, outward = 1 - y, y
    at = [b + k * (cols - 1 - 2 * b) for b in range(HALF)]
    inside = jnp.where(col == k * (n_col - 1), 0.0, 1.0)
    tiles = [None] * PACKED
    for h in range(ROWS):
        for b in range(HALF):
            tiles[OWN + h * HALF + b] = (None, rows[h], at[b], None)
            tiles[SIDE_A + h * HALF + b] = (3 - k, rows[h], at[b], None)
            tiles[SIDE_B + h * HALF + b] = (2 + k, rows[h], at[b], inside if b == 0 else None)
        tiles[FACING + h] = (2 + k, rows[h], HALF - k, None)
    for b in range(HALF):
        tiles[OUT_IN + b] = (inward, rows[0], at[b], None)
        tiles[IN_OUT + b] = (outward, rows[1], at[b], None)
        tiles[IN_IN + b] = (inward, rows[1], at[b], None)
    return tiles


def pack_kernel(n_col, sent, first, count, place_ref, pattern_ref, own_hbm, nb_hbm, out, *rest):
    sems = rest[-1]
    tiles = half_tiles(place_ref[0], place_ref[1], n_col, own_hbm.shape[1], sent)
    copies = []
    for i in range(count):
        direction, row, at, _ = tiles[first + i]
        source = own_hbm.at[row, at] if direction is None else nb_hbm.at[direction, row, at]
        copies.append(pltpu.make_async_copy(source, out.at[i], sems.at[i]))
    for copy in copies:
        copy.start()
    for i in range(count):
        direction, row, at, weight = tiles[first + i]
        copies[i].wait()
        if direction is not None:
            scale = pattern_ref[row, at, direction].astype(jnp.float32)
            out[i] = out[i] * (scale if weight is None else scale * weight)
    if not sent:
        for h in range(ROWS):
            rest[0][h] = out[SIDE_B + h * HALF]


def block_of(refs, sizes, slot):
    for ref, size in zip(refs, sizes):
        if slot < size:
            return lambda g, n: ref[slot, g:g + n, :]
        slot -= size


def half_block(halves, i, slot):
    return block_of(halves[i], SPLIT[i], slot)


def tile_terms(halves, j, b):
    i, h = ORIGIN[j]
    terms = [(OWN + h * HALF + b, (j, b))]
    if h == 0:
        terms.append((OUT_IN + b, ((1, 2)[i], b)))
    else:
        terms.append((IN_OUT + b, ((0, 3)[i], b)))
        terms.append((IN_IN + b, ((2, 1)[i], b)))
    terms.append(((SIDE_A if b == 0 else SIDE_B) + h * HALF + b, (j, 1 - b)))
    return [(half_block(halves, i, slot), at) for slot, at in terms]


def halo_block(halves, j, b):
    i, h = ORIGIN[j]
    return half_block(halves, i, (SIDE_B if b == 0 else SIDE_A) + h * HALF + b)


def facing_block(halves, beyond_0, first_b, j, b):
    i, h = ORIGIN[j]
    if b == 1:
        return half_block(halves, i, FACING + h)
    if i == 0:
        return lambda g, n: beyond_0[h, g:g + n, :]
    start = 2 * N + h * first_b.shape[1]
    return lambda g, n: first_b[start + g:start + g + n, :]


def matvec(terms, chunk=32):
    width = terms[0][1].shape[1]
    lane = lax.broadcasted_iota(jnp.int32, (chunk, width), 1)
    sub = lax.broadcasted_iota(jnp.int32, (chunk, width), 0)
    spread = jnp.zeros((chunk, width), jnp.float32)
    for g in range(0, width, chunk):
        acc = None
        for block, vec in terms:
            part = block(g, chunk) * vec
            acc = part if acc is None else acc + part
        total = jnp.sum(acc, axis=1, keepdims=True)
        spread = jnp.where(lane == sub + g, total, spread)
    return jnp.sum(spread, axis=0, keepdims=True)


def row_of(x, j, b):
    i = j * HALF + b
    return x[i:i + 1]


def inner_product(f, halves):
    return jnp.concatenate(
        [matvec([(block, row_of(f, *at)) for block, at in tile_terms(halves, j, b)]) for j, b in TILES], axis=0
    )


def messages(f, g):
    return [
        jnp.concatenate([row_of(x, j, b) for x in (f, g) for j in order], axis=0)
        for b, order in ((1, range(N)[::-1]), (0, range(N)))
    ]


def ahead(first, sweep, f, q, residue, capacity, injected):
    if first:
        return injected - q
    return residue - STRIDES[sweep] * (q + capacity * f) + MOMENTA[sweep + 1] * f


def small_part(small, index):
    keep, recv = small
    n = ROWS * HALF
    i = index * n
    return jnp.concatenate([keep[i:i + n, :], recv[i + HALF:i + n, :], recv[i:i + HALF, :]], axis=0)


def start_kernel(keep, recv_0, recv_1, small_keep, small_recv, msg_a, msg_b, q_out):
    small = (small_keep, small_recv)
    halves = ((keep,), (recv_0, recv_1))
    f = small_part(small, INITIAL)
    q = inner_product(f, halves)
    q_out[...] = q
    msg_a[...], to_b = messages(f, ahead(True, 0, f, q, None, None, small_part(small, 0)))
    msg_b[:2 * N, :] = to_b
    width = f.shape[1]
    for h in range(ROWS):
        start = 2 * N + h * width
        msg_b[start:start + width, :] = recv_0[SIDE_B + h * HALF]


def small_kernel(place_ref, arrived, capacity, initial, keep, send, injected):
    y, col = place_ref[0], place_ref[1]
    tiles, frames = injected.shape
    _, cols, width = capacity.shape
    slots = (arrived.shape[1] - width) // frames
    for t in range(tiles):
        total = jnp.zeros((arrived.shape[0], frames), jnp.float32)
        for k in range(slots):
            feeds = arrived[:, slots * frames + k:slots * frames + k + 1] == float(t)
            total = total + jnp.where(feeds, 1.0, 0.0) * arrived[:, k * frames:(k + 1) * frames]
        injected[t:t + 1, :] = jnp.sum(total, axis=0, keepdims=True)
    for sent, out in ((0, keep), (1, send)):
        parity = (y + col + sent) % 2
        for h in range(ROWS):
            row = y if h == 0 else 1 - y
            for b in range(HALF):
                at = b + parity * (cols - 1 - 2 * b)
                currents = injected[pl.ds(row * cols + at, 1), :]
                parts = [currents[:, n * width:(n + 1) * width] for n in range(STEPS)]
                parts += [x[row, pl.ds(at, 1), :] for x in (capacity, initial)]
                for n, part in enumerate(parts):
                    i = n * ROWS * HALF + h * HALF + b
                    out[i:i + 1, :] = part


def beside_kernel(begin, keep, recv_0, recv_1, beyond_0, first_b, got_a, q_ref, *refs):
    halves = ((keep,), (recv_0, recv_1))
    response_out, q_out = refs[-2:]
    f = small_part(refs[:2], INITIAL) if begin else refs[0][...]
    q = q_ref[...]
    response, total = [], []
    for j, b in TILES:
        response.append(matvec([(facing_block(halves, beyond_0, first_b, j, b), row_of(f, j, b))]))
        mine = row_of(q, j, b)
        if b == 1:
            mine = mine + matvec([(halo_block(halves, j, b), got_a[j:j + 1, :])])
        total.append(mine)
    response_out[...] = jnp.concatenate(response, axis=0)
    q_out[...] = jnp.concatenate(total, axis=0)


def pair_kernel(instant, pair, last, keep, recv_0, recv_1, small_keep, small_recv, got_a, got_b, response_ref, q_ref,
                *refs):
    small = (small_keep, small_recv)
    halves = ((keep,), (recv_0, recv_1))
    first = pair == 0
    capacity = small_part(small, CAPACITY)
    q, response = q_ref[...], response_ref[...]
    if first and instant == 0:
        f = small_part(small, INITIAL)
    else:
        f, refs = refs[0][...], refs[1:]
    if not first:
        residue, estimate, refs = refs[0][...], refs[1][...], refs[2:]
    got = (got_b, got_a)
    sweep = 2 * pair - 1

    product = []
    for j, b in TILES:
        mine = row_of(q, j, b)
        if b == 0:
            mine = mine + matvec([(halo_block(halves, j, b), got_b[j:j + 1, :])])
        product.append(mine)
    product = jnp.concatenate(product, axis=0)
    if first:
        residue = small_part(small, instant) - product
        f2 = residue
        estimate = f + STRIDES[0] * f2
        scale = 1.0
    else:
        residue = residue - STRIDES[sweep] * (product + capacity * f)
        f2 = residue + MOMENTA[sweep + 1] * f
        estimate = estimate + STRIDES[sweep + 1] * f2
        scale = STRIDES[sweep]

    outs = []
    for j, b in TILES:
        beside = got[b][N + j:N + j + 1, :] - scale * row_of(response, j, b)
        terms = [(block, row_of(f2, *at)) for block, at in tile_terms(halves, j, b)]
        outs.append(matvec(terms + [(halo_block(halves, j, b), beside)]))
    sweep = 2 * pair
    residue = residue - STRIDES[sweep] * (jnp.concatenate(outs, axis=0) + capacity * f2)
    f3 = residue + MOMENTA[sweep + 1] * f2
    estimate = estimate + STRIDES[sweep + 1] * f3
    closing = sweep + 2 == ITERS
    if closing:
        f3 = estimate
    f_out, refs = refs[0], refs[1:]
    f_out[...] = f3
    if last:
        return
    q = inner_product(f3, halves)
    q_out, msg_a, msg_b = refs[:3]
    q_out[...] = q
    upcoming = small_part(small, instant + 1) if closing else None
    msg_a[...], msg_b[...] = messages(f3, ahead(closing, sweep + 1, f3, q, residue, capacity, upcoming))
    if not closing:
        refs[3][...] = residue
        refs[4][...] = estimate


def shards_chain(own_block, neighbor_block, pattern, capacity, initial, currents, slot_tile):
    tile_rows, tile_cols, width = initial.shape
    n_col = lax.axis_size("col")
    row, col = lax.axis_index("row"), lax.axis_index("col")
    both = ("row", "col")
    swap = [(0, 1), (1, 0)]
    b_pairs = []
    for unit in range(1, 2 * n_col - 1, 2):
        ends = [r * n_col + c for r, c in (unit_device(unit, n_col), unit_device(unit + 1, n_col))]
        b_pairs += [tuple(ends), tuple(ends[::-1])]
    parity = (row + col) % 2

    vmem = pl.BlockSpec(memory_space=pltpu.VMEM)
    smem = pl.BlockSpec(memory_space=pltpu.SMEM)
    hbm = pl.BlockSpec(memory_space=pltpu.HBM)
    limit = pltpu.CompilerParams(vmem_limit_bytes=16 * 2**20)
    place = jnp.stack([row, col]).astype(jnp.int32)
    blocks = [pltpu.with_memory_space_constraint(x, pltpu.HBM) for x in (pattern, own_block, neighbor_block)]

    def pack(sent, first, count, extra=()):
        return pl.pallas_call(
            functools.partial(pack_kernel, n_col, sent, first, count),
            out_shape=[jax.ShapeDtypeStruct((n, width, width), jnp.float32) for n in (count, *extra)],
            in_specs=[smem, smem, hbm, hbm],
            out_specs=[vmem] * (1 + len(extra)),
            scratch_shapes=[pltpu.SemaphoreType.DMA((count,))],
            compiler_params=limit,
            name="pack",
        )(place, *blocks)

    recv = []
    for first, count in ((0, SPLIT[1][0]), SPLIT[1]):
        (send,) = pack(1, first, count)
        recv.append(lax.ppermute(send, "row", swap))
    keep, facing_0 = pack(0, 0, PACKED, (ROWS,))

    def beside(currents, slot_tile, capacity, initial, facing_0):
        beyond_0 = lax.ppermute(facing_0, both, b_pairs)
        slots, frames = currents.shape[3:]
        names = jnp.pad(slot_tile.astype(jnp.float32), ((0, 0), (0, 0), (0, 0), (0, width - slots)))
        packed = jnp.concatenate([currents.reshape(*currents.shape[:3], slots * frames), names], axis=3)
        arrived = lax.all_to_all(packed, "col", split_axis=2, concat_axis=1, tiled=True)
        half = jax.ShapeDtypeStruct(((STEPS + 2) * ROWS * HALF, width), jnp.float32)
        small, send = pl.pallas_call(
            small_kernel,
            out_shape=(half, half),
            in_specs=[smem, vmem, vmem, vmem],
            out_specs=(vmem, vmem),
            scratch_shapes=[pltpu.VMEM((tile_rows * tile_cols, frames), jnp.float32)],
            compiler_params=limit,
            name="small",
        )(place, arrived.reshape(n_col, slots * frames + width), capacity, initial)
        return small, lax.ppermute(send, "row", swap), beyond_0

    *small, beyond_0 = lax.cond(
        row < lax.axis_size("row"),
        beside,
        lambda currents, slot_tile, capacity, initial, facing_0: (
            *jnp.zeros((2, (STEPS + 2) * ROWS * HALF, width), jnp.float32), facing_0
        ),
        currents, slot_tile, capacity, initial, facing_0,
    )

    shape = jax.ShapeDtypeStruct((N * HALF, width), jnp.float32)
    halves = (keep, *recv)

    def call(body, outs, blocks, *ins):
        return pl.pallas_call(
            body,
            out_shape=outs,
            in_specs=[vmem] * len(ins),
            out_specs=(vmem,) * len(outs),
            compiler_params=limit,
            cost_estimate=pl.CostEstimate(flops=2 * blocks * width * width, bytes_accessed=blocks * width * width * 4,
                                          transcendentals=0),
            name="pair",
        )(*ins)

    first_shape = jax.ShapeDtypeStruct((2 * N + ROWS * width, width), jnp.float32)
    msg_a, msg_b, q = call(start_kernel, (shape, first_shape, shape), 28, *halves, *small)
    field, first_b = (), None
    frames = []
    state = ()
    for instant in range(STEPS):
        for pair in range(ITERS // 2):
            closing = pair + 1 == ITERS // 2
            last = closing and instant + 1 == STEPS
            got_b = lax.ppermute(msg_b, both, b_pairs)
            got_a = lax.ppermute(msg_a, "row", swap)
            if first_b is None:
                first_b = got_b
            response, q = call(functools.partial(beside_kernel, not field), (shape,) * 2, 12, *halves, beyond_0, first_b,
                               got_a, q, *(field or small))
            out = call(functools.partial(pair_kernel, instant, pair, last), (shape,) * (1 if last else 4 if closing else 6),
                       68, *halves, *small, got_a, got_b, response, q, *field, *state)
            field = out[:1]
            if not last:
                q, msg_a, msg_b = out[1:4]
                state = out[4:]
        frames.append(out[0])

    done = jnp.stack(frames).reshape(STEPS, N, HALF, width)
    got = lax.ppermute(jnp.flip(done[:, ROWS:], 1), "row", swap)
    mine = done[:, :ROWS]
    unit_0, unit_1 = jnp.where(parity == 1, got, mine), jnp.where(parity == 1, mine, got)
    done = jnp.concatenate([unit_0, jnp.flip(unit_1, 2)], axis=2)
    return jnp.where(row == 1, jnp.flip(done, 1), done)


def solution(mesh):
    rows, cols = mesh.shape["row"], mesh.shape["col"]
    return jax.shard_map(
        shards_chain if rows == 2 else shards_general,
        mesh=mesh,
        in_specs=(
            P("row", "col", None, None),
            P(None, "row", "col", None, None),
            P("row", "col", None),
            P("row", "col", None),
            P("row", "col", None),
            P("row", "col", None, None, None),
            P("row", "col", None, None),
        ),
        out_specs=P(None, "row", "col", None),
        check_vma=False,
    )
```

```python
import functools

import jax
import jax.numpy as jnp
from jax import lax
from jax.experimental import pallas as pl
from jax.experimental.pallas import tpu as pltpu
from jax.sharding import PartitionSpec as P

STEPS = 4
ITERS = 8

spec_center = 6.4
spec_radius = 5.6


def schedule():
    strides, momenta = [], []
    stride = 1.0 / spec_center
    for sweep in range(ITERS):
        if sweep == 0:
            momentum = 0.0
        else:
            if sweep == 1:
                momentum = 0.5 * (spec_radius * stride) ** 2
            else:
                momentum = (spec_radius * stride / 2.0) ** 2
            stride = 1.0 / (spec_center - momentum / stride)
        strides.append(stride)
        momenta.append(momentum)
    return strides, momenta


STRIDES, MOMENTA = schedule()


def swap_pairs(count, first):
    pairs = []
    for i in range(first, count - 1, 2):
        pairs += [(i, i + 1), (i + 1, i)]
    return pairs


def exchange(field):
    arrived = []
    for axis in ("row", "col"):
        count = lax.axis_size(axis)
        for first in (0, 1):
            pairs = swap_pairs(count, first)
            arrived.append(lax.ppermute(field, axis, pairs) if pairs else None)
    return arrived


def beside(field, halos, odd_row, odd_col, cols):
    tiles = field.shape[0]
    row_a, row_b, col_a, col_b = halos
    zero = jnp.zeros_like(field)
    row_a, row_b, col_a, col_b = [zero if h is None else h for h in (row_a, row_b, col_a, col_b)]
    above = jnp.where(odd_row, row_a, row_b)
    below = jnp.where(odd_row, row_b, row_a)
    west = jnp.where(odd_col, col_a, col_b)
    east = jnp.where(odd_col, col_b, col_a)
    up = jnp.concatenate([above[tiles - cols:], field[: tiles - cols]], axis=0)
    down = jnp.concatenate([field[cols:], below[:cols]], axis=0)
    column = lax.broadcasted_iota(jnp.int32, field.shape, 0) % cols
    rolled = jnp.concatenate([field[tiles - 1:], field[: tiles - 1]], axis=0)
    west_edge = jnp.concatenate([west[cols - 1:], west[: cols - 1]], axis=0)
    left = jnp.where(column == 0, west_edge, rolled)
    rolled = jnp.concatenate([field[1:], field[:1]], axis=0)
    east_edge = jnp.concatenate([east[tiles - cols + 1:], east[: tiles - cols + 1]], axis=0)
    right = jnp.where(column == cols - 1, east_edge, rolled)
    return up, down, left, right


def blocks_times(field, around, own_ref, nb_ref):
    tiles, width = field.shape
    chunk = 32
    lane = lax.broadcasted_iota(jnp.int32, (chunk, width), 1)
    sub = lax.broadcasted_iota(jnp.int32, (chunk, width), 0)
    outs = []
    for t in range(tiles):
        vecs = [f[t:t + 1] for f in around]
        mine = field[t:t + 1]
        spread = jnp.zeros((chunk, width), jnp.float32)
        for g in range(0, width, chunk):
            acc = own_ref[t, g:g + chunk, :] * mine
            for n, vec in enumerate(vecs):
                acc = acc + nb_ref[n, t, g:g + chunk, :] * vec
            total = jnp.sum(acc, axis=1, keepdims=True)
            spread = jnp.where(lane == sub + g, total, spread)
        outs.append(jnp.sum(spread, axis=0, keepdims=True))
    return jnp.concatenate(outs, axis=0)


def kernel(sweep, cols, present, flags, own_ref, nb_ref, weights, *refs):
    n_halo = sum(present)
    halo_refs, refs = refs[:n_halo], refs[n_halo:]
    halo_iter = iter(halo_refs)
    halos = [next(halo_iter)[...] if p else None for p in present]
    odd_row, odd_col = flags[0] == 1, flags[1] == 1
    field_ref, refs = refs[0], refs[1:]
    field = field_ref[...]
    around = beside(field, halos, odd_row, odd_col, cols)
    around = [f * weights[n] for n, f in enumerate(around)]
    product = blocks_times(field, around, own_ref, nb_ref)
    if sweep < 0:
        injected, search_out, residue_out, estimate_out = refs
        residue = injected[...] - product
        search_out[...] = residue
        residue_out[...] = residue
        estimate_out[...] = field + STRIDES[0] * residue
    else:
        capacity, residue_in, estimate_in = refs[:3]
        outs = refs[3:]
        residue = residue_in[...] - STRIDES[sweep] * (product + capacity[...] * field)
        search = residue + MOMENTA[sweep + 1] * field
        estimate = estimate_in[...] + STRIDES[sweep + 1] * search
        if sweep + 2 < ITERS:
            outs[0][...] = search
            outs[1][...] = residue
            outs[2][...] = estimate
        else:
            outs[0][...] = estimate


def collect(currents, slot_tile, tiles, width):
    slots, frames = currents.shape[3:]
    names = jnp.pad(slot_tile.astype(jnp.float32)[..., None, :],
                    ((0, 0), (0, 0), (0, 0), (0, 0), (0, frames - slots)))
    packed = jnp.concatenate([currents, names], axis=3)
    arrived = lax.all_to_all(packed, "col", split_axis=2, concat_axis=1, tiled=True)[0, :, 0]
    targets = arrived[:, slots, :slots]
    chooser = (targets[..., None] == jnp.arange(tiles, dtype=jnp.float32)).astype(jnp.float32)
    injected = jnp.einsum("skt,skf->tf", chooser, arrived[:, :slots], precision=lax.Precision.HIGHEST)
    return injected.reshape(tiles, STEPS, width)


def shards_general(own_block, neighbor_block, pattern, capacity, initial, currents, slot_tile):
    tile_rows, tile_cols, width = initial.shape
    tiles = tile_rows * tile_cols
    flags = jnp.stack([lax.axis_index("row") % 2, lax.axis_index("col") % 2]).astype(jnp.int32)

    voltage = initial.reshape(tiles, width)
    halos = exchange(voltage)

    injected = collect(currents, slot_tile, tiles, width)

    own = own_block.reshape(tiles, width, width)
    nb = neighbor_block.reshape(4, tiles, width, width)
    weights = jnp.broadcast_to(
        jnp.moveaxis(pattern.reshape(tiles, 4), 1, 0).astype(jnp.float32)[..., None], (4, tiles, width)
    )
    cap = capacity.reshape(tiles, width)
    shape = jax.ShapeDtypeStruct((tiles, width), jnp.float32)
    vmem = pl.BlockSpec(memory_space=pltpu.VMEM)
    smem = pl.BlockSpec(memory_space=pltpu.SMEM)

    def call(sweep, halos, *state):
        present = tuple(h is not None for h in halos)
        ins = (flags, own, nb, weights) + tuple(h for h in halos if h is not None) + state
        n_out = 1 if sweep + 2 == ITERS else 3
        out = pl.pallas_call(
            functools.partial(kernel, sweep, tile_cols, present),
            out_shape=(shape,) * n_out,
            in_specs=[smem] + [vmem] * (len(ins) - 1),
            out_specs=(vmem,) * n_out,
            compiler_params=pltpu.CompilerParams(vmem_limit_bytes=8 * 2**20),
            cost_estimate=pl.CostEstimate(flops=2 * 5 * tiles * width * width, bytes_accessed=5 * tiles * width * width * 4,
                                          transcendentals=0),
            name="couple",
        )(*ins)
        return out

    frames_out = []
    for instant in range(STEPS):
        if instant:
            halos = exchange(voltage)
        search, residue, estimate = call(-1, halos, voltage, injected[:, instant])
        for sweep in range(ITERS - 1):
            halos = exchange(search)
            out = call(sweep, halos, search, cap, residue, estimate)
            if sweep + 2 < ITERS:
                search, residue, estimate = out
            else:
                (voltage,) = out
        frames_out.append(voltage)
    return jnp.stack(frames_out).reshape(STEPS, tile_rows, tile_cols, width)


ROWS, HALF = 2, 2
N = 2 * ROWS
OWN, SIDE_A, SIDE_B, OUT_IN, IN_OUT, IN_IN, FACING, PACKED = 0, 4, 8, 12, 14, 16, 18, 20
TILES = [(j, b) for j in range(N) for b in range(HALF)]
ORIGIN = [(0, 0), (0, 1), (1, 1), (1, 0)]
CAPACITY, INITIAL = STEPS, STEPS + 1
SPLIT = ((PACKED,), (OUT_IN, PACKED - OUT_IN))


def unit_device(unit, n_col):
    col = unit // 2
    return (unit + col) % 2, col


def half_tiles(y, col, n_col, cols, sent):
    k = (y + col + sent) % 2
    rows = (y, 1 - y)
    inward, outward = 1 - y, y
    at = [b + k * (cols - 1 - 2 * b) for b in range(HALF)]
    inside = jnp.where(col == k * (n_col - 1), 0.0, 1.0)
    tiles = [None] * PACKED
    for h in range(ROWS):
        for b in range(HALF):
            tiles[OWN + h * HALF + b] = (None, rows[h], at[b], None)
            tiles[SIDE_A + h * HALF + b] = (3 - k, rows[h], at[b], None)
            tiles[SIDE_B + h * HALF + b] = (2 + k, rows[h], at[b], inside if b == 0 else None)
        tiles[FACING + h] = (2 + k, rows[h], HALF - k, None)
    for b in range(HALF):
        tiles[OUT_IN + b] = (inward, rows[0], at[b], None)
        tiles[IN_OUT + b] = (outward, rows[1], at[b], None)
        tiles[IN_IN + b] = (inward, rows[1], at[b], None)
    return tiles


def pack_kernel(n_col, sent, first, count, place_ref, pattern_ref, own_hbm, nb_hbm, out, *rest):
    sems = rest[-1]
    tiles = half_tiles(place_ref[0], place_ref[1], n_col, own_hbm.shape[1], sent)
    copies = []
    for i in range(count):
        direction, row, at, _ = tiles[first + i]
        source = own_hbm.at[row, at] if direction is None else nb_hbm.at[direction, row, at]
        copies.append(pltpu.make_async_copy(source, out.at[i], sems.at[i]))
    for copy in copies:
        copy.start()
    for i in range(count):
        direction, row, at, weight = tiles[first + i]
        copies[i].wait()
        if direction is not None:
            scale = pattern_ref[row, at, direction].astype(jnp.float32)
            out[i] = out[i] * (scale if weight is None else scale * weight)
    if not sent:
        for h in range(ROWS):
            rest[0][h] = out[SIDE_B + h * HALF]


def block_of(refs, sizes, slot):
    for ref, size in zip(refs, sizes):
        if slot < size:
            return lambda g, n: ref[slot, g:g + n, :]
        slot -= size


def half_block(halves, i, slot):
    return block_of(halves[i], SPLIT[i], slot)


def tile_terms(halves, j, b):
    i, h = ORIGIN[j]
    terms = [(OWN + h * HALF + b, (j, b))]
    if h == 0:
        terms.append((OUT_IN + b, ((1, 2)[i], b)))
    else:
        terms.append((IN_OUT + b, ((0, 3)[i], b)))
        terms.append((IN_IN + b, ((2, 1)[i], b)))
    terms.append(((SIDE_A if b == 0 else SIDE_B) + h * HALF + b, (j, 1 - b)))
    return [(half_block(halves, i, slot), at) for slot, at in terms]


def halo_block(halves, j, b):
    i, h = ORIGIN[j]
    return half_block(halves, i, (SIDE_B if b == 0 else SIDE_A) + h * HALF + b)


def facing_block(halves, beyond_0, first_b, j, b):
    i, h = ORIGIN[j]
    if b == 1:
        return half_block(halves, i, FACING + h)
    if i == 0:
        return lambda g, n: beyond_0[h, g:g + n, :]
    start = 2 * N + h * first_b.shape[1]
    return lambda g, n: first_b[start + g:start + g + n, :]


def matvec(terms, chunk=32):
    width = terms[0][1].shape[1]
    lane = lax.broadcasted_iota(jnp.int32, (chunk, width), 1)
    sub = lax.broadcasted_iota(jnp.int32, (chunk, width), 0)
    spread = jnp.zeros((chunk, width), jnp.float32)
    for g in range(0, width, chunk):
        acc = None
        for block, vec in terms:
            part = block(g, chunk) * vec
            acc = part if acc is None else acc + part
        total = jnp.sum(acc, axis=1, keepdims=True)
        spread = jnp.where(lane == sub + g, total, spread)
    return jnp.sum(spread, axis=0, keepdims=True)


def row_of(x, j, b):
    i = j * HALF + b
    return x[i:i + 1]


def inner_product(f, halves):
    return jnp.concatenate(
        [matvec([(block, row_of(f, *at)) for block, at in tile_terms(halves, j, b)]) for j, b in TILES], axis=0
    )


def messages(f, g):
    return [
        jnp.concatenate([row_of(x, j, b) for x in (f, g) for j in order], axis=0)
        for b, order in ((1, range(N)[::-1]), (0, range(N)))
    ]


def ahead(first, sweep, f, q, residue, capacity, injected):
    if first:
        return injected - q
    return residue - STRIDES[sweep] * (q + capacity * f) + MOMENTA[sweep + 1] * f


def small_part(small, index):
    n = N * HALF
    return small[index * n:(index + 1) * n, :]


def start_kernel(keep, recv_0, recv_1, small_keep, small_recv, msg_a, msg_b, q_out, small):
    n = ROWS * HALF
    for i in range(0, small_keep.shape[0], n):
        small[2 * i:2 * i + n, :] = small_keep[i:i + n, :]
        small[2 * i + n:2 * i + n + HALF, :] = small_recv[i + HALF:i + n, :]
        small[2 * i + n + HALF:2 * i + 2 * n, :] = small_recv[i:i + HALF, :]
    halves = ((keep,), (recv_0, recv_1))
    f = small_part(small, INITIAL)
    q = inner_product(f, halves)
    q_out[...] = q
    msg_a[...], to_b = messages(f, ahead(True, 0, f, q, None, None, small_part(small, 0)))
    msg_b[:2 * N, :] = to_b
    width = f.shape[1]
    for h in range(ROWS):
        start = 2 * N + h * width
        msg_b[start:start + width, :] = recv_0[SIDE_B + h * HALF]


def small_kernel(place_ref, arrived, capacity, initial, keep, send, injected):
    y, col = place_ref[0], place_ref[1]
    tiles, frames = injected.shape
    _, cols, width = capacity.shape
    slots = (arrived.shape[1] - width) // frames
    for t in range(tiles):
        total = jnp.zeros((arrived.shape[0], frames), jnp.float32)
        for k in range(slots):
            feeds = arrived[:, slots * frames + k:slots * frames + k + 1] == float(t)
            total = total + jnp.where(feeds, 1.0, 0.0) * arrived[:, k * frames:(k + 1) * frames]
        injected[t:t + 1, :] = jnp.sum(total, axis=0, keepdims=True)
    for sent, out in ((0, keep), (1, send)):
        parity = (y + col + sent) % 2
        for h in range(ROWS):
            row = y if h == 0 else 1 - y
            for b in range(HALF):
                at = b + parity * (cols - 1 - 2 * b)
                currents = injected[pl.ds(row * cols + at, 1), :]
                parts = [currents[:, n * width:(n + 1) * width] for n in range(STEPS)]
                parts += [x[row, pl.ds(at, 1), :] for x in (capacity, initial)]
                for n, part in enumerate(parts):
                    i = n * ROWS * HALF + h * HALF + b
                    out[i:i + 1, :] = part


def beside_kernel(begin, keep, recv_0, recv_1, beyond_0, first_b, got_a, q_ref, *refs):
    halves = ((keep,), (recv_0, recv_1))
    response_out, q_out = refs[-2:]
    f = small_part(refs[0], INITIAL) if begin else refs[0][...]
    q = q_ref[...]
    response, total = [], []
    for j, b in TILES:
        response.append(matvec([(facing_block(halves, beyond_0, first_b, j, b), row_of(f, j, b))]))
        mine = row_of(q, j, b)
        if b == 1:
            mine = mine + matvec([(halo_block(halves, j, b), got_a[j:j + 1, :])])
        total.append(mine)
    response_out[...] = jnp.concatenate(response, axis=0)
    q_out[...] = jnp.concatenate(total, axis=0)


def pair_kernel(instant, pair, last, keep, recv_0, recv_1, small, got_a, got_b, response_ref, q_ref, *refs):
    halves = ((keep,), (recv_0, recv_1))
    first = pair == 0
    capacity = small_part(small, CAPACITY)
    q, response = q_ref[...], response_ref[...]
    if first and instant == 0:
        f = small_part(small, INITIAL)
    else:
        f, refs = refs[0][...], refs[1:]
    if not first:
        residue, estimate, refs = refs[0][...], refs[1][...], refs[2:]
    got = (got_b, got_a)
    sweep = 2 * pair - 1

    product = []
    for j, b in TILES:
        mine = row_of(q, j, b)
        if b == 0:
            mine = mine + matvec([(halo_block(halves, j, b), got_b[j:j + 1, :])])
        product.append(mine)
    product = jnp.concatenate(product, axis=0)
    if first:
        residue = small_part(small, instant) - product
        f2 = residue
        estimate = f + STRIDES[0] * f2
        scale = 1.0
    else:
        residue = residue - STRIDES[sweep] * (product + capacity * f)
        f2 = residue + MOMENTA[sweep + 1] * f
        estimate = estimate + STRIDES[sweep + 1] * f2
        scale = STRIDES[sweep]

    outs = []
    for j, b in TILES:
        beside = got[b][N + j:N + j + 1, :] - scale * row_of(response, j, b)
        terms = [(block, row_of(f2, *at)) for block, at in tile_terms(halves, j, b)]
        outs.append(matvec(terms + [(halo_block(halves, j, b), beside)]))
    sweep = 2 * pair
    residue = residue - STRIDES[sweep] * (jnp.concatenate(outs, axis=0) + capacity * f2)
    f3 = residue + MOMENTA[sweep + 1] * f2
    estimate = estimate + STRIDES[sweep + 1] * f3
    closing = sweep + 2 == ITERS
    if closing:
        f3 = estimate
    f_out, refs = refs[0], refs[1:]
    f_out[...] = f3
    if last:
        return
    q = inner_product(f3, halves)
    q_out, msg_a, msg_b = refs[:3]
    q_out[...] = q
    upcoming = small_part(small, instant + 1) if closing else None
    msg_a[...], msg_b[...] = messages(f3, ahead(closing, sweep + 1, f3, q, residue, capacity, upcoming))
    if not closing:
        refs[3][...] = residue
        refs[4][...] = estimate


def shards_chain(own_block, neighbor_block, pattern, capacity, initial, currents, slot_tile):
    tile_rows, tile_cols, width = initial.shape
    n_col = lax.axis_size("col")
    row, col = lax.axis_index("row"), lax.axis_index("col")
    both = ("row", "col")
    swap = [(0, 1), (1, 0)]
    b_pairs = []
    for unit in range(1, 2 * n_col - 1, 2):
        ends = [r * n_col + c for r, c in (unit_device(unit, n_col), unit_device(unit + 1, n_col))]
        b_pairs += [tuple(ends), tuple(ends[::-1])]
    parity = (row + col) % 2

    vmem = pl.BlockSpec(memory_space=pltpu.VMEM)
    smem = pl.BlockSpec(memory_space=pltpu.SMEM)
    hbm = pl.BlockSpec(memory_space=pltpu.HBM)
    limit = pltpu.CompilerParams(vmem_limit_bytes=16 * 2**20)
    place = jnp.stack([row, col]).astype(jnp.int32)
    blocks = [pltpu.with_memory_space_constraint(x, pltpu.HBM) for x in (pattern, own_block, neighbor_block)]

    def pack(sent, first, count, extra=()):
        return pl.pallas_call(
            functools.partial(pack_kernel, n_col, sent, first, count),
            out_shape=[jax.ShapeDtypeStruct((n, width, width), jnp.float32) for n in (count, *extra)],
            in_specs=[smem, smem, hbm, hbm],
            out_specs=[vmem] * (1 + len(extra)),
            scratch_shapes=[pltpu.SemaphoreType.DMA((count,))],
            compiler_params=limit,
            name="pack",
        )(place, *blocks)

    recv = []
    for first, count in ((0, SPLIT[1][0]), SPLIT[1]):
        (send,) = pack(1, first, count)
        recv.append(lax.ppermute(send, "row", swap))
    keep, facing_0 = pack(0, 0, PACKED, (ROWS,))

    def beside(currents, slot_tile, capacity, initial, facing_0):
        beyond_0 = lax.ppermute(facing_0, both, b_pairs)
        slots, frames = currents.shape[3:]
        names = jnp.pad(slot_tile.astype(jnp.float32), ((0, 0), (0, 0), (0, 0), (0, width - slots)))
        packed = jnp.concatenate([currents.reshape(*currents.shape[:3], slots * frames), names], axis=3)
        arrived = lax.all_to_all(packed, "col", split_axis=2, concat_axis=1, tiled=True)
        half = jax.ShapeDtypeStruct(((STEPS + 2) * ROWS * HALF, width), jnp.float32)
        small, send = pl.pallas_call(
            small_kernel,
            out_shape=(half, half),
            in_specs=[smem, vmem, vmem, vmem],
            out_specs=(vmem, vmem),
            scratch_shapes=[pltpu.VMEM((tile_rows * tile_cols, frames), jnp.float32)],
            compiler_params=limit,
            name="small",
        )(place, arrived.reshape(n_col, slots * frames + width), capacity, initial)
        return small, lax.ppermute(send, "row", swap), beyond_0

    *small, beyond_0 = lax.cond(
        row < lax.axis_size("row"),
        beside,
        lambda currents, slot_tile, capacity, initial, facing_0: (
            *jnp.zeros((2, (STEPS + 2) * ROWS * HALF, width), jnp.float32), facing_0
        ),
        currents, slot_tile, capacity, initial, facing_0,
    )

    shape = jax.ShapeDtypeStruct((N * HALF, width), jnp.float32)
    halves = (keep, *recv)

    def call(body, outs, blocks, *ins):
        return pl.pallas_call(
            body,
            out_shape=outs,
            in_specs=[vmem] * len(ins),
            out_specs=(vmem,) * len(outs),
            compiler_params=limit,
            cost_estimate=pl.CostEstimate(flops=2 * blocks * width * width, bytes_accessed=blocks * width * width * 4,
                                          transcendentals=0),
            name="pair",
        )(*ins)

    first_shape = jax.ShapeDtypeStruct((2 * N + ROWS * width, width), jnp.float32)
    unit_small = jax.ShapeDtypeStruct(((STEPS + 2) * N * HALF, width), jnp.float32)
    msg_a, msg_b, q, small = call(start_kernel, (shape, first_shape, shape, unit_small), 28, *halves, *small)
    field, first_b = (), None
    frames = []
    state = ()
    for instant in range(STEPS):
        for pair in range(ITERS // 2):
            closing = pair + 1 == ITERS // 2
            last = closing and instant + 1 == STEPS
            got_b = lax.ppermute(msg_b, both, b_pairs)
            got_a = lax.ppermute(msg_a, "row", swap)
            if first_b is None:
                first_b = got_b
            response, q = call(functools.partial(beside_kernel, not field), (shape,) * 2, 12, *halves, beyond_0, first_b,
                               got_a, q, *(field or (small,)))
            out = call(functools.partial(pair_kernel, instant, pair, last), (shape,) * (1 if last else 4 if closing else 6),
                       68, *halves, small, got_a, got_b, response, q, *field, *state)
            field = out[:1]
            if not last:
                q, msg_a, msg_b = out[1:4]
                state = out[4:]
        frames.append(out[0])

    done = jnp.stack(frames).reshape(STEPS, N, HALF, width)
    got = lax.ppermute(jnp.flip(done[:, ROWS:], 1), "row", swap)
    mine = done[:, :ROWS]
    unit_0, unit_1 = jnp.where(parity == 1, got, mine), jnp.where(parity == 1, mine, got)
    done = jnp.concatenate([unit_0, jnp.flip(unit_1, 2)], axis=2)
    return jnp.where(row == 1, jnp.flip(done, 1), done)


def solution(mesh):
    rows, cols = mesh.shape["row"], mesh.shape["col"]
    return jax.shard_map(
        shards_chain if rows == 2 else shards_general,
        mesh=mesh,
        in_specs=(
            P("row", "col", None, None),
            P(None, "row", "col", None, None),
            P("row", "col", None),
            P("row", "col", None),
            P("row", "col", None),
            P("row", "col", None, None, None),
            P("row", "col", None, None),
        ),
        out_specs=P(None, "row", "col", None),
        check_vma=False,
    )
```

```python
import functools

import jax
import jax.numpy as jnp
from jax import lax
from jax.experimental import pallas as pl
from jax.experimental.pallas import tpu as pltpu
from jax.sharding import PartitionSpec as P

STEPS = 4
ITERS = 8

spec_center = 6.4
spec_radius = 5.6


def schedule():
    strides, momenta = [], []
    stride = 1.0 / spec_center
    for sweep in range(ITERS):
        if sweep == 0:
            momentum = 0.0
        else:
            if sweep == 1:
                momentum = 0.5 * (spec_radius * stride) ** 2
            else:
                momentum = (spec_radius * stride / 2.0) ** 2
            stride = 1.0 / (spec_center - momentum / stride)
        strides.append(stride)
        momenta.append(momentum)
    return strides, momenta


STRIDES, MOMENTA = schedule()


def swap_pairs(count, first):
    pairs = []
    for i in range(first, count - 1, 2):
        pairs += [(i, i + 1), (i + 1, i)]
    return pairs


def exchange(field):
    arrived = []
    for axis in ("row", "col"):
        count = lax.axis_size(axis)
        for first in (0, 1):
            pairs = swap_pairs(count, first)
            arrived.append(lax.ppermute(field, axis, pairs) if pairs else None)
    return arrived


def beside(field, halos, odd_row, odd_col, cols):
    tiles = field.shape[0]
    row_a, row_b, col_a, col_b = halos
    zero = jnp.zeros_like(field)
    row_a, row_b, col_a, col_b = [zero if h is None else h for h in (row_a, row_b, col_a, col_b)]
    above = jnp.where(odd_row, row_a, row_b)
    below = jnp.where(odd_row, row_b, row_a)
    west = jnp.where(odd_col, col_a, col_b)
    east = jnp.where(odd_col, col_b, col_a)
    up = jnp.concatenate([above[tiles - cols:], field[: tiles - cols]], axis=0)
    down = jnp.concatenate([field[cols:], below[:cols]], axis=0)
    column = lax.broadcasted_iota(jnp.int32, field.shape, 0) % cols
    rolled = jnp.concatenate([field[tiles - 1:], field[: tiles - 1]], axis=0)
    west_edge = jnp.concatenate([west[cols - 1:], west[: cols - 1]], axis=0)
    left = jnp.where(column == 0, west_edge, rolled)
    rolled = jnp.concatenate([field[1:], field[:1]], axis=0)
    east_edge = jnp.concatenate([east[tiles - cols + 1:], east[: tiles - cols + 1]], axis=0)
    right = jnp.where(column == cols - 1, east_edge, rolled)
    return up, down, left, right


def blocks_times(field, around, own_ref, nb_ref):
    tiles, width = field.shape
    chunk = 32
    lane = lax.broadcasted_iota(jnp.int32, (chunk, width), 1)
    sub = lax.broadcasted_iota(jnp.int32, (chunk, width), 0)
    outs = []
    for t in range(tiles):
        vecs = [f[t:t + 1] for f in around]
        mine = field[t:t + 1]
        spread = jnp.zeros((chunk, width), jnp.float32)
        for g in range(0, width, chunk):
            acc = own_ref[t, g:g + chunk, :] * mine
            for n, vec in enumerate(vecs):
                acc = acc + nb_ref[n, t, g:g + chunk, :] * vec
            total = jnp.sum(acc, axis=1, keepdims=True)
            spread = jnp.where(lane == sub + g, total, spread)
        outs.append(jnp.sum(spread, axis=0, keepdims=True))
    return jnp.concatenate(outs, axis=0)


def kernel(sweep, cols, present, flags, own_ref, nb_ref, weights, *refs):
    n_halo = sum(present)
    halo_refs, refs = refs[:n_halo], refs[n_halo:]
    halo_iter = iter(halo_refs)
    halos = [next(halo_iter)[...] if p else None for p in present]
    odd_row, odd_col = flags[0] == 1, flags[1] == 1
    field_ref, refs = refs[0], refs[1:]
    field = field_ref[...]
    around = beside(field, halos, odd_row, odd_col, cols)
    around = [f * weights[n] for n, f in enumerate(around)]
    product = blocks_times(field, around, own_ref, nb_ref)
    if sweep < 0:
        injected, search_out, residue_out, estimate_out = refs
        residue = injected[...] - product
        search_out[...] = residue
        residue_out[...] = residue
        estimate_out[...] = field + STRIDES[0] * residue
    else:
        capacity, residue_in, estimate_in = refs[:3]
        outs = refs[3:]
        residue = residue_in[...] - STRIDES[sweep] * (product + capacity[...] * field)
        search = residue + MOMENTA[sweep + 1] * field
        estimate = estimate_in[...] + STRIDES[sweep + 1] * search
        if sweep + 2 < ITERS:
            outs[0][...] = search
            outs[1][...] = residue
            outs[2][...] = estimate
        else:
            outs[0][...] = estimate


def collect(currents, slot_tile, tiles, width):
    slots, frames = currents.shape[3:]
    names = jnp.pad(slot_tile.astype(jnp.float32)[..., None, :],
                    ((0, 0), (0, 0), (0, 0), (0, 0), (0, frames - slots)))
    packed = jnp.concatenate([currents, names], axis=3)
    arrived = lax.all_to_all(packed, "col", split_axis=2, concat_axis=1, tiled=True)[0, :, 0]
    targets = arrived[:, slots, :slots]
    chooser = (targets[..., None] == jnp.arange(tiles, dtype=jnp.float32)).astype(jnp.float32)
    injected = jnp.einsum("skt,skf->tf", chooser, arrived[:, :slots], precision=lax.Precision.HIGHEST)
    return injected.reshape(tiles, STEPS, width)


def shards_general(own_block, neighbor_block, pattern, capacity, initial, currents, slot_tile):
    tile_rows, tile_cols, width = initial.shape
    tiles = tile_rows * tile_cols
    flags = jnp.stack([lax.axis_index("row") % 2, lax.axis_index("col") % 2]).astype(jnp.int32)

    voltage = initial.reshape(tiles, width)
    halos = exchange(voltage)

    injected = collect(currents, slot_tile, tiles, width)

    own = own_block.reshape(tiles, width, width)
    nb = neighbor_block.reshape(4, tiles, width, width)
    weights = jnp.broadcast_to(
        jnp.moveaxis(pattern.reshape(tiles, 4), 1, 0).astype(jnp.float32)[..., None], (4, tiles, width)
    )
    cap = capacity.reshape(tiles, width)
    shape = jax.ShapeDtypeStruct((tiles, width), jnp.float32)
    vmem = pl.BlockSpec(memory_space=pltpu.VMEM)
    smem = pl.BlockSpec(memory_space=pltpu.SMEM)

    def call(sweep, halos, *state):
        present = tuple(h is not None for h in halos)
        ins = (flags, own, nb, weights) + tuple(h for h in halos if h is not None) + state
        n_out = 1 if sweep + 2 == ITERS else 3
        out = pl.pallas_call(
            functools.partial(kernel, sweep, tile_cols, present),
            out_shape=(shape,) * n_out,
            in_specs=[smem] + [vmem] * (len(ins) - 1),
            out_specs=(vmem,) * n_out,
            compiler_params=pltpu.CompilerParams(vmem_limit_bytes=8 * 2**20),
            cost_estimate=pl.CostEstimate(flops=2 * 5 * tiles * width * width, bytes_accessed=5 * tiles * width * width * 4,
                                          transcendentals=0),
            name="couple",
        )(*ins)
        return out

    frames_out = []
    for instant in range(STEPS):
        if instant:
            halos = exchange(voltage)
        search, residue, estimate = call(-1, halos, voltage, injected[:, instant])
        for sweep in range(ITERS - 1):
            halos = exchange(search)
            out = call(sweep, halos, search, cap, residue, estimate)
            if sweep + 2 < ITERS:
                search, residue, estimate = out
            else:
                (voltage,) = out
        frames_out.append(voltage)
    return jnp.stack(frames_out).reshape(STEPS, tile_rows, tile_cols, width)


ROWS, HALF = 2, 2
N = 2 * ROWS
OWN, SIDE_A, SIDE_B, OUT_IN, IN_OUT, IN_IN, FACING, PACKED = 0, 4, 8, 12, 14, 16, 18, 20
TILES = [(j, b) for j in range(N) for b in range(HALF)]
ORIGIN = [(0, 0), (0, 1), (1, 1), (1, 0)]
CAPACITY, INITIAL = STEPS, STEPS + 1
SPLIT = ((PACKED,), (OUT_IN, FACING - OUT_IN))


def unit_device(unit, n_col):
    col = unit // 2
    return (unit + col) % 2, col


def half_tiles(y, col, n_col, cols, sent):
    k = (y + col + sent) % 2
    rows = (y, 1 - y)
    inward, outward = 1 - y, y
    at = [b + k * (cols - 1 - 2 * b) for b in range(HALF)]
    inside = jnp.where(col == k * (n_col - 1), 0.0, 1.0)
    tiles = [None] * PACKED
    for h in range(ROWS):
        for b in range(HALF):
            tiles[OWN + h * HALF + b] = (None, rows[h], at[b], None)
            tiles[SIDE_A + h * HALF + b] = (3 - k, rows[h], at[b], None)
            tiles[SIDE_B + h * HALF + b] = (2 + k, rows[h], at[b], inside if b == 0 else None)
        tiles[FACING + h] = (2 + k, rows[h], HALF - k, None)
    for b in range(HALF):
        tiles[OUT_IN + b] = (inward, rows[0], at[b], None)
        tiles[IN_OUT + b] = (outward, rows[1], at[b], None)
        tiles[IN_IN + b] = (inward, rows[1], at[b], None)
    return tiles


def pack_kernel(n_col, sent, first, count, place_ref, pattern_ref, own_hbm, nb_hbm, out, *rest):
    sems = rest[-1]
    tiles = half_tiles(place_ref[0], place_ref[1], n_col, own_hbm.shape[1], sent)
    copies = []
    for i in range(count):
        direction, row, at, _ = tiles[first + i]
        source = own_hbm.at[row, at] if direction is None else nb_hbm.at[direction, row, at]
        copies.append(pltpu.make_async_copy(source, out.at[i], sems.at[i]))
    for copy in copies:
        copy.start()
    for i in range(count):
        direction, row, at, weight = tiles[first + i]
        copies[i].wait()
        if direction is not None:
            scale = pattern_ref[row, at, direction].astype(jnp.float32)
            out[i] = out[i] * (scale if weight is None else scale * weight)
    if not sent:
        for h in range(ROWS):
            rest[0][h] = out[SIDE_B + h * HALF]


def block_of(refs, sizes, slot):
    for ref, size in zip(refs, sizes):
        if slot < size:
            return lambda g, n: ref[slot, g:g + n, :]
        slot -= size


def half_block(halves, i, slot):
    return block_of(halves[i], SPLIT[i], slot)


def tile_terms(halves, j, b):
    i, h = ORIGIN[j]
    terms = [(OWN + h * HALF + b, (j, b))]
    if h == 0:
        terms.append((OUT_IN + b, ((1, 2)[i], b)))
    else:
        terms.append((IN_OUT + b, ((0, 3)[i], b)))
        terms.append((IN_IN + b, ((2, 1)[i], b)))
    terms.append(((SIDE_A if b == 0 else SIDE_B) + h * HALF + b, (j, 1 - b)))
    return [(half_block(halves, i, slot), at) for slot, at in terms]


def halo_block(halves, j, b):
    i, h = ORIGIN[j]
    return half_block(halves, i, (SIDE_B if b == 0 else SIDE_A) + h * HALF + b)


def facing_block(halves, beyond_0, first_a, first_b, j, b):
    i, h = ORIGIN[j]
    if i == 0:
        return half_block(halves, i, FACING + h) if b == 1 else lambda g, n: beyond_0[h, g:g + n, :]
    first = first_a if b == 1 else first_b
    start = 2 * N + h * first.shape[1]
    return lambda g, n: first[start + g:start + g + n, :]


def matvec(terms, chunk=32):
    width = terms[0][1].shape[1]
    lane = lax.broadcasted_iota(jnp.int32, (chunk, width), 1)
    sub = lax.broadcasted_iota(jnp.int32, (chunk, width), 0)
    spread = jnp.zeros((chunk, width), jnp.float32)
    for g in range(0, width, chunk):
        acc = None
        for block, vec in terms:
            part = block(g, chunk) * vec
            acc = part if acc is None else acc + part
        total = jnp.sum(acc, axis=1, keepdims=True)
        spread = jnp.where(lane == sub + g, total, spread)
    return jnp.sum(spread, axis=0, keepdims=True)


def row_of(x, j, b):
    i = j * HALF + b
    return x[i:i + 1]


def inner_product(f, halves):
    return jnp.concatenate(
        [matvec([(block, row_of(f, *at)) for block, at in tile_terms(halves, j, b)]) for j, b in TILES], axis=0
    )


def messages(f, g):
    return [
        jnp.concatenate([row_of(x, j, b) for x in (f, g) for j in order], axis=0)
        for b, order in ((1, range(N)[::-1]), (0, range(N)))
    ]


def ahead(first, sweep, f, q, residue, capacity, injected):
    if first:
        return injected - q
    return residue - STRIDES[sweep] * (q + capacity * f) + MOMENTA[sweep + 1] * f


def small_part(small, index):
    n = N * HALF
    return small[index * n:(index + 1) * n, :]


def start_kernel(keep, recv_0, recv_1, small_keep, small_recv, msg_a, msg_b, q_out, small):
    n = ROWS * HALF
    for i in range(0, small_keep.shape[0], n):
        small[2 * i:2 * i + n, :] = small_keep[i:i + n, :]
        small[2 * i + n:2 * i + n + HALF, :] = small_recv[i + HALF:i + n, :]
        small[2 * i + n + HALF:2 * i + 2 * n, :] = small_recv[i:i + HALF, :]
    halves = ((keep,), (recv_0, recv_1))
    f = small_part(small, INITIAL)
    q = inner_product(f, halves)
    q_out[...] = q
    to_a, to_b = messages(f, ahead(True, 0, f, q, None, None, small_part(small, 0)))
    msg_a[:2 * N, :], msg_b[:2 * N, :] = to_a, to_b
    width = f.shape[1]
    for h in range(ROWS):
        start = 2 * N + h * width
        msg_a[start:start + width, :] = keep[SIDE_A + h * HALF + 1]
        msg_b[start:start + width, :] = recv_0[SIDE_B + h * HALF]


def by_target_kernel(currents, slot_tile, out):
    targets, slots, frames = currents.shape
    width = out.shape[2] - slots * frames
    names = slot_tile[...].astype(jnp.float32)
    names = jnp.concatenate([names, jnp.zeros((targets, width - slots), jnp.float32)], axis=1)
    for d in range(targets):
        for k in range(slots):
            out[d, :, k * frames:(k + 1) * frames] = currents[d, k:k + 1, :]
        out[d, :, slots * frames:] = names[d:d + 1, :]


def small_kernel(place_ref, arrived, capacity, initial, keep, send, injected):
    y, col = place_ref[0], place_ref[1]
    tiles, frames = injected.shape
    _, cols, width = capacity.shape
    slots = (arrived.shape[1] - width) // frames
    for t in range(tiles):
        total = jnp.zeros((arrived.shape[0], frames), jnp.float32)
        for k in range(slots):
            feeds = arrived[:, slots * frames + k:slots * frames + k + 1] == float(t)
            total = total + jnp.where(feeds, 1.0, 0.0) * arrived[:, k * frames:(k + 1) * frames]
        injected[t:t + 1, :] = jnp.sum(total, axis=0, keepdims=True)
    for sent, out in ((0, keep), (1, send)):
        parity = (y + col + sent) % 2
        for h in range(ROWS):
            row = y if h == 0 else 1 - y
            for b in range(HALF):
                at = b + parity * (cols - 1 - 2 * b)
                currents = injected[pl.ds(row * cols + at, 1), :]
                parts = [currents[:, n * width:(n + 1) * width] for n in range(STEPS)]
                parts += [x[row, pl.ds(at, 1), :] for x in (capacity, initial)]
                for n, part in enumerate(parts):
                    i = n * ROWS * HALF + h * HALF + b
                    out[i:i + 1, :] = part


def beside_kernel(begin, keep, recv_0, recv_1, beyond_0, first_a, first_b, got_a, q_ref, *refs):
    halves = ((keep,), (recv_0, recv_1))
    response_out, q_out = refs[-2:]
    f = small_part(refs[0], INITIAL) if begin else refs[0][...]
    q = q_ref[...]
    response, total = [], []
    for j, b in TILES:
        response.append(matvec([(facing_block(halves, beyond_0, first_a, first_b, j, b), row_of(f, j, b))]))
        mine = row_of(q, j, b)
        if b == 1:
            mine = mine + matvec([(halo_block(halves, j, b), got_a[j:j + 1, :])])
        total.append(mine)
    response_out[...] = jnp.concatenate(response, axis=0)
    q_out[...] = jnp.concatenate(total, axis=0)


def pair_kernel(instant, pair, last, keep, recv_0, recv_1, small, got_a, got_b, response_ref, q_ref, *refs):
    halves = ((keep,), (recv_0, recv_1))
    first = pair == 0
    capacity = small_part(small, CAPACITY)
    q, response = q_ref[...], response_ref[...]
    if first and instant == 0:
        f = small_part(small, INITIAL)
    else:
        f, refs = refs[0][...], refs[1:]
    if not first:
        residue, estimate, refs = refs[0][...], refs[1][...], refs[2:]
    got = (got_b, got_a)
    sweep = 2 * pair - 1

    product = []
    for j, b in TILES:
        mine = row_of(q, j, b)
        if b == 0:
            mine = mine + matvec([(halo_block(halves, j, b), got_b[j:j + 1, :])])
        product.append(mine)
    product = jnp.concatenate(product, axis=0)
    if first:
        residue = small_part(small, instant) - product
        f2 = residue
        estimate = f + STRIDES[0] * f2
        scale = 1.0
    else:
        residue = residue - STRIDES[sweep] * (product + capacity * f)
        f2 = residue + MOMENTA[sweep + 1] * f
        estimate = estimate + STRIDES[sweep + 1] * f2
        scale = STRIDES[sweep]

    outs = []
    for j, b in TILES:
        beside = got[b][N + j:N + j + 1, :] - scale * row_of(response, j, b)
        terms = [(block, row_of(f2, *at)) for block, at in tile_terms(halves, j, b)]
        outs.append(matvec(terms + [(halo_block(halves, j, b), beside)]))
    sweep = 2 * pair
    residue = residue - STRIDES[sweep] * (jnp.concatenate(outs, axis=0) + capacity * f2)
    f3 = residue + MOMENTA[sweep + 1] * f2
    estimate = estimate + STRIDES[sweep + 1] * f3
    closing = sweep + 2 == ITERS
    if closing:
        f3 = estimate
    f_out, refs = refs[0], refs[1:]
    f_out[...] = f3
    if last:
        return
    q = inner_product(f3, halves)
    q_out, msg_a, msg_b = refs[:3]
    q_out[...] = q
    upcoming = small_part(small, instant + 1) if closing else None
    msg_a[...], msg_b[...] = messages(f3, ahead(closing, sweep + 1, f3, q, residue, capacity, upcoming))
    if not closing:
        refs[3][...] = residue
        refs[4][...] = estimate


def shards_chain(own_block, neighbor_block, pattern, capacity, initial, currents, slot_tile):
    tile_rows, tile_cols, width = initial.shape
    n_col = lax.axis_size("col")
    row, col = lax.axis_index("row"), lax.axis_index("col")
    both = ("row", "col")
    swap = [(0, 1), (1, 0)]
    b_pairs = []
    for unit in range(1, 2 * n_col - 1, 2):
        ends = [r * n_col + c for r, c in (unit_device(unit, n_col), unit_device(unit + 1, n_col))]
        b_pairs += [tuple(ends), tuple(ends[::-1])]
    parity = (row + col) % 2

    vmem = pl.BlockSpec(memory_space=pltpu.VMEM)
    smem = pl.BlockSpec(memory_space=pltpu.SMEM)
    hbm = pl.BlockSpec(memory_space=pltpu.HBM)
    limit = pltpu.CompilerParams(vmem_limit_bytes=16 * 2**20)
    place = jnp.stack([row, col]).astype(jnp.int32)
    blocks = [pltpu.with_memory_space_constraint(x, pltpu.HBM) for x in (pattern, own_block, neighbor_block)]

    def pack(sent, first, count, extra=()):
        return pl.pallas_call(
            functools.partial(pack_kernel, n_col, sent, first, count),
            out_shape=[jax.ShapeDtypeStruct((n, width, width), jnp.float32) for n in (count, *extra)],
            in_specs=[smem, smem, hbm, hbm],
            out_specs=[vmem] * (1 + len(extra)),
            scratch_shapes=[pltpu.SemaphoreType.DMA((count,))],
            compiler_params=limit,
            name="pack",
        )(place, *blocks)

    recv = []
    for first, count in ((0, SPLIT[1][0]), SPLIT[1]):
        (send,) = pack(1, first, count)
        recv.append(lax.ppermute(send, "row", swap))
    keep, facing_0 = pack(0, 0, PACKED, (ROWS,))

    def beside(currents, slot_tile, capacity, initial, facing_0):
        beyond_0 = lax.ppermute(facing_0, both, b_pairs)
        slots, frames = currents.shape[3:]
        by_target = pl.pallas_call(
            by_target_kernel,
            out_shape=jax.ShapeDtypeStruct((n_col, 1, slots * frames + width), jnp.float32),
            in_specs=[vmem, vmem],
            out_specs=vmem,
            compiler_params=limit,
            name="by_target",
        )(currents.reshape(n_col, slots, frames), slot_tile.reshape(n_col, slots))
        arrived = lax.all_to_all(by_target, "col", split_axis=0, concat_axis=0, tiled=True)
        half = jax.ShapeDtypeStruct(((STEPS + 2) * ROWS * HALF, width), jnp.float32)
        small, send = pl.pallas_call(
            small_kernel,
            out_shape=(half, half),
            in_specs=[smem, vmem, vmem, vmem],
            out_specs=(vmem, vmem),
            scratch_shapes=[pltpu.VMEM((tile_rows * tile_cols, frames), jnp.float32)],
            compiler_params=limit,
            name="small",
        )(place, arrived.reshape(n_col, slots * frames + width), capacity, initial)
        return small, lax.ppermute(send, "row", swap), beyond_0

    *small, beyond_0 = lax.cond(
        row < lax.axis_size("row"),
        beside,
        lambda currents, slot_tile, capacity, initial, facing_0: (
            *jnp.zeros((2, (STEPS + 2) * ROWS * HALF, width), jnp.float32), facing_0
        ),
        currents, slot_tile, capacity, initial, facing_0,
    )

    shape = jax.ShapeDtypeStruct((N * HALF, width), jnp.float32)
    halves = (keep, *recv)

    def call(body, outs, blocks, *ins):
        return pl.pallas_call(
            body,
            out_shape=outs,
            in_specs=[vmem] * len(ins),
            out_specs=(vmem,) * len(outs),
            compiler_params=limit,
            cost_estimate=pl.CostEstimate(flops=2 * blocks * width * width, bytes_accessed=blocks * width * width * 4,
                                          transcendentals=0),
            name="pair",
        )(*ins)

    first_shape = jax.ShapeDtypeStruct((2 * N + ROWS * width, width), jnp.float32)
    unit_small = jax.ShapeDtypeStruct(((STEPS + 2) * N * HALF, width), jnp.float32)
    msg_a, msg_b, q, small = call(start_kernel, (first_shape, first_shape, shape, unit_small), 28, *halves, *small)
    field, first_a, first_b = (), None, None
    frames = []
    state = ()
    for instant in range(STEPS):
        for pair in range(ITERS // 2):
            closing = pair + 1 == ITERS // 2
            last = closing and instant + 1 == STEPS
            got_b = lax.ppermute(msg_b, both, b_pairs)
            got_a = lax.ppermute(msg_a, "row", swap)
            if first_b is None:
                first_a, first_b = got_a, got_b
            response, q = call(functools.partial(beside_kernel, not field), (shape,) * 2, 12, *halves, beyond_0, first_a, first_b,
                               got_a, q, *(field or (small,)))
            out = call(functools.partial(pair_kernel, instant, pair, last), (shape,) * (1 if last else 4 if closing else 6),
                       68, *halves, small, got_a, got_b, response, q, *field, *state)
            field = out[:1]
            if not last:
                q, msg_a, msg_b = out[1:4]
                state = out[4:]
        frames.append(out[0])

    done = jnp.stack(frames).reshape(STEPS, N, HALF, width)
    got = lax.ppermute(jnp.flip(done[:, ROWS:], 1), "row", swap)
    mine = done[:, :ROWS]
    unit_0, unit_1 = jnp.where(parity == 1, got, mine), jnp.where(parity == 1, mine, got)
    done = jnp.concatenate([unit_0, jnp.flip(unit_1, 2)], axis=2)
    return jnp.where(row == 1, jnp.flip(done, 1), done)


def solution(mesh):
    rows, cols = mesh.shape["row"], mesh.shape["col"]
    return jax.shard_map(
        shards_chain if rows == 2 else shards_general,
        mesh=mesh,
        in_specs=(
            P("row", "col", None, None),
            P(None, "row", "col", None, None),
            P("row", "col", None),
            P("row", "col", None),
            P("row", "col", None),
            P("row", "col", None, None, None),
            P("row", "col", None, None),
        ),
        out_specs=P(None, "row", "col", None),
        check_vma=False,
    )
```

```python
import functools

import jax
import jax.numpy as jnp
from jax import lax
from jax.experimental import pallas as pl
from jax.experimental.pallas import tpu as pltpu
from jax.sharding import PartitionSpec as P

STEPS = 4
ITERS = 8

spec_center = 6.4
spec_radius = 5.6


def schedule():
    strides, momenta = [], []
    stride = 1.0 / spec_center
    for sweep in range(ITERS):
        if sweep == 0:
            momentum = 0.0
        else:
            if sweep == 1:
                momentum = 0.5 * (spec_radius * stride) ** 2
            else:
                momentum = (spec_radius * stride / 2.0) ** 2
            stride = 1.0 / (spec_center - momentum / stride)
        strides.append(stride)
        momenta.append(momentum)
    return strides, momenta


STRIDES, MOMENTA = schedule()


def swap_pairs(count, first):
    pairs = []
    for i in range(first, count - 1, 2):
        pairs += [(i, i + 1), (i + 1, i)]
    return pairs


def exchange(field):
    arrived = []
    for axis in ("row", "col"):
        count = lax.axis_size(axis)
        for first in (0, 1):
            pairs = swap_pairs(count, first)
            arrived.append(lax.ppermute(field, axis, pairs) if pairs else None)
    return arrived


def beside(field, halos, odd_row, odd_col, cols):
    tiles = field.shape[0]
    row_a, row_b, col_a, col_b = halos
    zero = jnp.zeros_like(field)
    row_a, row_b, col_a, col_b = [zero if h is None else h for h in (row_a, row_b, col_a, col_b)]
    above = jnp.where(odd_row, row_a, row_b)
    below = jnp.where(odd_row, row_b, row_a)
    west = jnp.where(odd_col, col_a, col_b)
    east = jnp.where(odd_col, col_b, col_a)
    up = jnp.concatenate([above[tiles - cols:], field[: tiles - cols]], axis=0)
    down = jnp.concatenate([field[cols:], below[:cols]], axis=0)
    column = lax.broadcasted_iota(jnp.int32, field.shape, 0) % cols
    rolled = jnp.concatenate([field[tiles - 1:], field[: tiles - 1]], axis=0)
    west_edge = jnp.concatenate([west[cols - 1:], west[: cols - 1]], axis=0)
    left = jnp.where(column == 0, west_edge, rolled)
    rolled = jnp.concatenate([field[1:], field[:1]], axis=0)
    east_edge = jnp.concatenate([east[tiles - cols + 1:], east[: tiles - cols + 1]], axis=0)
    right = jnp.where(column == cols - 1, east_edge, rolled)
    return up, down, left, right


def blocks_times(field, around, own_ref, nb_ref):
    tiles, width = field.shape
    chunk = 32
    lane = lax.broadcasted_iota(jnp.int32, (chunk, width), 1)
    sub = lax.broadcasted_iota(jnp.int32, (chunk, width), 0)
    outs = []
    for t in range(tiles):
        vecs = [f[t:t + 1] for f in around]
        mine = field[t:t + 1]
        spread = jnp.zeros((chunk, width), jnp.float32)
        for g in range(0, width, chunk):
            acc = own_ref[t, g:g + chunk, :] * mine
            for n, vec in enumerate(vecs):
                acc = acc + nb_ref[n, t, g:g + chunk, :] * vec
            total = jnp.sum(acc, axis=1, keepdims=True)
            spread = jnp.where(lane == sub + g, total, spread)
        outs.append(jnp.sum(spread, axis=0, keepdims=True))
    return jnp.concatenate(outs, axis=0)


def kernel(sweep, cols, present, flags, own_ref, nb_ref, weights, *refs):
    n_halo = sum(present)
    halo_refs, refs = refs[:n_halo], refs[n_halo:]
    halo_iter = iter(halo_refs)
    halos = [next(halo_iter)[...] if p else None for p in present]
    odd_row, odd_col = flags[0] == 1, flags[1] == 1
    field_ref, refs = refs[0], refs[1:]
    field = field_ref[...]
    around = beside(field, halos, odd_row, odd_col, cols)
    around = [f * weights[n] for n, f in enumerate(around)]
    product = blocks_times(field, around, own_ref, nb_ref)
    if sweep < 0:
        injected, search_out, residue_out, estimate_out = refs
        residue = injected[...] - product
        search_out[...] = residue
        residue_out[...] = residue
        estimate_out[...] = field + STRIDES[0] * residue
    else:
        capacity, residue_in, estimate_in = refs[:3]
        outs = refs[3:]
        residue = residue_in[...] - STRIDES[sweep] * (product + capacity[...] * field)
        search = residue + MOMENTA[sweep + 1] * field
        estimate = estimate_in[...] + STRIDES[sweep + 1] * search
        if sweep + 2 < ITERS:
            outs[0][...] = search
            outs[1][...] = residue
            outs[2][...] = estimate
        else:
            outs[0][...] = estimate


def collect(currents, slot_tile, tiles, width):
    slots, frames = currents.shape[3:]
    names = jnp.pad(slot_tile.astype(jnp.float32)[..., None, :],
                    ((0, 0), (0, 0), (0, 0), (0, 0), (0, frames - slots)))
    packed = jnp.concatenate([currents, names], axis=3)
    arrived = lax.all_to_all(packed, "col", split_axis=2, concat_axis=1, tiled=True)[0, :, 0]
    targets = arrived[:, slots, :slots]
    chooser = (targets[..., None] == jnp.arange(tiles, dtype=jnp.float32)).astype(jnp.float32)
    injected = jnp.einsum("skt,skf->tf", chooser, arrived[:, :slots], precision=lax.Precision.HIGHEST)
    return injected.reshape(tiles, STEPS, width)


def shards_general(own_block, neighbor_block, pattern, capacity, initial, currents, slot_tile):
    tile_rows, tile_cols, width = initial.shape
    tiles = tile_rows * tile_cols
    flags = jnp.stack([lax.axis_index("row") % 2, lax.axis_index("col") % 2]).astype(jnp.int32)

    voltage = initial.reshape(tiles, width)
    halos = exchange(voltage)

    injected = collect(currents, slot_tile, tiles, width)

    own = own_block.reshape(tiles, width, width)
    nb = neighbor_block.reshape(4, tiles, width, width)
    weights = jnp.broadcast_to(
        jnp.moveaxis(pattern.reshape(tiles, 4), 1, 0).astype(jnp.float32)[..., None], (4, tiles, width)
    )
    cap = capacity.reshape(tiles, width)
    shape = jax.ShapeDtypeStruct((tiles, width), jnp.float32)
    vmem = pl.BlockSpec(memory_space=pltpu.VMEM)
    smem = pl.BlockSpec(memory_space=pltpu.SMEM)

    def call(sweep, halos, *state):
        present = tuple(h is not None for h in halos)
        ins = (flags, own, nb, weights) + tuple(h for h in halos if h is not None) + state
        n_out = 1 if sweep + 2 == ITERS else 3
        out = pl.pallas_call(
            functools.partial(kernel, sweep, tile_cols, present),
            out_shape=(shape,) * n_out,
            in_specs=[smem] + [vmem] * (len(ins) - 1),
            out_specs=(vmem,) * n_out,
            compiler_params=pltpu.CompilerParams(vmem_limit_bytes=8 * 2**20),
            cost_estimate=pl.CostEstimate(flops=2 * 5 * tiles * width * width, bytes_accessed=5 * tiles * width * width * 4,
                                          transcendentals=0),
            name="couple",
        )(*ins)
        return out

    frames_out = []
    for instant in range(STEPS):
        if instant:
            halos = exchange(voltage)
        search, residue, estimate = call(-1, halos, voltage, injected[:, instant])
        for sweep in range(ITERS - 1):
            halos = exchange(search)
            out = call(sweep, halos, search, cap, residue, estimate)
            if sweep + 2 < ITERS:
                search, residue, estimate = out
            else:
                (voltage,) = out
        frames_out.append(voltage)
    return jnp.stack(frames_out).reshape(STEPS, tile_rows, tile_cols, width)


ROWS, HALF = 2, 2
N = 2 * ROWS
OWN, SIDE_A, SIDE_B, OUT_IN, IN_OUT, IN_IN, FACING, PACKED = 0, 4, 8, 12, 14, 16, 18, 20
TILES = [(j, b) for j in range(N) for b in range(HALF)]
ORIGIN = [(0, 0), (0, 1), (1, 1), (1, 0)]
CAPACITY, INITIAL = STEPS, STEPS + 1
SPLIT = ((PACKED,), (OUT_IN, FACING - OUT_IN))


def unit_device(unit, n_col):
    col = unit // 2
    return (unit + col) % 2, col


def half_tiles(y, col, n_col, cols, sent):
    k = (y + col + sent) % 2
    rows = (y, 1 - y)
    inward, outward = 1 - y, y
    at = [b + k * (cols - 1 - 2 * b) for b in range(HALF)]
    inside = jnp.where(col == k * (n_col - 1), 0.0, 1.0)
    tiles = [None] * PACKED
    for h in range(ROWS):
        for b in range(HALF):
            tiles[OWN + h * HALF + b] = (None, rows[h], at[b], None)
            tiles[SIDE_A + h * HALF + b] = (3 - k, rows[h], at[b], None)
            tiles[SIDE_B + h * HALF + b] = (2 + k, rows[h], at[b], inside if b == 0 else None)
        tiles[FACING + h] = (2 + k, rows[h], HALF - k, None)
    for b in range(HALF):
        tiles[OUT_IN + b] = (inward, rows[0], at[b], None)
        tiles[IN_OUT + b] = (outward, rows[1], at[b], None)
        tiles[IN_IN + b] = (inward, rows[1], at[b], None)
    return tiles


def pack_kernel(n_col, sent, first, count, place_ref, pattern_ref, own_hbm, nb_hbm, out, *rest):
    sems = rest[-1]
    tiles = half_tiles(place_ref[0], place_ref[1], n_col, own_hbm.shape[1], sent)
    copies = []
    for i in range(count):
        direction, row, at, _ = tiles[first + i]
        source = own_hbm.at[row, at] if direction is None else nb_hbm.at[direction, row, at]
        copies.append(pltpu.make_async_copy(source, out.at[i], sems.at[i]))
    for copy in copies:
        copy.start()
    for i in range(count):
        direction, row, at, weight = tiles[first + i]
        copies[i].wait()
        if direction is not None:
            scale = pattern_ref[row, at, direction].astype(jnp.float32)
            out[i] = out[i] * (scale if weight is None else scale * weight)
    if not sent:
        for h in range(ROWS):
            rest[0][h] = out[SIDE_B + h * HALF]


def block_of(refs, sizes, slot):
    for ref, size in zip(refs, sizes):
        if slot < size:
            return lambda g, n: ref[slot, g:g + n, :]
        slot -= size


def half_block(halves, i, slot):
    return block_of(halves[i], SPLIT[i], slot)


def tile_terms(halves, j, b):
    i, h = ORIGIN[j]
    terms = [(OWN + h * HALF + b, (j, b))]
    if h == 0:
        terms.append((OUT_IN + b, ((1, 2)[i], b)))
    else:
        terms.append((IN_OUT + b, ((0, 3)[i], b)))
        terms.append((IN_IN + b, ((2, 1)[i], b)))
    terms.append(((SIDE_A if b == 0 else SIDE_B) + h * HALF + b, (j, 1 - b)))
    return [(half_block(halves, i, slot), at) for slot, at in terms]


def halo_block(halves, j, b):
    i, h = ORIGIN[j]
    return half_block(halves, i, (SIDE_B if b == 0 else SIDE_A) + h * HALF + b)


def facing_block(halves, beyond_0, first_a, first_b, j, b):
    i, h = ORIGIN[j]
    if i == 0:
        return half_block(halves, i, FACING + h) if b == 1 else lambda g, n: beyond_0[h, g:g + n, :]
    first = first_a if b == 1 else first_b
    start = 2 * N + h * first.shape[1]
    return lambda g, n: first[start + g:start + g + n, :]


def matvec(terms, chunk=32):
    width = terms[0][1].shape[1]
    lane = lax.broadcasted_iota(jnp.int32, (chunk, width), 1)
    sub = lax.broadcasted_iota(jnp.int32, (chunk, width), 0)
    spread = jnp.zeros((chunk, width), jnp.float32)
    for g in range(0, width, chunk):
        acc = None
        for block, vec in terms:
            part = block(g, chunk) * vec
            acc = part if acc is None else acc + part
        total = jnp.sum(acc, axis=1, keepdims=True)
        spread = jnp.where(lane == sub + g, total, spread)
    return jnp.sum(spread, axis=0, keepdims=True)


def row_of(x, j, b):
    i = j * HALF + b
    return x[i:i + 1]


def inner_product(f, halves):
    return jnp.concatenate(
        [matvec([(block, row_of(f, *at)) for block, at in tile_terms(halves, j, b)]) for j, b in TILES], axis=0
    )


def message(f, g, b):
    order = range(N)[::-1] if b == 1 else range(N)
    return jnp.concatenate([row_of(x, j, b) for x in (f, g) for j in order], axis=0)


def ahead(first, sweep, f, residue, capacity, injected):
    if first:
        return injected, 1.0
    return residue - STRIDES[sweep] * (capacity * f) + MOMENTA[sweep + 1] * f, STRIDES[sweep]


def small_part(small, index):
    n = N * HALF
    return small[index * n:(index + 1) * n, :]


def start_kernel(keep, recv_0, recv_1, small_keep, small_recv, msg_a, msg_b, q_out, small):
    n = ROWS * HALF
    for i in range(0, small_keep.shape[0], n):
        small[2 * i:2 * i + n, :] = small_keep[i:i + n, :]
        small[2 * i + n:2 * i + n + HALF, :] = small_recv[i + HALF:i + n, :]
        small[2 * i + n + HALF:2 * i + 2 * n, :] = small_recv[i:i + HALF, :]
    halves = ((keep,), (recv_0, recv_1))
    f = small_part(small, INITIAL)
    q = inner_product(f, halves)
    q_out[...] = q
    g = small_part(small, 0) - q
    msg_a[:2 * N, :], msg_b[:2 * N, :] = message(f, g, 1), message(f, g, 0)
    width = f.shape[1]
    for h in range(ROWS):
        start = 2 * N + h * width
        msg_a[start:start + width, :] = keep[SIDE_A + h * HALF + 1]
        msg_b[start:start + width, :] = recv_0[SIDE_B + h * HALF]


def by_target_kernel(currents, slot_tile, out):
    targets, slots, frames = currents.shape
    width = out.shape[2] - slots * frames
    names = slot_tile[...].astype(jnp.float32)
    names = jnp.concatenate([names, jnp.zeros((targets, width - slots), jnp.float32)], axis=1)
    for d in range(targets):
        for k in range(slots):
            out[d, :, k * frames:(k + 1) * frames] = currents[d, k:k + 1, :]
        out[d, :, slots * frames:] = names[d:d + 1, :]


def small_kernel(place_ref, arrived, capacity, initial, keep, send, injected):
    y, col = place_ref[0], place_ref[1]
    tiles, frames = injected.shape
    _, cols, width = capacity.shape
    slots = (arrived.shape[1] - width) // frames
    for t in range(tiles):
        total = jnp.zeros((arrived.shape[0], frames), jnp.float32)
        for k in range(slots):
            feeds = arrived[:, slots * frames + k:slots * frames + k + 1] == float(t)
            total = total + jnp.where(feeds, 1.0, 0.0) * arrived[:, k * frames:(k + 1) * frames]
        injected[t:t + 1, :] = jnp.sum(total, axis=0, keepdims=True)
    for sent, out in ((0, keep), (1, send)):
        parity = (y + col + sent) % 2
        for h in range(ROWS):
            row = y if h == 0 else 1 - y
            for b in range(HALF):
                at = b + parity * (cols - 1 - 2 * b)
                currents = injected[pl.ds(row * cols + at, 1), :]
                parts = [currents[:, n * width:(n + 1) * width] for n in range(STEPS)]
                parts += [x[row, pl.ds(at, 1), :] for x in (capacity, initial)]
                for n, part in enumerate(parts):
                    i = n * ROWS * HALF + h * HALF + b
                    out[i:i + 1, :] = part


def stacked(rows):
    return jnp.concatenate(rows, axis=0)


def responses(halves, beyond_0, first_a, first_b, f):
    return stacked([
        matvec([(facing_block(halves, beyond_0, first_a, first_b, j, b), row_of(f, j, b))]) for j, b in TILES
    ])


def response_kernel(keep, recv_0, recv_1, beyond_0, first_a, first_b, small, out):
    out[...] = responses(((keep,), (recv_0, recv_1)), beyond_0, first_a, first_b, small_part(small, INITIAL))


def to_a_kernel(factor, keep, recv_0, recv_1, beyond_0, first_a, first_b, f_ref, q_ref, base, response_out, q_out, msg_a):
    halves = ((keep,), (recv_0, recv_1))
    f, q = f_ref[...], q_ref[...]
    q = stacked([
        matvec([(block, row_of(f, *at)) for block, at in tile_terms(halves, j, b)]) if b == 1 else row_of(q, j, b)
        for j, b in TILES
    ])
    q_out[...] = q
    msg_a[...] = message(f, base[...] - factor * q, 1)
    response_out[...] = responses(halves, beyond_0, first_a, first_b, f)


def advance(instant, pair, small, product, f, residue):
    if pair == 0:
        residue = small_part(small, instant) - product
        return residue, residue, 1.0
    sweep = 2 * pair - 1
    residue = residue - STRIDES[sweep] * (product + small_part(small, CAPACITY) * f)
    return residue, residue + MOMENTA[sweep + 1] * f, STRIDES[sweep]


def inner_and_side(halves, j, b, f):
    terms = [(block, row_of(f, *at)) for block, at in tile_terms(halves, j, b)]
    return terms[:-1], terms[-1:]


def beside_kernel(instant, pair, keep, recv_0, recv_1, small, got_a, response_ref, q_ref, *refs):
    halves = ((keep,), (recv_0, recv_1))
    product_out, part_out = refs[-2:]
    f = small_part(small, INITIAL) if instant == pair == 0 else refs[0][...]
    residue = None if pair == 0 else refs[1][...]
    q, response = q_ref[...], response_ref[...]
    product = stacked([
        row_of(q, j, b) + matvec([(halo_block(halves, j, b), got_a[j:j + 1, :])]) if b == 1 else row_of(q, j, b)
        for j, b in TILES
    ])
    product_out[...] = product
    _, f2, scale = advance(instant, pair, small, product, f, residue)
    part = []
    for j, b in TILES:
        inner, side = inner_and_side(halves, j, b, f2)
        if b == 1:
            beside = got_a[N + j:N + j + 1, :] - scale * row_of(response, j, b)
            part.append(matvec(inner + [(halo_block(halves, j, b), beside)]))
        else:
            part.append(matvec(side))
    part_out[...] = stacked(part)


def pair_kernel(instant, pair, last, keep, recv_0, recv_1, small, got_b, response_ref, product_ref, part_ref, *refs):
    halves = ((keep,), (recv_0, recv_1))
    first = pair == 0
    capacity = small_part(small, CAPACITY)
    if first and instant == 0:
        f = small_part(small, INITIAL)
    else:
        f, refs = refs[0][...], refs[1:]
    residue = estimate = None
    if not first:
        residue, estimate, refs = refs[0][...], refs[1][...], refs[2:]
    response, product, part = response_ref[...], product_ref[...], part_ref[...]

    product = stacked([
        row_of(product, j, b) + matvec([(halo_block(halves, j, b), got_b[j:j + 1, :])]) if b == 0
        else row_of(product, j, b) for j, b in TILES
    ])
    residue, f2, scale = advance(instant, pair, small, product, f, residue)
    estimate = f + STRIDES[0] * f2 if first else estimate + STRIDES[2 * pair] * f2

    outs = []
    for j, b in TILES:
        inner, side = inner_and_side(halves, j, b, f2)
        if b == 0:
            beside = got_b[N + j:N + j + 1, :] - scale * row_of(response, j, b)
            rest = matvec(inner + [(halo_block(halves, j, b), beside)])
        else:
            rest = matvec(side)
        outs.append(row_of(part, j, b) + rest)
    sweep = 2 * pair
    residue = residue - STRIDES[sweep] * (stacked(outs) + capacity * f2)
    f3 = residue + MOMENTA[sweep + 1] * f2
    estimate = estimate + STRIDES[sweep + 1] * f3
    closing = sweep + 2 == ITERS
    if closing:
        f3 = estimate
    f_out, refs = refs[0], refs[1:]
    f_out[...] = f3
    if last:
        return
    zero = jnp.zeros_like(f3[:1])
    q = stacked([
        matvec([(block, row_of(f3, *at)) for block, at in tile_terms(halves, j, b)]) if b == 0 else zero for j, b in TILES
    ])
    upcoming = small_part(small, instant + 1) if closing else None
    base, factor = ahead(closing, sweep + 1, f3, residue, capacity, upcoming)
    q_out, base_out, msg_b = refs[:3]
    q_out[...] = q
    base_out[...] = base
    to_b = message(f3, base - factor * q, 0)
    msg_b[...] = stacked([to_b, jnp.zeros_like(to_b)])
    if not closing:
        refs[3][...] = residue
        refs[4][...] = estimate


def shards_chain(own_block, neighbor_block, pattern, capacity, initial, currents, slot_tile):
    tile_rows, tile_cols, width = initial.shape
    n_col = lax.axis_size("col")
    row, col = lax.axis_index("row"), lax.axis_index("col")
    both = ("row", "col")
    swap = [(0, 1), (1, 0)]
    b_pairs = []
    for unit in range(1, 2 * n_col - 1, 2):
        ends = [r * n_col + c for r, c in (unit_device(unit, n_col), unit_device(unit + 1, n_col))]
        b_pairs += [tuple(ends), tuple(ends[::-1])]
    parity = (row + col) % 2

    vmem = pl.BlockSpec(memory_space=pltpu.VMEM)
    smem = pl.BlockSpec(memory_space=pltpu.SMEM)
    hbm = pl.BlockSpec(memory_space=pltpu.HBM)
    limit = pltpu.CompilerParams(vmem_limit_bytes=16 * 2**20)
    place = jnp.stack([row, col]).astype(jnp.int32)
    blocks = [pltpu.with_memory_space_constraint(x, pltpu.HBM) for x in (pattern, own_block, neighbor_block)]

    def pack(sent, first, count, extra=()):
        return pl.pallas_call(
            functools.partial(pack_kernel, n_col, sent, first, count),
            out_shape=[jax.ShapeDtypeStruct((n, width, width), jnp.float32) for n in (count, *extra)],
            in_specs=[smem, smem, hbm, hbm],
            out_specs=[vmem] * (1 + len(extra)),
            scratch_shapes=[pltpu.SemaphoreType.DMA((count,))],
            compiler_params=limit,
            name="pack",
        )(place, *blocks)

    recv = []
    for first, count in ((0, SPLIT[1][0]), SPLIT[1]):
        (send,) = pack(1, first, count)
        recv.append(lax.ppermute(send, "row", swap))
    keep, facing_0 = pack(0, 0, PACKED, (ROWS,))

    def beside(currents, slot_tile, capacity, initial, facing_0):
        beyond_0 = lax.ppermute(facing_0, both, b_pairs)
        slots, frames = currents.shape[3:]
        by_target = pl.pallas_call(
            by_target_kernel,
            out_shape=jax.ShapeDtypeStruct((n_col, 1, slots * frames + width), jnp.float32),
            in_specs=[vmem, vmem],
            out_specs=vmem,
            compiler_params=limit,
            name="by_target",
        )(currents.reshape(n_col, slots, frames), slot_tile.reshape(n_col, slots))
        arrived = lax.all_to_all(by_target, "col", split_axis=0, concat_axis=0, tiled=True)
        half = jax.ShapeDtypeStruct(((STEPS + 2) * ROWS * HALF, width), jnp.float32)
        small, send = pl.pallas_call(
            small_kernel,
            out_shape=(half, half),
            in_specs=[smem, vmem, vmem, vmem],
            out_specs=(vmem, vmem),
            scratch_shapes=[pltpu.VMEM((tile_rows * tile_cols, frames), jnp.float32)],
            compiler_params=limit,
            name="small",
        )(place, arrived.reshape(n_col, slots * frames + width), capacity, initial)
        return small, lax.ppermute(send, "row", swap), beyond_0

    *small, beyond_0 = lax.cond(
        row < lax.axis_size("row"),
        beside,
        lambda currents, slot_tile, capacity, initial, facing_0: (
            *jnp.zeros((2, (STEPS + 2) * ROWS * HALF, width), jnp.float32), facing_0
        ),
        currents, slot_tile, capacity, initial, facing_0,
    )

    shape = jax.ShapeDtypeStruct((N * HALF, width), jnp.float32)
    halves = (keep, *recv)

    def call(body, outs, blocks, *ins):
        return pl.pallas_call(
            body,
            out_shape=outs,
            in_specs=[vmem] * len(ins),
            out_specs=(vmem,) * len(outs),
            compiler_params=limit,
            cost_estimate=pl.CostEstimate(flops=2 * blocks * width * width, bytes_accessed=blocks * width * width * 4,
                                          transcendentals=0),
            name="pair",
        )(*ins)

    first_shape = jax.ShapeDtypeStruct((2 * N + ROWS * width, width), jnp.float32)
    unit_small = jax.ShapeDtypeStruct(((STEPS + 2) * N * HALF, width), jnp.float32)
    msg_a, msg_b, q, small = call(start_kernel, (first_shape, first_shape, shape, unit_small), 28, *halves, *small)
    got_b = first_b = lax.ppermute(msg_b, both, b_pairs)
    got_a = first_a = lax.ppermute(msg_a, "row", swap)
    blocks = (*halves, beyond_0, first_a, first_b)
    (response,) = call(response_kernel, (shape,), 8, *blocks, small)
    b_shape = jax.ShapeDtypeStruct((4 * N, width), jnp.float32)
    field, state, frames = (), (), []
    for instant in range(STEPS):
        for pair in range(ITERS // 2):
            closing = pair + 1 == ITERS // 2
            last = closing and instant + 1 == STEPS
            product, part = call(functools.partial(beside_kernel, instant, pair), (shape,) * 2, 22,
                                 *halves, small, got_a, response, q, *field, *state[:1])
            out = call(functools.partial(pair_kernel, instant, pair, last), (shape,) if last else (shape,) * 3 + (b_shape,) + (shape,) * (0 if closing else 2),
                       36, *halves, small, got_b, response, product, part, *field, *state)
            field = out[:1]
            if last:
                break
            q, base, msg_b = out[1:4]
            state = out[4:]
            got_b = lax.ppermute(msg_b, both, b_pairs)
            factor = 1.0 if closing else STRIDES[2 * pair + 1]
            response, q, msg_a = call(functools.partial(to_a_kernel, factor), (shape,) * 3, 22, *blocks, *field, q, base)
            got_a = lax.ppermute(msg_a, "row", swap)
        frames.append(field[0])

    done = jnp.stack(frames).reshape(STEPS, N, HALF, width)
    got = lax.ppermute(jnp.flip(done[:, ROWS:], 1), "row", swap)
    mine = done[:, :ROWS]
    unit_0, unit_1 = jnp.where(parity == 1, got, mine), jnp.where(parity == 1, mine, got)
    done = jnp.concatenate([unit_0, jnp.flip(unit_1, 2)], axis=2)
    return jnp.where(row == 1, jnp.flip(done, 1), done)


def solution(mesh):
    rows, cols = mesh.shape["row"], mesh.shape["col"]
    return jax.shard_map(
        shards_chain if rows == 2 else shards_general,
        mesh=mesh,
        in_specs=(
            P("row", "col", None, None),
            P(None, "row", "col", None, None),
            P("row", "col", None),
            P("row", "col", None),
            P("row", "col", None),
            P("row", "col", None, None, None),
            P("row", "col", None, None),
        ),
        out_specs=P(None, "row", "col", None),
        check_vma=False,
    )
```

```python
import functools

import jax
import jax.numpy as jnp
from jax import lax
from jax.experimental import pallas as pl
from jax.experimental.pallas import tpu as pltpu
from jax.sharding import PartitionSpec as P

STEPS = 4
ITERS = 8

spec_center = 6.4
spec_radius = 5.6


def schedule():
    strides, momenta = [], []
    stride = 1.0 / spec_center
    for sweep in range(ITERS):
        if sweep == 0:
            momentum = 0.0
        else:
            if sweep == 1:
                momentum = 0.5 * (spec_radius * stride) ** 2
            else:
                momentum = (spec_radius * stride / 2.0) ** 2
            stride = 1.0 / (spec_center - momentum / stride)
        strides.append(stride)
        momenta.append(momentum)
    return strides, momenta


STRIDES, MOMENTA = schedule()


def swap_pairs(count, first):
    pairs = []
    for i in range(first, count - 1, 2):
        pairs += [(i, i + 1), (i + 1, i)]
    return pairs


def exchange(field):
    arrived = []
    for axis in ("row", "col"):
        count = lax.axis_size(axis)
        for first in (0, 1):
            pairs = swap_pairs(count, first)
            arrived.append(lax.ppermute(field, axis, pairs) if pairs else None)
    return arrived


def beside(field, halos, odd_row, odd_col, cols):
    tiles = field.shape[0]
    row_a, row_b, col_a, col_b = halos
    zero = jnp.zeros_like(field)
    row_a, row_b, col_a, col_b = [zero if h is None else h for h in (row_a, row_b, col_a, col_b)]
    above = jnp.where(odd_row, row_a, row_b)
    below = jnp.where(odd_row, row_b, row_a)
    west = jnp.where(odd_col, col_a, col_b)
    east = jnp.where(odd_col, col_b, col_a)
    up = jnp.concatenate([above[tiles - cols:], field[: tiles - cols]], axis=0)
    down = jnp.concatenate([field[cols:], below[:cols]], axis=0)
    column = lax.broadcasted_iota(jnp.int32, field.shape, 0) % cols
    rolled = jnp.concatenate([field[tiles - 1:], field[: tiles - 1]], axis=0)
    west_edge = jnp.concatenate([west[cols - 1:], west[: cols - 1]], axis=0)
    left = jnp.where(column == 0, west_edge, rolled)
    rolled = jnp.concatenate([field[1:], field[:1]], axis=0)
    east_edge = jnp.concatenate([east[tiles - cols + 1:], east[: tiles - cols + 1]], axis=0)
    right = jnp.where(column == cols - 1, east_edge, rolled)
    return up, down, left, right


def blocks_times(field, around, own_ref, nb_ref):
    tiles, width = field.shape
    chunk = 32
    lane = lax.broadcasted_iota(jnp.int32, (chunk, width), 1)
    sub = lax.broadcasted_iota(jnp.int32, (chunk, width), 0)
    outs = []
    for t in range(tiles):
        vecs = [f[t:t + 1] for f in around]
        mine = field[t:t + 1]
        spread = jnp.zeros((chunk, width), jnp.float32)
        for g in range(0, width, chunk):
            acc = own_ref[t, g:g + chunk, :] * mine
            for n, vec in enumerate(vecs):
                acc = acc + nb_ref[n, t, g:g + chunk, :] * vec
            total = jnp.sum(acc, axis=1, keepdims=True)
            spread = jnp.where(lane == sub + g, total, spread)
        outs.append(jnp.sum(spread, axis=0, keepdims=True))
    return jnp.concatenate(outs, axis=0)


def kernel(sweep, cols, present, flags, own_ref, nb_ref, weights, *refs):
    n_halo = sum(present)
    halo_refs, refs = refs[:n_halo], refs[n_halo:]
    halo_iter = iter(halo_refs)
    halos = [next(halo_iter)[...] if p else None for p in present]
    odd_row, odd_col = flags[0] == 1, flags[1] == 1
    field_ref, refs = refs[0], refs[1:]
    field = field_ref[...]
    around = beside(field, halos, odd_row, odd_col, cols)
    around = [f * weights[n] for n, f in enumerate(around)]
    product = blocks_times(field, around, own_ref, nb_ref)
    if sweep < 0:
        injected, search_out, residue_out, estimate_out = refs
        residue = injected[...] - product
        search_out[...] = residue
        residue_out[...] = residue
        estimate_out[...] = field + STRIDES[0] * residue
    else:
        capacity, residue_in, estimate_in = refs[:3]
        outs = refs[3:]
        residue = residue_in[...] - STRIDES[sweep] * (product + capacity[...] * field)
        search = residue + MOMENTA[sweep + 1] * field
        estimate = estimate_in[...] + STRIDES[sweep + 1] * search
        if sweep + 2 < ITERS:
            outs[0][...] = search
            outs[1][...] = residue
            outs[2][...] = estimate
        else:
            outs[0][...] = estimate


def collect(currents, slot_tile, tiles, width):
    slots, frames = currents.shape[3:]
    names = jnp.pad(slot_tile.astype(jnp.float32)[..., None, :],
                    ((0, 0), (0, 0), (0, 0), (0, 0), (0, frames - slots)))
    packed = jnp.concatenate([currents, names], axis=3)
    arrived = lax.all_to_all(packed, "col", split_axis=2, concat_axis=1, tiled=True)[0, :, 0]
    targets = arrived[:, slots, :slots]
    chooser = (targets[..., None] == jnp.arange(tiles, dtype=jnp.float32)).astype(jnp.float32)
    injected = jnp.einsum("skt,skf->tf", chooser, arrived[:, :slots], precision=lax.Precision.HIGHEST)
    return injected.reshape(tiles, STEPS, width)


def shards_general(own_block, neighbor_block, pattern, capacity, initial, currents, slot_tile):
    tile_rows, tile_cols, width = initial.shape
    tiles = tile_rows * tile_cols
    flags = jnp.stack([lax.axis_index("row") % 2, lax.axis_index("col") % 2]).astype(jnp.int32)

    voltage = initial.reshape(tiles, width)
    halos = exchange(voltage)

    injected = collect(currents, slot_tile, tiles, width)

    own = own_block.reshape(tiles, width, width)
    nb = neighbor_block.reshape(4, tiles, width, width)
    weights = jnp.broadcast_to(
        jnp.moveaxis(pattern.reshape(tiles, 4), 1, 0).astype(jnp.float32)[..., None], (4, tiles, width)
    )
    cap = capacity.reshape(tiles, width)
    shape = jax.ShapeDtypeStruct((tiles, width), jnp.float32)
    vmem = pl.BlockSpec(memory_space=pltpu.VMEM)
    smem = pl.BlockSpec(memory_space=pltpu.SMEM)

    def call(sweep, halos, *state):
        present = tuple(h is not None for h in halos)
        ins = (flags, own, nb, weights) + tuple(h for h in halos if h is not None) + state
        n_out = 1 if sweep + 2 == ITERS else 3
        out = pl.pallas_call(
            functools.partial(kernel, sweep, tile_cols, present),
            out_shape=(shape,) * n_out,
            in_specs=[smem] + [vmem] * (len(ins) - 1),
            out_specs=(vmem,) * n_out,
            compiler_params=pltpu.CompilerParams(vmem_limit_bytes=8 * 2**20),
            cost_estimate=pl.CostEstimate(flops=2 * 5 * tiles * width * width, bytes_accessed=5 * tiles * width * width * 4,
                                          transcendentals=0),
            name="couple",
        )(*ins)
        return out

    frames_out = []
    for instant in range(STEPS):
        if instant:
            halos = exchange(voltage)
        search, residue, estimate = call(-1, halos, voltage, injected[:, instant])
        for sweep in range(ITERS - 1):
            halos = exchange(search)
            out = call(sweep, halos, search, cap, residue, estimate)
            if sweep + 2 < ITERS:
                search, residue, estimate = out
            else:
                (voltage,) = out
        frames_out.append(voltage)
    return jnp.stack(frames_out).reshape(STEPS, tile_rows, tile_cols, width)


ROWS, HALF = 2, 2
N = 2 * ROWS
OWN, SIDE_A, SIDE_B, OUT_IN, IN_OUT, IN_IN, FACING, PACKED = 0, 4, 8, 12, 14, 16, 18, 20
TILES = [(j, b) for j in range(N) for b in range(HALF)]
ORIGIN = [(0, 0), (0, 1), (1, 1), (1, 0)]
CAPACITY, INITIAL = STEPS, STEPS + 1
SPLIT = ((PACKED,), (OUT_IN, FACING - OUT_IN))


def unit_device(unit, n_col):
    col = unit // 2
    return (unit + col) % 2, col


def half_tiles(y, col, n_col, cols, sent):
    k = (y + col + sent) % 2
    rows = (y, 1 - y)
    inward, outward = 1 - y, y
    at = [b + k * (cols - 1 - 2 * b) for b in range(HALF)]
    inside = jnp.where(col == k * (n_col - 1), 0.0, 1.0)
    tiles = [None] * PACKED
    for h in range(ROWS):
        for b in range(HALF):
            tiles[OWN + h * HALF + b] = (None, rows[h], at[b], None)
            tiles[SIDE_A + h * HALF + b] = (3 - k, rows[h], at[b], None)
            tiles[SIDE_B + h * HALF + b] = (2 + k, rows[h], at[b], inside if b == 0 else None)
        tiles[FACING + h] = (2 + k, rows[h], HALF - k, None)
    for b in range(HALF):
        tiles[OUT_IN + b] = (inward, rows[0], at[b], None)
        tiles[IN_OUT + b] = (outward, rows[1], at[b], None)
        tiles[IN_IN + b] = (inward, rows[1], at[b], None)
    return tiles


def pack_kernel(n_col, sent, first, count, place_ref, pattern_ref, own_hbm, nb_hbm, out, *rest):
    sems = rest[-1]
    tiles = half_tiles(place_ref[0], place_ref[1], n_col, own_hbm.shape[1], sent)
    copies = []
    for i in range(count):
        direction, row, at, _ = tiles[first + i]
        source = own_hbm.at[row, at] if direction is None else nb_hbm.at[direction, row, at]
        copies.append(pltpu.make_async_copy(source, out.at[i], sems.at[i]))
    for copy in copies:
        copy.start()
    for i in range(count):
        direction, row, at, weight = tiles[first + i]
        copies[i].wait()
        if direction is not None:
            scale = pattern_ref[row, at, direction].astype(jnp.float32)
            out[i] = out[i] * (scale if weight is None else scale * weight)
    if not sent:
        for h in range(ROWS):
            rest[0][h] = out[SIDE_B + h * HALF]


def block_of(refs, sizes, slot):
    for ref, size in zip(refs, sizes):
        if slot < size:
            return lambda g, n: ref[slot, g:g + n, :]
        slot -= size


def half_block(halves, i, slot):
    return block_of(halves[i], SPLIT[i], slot)


def tile_terms(halves, j, b):
    i, h = ORIGIN[j]
    terms = [(OWN + h * HALF + b, (j, b))]
    if h == 0:
        terms.append((OUT_IN + b, ((1, 2)[i], b)))
    else:
        terms.append((IN_OUT + b, ((0, 3)[i], b)))
        terms.append((IN_IN + b, ((2, 1)[i], b)))
    terms.append(((SIDE_A if b == 0 else SIDE_B) + h * HALF + b, (j, 1 - b)))
    return [(half_block(halves, i, slot), at) for slot, at in terms]


def halo_block(halves, j, b):
    i, h = ORIGIN[j]
    return half_block(halves, i, (SIDE_B if b == 0 else SIDE_A) + h * HALF + b)


def facing_block(halves, beyond_0, first_a, first_b, j, b):
    i, h = ORIGIN[j]
    if i == 0:
        return half_block(halves, i, FACING + h) if b == 1 else lambda g, n: beyond_0[h, g:g + n, :]
    first = first_a if b == 1 else first_b
    start = 2 * N + h * first.shape[1]
    return lambda g, n: first[start + g:start + g + n, :]


def matvec(terms, chunk=32):
    width = terms[0][1].shape[1]
    lane = lax.broadcasted_iota(jnp.int32, (chunk, width), 1)
    sub = lax.broadcasted_iota(jnp.int32, (chunk, width), 0)
    spread = jnp.zeros((chunk, width), jnp.float32)
    for g in range(0, width, chunk):
        acc = None
        for block, vec in terms:
            part = block(g, chunk) * vec
            acc = part if acc is None else acc + part
        total = jnp.sum(acc, axis=1, keepdims=True)
        spread = jnp.where(lane == sub + g, total, spread)
    return jnp.sum(spread, axis=0, keepdims=True)


def row_of(x, j, b):
    i = j * HALF + b
    return x[i:i + 1]


def inner_product(f, halves):
    return jnp.concatenate(
        [matvec([(block, row_of(f, *at)) for block, at in tile_terms(halves, j, b)]) for j, b in TILES], axis=0
    )


def message(f, g, b):
    order = range(N)[::-1] if b == 1 else range(N)
    return jnp.concatenate([row_of(x, j, b) for x in (f, g) for j in order], axis=0)


def ahead(first, sweep, f, residue, capacity, injected):
    if first:
        return injected, 1.0
    return residue - STRIDES[sweep] * (capacity * f) + MOMENTA[sweep + 1] * f, STRIDES[sweep]


def small_part(small, index):
    n = N * HALF
    return small[index * n:(index + 1) * n, :]


def start_kernel(keep, recv_0, recv_1, small_keep, small_recv, msg_a, msg_b, q_out, small):
    n = ROWS * HALF
    for i in range(0, small_keep.shape[0], n):
        small[2 * i:2 * i + n, :] = small_keep[i:i + n, :]
        small[2 * i + n:2 * i + n + HALF, :] = small_recv[i + HALF:i + n, :]
        small[2 * i + n + HALF:2 * i + 2 * n, :] = small_recv[i:i + HALF, :]
    halves = ((keep,), (recv_0, recv_1))
    f = small_part(small, INITIAL)
    q = inner_product(f, halves)
    q_out[...] = q
    g = small_part(small, 0) - q
    msg_a[:2 * N, :], msg_b[:2 * N, :] = message(f, g, 1), message(f, g, 0)
    width = f.shape[1]
    for h in range(ROWS):
        start = 2 * N + h * width
        msg_a[start:start + width, :] = keep[SIDE_A + h * HALF + 1]
        msg_b[start:start + width, :] = recv_0[SIDE_B + h * HALF]


def by_target_kernel(currents, slot_tile, out):
    targets, slots, frames = currents.shape
    width = out.shape[2] - slots * frames
    names = slot_tile[...].astype(jnp.float32)
    names = jnp.concatenate([names, jnp.zeros((targets, width - slots), jnp.float32)], axis=1)
    for d in range(targets):
        for k in range(slots):
            out[d, :, k * frames:(k + 1) * frames] = currents[d, k:k + 1, :]
        out[d, :, slots * frames:] = names[d:d + 1, :]


def small_kernel(place_ref, arrived, capacity, initial, keep, send, injected):
    y, col = place_ref[0], place_ref[1]
    tiles, frames = injected.shape
    _, cols, width = capacity.shape
    slots = (arrived.shape[1] - width) // frames
    for t in range(tiles):
        total = jnp.zeros((arrived.shape[0], frames), jnp.float32)
        for k in range(slots):
            feeds = arrived[:, slots * frames + k:slots * frames + k + 1] == float(t)
            total = total + jnp.where(feeds, 1.0, 0.0) * arrived[:, k * frames:(k + 1) * frames]
        injected[t:t + 1, :] = jnp.sum(total, axis=0, keepdims=True)
    for sent, out in ((0, keep), (1, send)):
        parity = (y + col + sent) % 2
        for h in range(ROWS):
            row = y if h == 0 else 1 - y
            for b in range(HALF):
                at = b + parity * (cols - 1 - 2 * b)
                currents = injected[pl.ds(row * cols + at, 1), :]
                parts = [currents[:, n * width:(n + 1) * width] for n in range(STEPS)]
                parts += [x[row, pl.ds(at, 1), :] for x in (capacity, initial)]
                for n, part in enumerate(parts):
                    i = n * ROWS * HALF + h * HALF + b
                    out[i:i + 1, :] = part


def stacked(rows):
    return jnp.concatenate(rows, axis=0)


def responses(halves, beyond_0, first_a, first_b, f):
    return stacked([
        matvec([(facing_block(halves, beyond_0, first_a, first_b, j, b), row_of(f, j, b))]) for j, b in TILES
    ])


def advance(instant, pair, small, product, f, residue):
    if pair == 0:
        residue = small_part(small, instant) - product
        return residue, residue, 1.0
    sweep = 2 * pair - 1
    residue = residue - STRIDES[sweep] * (product + small_part(small, CAPACITY) * f)
    return residue, residue + MOMENTA[sweep + 1] * f, STRIDES[sweep]


def inner_and_side(halves, j, b, f):
    terms = [(block, row_of(f, *at)) for block, at in tile_terms(halves, j, b)]
    return terms[:-1], terms[-1:]


def beside_kernel(instant, pair, keep, recv_0, recv_1, beyond_0, first_a, first_b, small, got_a, q_ref, *refs):
    halves = ((keep,), (recv_0, recv_1))
    response_out, product_out, part_out = refs[-3:]
    f = small_part(small, INITIAL) if instant == pair == 0 else refs[0][...]
    residue = None if pair == 0 else refs[1][...]
    q, response = q_ref[...], responses(halves, beyond_0, first_a, first_b, f)
    response_out[...] = response
    product = stacked([
        row_of(q, j, b) + matvec([(halo_block(halves, j, b), got_a[j:j + 1, :])]) if b == 1 else row_of(q, j, b)
        for j, b in TILES
    ])
    product_out[...] = product
    _, f2, scale = advance(instant, pair, small, product, f, residue)
    part = []
    for j, b in TILES:
        inner, side = inner_and_side(halves, j, b, f2)
        if b == 1:
            beside = got_a[N + j:N + j + 1, :] - scale * row_of(response, j, b)
            part.append(matvec(inner + [(halo_block(halves, j, b), beside)]))
        else:
            part.append(matvec(side))
    part_out[...] = stacked(part)


def pair_kernel(instant, pair, last, keep, recv_0, recv_1, small, got_b, response_ref, product_ref, part_ref, *refs):
    halves = ((keep,), (recv_0, recv_1))
    first = pair == 0
    capacity = small_part(small, CAPACITY)
    if first and instant == 0:
        f = small_part(small, INITIAL)
    else:
        f, refs = refs[0][...], refs[1:]
    residue = estimate = None
    if not first:
        residue, estimate, refs = refs[0][...], refs[1][...], refs[2:]
    response, product, part = response_ref[...], product_ref[...], part_ref[...]

    product = stacked([
        row_of(product, j, b) + matvec([(halo_block(halves, j, b), got_b[j:j + 1, :])]) if b == 0
        else row_of(product, j, b) for j, b in TILES
    ])
    residue, f2, scale = advance(instant, pair, small, product, f, residue)
    estimate = f + STRIDES[0] * f2 if first else estimate + STRIDES[2 * pair] * f2

    outs = []
    for j, b in TILES:
        inner, side = inner_and_side(halves, j, b, f2)
        if b == 0:
            beside = got_b[N + j:N + j + 1, :] - scale * row_of(response, j, b)
            rest = matvec(inner + [(halo_block(halves, j, b), beside)])
        else:
            rest = matvec(side)
        outs.append(row_of(part, j, b) + rest)
    sweep = 2 * pair
    residue = residue - STRIDES[sweep] * (stacked(outs) + capacity * f2)
    f3 = residue + MOMENTA[sweep + 1] * f2
    estimate = estimate + STRIDES[sweep + 1] * f3
    closing = sweep + 2 == ITERS
    if closing:
        f3 = estimate
    f_out, refs = refs[0], refs[1:]
    f_out[...] = f3
    if last:
        return
    q = inner_product(f3, halves)
    upcoming = small_part(small, instant + 1) if closing else None
    base, factor = ahead(closing, sweep + 1, f3, residue, capacity, upcoming)
    g = base - factor * q
    q_out, msg_a, msg_b = refs[:3]
    q_out[...] = q
    msg_a[...], msg_b[...] = message(f3, g, 1), message(f3, g, 0)
    if not closing:
        refs[3][...] = residue
        refs[4][...] = estimate


def shards_chain(own_block, neighbor_block, pattern, capacity, initial, currents, slot_tile):
    tile_rows, tile_cols, width = initial.shape
    n_col = lax.axis_size("col")
    row, col = lax.axis_index("row"), lax.axis_index("col")
    both = ("row", "col")
    swap = [(0, 1), (1, 0)]
    b_pairs = []
    for unit in range(1, 2 * n_col - 1, 2):
        ends = [r * n_col + c for r, c in (unit_device(unit, n_col), unit_device(unit + 1, n_col))]
        b_pairs += [tuple(ends), tuple(ends[::-1])]
    parity = (row + col) % 2

    vmem = pl.BlockSpec(memory_space=pltpu.VMEM)
    smem = pl.BlockSpec(memory_space=pltpu.SMEM)
    hbm = pl.BlockSpec(memory_space=pltpu.HBM)
    limit = pltpu.CompilerParams(vmem_limit_bytes=16 * 2**20)
    place = jnp.stack([row, col]).astype(jnp.int32)
    blocks = [pltpu.with_memory_space_constraint(x, pltpu.HBM) for x in (pattern, own_block, neighbor_block)]

    def pack(sent, first, count, extra=()):
        return pl.pallas_call(
            functools.partial(pack_kernel, n_col, sent, first, count),
            out_shape=[jax.ShapeDtypeStruct((n, width, width), jnp.float32) for n in (count, *extra)],
            in_specs=[smem, smem, hbm, hbm],
            out_specs=[vmem] * (1 + len(extra)),
            scratch_shapes=[pltpu.SemaphoreType.DMA((count,))],
            compiler_params=limit,
            name="pack",
        )(place, *blocks)

    recv = []
    for first, count in ((0, SPLIT[1][0]), SPLIT[1]):
        (send,) = pack(1, first, count)
        recv.append(lax.ppermute(send, "row", swap))
    keep, facing_0 = pack(0, 0, PACKED, (ROWS,))

    def beside(currents, slot_tile, capacity, initial, facing_0):
        beyond_0 = lax.ppermute(facing_0, both, b_pairs)
        slots, frames = currents.shape[3:]
        by_target = pl.pallas_call(
            by_target_kernel,
            out_shape=jax.ShapeDtypeStruct((n_col, 1, slots * frames + width), jnp.float32),
            in_specs=[vmem, vmem],
            out_specs=vmem,
            compiler_params=limit,
            name="by_target",
        )(currents.reshape(n_col, slots, frames), slot_tile.reshape(n_col, slots))
        arrived = lax.all_to_all(by_target, "col", split_axis=0, concat_axis=0, tiled=True)
        half = jax.ShapeDtypeStruct(((STEPS + 2) * ROWS * HALF, width), jnp.float32)
        small, send = pl.pallas_call(
            small_kernel,
            out_shape=(half, half),
            in_specs=[smem, vmem, vmem, vmem],
            out_specs=(vmem, vmem),
            scratch_shapes=[pltpu.VMEM((tile_rows * tile_cols, frames), jnp.float32)],
            compiler_params=limit,
            name="small",
        )(place, arrived.reshape(n_col, slots * frames + width), capacity, initial)
        return small, lax.ppermute(send, "row", swap), beyond_0

    *small, beyond_0 = lax.cond(
        row < lax.axis_size("row"),
        beside,
        lambda currents, slot_tile, capacity, initial, facing_0: (
            *jnp.zeros((2, (STEPS + 2) * ROWS * HALF, width), jnp.float32), facing_0
        ),
        currents, slot_tile, capacity, initial, facing_0,
    )

    shape = jax.ShapeDtypeStruct((N * HALF, width), jnp.float32)
    halves = (keep, *recv)

    def call(body, outs, blocks, *ins):
        return pl.pallas_call(
            body,
            out_shape=outs,
            in_specs=[vmem] * len(ins),
            out_specs=(vmem,) * len(outs),
            compiler_params=limit,
            cost_estimate=pl.CostEstimate(flops=2 * blocks * width * width, bytes_accessed=blocks * width * width * 4,
                                          transcendentals=0),
            name="pair",
        )(*ins)

    first_shape = jax.ShapeDtypeStruct((2 * N + ROWS * width, width), jnp.float32)
    unit_small = jax.ShapeDtypeStruct(((STEPS + 2) * N * HALF, width), jnp.float32)
    msg_a, msg_b, q, small = call(start_kernel, (first_shape, first_shape, shape, unit_small), 28, *halves, *small)
    field, state, frames, first = (), (), [], None
    for instant in range(STEPS):
        for pair in range(ITERS // 2):
            closing = pair + 1 == ITERS // 2
            last = closing and instant + 1 == STEPS
            got_b = lax.ppermute(msg_b, both, b_pairs)
            got_a = lax.ppermute(msg_a, "row", swap)
            first = first or (got_a, got_b)
            response, product, part = call(functools.partial(beside_kernel, instant, pair), (shape,) * 3, 30,
                                           *halves, beyond_0, *first, small, got_a, q, *field, *state[:1])
            out = call(functools.partial(pair_kernel, instant, pair, last), (shape,) * (1 if last else 4 if closing else 6),
                       50, *halves, small, got_b, response, product, part, *field, *state)
            field = out[:1]
            if not last:
                q, msg_a, msg_b = out[1:4]
                state = out[4:]
        frames.append(field[0])

    done = jnp.stack(frames).reshape(STEPS, N, HALF, width)
    got = lax.ppermute(jnp.flip(done[:, ROWS:], 1), "row", swap)
    mine = done[:, :ROWS]
    unit_0, unit_1 = jnp.where(parity == 1, got, mine), jnp.where(parity == 1, mine, got)
    done = jnp.concatenate([unit_0, jnp.flip(unit_1, 2)], axis=2)
    return jnp.where(row == 1, jnp.flip(done, 1), done)


def solution(mesh):
    rows, cols = mesh.shape["row"], mesh.shape["col"]
    return jax.shard_map(
        shards_chain if rows == 2 else shards_general,
        mesh=mesh,
        in_specs=(
            P("row", "col", None, None),
            P(None, "row", "col", None, None),
            P("row", "col", None),
            P("row", "col", None),
            P("row", "col", None),
            P("row", "col", None, None, None),
            P("row", "col", None, None),
        ),
        out_specs=P(None, "row", "col", None),
        check_vma=False,
    )
```

```python
import functools

import jax
import jax.numpy as jnp
from jax import lax
from jax.experimental import pallas as pl
from jax.experimental.pallas import tpu as pltpu
from jax.sharding import PartitionSpec as P

STEPS = 4
ITERS = 8

spec_center = 6.4
spec_radius = 5.6


def schedule():
    strides, momenta = [], []
    stride = 1.0 / spec_center
    for sweep in range(ITERS):
        if sweep == 0:
            momentum = 0.0
        else:
            if sweep == 1:
                momentum = 0.5 * (spec_radius * stride) ** 2
            else:
                momentum = (spec_radius * stride / 2.0) ** 2
            stride = 1.0 / (spec_center - momentum / stride)
        strides.append(stride)
        momenta.append(momentum)
    return strides, momenta


STRIDES, MOMENTA = schedule()


def swap_pairs(count, first):
    pairs = []
    for i in range(first, count - 1, 2):
        pairs += [(i, i + 1), (i + 1, i)]
    return pairs


def exchange(field):
    arrived = []
    for axis in ("row", "col"):
        count = lax.axis_size(axis)
        for first in (0, 1):
            pairs = swap_pairs(count, first)
            arrived.append(lax.ppermute(field, axis, pairs) if pairs else None)
    return arrived


def beside(field, halos, odd_row, odd_col, cols):
    tiles = field.shape[0]
    row_a, row_b, col_a, col_b = halos
    zero = jnp.zeros_like(field)
    row_a, row_b, col_a, col_b = [zero if h is None else h for h in (row_a, row_b, col_a, col_b)]
    above = jnp.where(odd_row, row_a, row_b)
    below = jnp.where(odd_row, row_b, row_a)
    west = jnp.where(odd_col, col_a, col_b)
    east = jnp.where(odd_col, col_b, col_a)
    up = jnp.concatenate([above[tiles - cols:], field[: tiles - cols]], axis=0)
    down = jnp.concatenate([field[cols:], below[:cols]], axis=0)
    column = lax.broadcasted_iota(jnp.int32, field.shape, 0) % cols
    rolled = jnp.concatenate([field[tiles - 1:], field[: tiles - 1]], axis=0)
    west_edge = jnp.concatenate([west[cols - 1:], west[: cols - 1]], axis=0)
    left = jnp.where(column == 0, west_edge, rolled)
    rolled = jnp.concatenate([field[1:], field[:1]], axis=0)
    east_edge = jnp.concatenate([east[tiles - cols + 1:], east[: tiles - cols + 1]], axis=0)
    right = jnp.where(column == cols - 1, east_edge, rolled)
    return up, down, left, right


def blocks_times(field, around, own_ref, nb_ref):
    tiles, width = field.shape
    chunk = 32
    lane = lax.broadcasted_iota(jnp.int32, (chunk, width), 1)
    sub = lax.broadcasted_iota(jnp.int32, (chunk, width), 0)
    outs = []
    for t in range(tiles):
        vecs = [f[t:t + 1] for f in around]
        mine = field[t:t + 1]
        spread = jnp.zeros((chunk, width), jnp.float32)
        for g in range(0, width, chunk):
            acc = own_ref[t, g:g + chunk, :] * mine
            for n, vec in enumerate(vecs):
                acc = acc + nb_ref[n, t, g:g + chunk, :] * vec
            total = jnp.sum(acc, axis=1, keepdims=True)
            spread = jnp.where(lane == sub + g, total, spread)
        outs.append(jnp.sum(spread, axis=0, keepdims=True))
    return jnp.concatenate(outs, axis=0)


def kernel(sweep, cols, present, flags, own_ref, nb_ref, weights, *refs):
    n_halo = sum(present)
    halo_refs, refs = refs[:n_halo], refs[n_halo:]
    halo_iter = iter(halo_refs)
    halos = [next(halo_iter)[...] if p else None for p in present]
    odd_row, odd_col = flags[0] == 1, flags[1] == 1
    field_ref, refs = refs[0], refs[1:]
    field = field_ref[...]
    around = beside(field, halos, odd_row, odd_col, cols)
    around = [f * weights[n] for n, f in enumerate(around)]
    product = blocks_times(field, around, own_ref, nb_ref)
    if sweep < 0:
        injected, search_out, residue_out, estimate_out = refs
        residue = injected[...] - product
        search_out[...] = residue
        residue_out[...] = residue
        estimate_out[...] = field + STRIDES[0] * residue
    else:
        capacity, residue_in, estimate_in = refs[:3]
        outs = refs[3:]
        residue = residue_in[...] - STRIDES[sweep] * (product + capacity[...] * field)
        search = residue + MOMENTA[sweep + 1] * field
        estimate = estimate_in[...] + STRIDES[sweep + 1] * search
        if sweep + 2 < ITERS:
            outs[0][...] = search
            outs[1][...] = residue
            outs[2][...] = estimate
        else:
            outs[0][...] = estimate


def collect(currents, slot_tile, tiles, width):
    slots, frames = currents.shape[3:]
    names = jnp.pad(slot_tile.astype(jnp.float32)[..., None, :],
                    ((0, 0), (0, 0), (0, 0), (0, 0), (0, frames - slots)))
    packed = jnp.concatenate([currents, names], axis=3)
    arrived = lax.all_to_all(packed, "col", split_axis=2, concat_axis=1, tiled=True)[0, :, 0]
    targets = arrived[:, slots, :slots]
    chooser = (targets[..., None] == jnp.arange(tiles, dtype=jnp.float32)).astype(jnp.float32)
    injected = jnp.einsum("skt,skf->tf", chooser, arrived[:, :slots], precision=lax.Precision.HIGHEST)
    return injected.reshape(tiles, STEPS, width)


def shards_general(own_block, neighbor_block, pattern, capacity, initial, currents, slot_tile):
    tile_rows, tile_cols, width = initial.shape
    tiles = tile_rows * tile_cols
    flags = jnp.stack([lax.axis_index("row") % 2, lax.axis_index("col") % 2]).astype(jnp.int32)

    voltage = initial.reshape(tiles, width)
    halos = exchange(voltage)

    injected = collect(currents, slot_tile, tiles, width)

    own = own_block.reshape(tiles, width, width)
    nb = neighbor_block.reshape(4, tiles, width, width)
    weights = jnp.broadcast_to(
        jnp.moveaxis(pattern.reshape(tiles, 4), 1, 0).astype(jnp.float32)[..., None], (4, tiles, width)
    )
    cap = capacity.reshape(tiles, width)
    shape = jax.ShapeDtypeStruct((tiles, width), jnp.float32)
    vmem = pl.BlockSpec(memory_space=pltpu.VMEM)
    smem = pl.BlockSpec(memory_space=pltpu.SMEM)

    def call(sweep, halos, *state):
        present = tuple(h is not None for h in halos)
        ins = (flags, own, nb, weights) + tuple(h for h in halos if h is not None) + state
        n_out = 1 if sweep + 2 == ITERS else 3
        out = pl.pallas_call(
            functools.partial(kernel, sweep, tile_cols, present),
            out_shape=(shape,) * n_out,
            in_specs=[smem] + [vmem] * (len(ins) - 1),
            out_specs=(vmem,) * n_out,
            compiler_params=pltpu.CompilerParams(vmem_limit_bytes=8 * 2**20),
            cost_estimate=pl.CostEstimate(flops=2 * 5 * tiles * width * width, bytes_accessed=5 * tiles * width * width * 4,
                                          transcendentals=0),
            name="couple",
        )(*ins)
        return out

    frames_out = []
    for instant in range(STEPS):
        if instant:
            halos = exchange(voltage)
        search, residue, estimate = call(-1, halos, voltage, injected[:, instant])
        for sweep in range(ITERS - 1):
            halos = exchange(search)
            out = call(sweep, halos, search, cap, residue, estimate)
            if sweep + 2 < ITERS:
                search, residue, estimate = out
            else:
                (voltage,) = out
        frames_out.append(voltage)
    return jnp.stack(frames_out).reshape(STEPS, tile_rows, tile_cols, width)


ROWS, HALF = 2, 2
N = 2 * ROWS
OWN, SIDE_A, SIDE_B, OUT_IN, IN_OUT, IN_IN, FACING, PACKED = 0, 4, 8, 12, 14, 16, 18, 20
TILES = [(j, b) for j in range(N) for b in range(HALF)]
ORIGIN = [(0, 0), (0, 1), (1, 1), (1, 0)]
CAPACITY, INITIAL = STEPS, STEPS + 1
SPLIT = ((PACKED,), (OUT_IN, FACING - OUT_IN))


def unit_device(unit, n_col):
    col = unit // 2
    return (unit + col) % 2, col


def half_tiles(y, col, n_col, cols, sent):
    k = (y + col + sent) % 2
    rows = (y, 1 - y)
    inward, outward = 1 - y, y
    at = [b + k * (cols - 1 - 2 * b) for b in range(HALF)]
    inside = jnp.where(col == k * (n_col - 1), 0.0, 1.0)
    tiles = [None] * PACKED
    for h in range(ROWS):
        for b in range(HALF):
            tiles[OWN + h * HALF + b] = (None, rows[h], at[b], None)
            tiles[SIDE_A + h * HALF + b] = (3 - k, rows[h], at[b], None)
            tiles[SIDE_B + h * HALF + b] = (2 + k, rows[h], at[b], inside if b == 0 else None)
        tiles[FACING + h] = (2 + k, rows[h], HALF - k, None)
    for b in range(HALF):
        tiles[OUT_IN + b] = (inward, rows[0], at[b], None)
        tiles[IN_OUT + b] = (outward, rows[1], at[b], None)
        tiles[IN_IN + b] = (inward, rows[1], at[b], None)
    return tiles


def pack_kernel(n_col, sent, first, count, place_ref, pattern_ref, own_hbm, nb_hbm, out, *rest):
    sems = rest[-1]
    tiles = half_tiles(place_ref[0], place_ref[1], n_col, own_hbm.shape[1], sent)
    copies = []
    for i in range(count):
        direction, row, at, _ = tiles[first + i]
        source = own_hbm.at[row, at] if direction is None else nb_hbm.at[direction, row, at]
        copies.append(pltpu.make_async_copy(source, out.at[i], sems.at[i]))
    for copy in copies:
        copy.start()
    for i in range(count):
        direction, row, at, weight = tiles[first + i]
        copies[i].wait()
        if direction is not None:
            scale = pattern_ref[row, at, direction].astype(jnp.float32)
            out[i] = out[i] * (scale if weight is None else scale * weight)
    if not sent:
        for h in range(ROWS):
            rest[0][h] = out[SIDE_B + h * HALF]


def block_of(refs, sizes, slot):
    for ref, size in zip(refs, sizes):
        if slot < size:
            return lambda g, n: ref[slot, g:g + n, :]
        slot -= size


def half_block(halves, i, slot):
    return block_of(halves[i], SPLIT[i], slot)


def tile_terms(halves, j, b):
    i, h = ORIGIN[j]
    terms = [(OWN + h * HALF + b, (j, b))]
    if h == 0:
        terms.append((OUT_IN + b, ((1, 2)[i], b)))
    else:
        terms.append((IN_OUT + b, ((0, 3)[i], b)))
        terms.append((IN_IN + b, ((2, 1)[i], b)))
    terms.append(((SIDE_A if b == 0 else SIDE_B) + h * HALF + b, (j, 1 - b)))
    return [(half_block(halves, i, slot), at) for slot, at in terms]


def halo_block(halves, j, b):
    i, h = ORIGIN[j]
    return half_block(halves, i, (SIDE_B if b == 0 else SIDE_A) + h * HALF + b)


def facing_block(halves, beyond_0, first_a, first_b, j, b):
    i, h = ORIGIN[j]
    if i == 0:
        return half_block(halves, i, FACING + h) if b == 1 else lambda g, n: beyond_0[h, g:g + n, :]
    first = first_a if b == 1 else first_b
    start = 2 * N + h * first.shape[1]
    return lambda g, n: first[start + g:start + g + n, :]


def matvec(terms, chunk=32):
    width = terms[0][1].shape[1]
    lane = lax.broadcasted_iota(jnp.int32, (chunk, width), 1)
    sub = lax.broadcasted_iota(jnp.int32, (chunk, width), 0)
    spread = jnp.zeros((chunk, width), jnp.float32)
    for g in range(0, width, chunk):
        acc = None
        for block, vec in terms:
            part = block(g, chunk) * vec
            acc = part if acc is None else acc + part
        total = jnp.sum(acc, axis=1, keepdims=True)
        spread = jnp.where(lane == sub + g, total, spread)
    return jnp.sum(spread, axis=0, keepdims=True)


def rows_of(ref, start=0, count=N * HALF):
    return [ref[start + i:start + i + 1, :] for i in range(count)]


def put(ref, rows, start=0):
    for i, row in enumerate(rows):
        ref[start + i:start + i + 1, :] = row


def each(body, *fields):
    return [body(*rows) for rows in zip(*fields)]


def tile(j, b):
    return j * HALF + b


def products(terms, f):
    return [(block, f[tile(*at)]) for block, at in terms]


def inner_product(f, halves):
    return [matvec(products(tile_terms(halves, j, b), f)) for j, b in TILES]


def message(f, g, b):
    order = range(N)[::-1] if b == 1 else range(N)
    return [x[tile(j, b)] for x in (f, g) for j in order]


def ahead(first, sweep, f, q, residue, capacity, injected):
    if first:
        return each(lambda source, a: source - a, injected, q)
    return each(
        lambda v, a, r, c: r - STRIDES[sweep] * (a + c * v) + MOMENTA[sweep + 1] * v, f, q, residue, capacity
    )


def small_part(small, index):
    return rows_of(small, index * N * HALF)


def start_kernel(keep, recv_0, recv_1, small_keep, small_recv, msg_a, msg_b, q_out, small):
    n = ROWS * HALF
    for i in range(0, small_keep.shape[0], n):
        small[2 * i:2 * i + n, :] = small_keep[i:i + n, :]
        small[2 * i + n:2 * i + n + HALF, :] = small_recv[i + HALF:i + n, :]
        small[2 * i + n + HALF:2 * i + 2 * n, :] = small_recv[i:i + HALF, :]
    halves = ((keep,), (recv_0, recv_1))
    f = small_part(small, INITIAL)
    q = inner_product(f, halves)
    put(q_out, q)
    g = ahead(True, 0, f, q, None, None, small_part(small, 0))
    put(msg_a, message(f, g, 1))
    put(msg_b, message(f, g, 0))
    width = small.shape[1]
    for h in range(ROWS):
        start = 2 * N + h * width
        msg_a[start:start + width, :] = keep[SIDE_A + h * HALF + 1]
        msg_b[start:start + width, :] = recv_0[SIDE_B + h * HALF]


def by_target_kernel(currents, slot_tile, out):
    targets, slots, frames = currents.shape
    width = out.shape[2] - slots * frames
    names = slot_tile[...].astype(jnp.float32)
    names = jnp.concatenate([names, jnp.zeros((targets, width - slots), jnp.float32)], axis=1)
    for d in range(targets):
        for k in range(slots):
            out[d, :, k * frames:(k + 1) * frames] = currents[d, k:k + 1, :]
        out[d, :, slots * frames:] = names[d:d + 1, :]


def small_kernel(place_ref, arrived, capacity, initial, keep, send, injected):
    y, col = place_ref[0], place_ref[1]
    tiles, frames = injected.shape
    _, cols, width = capacity.shape
    slots = (arrived.shape[1] - width) // frames
    for t in range(tiles):
        total = jnp.zeros((arrived.shape[0], frames), jnp.float32)
        for k in range(slots):
            feeds = arrived[:, slots * frames + k:slots * frames + k + 1] == float(t)
            total = total + jnp.where(feeds, 1.0, 0.0) * arrived[:, k * frames:(k + 1) * frames]
        injected[t:t + 1, :] = jnp.sum(total, axis=0, keepdims=True)
    for sent, out in ((0, keep), (1, send)):
        parity = (y + col + sent) % 2
        for h in range(ROWS):
            row = y if h == 0 else 1 - y
            for b in range(HALF):
                at = b + parity * (cols - 1 - 2 * b)
                currents = injected[pl.ds(row * cols + at, 1), :]
                parts = [currents[:, n * width:(n + 1) * width] for n in range(STEPS)]
                parts += [x[row, pl.ds(at, 1), :] for x in (capacity, initial)]
                for n, part in enumerate(parts):
                    i = n * ROWS * HALF + h * HALF + b
                    out[i:i + 1, :] = part


def advance(instant, pair, small, product, f, residue):
    if pair == 0:
        residue = each(lambda source, a: source - a, small_part(small, instant), product)
        return residue, residue, 1.0
    sweep = 2 * pair - 1
    residue = each(lambda r, a, c, v: r - STRIDES[sweep] * (a + c * v), residue, product, small_part(small, CAPACITY), f)
    return residue, each(lambda r, v: r + MOMENTA[sweep + 1] * v, residue, f), STRIDES[sweep]


def beside_kernel(instant, pair, keep, recv_0, recv_1, beyond_0, first_a, first_b, small, got_a, q_ref, *refs):
    halves = ((keep,), (recv_0, recv_1))
    response_out, product_out, part_out = refs[-3:]
    f = small_part(small, INITIAL) if instant == pair == 0 else rows_of(refs[0])
    residue = None if pair == 0 else rows_of(refs[1])
    product = rows_of(q_ref)
    for j in range(N):
        product[tile(j, 1)] += matvec([(halo_block(halves, j, 1), got_a[j:j + 1, :])])
    put(product_out, product)
    response = [
        matvec([(facing_block(halves, beyond_0, first_a, first_b, j, b), f[tile(j, b)])]) for j, b in TILES
    ]
    put(response_out, response)
    _, f2, scale = advance(instant, pair, small, product, f, residue)
    part = []
    for j, b in TILES:
        terms = products(tile_terms(halves, j, b), f2)
        if b == 1:
            beside = got_a[N + j:N + j + 1, :] - scale * response[tile(j, b)]
            part.append(matvec(terms[:-1] + [(halo_block(halves, j, b), beside)]))
        else:
            part.append(matvec(terms[-1:]))
    put(part_out, part)


def pair_kernel(instant, pair, last, keep, recv_0, recv_1, small, got_b, response, product_ref, part_ref, *refs):
    halves = ((keep,), (recv_0, recv_1))
    first = pair == 0
    capacity = small_part(small, CAPACITY)
    if first and instant == 0:
        f = small_part(small, INITIAL)
    else:
        f, refs = rows_of(refs[0]), refs[1:]
    residue = estimate = None
    if not first:
        residue, estimate, refs = rows_of(refs[0]), rows_of(refs[1]), refs[2:]

    product = rows_of(product_ref)
    for j in range(N):
        product[tile(j, 0)] += matvec([(halo_block(halves, j, 0), got_b[j:j + 1, :])])
    residue, f2, scale = advance(instant, pair, small, product, f, residue)
    if first:
        estimate = each(lambda v, p: v + STRIDES[0] * p, f, f2)
    else:
        estimate = each(lambda e, p: e + STRIDES[2 * pair] * p, estimate, f2)

    total = rows_of(part_ref)
    for j, b in TILES:
        i = tile(j, b)
        terms = products(tile_terms(halves, j, b), f2)
        if b == 0:
            beside = got_b[N + j:N + j + 1, :] - scale * response[i:i + 1, :]
            total[i] += matvec(terms[:-1] + [(halo_block(halves, j, b), beside)])
        else:
            total[i] += matvec(terms[-1:])
    sweep = 2 * pair
    residue = each(lambda r, a, c, v: r - STRIDES[sweep] * (a + c * v), residue, total, capacity, f2)
    f3 = each(lambda r, v: r + MOMENTA[sweep + 1] * v, residue, f2)
    estimate = each(lambda e, p: e + STRIDES[sweep + 1] * p, estimate, f3)
    closing = sweep + 2 == ITERS
    if closing:
        f3 = estimate
    f_out, refs = refs[0], refs[1:]
    put(f_out, f3)
    if last:
        return
    q = inner_product(f3, halves)
    upcoming = small_part(small, instant + 1) if closing else None
    g = ahead(closing, sweep + 1, f3, q, residue, capacity, upcoming)
    q_out, msg_a, msg_b = refs[:3]
    put(msg_a, message(f3, g, 1))
    put(msg_b, message(f3, g, 0))
    put(q_out, q)
    if not closing:
        put(refs[3], residue)
        put(refs[4], estimate)


def shards_chain(own_block, neighbor_block, pattern, capacity, initial, currents, slot_tile):
    tile_rows, tile_cols, width = initial.shape
    n_col = lax.axis_size("col")
    row, col = lax.axis_index("row"), lax.axis_index("col")
    both = ("row", "col")
    swap = [(0, 1), (1, 0)]
    b_pairs = []
    for unit in range(1, 2 * n_col - 1, 2):
        ends = [r * n_col + c for r, c in (unit_device(unit, n_col), unit_device(unit + 1, n_col))]
        b_pairs += [tuple(ends), tuple(ends[::-1])]
    parity = (row + col) % 2

    vmem = pl.BlockSpec(memory_space=pltpu.VMEM)
    smem = pl.BlockSpec(memory_space=pltpu.SMEM)
    hbm = pl.BlockSpec(memory_space=pltpu.HBM)
    limit = pltpu.CompilerParams(vmem_limit_bytes=16 * 2**20)
    place = jnp.stack([row, col]).astype(jnp.int32)
    blocks = [pltpu.with_memory_space_constraint(x, pltpu.HBM) for x in (pattern, own_block, neighbor_block)]

    def pack(sent, first, count, extra=()):
        return pl.pallas_call(
            functools.partial(pack_kernel, n_col, sent, first, count),
            out_shape=[jax.ShapeDtypeStruct((n, width, width), jnp.float32) for n in (count, *extra)],
            in_specs=[smem, smem, hbm, hbm],
            out_specs=[vmem] * (1 + len(extra)),
            scratch_shapes=[pltpu.SemaphoreType.DMA((count,))],
            compiler_params=limit,
            name="pack",
        )(place, *blocks)

    recv = []
    for first, count in ((0, SPLIT[1][0]), SPLIT[1]):
        (send,) = pack(1, first, count)
        recv.append(lax.ppermute(send, "row", swap))
    keep, facing_0 = pack(0, 0, PACKED, (ROWS,))

    def beside(currents, slot_tile, capacity, initial, facing_0):
        beyond_0 = lax.ppermute(facing_0, both, b_pairs)
        slots, frames = currents.shape[3:]
        by_target = pl.pallas_call(
            by_target_kernel,
            out_shape=jax.ShapeDtypeStruct((n_col, 1, slots * frames + width), jnp.float32),
            in_specs=[vmem, vmem],
            out_specs=vmem,
            compiler_params=limit,
            name="by_target",
        )(currents.reshape(n_col, slots, frames), slot_tile.reshape(n_col, slots))
        arrived = lax.all_to_all(by_target, "col", split_axis=0, concat_axis=0, tiled=True)
        half = jax.ShapeDtypeStruct(((STEPS + 2) * ROWS * HALF, width), jnp.float32)
        small, send = pl.pallas_call(
            small_kernel,
            out_shape=(half, half),
            in_specs=[smem, vmem, vmem, vmem],
            out_specs=(vmem, vmem),
            scratch_shapes=[pltpu.VMEM((tile_rows * tile_cols, frames), jnp.float32)],
            compiler_params=limit,
            name="small",
        )(place, arrived.reshape(n_col, slots * frames + width), capacity, initial)
        return small, lax.ppermute(send, "row", swap), beyond_0

    *small, beyond_0 = lax.cond(
        row < lax.axis_size("row"),
        beside,
        lambda currents, slot_tile, capacity, initial, facing_0: (
            *jnp.zeros((2, (STEPS + 2) * ROWS * HALF, width), jnp.float32), facing_0
        ),
        currents, slot_tile, capacity, initial, facing_0,
    )

    shape = jax.ShapeDtypeStruct((N * HALF, width), jnp.float32)
    halves = (keep, *recv)

    def call(body, outs, blocks, *ins):
        return pl.pallas_call(
            body,
            out_shape=outs,
            in_specs=[vmem] * len(ins),
            out_specs=(vmem,) * len(outs),
            compiler_params=limit,
            cost_estimate=pl.CostEstimate(flops=2 * blocks * width * width, bytes_accessed=blocks * width * width * 4,
                                          transcendentals=0),
            name="pair",
        )(*ins)

    first_shape = jax.ShapeDtypeStruct((2 * N + ROWS * width, width), jnp.float32)
    unit_small = jax.ShapeDtypeStruct(((STEPS + 2) * N * HALF, width), jnp.float32)
    msg_a, msg_b, q, small = call(start_kernel, (first_shape, first_shape, shape, unit_small), 28, *halves, *small)
    field, state, frames, first = (), (), [], None
    for instant in range(STEPS):
        for pair in range(ITERS // 2):
            closing = pair + 1 == ITERS // 2
            last = closing and instant + 1 == STEPS
            got_b = lax.ppermute(msg_b, both, b_pairs)
            got_a = lax.ppermute(msg_a, "row", swap)
            first = first or (got_a, got_b)
            response, product, part = call(functools.partial(beside_kernel, instant, pair), (shape,) * 3, 30,
                                           *halves, beyond_0, *first, small, got_a, q, *field, *state[:1])
            out = call(functools.partial(pair_kernel, instant, pair, last), (shape,) * (1 if last else 4 if closing else 6),
                       50, *halves, small, got_b, response, product, part, *field, *state)
            field = out[:1]
            if not last:
                q, msg_a, msg_b = out[1:4]
                state = out[4:]
        frames.append(field[0])

    done = jnp.stack(frames).reshape(STEPS, N, HALF, width)
    got = lax.ppermute(jnp.flip(done[:, ROWS:], 1), "row", swap)
    mine = done[:, :ROWS]
    unit_0, unit_1 = jnp.where(parity == 1, got, mine), jnp.where(parity == 1, mine, got)
    done = jnp.concatenate([unit_0, jnp.flip(unit_1, 2)], axis=2)
    return jnp.where(row == 1, jnp.flip(done, 1), done)


def solution(mesh):
    rows, cols = mesh.shape["row"], mesh.shape["col"]
    return jax.shard_map(
        shards_chain if rows == 2 else shards_general,
        mesh=mesh,
        in_specs=(
            P("row", "col", None, None),
            P(None, "row", "col", None, None),
            P("row", "col", None),
            P("row", "col", None),
            P("row", "col", None),
            P("row", "col", None, None, None),
            P("row", "col", None, None),
        ),
        out_specs=P(None, "row", "col", None),
        check_vma=False,
    )
```

```python
import functools

import jax
import jax.numpy as jnp
from jax import lax
from jax.experimental import pallas as pl
from jax.experimental.pallas import tpu as pltpu
from jax.sharding import PartitionSpec as P

STEPS = 4
ITERS = 8

spec_center = 6.4
spec_radius = 5.6


def schedule():
    strides, momenta = [], []
    stride = 1.0 / spec_center
    for sweep in range(ITERS):
        if sweep == 0:
            momentum = 0.0
        else:
            if sweep == 1:
                momentum = 0.5 * (spec_radius * stride) ** 2
            else:
                momentum = (spec_radius * stride / 2.0) ** 2
            stride = 1.0 / (spec_center - momentum / stride)
        strides.append(stride)
        momenta.append(momentum)
    return strides, momenta


STRIDES, MOMENTA = schedule()


def swap_pairs(count, first):
    pairs = []
    for i in range(first, count - 1, 2):
        pairs += [(i, i + 1), (i + 1, i)]
    return pairs


def exchange(field):
    arrived = []
    for axis in ("row", "col"):
        count = lax.axis_size(axis)
        for first in (0, 1):
            pairs = swap_pairs(count, first)
            arrived.append(lax.ppermute(field, axis, pairs) if pairs else None)
    return arrived


def beside(field, halos, odd_row, odd_col, cols):
    tiles = field.shape[0]
    row_a, row_b, col_a, col_b = halos
    zero = jnp.zeros_like(field)
    row_a, row_b, col_a, col_b = [zero if h is None else h for h in (row_a, row_b, col_a, col_b)]
    above = jnp.where(odd_row, row_a, row_b)
    below = jnp.where(odd_row, row_b, row_a)
    west = jnp.where(odd_col, col_a, col_b)
    east = jnp.where(odd_col, col_b, col_a)
    up = jnp.concatenate([above[tiles - cols:], field[: tiles - cols]], axis=0)
    down = jnp.concatenate([field[cols:], below[:cols]], axis=0)
    column = lax.broadcasted_iota(jnp.int32, field.shape, 0) % cols
    rolled = jnp.concatenate([field[tiles - 1:], field[: tiles - 1]], axis=0)
    west_edge = jnp.concatenate([west[cols - 1:], west[: cols - 1]], axis=0)
    left = jnp.where(column == 0, west_edge, rolled)
    rolled = jnp.concatenate([field[1:], field[:1]], axis=0)
    east_edge = jnp.concatenate([east[tiles - cols + 1:], east[: tiles - cols + 1]], axis=0)
    right = jnp.where(column == cols - 1, east_edge, rolled)
    return up, down, left, right


def blocks_times(field, around, own_ref, nb_ref):
    tiles, width = field.shape
    chunk = 32
    lane = lax.broadcasted_iota(jnp.int32, (chunk, width), 1)
    sub = lax.broadcasted_iota(jnp.int32, (chunk, width), 0)
    outs = []
    for t in range(tiles):
        vecs = [f[t:t + 1] for f in around]
        mine = field[t:t + 1]
        spread = jnp.zeros((chunk, width), jnp.float32)
        for g in range(0, width, chunk):
            acc = own_ref[t, g:g + chunk, :] * mine
            for n, vec in enumerate(vecs):
                acc = acc + nb_ref[n, t, g:g + chunk, :] * vec
            total = jnp.sum(acc, axis=1, keepdims=True)
            spread = jnp.where(lane == sub + g, total, spread)
        outs.append(jnp.sum(spread, axis=0, keepdims=True))
    return jnp.concatenate(outs, axis=0)


def kernel(sweep, cols, present, flags, own_ref, nb_ref, weights, *refs):
    n_halo = sum(present)
    halo_refs, refs = refs[:n_halo], refs[n_halo:]
    halo_iter = iter(halo_refs)
    halos = [next(halo_iter)[...] if p else None for p in present]
    odd_row, odd_col = flags[0] == 1, flags[1] == 1
    field_ref, refs = refs[0], refs[1:]
    field = field_ref[...]
    around = beside(field, halos, odd_row, odd_col, cols)
    around = [f * weights[n] for n, f in enumerate(around)]
    product = blocks_times(field, around, own_ref, nb_ref)
    if sweep < 0:
        injected, search_out, residue_out, estimate_out = refs
        residue = injected[...] - product
        search_out[...] = residue
        residue_out[...] = residue
        estimate_out[...] = field + STRIDES[0] * residue
    else:
        capacity, residue_in, estimate_in = refs[:3]
        outs = refs[3:]
        residue = residue_in[...] - STRIDES[sweep] * (product + capacity[...] * field)
        search = residue + MOMENTA[sweep + 1] * field
        estimate = estimate_in[...] + STRIDES[sweep + 1] * search
        if sweep + 2 < ITERS:
            outs[0][...] = search
            outs[1][...] = residue
            outs[2][...] = estimate
        else:
            outs[0][...] = estimate


def collect(currents, slot_tile, tiles, width):
    slots, frames = currents.shape[3:]
    names = jnp.pad(slot_tile.astype(jnp.float32)[..., None, :],
                    ((0, 0), (0, 0), (0, 0), (0, 0), (0, frames - slots)))
    packed = jnp.concatenate([currents, names], axis=3)
    arrived = lax.all_to_all(packed, "col", split_axis=2, concat_axis=1, tiled=True)[0, :, 0]
    targets = arrived[:, slots, :slots]
    chooser = (targets[..., None] == jnp.arange(tiles, dtype=jnp.float32)).astype(jnp.float32)
    injected = jnp.einsum("skt,skf->tf", chooser, arrived[:, :slots], precision=lax.Precision.HIGHEST)
    return injected.reshape(tiles, STEPS, width)


def shards_general(own_block, neighbor_block, pattern, capacity, initial, currents, slot_tile):
    tile_rows, tile_cols, width = initial.shape
    tiles = tile_rows * tile_cols
    flags = jnp.stack([lax.axis_index("row") % 2, lax.axis_index("col") % 2]).astype(jnp.int32)

    voltage = initial.reshape(tiles, width)
    halos = exchange(voltage)

    injected = collect(currents, slot_tile, tiles, width)

    own = own_block.reshape(tiles, width, width)
    nb = neighbor_block.reshape(4, tiles, width, width)
    weights = jnp.broadcast_to(
        jnp.moveaxis(pattern.reshape(tiles, 4), 1, 0).astype(jnp.float32)[..., None], (4, tiles, width)
    )
    cap = capacity.reshape(tiles, width)
    shape = jax.ShapeDtypeStruct((tiles, width), jnp.float32)
    vmem = pl.BlockSpec(memory_space=pltpu.VMEM)
    smem = pl.BlockSpec(memory_space=pltpu.SMEM)

    def call(sweep, halos, *state):
        present = tuple(h is not None for h in halos)
        ins = (flags, own, nb, weights) + tuple(h for h in halos if h is not None) + state
        n_out = 1 if sweep + 2 == ITERS else 3
        out = pl.pallas_call(
            functools.partial(kernel, sweep, tile_cols, present),
            out_shape=(shape,) * n_out,
            in_specs=[smem] + [vmem] * (len(ins) - 1),
            out_specs=(vmem,) * n_out,
            compiler_params=pltpu.CompilerParams(vmem_limit_bytes=8 * 2**20),
            cost_estimate=pl.CostEstimate(flops=2 * 5 * tiles * width * width, bytes_accessed=5 * tiles * width * width * 4,
                                          transcendentals=0),
            name="couple",
        )(*ins)
        return out

    frames_out = []
    for instant in range(STEPS):
        if instant:
            halos = exchange(voltage)
        search, residue, estimate = call(-1, halos, voltage, injected[:, instant])
        for sweep in range(ITERS - 1):
            halos = exchange(search)
            out = call(sweep, halos, search, cap, residue, estimate)
            if sweep + 2 < ITERS:
                search, residue, estimate = out
            else:
                (voltage,) = out
        frames_out.append(voltage)
    return jnp.stack(frames_out).reshape(STEPS, tile_rows, tile_cols, width)


ROWS, HALF = 2, 2
N = 2 * ROWS
OWN, SIDE_A, SIDE_B, OUT_IN, IN_OUT, IN_IN, FACING, PACKED = 0, 4, 8, 12, 14, 16, 18, 20
TILES = [(j, b) for j in range(N) for b in range(HALF)]
ORIGIN = [(0, 0), (0, 1), (1, 1), (1, 0)]
CAPACITY, INITIAL = STEPS, STEPS + 1
SPLIT = ((PACKED,), (OUT_IN, FACING - OUT_IN))


def unit_device(unit, n_col):
    col = unit // 2
    return (unit + col) % 2, col


def half_tiles(y, col, n_col, cols, sent):
    k = (y + col + sent) % 2
    rows = (y, 1 - y)
    inward, outward = 1 - y, y
    at = [b + k * (cols - 1 - 2 * b) for b in range(HALF)]
    inside = jnp.where(col == k * (n_col - 1), 0.0, 1.0)
    tiles = [None] * PACKED
    for h in range(ROWS):
        for b in range(HALF):
            tiles[OWN + h * HALF + b] = (None, rows[h], at[b], None)
            tiles[SIDE_A + h * HALF + b] = (3 - k, rows[h], at[b], None)
            tiles[SIDE_B + h * HALF + b] = (2 + k, rows[h], at[b], inside if b == 0 else None)
        tiles[FACING + h] = (2 + k, rows[h], HALF - k, None)
    for b in range(HALF):
        tiles[OUT_IN + b] = (inward, rows[0], at[b], None)
        tiles[IN_OUT + b] = (outward, rows[1], at[b], None)
        tiles[IN_IN + b] = (inward, rows[1], at[b], None)
    return tiles


def pack_kernel(n_col, sent, first, count, pattern_hbm, own_hbm, nb_hbm, out, *rest):
    pattern_ref, sems = rest[-2:]
    tiles = half_tiles(lax.axis_index("row"), lax.axis_index("col"), n_col, own_hbm.shape[1], sent)
    pattern_copy = pltpu.make_async_copy(pattern_hbm, pattern_ref, sems.at[count])
    pattern_copy.start()
    copies = []
    for i in range(count):
        direction, row, at, _ = tiles[first + i]
        source = own_hbm.at[row, at] if direction is None else nb_hbm.at[direction, row, at]
        copies.append(pltpu.make_async_copy(source, out.at[i], sems.at[i]))
    for copy in copies:
        copy.start()
    pattern_copy.wait()
    for i in range(count):
        direction, row, at, weight = tiles[first + i]
        copies[i].wait()
        if direction is not None:
            scale = pattern_ref[row, at, direction].astype(jnp.float32)
            out[i] = out[i] * (scale if weight is None else scale * weight)
    if not sent:
        for h in range(ROWS):
            rest[0][h] = out[SIDE_B + h * HALF]


def block_of(refs, sizes, slot):
    for ref, size in zip(refs, sizes):
        if slot < size:
            return lambda g, n: ref[slot, g:g + n, :]
        slot -= size


def half_block(halves, i, slot):
    return block_of(halves[i], SPLIT[i], slot)


def tile_terms(halves, j, b):
    i, h = ORIGIN[j]
    terms = [(OWN + h * HALF + b, (j, b))]
    if h == 0:
        terms.append((OUT_IN + b, ((1, 2)[i], b)))
    else:
        terms.append((IN_OUT + b, ((0, 3)[i], b)))
        terms.append((IN_IN + b, ((2, 1)[i], b)))
    terms.append(((SIDE_A if b == 0 else SIDE_B) + h * HALF + b, (j, 1 - b)))
    return [(half_block(halves, i, slot), at) for slot, at in terms]


def halo_block(halves, j, b):
    i, h = ORIGIN[j]
    return half_block(halves, i, (SIDE_B if b == 0 else SIDE_A) + h * HALF + b)


def facing_block(halves, beyond_0, first_a, first_b, j, b):
    i, h = ORIGIN[j]
    if i == 0:
        return half_block(halves, i, FACING + h) if b == 1 else lambda g, n: beyond_0[h, g:g + n, :]
    first = first_a if b == 1 else first_b
    start = 2 * N + h * first.shape[1]
    return lambda g, n: first[start + g:start + g + n, :]


def matvec(terms, chunk=32):
    width = terms[0][1].shape[1]
    lane = lax.broadcasted_iota(jnp.int32, (chunk, width), 1)
    sub = lax.broadcasted_iota(jnp.int32, (chunk, width), 0)
    spread = jnp.zeros((chunk, width), jnp.float32)
    for g in range(0, width, chunk):
        acc = None
        for block, vec in terms:
            part = block(g, chunk) * vec
            acc = part if acc is None else acc + part
        total = jnp.sum(acc, axis=1, keepdims=True)
        spread = jnp.where(lane == sub + g, total, spread)
    return jnp.sum(spread, axis=0, keepdims=True)


def rows_of(ref, start=0, count=N * HALF):
    return [ref[start + i:start + i + 1, :] for i in range(count)]


def put(ref, rows, start=0):
    for i, row in enumerate(rows):
        ref[start + i:start + i + 1, :] = row


def each(body, *fields):
    return [body(*rows) for rows in zip(*fields)]


def tile(j, b):
    return j * HALF + b


def products(terms, f):
    return [(block, f[tile(*at)]) for block, at in terms]


def inner_product(f, halves):
    return [matvec(products(tile_terms(halves, j, b), f)) for j, b in TILES]


def message(f, g, b):
    order = range(N)[::-1] if b == 1 else range(N)
    return [x[tile(j, b)] for x in (f, g) for j in order]


def ahead(first, sweep, f, q, residue, capacity, injected):
    if first:
        return each(lambda source, a: source - a, injected, q)
    return each(
        lambda v, a, r, c: r - STRIDES[sweep] * (a + c * v) + MOMENTA[sweep + 1] * v, f, q, residue, capacity
    )


def small_part(small, index):
    return rows_of(small, index * N * HALF)


def join_kernel(keep, recv, small):
    n = ROWS * HALF
    for i in range(0, keep.shape[0], n):
        small[2 * i:2 * i + n, :] = keep[i:i + n, :]
        small[2 * i + n:2 * i + n + HALF, :] = recv[i + HALF:i + n, :]
        small[2 * i + n + HALF:2 * i + 2 * n, :] = recv[i:i + HALF, :]


def start_kernel(keep, recv_0, recv_1, small, msg_a, msg_b, q_out):
    halves = ((keep,), (recv_0, recv_1))
    f = small_part(small, INITIAL)
    q = inner_product(f, halves)
    put(q_out, q)
    g = ahead(True, 0, f, q, None, None, small_part(small, 0))
    put(msg_a, message(f, g, 1))
    put(msg_b, message(f, g, 0))
    width = small.shape[1]
    for h in range(ROWS):
        start = 2 * N + h * width
        msg_a[start:start + width, :] = keep[SIDE_A + h * HALF + 1]
        msg_b[start:start + width, :] = recv_0[SIDE_B + h * HALF]


def by_target_kernel(currents, slot_tile, out):
    targets, slots, frames = currents.shape
    width = out.shape[2] - slots * frames
    names = slot_tile[...].astype(jnp.float32)
    names = jnp.concatenate([names, jnp.zeros((targets, width - slots), jnp.float32)], axis=1)
    for d in range(targets):
        for k in range(slots):
            out[d, :, k * frames:(k + 1) * frames] = currents[d, k:k + 1, :]
        out[d, :, slots * frames:] = names[d:d + 1, :]


def small_kernel(place_ref, arrived, capacity, initial, keep, send, injected):
    y, col = place_ref[0], place_ref[1]
    tiles, frames = injected.shape
    _, cols, width = capacity.shape
    slots = (arrived.shape[1] - width) // frames
    for t in range(tiles):
        total = jnp.zeros((arrived.shape[0], frames), jnp.float32)
        for k in range(slots):
            feeds = arrived[:, slots * frames + k:slots * frames + k + 1] == float(t)
            total = total + jnp.where(feeds, 1.0, 0.0) * arrived[:, k * frames:(k + 1) * frames]
        injected[t:t + 1, :] = jnp.sum(total, axis=0, keepdims=True)
    for sent, out in ((0, keep), (1, send)):
        parity = (y + col + sent) % 2
        for h in range(ROWS):
            row = y if h == 0 else 1 - y
            for b in range(HALF):
                at = b + parity * (cols - 1 - 2 * b)
                currents = injected[pl.ds(row * cols + at, 1), :]
                parts = [currents[:, n * width:(n + 1) * width] for n in range(STEPS)]
                parts += [x[row, pl.ds(at, 1), :] for x in (capacity, initial)]
                for n, part in enumerate(parts):
                    i = n * ROWS * HALF + h * HALF + b
                    out[i:i + 1, :] = part


def advance(instant, pair, small, product, f, residue):
    if pair == 0:
        residue = each(lambda source, a: source - a, small_part(small, instant), product)
        return residue, residue, 1.0
    sweep = 2 * pair - 1
    residue = each(lambda r, a, c, v: r - STRIDES[sweep] * (a + c * v), residue, product, small_part(small, CAPACITY), f)
    return residue, each(lambda r, v: r + MOMENTA[sweep + 1] * v, residue, f), STRIDES[sweep]


def beside_kernel(instant, pair, keep, recv_0, recv_1, beyond_0, first_a, first_b, small, got_a, q_ref, *refs):
    halves = ((keep,), (recv_0, recv_1))
    response_out, product_out, part_out = refs[-3:]
    f = small_part(small, INITIAL) if instant == pair == 0 else rows_of(refs[0])
    residue = None if pair == 0 else rows_of(refs[1])
    product = rows_of(q_ref)
    for j in range(N):
        product[tile(j, 1)] += matvec([(halo_block(halves, j, 1), got_a[j:j + 1, :])])
    put(product_out, product)
    response = [
        matvec([(facing_block(halves, beyond_0, first_a, first_b, j, b), f[tile(j, b)])]) for j, b in TILES
    ]
    put(response_out, response)
    _, f2, scale = advance(instant, pair, small, product, f, residue)
    part = []
    for j, b in TILES:
        terms = products(tile_terms(halves, j, b), f2)
        if b == 1:
            beside = got_a[N + j:N + j + 1, :] - scale * response[tile(j, b)]
            part.append(matvec(terms[:-1] + [(halo_block(halves, j, b), beside)]))
        else:
            part.append(matvec(terms[-1:]))
    put(part_out, part)


def pair_kernel(instant, pair, last, keep, recv_0, recv_1, small, got_b, response, product_ref, part_ref, *refs):
    halves = ((keep,), (recv_0, recv_1))
    first = pair == 0
    capacity = small_part(small, CAPACITY)
    if first and instant == 0:
        f = small_part(small, INITIAL)
    else:
        f, refs = rows_of(refs[0]), refs[1:]
    residue = estimate = None
    if not first:
        residue, estimate, refs = rows_of(refs[0]), rows_of(refs[1]), refs[2:]

    product = rows_of(product_ref)
    for j in range(N):
        product[tile(j, 0)] += matvec([(halo_block(halves, j, 0), got_b[j:j + 1, :])])
    residue, f2, scale = advance(instant, pair, small, product, f, residue)
    if first:
        estimate = each(lambda v, p: v + STRIDES[0] * p, f, f2)
    else:
        estimate = each(lambda e, p: e + STRIDES[2 * pair] * p, estimate, f2)

    total = rows_of(part_ref)
    for j, b in TILES:
        i = tile(j, b)
        terms = products(tile_terms(halves, j, b), f2)
        if b == 0:
            beside = got_b[N + j:N + j + 1, :] - scale * response[i:i + 1, :]
            total[i] += matvec(terms[:-1] + [(halo_block(halves, j, b), beside)])
        else:
            total[i] += matvec(terms[-1:])
    sweep = 2 * pair
    residue = each(lambda r, a, c, v: r - STRIDES[sweep] * (a + c * v), residue, total, capacity, f2)
    f3 = each(lambda r, v: r + MOMENTA[sweep + 1] * v, residue, f2)
    estimate = each(lambda e, p: e + STRIDES[sweep + 1] * p, estimate, f3)
    closing = sweep + 2 == ITERS
    if closing:
        f3 = estimate
    f_out, refs = refs[0], refs[1:]
    put(f_out, f3)
    if last:
        return
    q = inner_product(f3, halves)
    upcoming = small_part(small, instant + 1) if closing else None
    g = ahead(closing, sweep + 1, f3, q, residue, capacity, upcoming)
    q_out, msg_a, msg_b = refs[:3]
    put(msg_a, message(f3, g, 1))
    put(msg_b, message(f3, g, 0))
    put(q_out, q)
    if not closing:
        put(refs[3], residue)
        put(refs[4], estimate)


def shards_chain(own_block, neighbor_block, pattern, capacity, initial, currents, slot_tile):
    tile_rows, tile_cols, width = initial.shape
    n_col = lax.axis_size("col")
    row, col = lax.axis_index("row"), lax.axis_index("col")
    both = ("row", "col")
    swap = [(0, 1), (1, 0)]
    b_pairs = []
    for unit in range(1, 2 * n_col - 1, 2):
        ends = [r * n_col + c for r, c in (unit_device(unit, n_col), unit_device(unit + 1, n_col))]
        b_pairs += [tuple(ends), tuple(ends[::-1])]
    parity = (row + col) % 2

    vmem = pl.BlockSpec(memory_space=pltpu.VMEM)
    smem = pl.BlockSpec(memory_space=pltpu.SMEM)
    hbm = pl.BlockSpec(memory_space=pltpu.HBM)
    limit = pltpu.CompilerParams(vmem_limit_bytes=16 * 2**20)
    place = jnp.stack([row, col]).astype(jnp.int32)
    blocks = [pltpu.with_memory_space_constraint(x, pltpu.HBM) for x in (pattern, own_block, neighbor_block)]

    def pack(sent, first, count, extra=()):
        return pl.pallas_call(
            functools.partial(pack_kernel, n_col, sent, first, count),
            out_shape=[jax.ShapeDtypeStruct((n, width, width), jnp.float32) for n in (count, *extra)],
            in_specs=[hbm, hbm, hbm],
            out_specs=[vmem] * (1 + len(extra)),
            scratch_shapes=[pltpu.SMEM(pattern.shape, jnp.int32), pltpu.SemaphoreType.DMA((count + 1,))],
            compiler_params=limit,
            name="pack",
        )(*blocks)

    recv = []
    for first, count in ((0, SPLIT[1][0]), SPLIT[1]):
        (send,) = pack(1, first, count)
        recv.append(lax.ppermute(send, "row", swap))
    keep, facing_0 = pack(0, 0, PACKED, (ROWS,))

    unit_small = jax.ShapeDtypeStruct(((STEPS + 2) * N * HALF, width), jnp.float32)

    def beside(currents, slot_tile, capacity, initial, facing_0):
        beyond_0 = lax.ppermute(facing_0, both, b_pairs)
        slots, frames = currents.shape[3:]
        by_target = pl.pallas_call(
            by_target_kernel,
            out_shape=jax.ShapeDtypeStruct((n_col, 1, slots * frames + width), jnp.float32),
            in_specs=[vmem, vmem],
            out_specs=vmem,
            compiler_params=limit,
            name="by_target",
        )(currents.reshape(n_col, slots, frames), slot_tile.reshape(n_col, slots))
        arrived = lax.all_to_all(by_target, "col", split_axis=0, concat_axis=0, tiled=True)
        half = jax.ShapeDtypeStruct(((STEPS + 2) * ROWS * HALF, width), jnp.float32)
        small, send = pl.pallas_call(
            small_kernel,
            out_shape=(half, half),
            in_specs=[smem, vmem, vmem, vmem],
            out_specs=(vmem, vmem),
            scratch_shapes=[pltpu.VMEM((tile_rows * tile_cols, frames), jnp.float32)],
            compiler_params=limit,
            name="small",
        )(place, arrived.reshape(n_col, slots * frames + width), capacity, initial)
        small = pl.pallas_call(
            join_kernel,
            out_shape=unit_small,
            in_specs=[vmem, vmem],
            out_specs=vmem,
            compiler_params=limit,
            name="join",
        )(small, lax.ppermute(send, "row", swap))
        return small, beyond_0

    small, beyond_0 = lax.cond(
        row < lax.axis_size("row"),
        beside,
        lambda currents, slot_tile, capacity, initial, facing_0: (
            jnp.zeros(unit_small.shape, jnp.float32), facing_0
        ),
        currents, slot_tile, capacity, initial, facing_0,
    )

    shape = jax.ShapeDtypeStruct((N * HALF, width), jnp.float32)
    halves = (keep, *recv)

    def call(body, outs, blocks, *ins):
        return pl.pallas_call(
            body,
            out_shape=outs,
            in_specs=[vmem] * len(ins),
            out_specs=(vmem,) * len(outs),
            compiler_params=limit,
            cost_estimate=pl.CostEstimate(flops=2 * blocks * width * width, bytes_accessed=blocks * width * width * 4,
                                          transcendentals=0),
            name="pair",
        )(*ins)

    first_shape = jax.ShapeDtypeStruct((2 * N + ROWS * width, width), jnp.float32)
    msg_a, msg_b, q = call(start_kernel, (first_shape, first_shape, shape), 28, *halves, small)
    field, state, frames, first = (), (), [], None
    for instant in range(STEPS):
        for pair in range(ITERS // 2):
            closing = pair + 1 == ITERS // 2
            last = closing and instant + 1 == STEPS
            got_b = lax.ppermute(msg_b, both, b_pairs)
            got_a = lax.ppermute(msg_a, "row", swap)
            first = first or (got_a, got_b)
            response, product, part = call(functools.partial(beside_kernel, instant, pair), (shape,) * 3, 30,
                                           *halves, beyond_0, *first, small, got_a, q, *field, *state[:1])
            out = call(functools.partial(pair_kernel, instant, pair, last), (shape,) * (1 if last else 4 if closing else 6),
                       50, *halves, small, got_b, response, product, part, *field, *state)
            field = out[:1]
            if not last:
                q, msg_a, msg_b = out[1:4]
                state = out[4:]
        frames.append(field[0])

    done = jnp.stack(frames).reshape(STEPS, N, HALF, width)
    got = lax.ppermute(jnp.flip(done[:, ROWS:], 1), "row", swap)
    mine = done[:, :ROWS]
    unit_0, unit_1 = jnp.where(parity == 1, got, mine), jnp.where(parity == 1, mine, got)
    done = jnp.concatenate([unit_0, jnp.flip(unit_1, 2)], axis=2)
    return jnp.where(row == 1, jnp.flip(done, 1), done)


def solution(mesh):
    rows, cols = mesh.shape["row"], mesh.shape["col"]
    return jax.shard_map(
        shards_chain if rows == 2 else shards_general,
        mesh=mesh,
        in_specs=(
            P("row", "col", None, None),
            P(None, "row", "col", None, None),
            P("row", "col", None),
            P("row", "col", None),
            P("row", "col", None),
            P("row", "col", None, None, None),
            P("row", "col", None, None),
        ),
        out_specs=P(None, "row", "col", None),
        check_vma=False,
    )
```

```python
import functools

import jax
import jax.numpy as jnp
from jax import lax
from jax.experimental import pallas as pl
from jax.experimental.pallas import tpu as pltpu
from jax.sharding import PartitionSpec as P

STEPS = 4
ITERS = 8

spec_center = 6.4
spec_radius = 5.6


def schedule():
    strides, momenta = [], []
    stride = 1.0 / spec_center
    for sweep in range(ITERS):
        if sweep == 0:
            momentum = 0.0
        else:
            if sweep == 1:
                momentum = 0.5 * (spec_radius * stride) ** 2
            else:
                momentum = (spec_radius * stride / 2.0) ** 2
            stride = 1.0 / (spec_center - momentum / stride)
        strides.append(stride)
        momenta.append(momentum)
    return strides, momenta


STRIDES, MOMENTA = schedule()


def swap_pairs(count, first):
    pairs = []
    for i in range(first, count - 1, 2):
        pairs += [(i, i + 1), (i + 1, i)]
    return pairs


def exchange(field):
    arrived = []
    for axis in ("row", "col"):
        count = lax.axis_size(axis)
        for first in (0, 1):
            pairs = swap_pairs(count, first)
            arrived.append(lax.ppermute(field, axis, pairs) if pairs else None)
    return arrived


def beside(field, halos, odd_row, odd_col, cols):
    tiles = field.shape[0]
    row_a, row_b, col_a, col_b = halos
    zero = jnp.zeros_like(field)
    row_a, row_b, col_a, col_b = [zero if h is None else h for h in (row_a, row_b, col_a, col_b)]
    above = jnp.where(odd_row, row_a, row_b)
    below = jnp.where(odd_row, row_b, row_a)
    west = jnp.where(odd_col, col_a, col_b)
    east = jnp.where(odd_col, col_b, col_a)
    up = jnp.concatenate([above[tiles - cols:], field[: tiles - cols]], axis=0)
    down = jnp.concatenate([field[cols:], below[:cols]], axis=0)
    column = lax.broadcasted_iota(jnp.int32, field.shape, 0) % cols
    rolled = jnp.concatenate([field[tiles - 1:], field[: tiles - 1]], axis=0)
    west_edge = jnp.concatenate([west[cols - 1:], west[: cols - 1]], axis=0)
    left = jnp.where(column == 0, west_edge, rolled)
    rolled = jnp.concatenate([field[1:], field[:1]], axis=0)
    east_edge = jnp.concatenate([east[tiles - cols + 1:], east[: tiles - cols + 1]], axis=0)
    right = jnp.where(column == cols - 1, east_edge, rolled)
    return up, down, left, right


def blocks_times(field, around, own_ref, nb_ref):
    tiles, width = field.shape
    chunk = 32
    lane = lax.broadcasted_iota(jnp.int32, (chunk, width), 1)
    sub = lax.broadcasted_iota(jnp.int32, (chunk, width), 0)
    outs = []
    for t in range(tiles):
        vecs = [f[t:t + 1] for f in around]
        mine = field[t:t + 1]
        spread = jnp.zeros((chunk, width), jnp.float32)
        for g in range(0, width, chunk):
            acc = own_ref[t, g:g + chunk, :] * mine
            for n, vec in enumerate(vecs):
                acc = acc + nb_ref[n, t, g:g + chunk, :] * vec
            total = jnp.sum(acc, axis=1, keepdims=True)
            spread = jnp.where(lane == sub + g, total, spread)
        outs.append(jnp.sum(spread, axis=0, keepdims=True))
    return jnp.concatenate(outs, axis=0)


def kernel(sweep, cols, present, flags, own_ref, nb_ref, weights, *refs):
    n_halo = sum(present)
    halo_refs, refs = refs[:n_halo], refs[n_halo:]
    halo_iter = iter(halo_refs)
    halos = [next(halo_iter)[...] if p else None for p in present]
    odd_row, odd_col = flags[0] == 1, flags[1] == 1
    field_ref, refs = refs[0], refs[1:]
    field = field_ref[...]
    around = beside(field, halos, odd_row, odd_col, cols)
    around = [f * weights[n] for n, f in enumerate(around)]
    product = blocks_times(field, around, own_ref, nb_ref)
    if sweep < 0:
        injected, search_out, residue_out, estimate_out = refs
        residue = injected[...] - product
        search_out[...] = residue
        residue_out[...] = residue
        estimate_out[...] = field + STRIDES[0] * residue
    else:
        capacity, residue_in, estimate_in = refs[:3]
        outs = refs[3:]
        residue = residue_in[...] - STRIDES[sweep] * (product + capacity[...] * field)
        search = residue + MOMENTA[sweep + 1] * field
        estimate = estimate_in[...] + STRIDES[sweep + 1] * search
        if sweep + 2 < ITERS:
            outs[0][...] = search
            outs[1][...] = residue
            outs[2][...] = estimate
        else:
            outs[0][...] = estimate


def collect(currents, slot_tile, tiles, width):
    slots, frames = currents.shape[3:]
    names = jnp.pad(slot_tile.astype(jnp.float32)[..., None, :],
                    ((0, 0), (0, 0), (0, 0), (0, 0), (0, frames - slots)))
    packed = jnp.concatenate([currents, names], axis=3)
    arrived = lax.all_to_all(packed, "col", split_axis=2, concat_axis=1, tiled=True)[0, :, 0]
    targets = arrived[:, slots, :slots]
    chooser = (targets[..., None] == jnp.arange(tiles, dtype=jnp.float32)).astype(jnp.float32)
    injected = jnp.einsum("skt,skf->tf", chooser, arrived[:, :slots], precision=lax.Precision.HIGHEST)
    return injected.reshape(tiles, STEPS, width)


def shards_general(own_block, neighbor_block, pattern, capacity, initial, currents, slot_tile):
    tile_rows, tile_cols, width = initial.shape
    tiles = tile_rows * tile_cols
    flags = jnp.stack([lax.axis_index("row") % 2, lax.axis_index("col") % 2]).astype(jnp.int32)

    voltage = initial.reshape(tiles, width)
    halos = exchange(voltage)

    injected = collect(currents, slot_tile, tiles, width)

    own = own_block.reshape(tiles, width, width)
    nb = neighbor_block.reshape(4, tiles, width, width)
    weights = jnp.broadcast_to(
        jnp.moveaxis(pattern.reshape(tiles, 4), 1, 0).astype(jnp.float32)[..., None], (4, tiles, width)
    )
    cap = capacity.reshape(tiles, width)
    shape = jax.ShapeDtypeStruct((tiles, width), jnp.float32)
    vmem = pl.BlockSpec(memory_space=pltpu.VMEM)
    smem = pl.BlockSpec(memory_space=pltpu.SMEM)

    def call(sweep, halos, *state):
        present = tuple(h is not None for h in halos)
        ins = (flags, own, nb, weights) + tuple(h for h in halos if h is not None) + state
        n_out = 1 if sweep + 2 == ITERS else 3
        out = pl.pallas_call(
            functools.partial(kernel, sweep, tile_cols, present),
            out_shape=(shape,) * n_out,
            in_specs=[smem] + [vmem] * (len(ins) - 1),
            out_specs=(vmem,) * n_out,
            compiler_params=pltpu.CompilerParams(vmem_limit_bytes=8 * 2**20),
            cost_estimate=pl.CostEstimate(flops=2 * 5 * tiles * width * width, bytes_accessed=5 * tiles * width * width * 4,
                                          transcendentals=0),
            name="couple",
        )(*ins)
        return out

    frames_out = []
    for instant in range(STEPS):
        if instant:
            halos = exchange(voltage)
        search, residue, estimate = call(-1, halos, voltage, injected[:, instant])
        for sweep in range(ITERS - 1):
            halos = exchange(search)
            out = call(sweep, halos, search, cap, residue, estimate)
            if sweep + 2 < ITERS:
                search, residue, estimate = out
            else:
                (voltage,) = out
        frames_out.append(voltage)
    return jnp.stack(frames_out).reshape(STEPS, tile_rows, tile_cols, width)


ROWS, HALF = 2, 2
N = 2 * ROWS
OWN, SIDE_A, SIDE_B, OUT_IN, IN_OUT, IN_IN, FACING, PACKED = 0, 4, 8, 12, 14, 16, 18, 20
TILES = [(j, b) for j in range(N) for b in range(HALF)]
ORIGIN = [(0, 0), (0, 1), (1, 1), (1, 0)]
CAPACITY, INITIAL = STEPS, STEPS + 1
SPLIT = ((PACKED,), (OUT_IN, FACING - OUT_IN))


def unit_device(unit, n_col):
    col = unit // 2
    return (unit + col) % 2, col


def half_tiles(y, col, n_col, cols, sent):
    k = (y + col + sent) % 2
    rows = (y, 1 - y)
    inward, outward = 1 - y, y
    at = [b + k * (cols - 1 - 2 * b) for b in range(HALF)]
    inside = jnp.where(col == k * (n_col - 1), 0.0, 1.0)
    tiles = [None] * PACKED
    for h in range(ROWS):
        for b in range(HALF):
            tiles[OWN + h * HALF + b] = (None, rows[h], at[b], None)
            tiles[SIDE_A + h * HALF + b] = (3 - k, rows[h], at[b], None)
            tiles[SIDE_B + h * HALF + b] = (2 + k, rows[h], at[b], inside if b == 0 else None)
        tiles[FACING + h] = (2 + k, rows[h], HALF - k, None)
    for b in range(HALF):
        tiles[OUT_IN + b] = (inward, rows[0], at[b], None)
        tiles[IN_OUT + b] = (outward, rows[1], at[b], None)
        tiles[IN_IN + b] = (inward, rows[1], at[b], None)
    return tiles


def pack_kernel(n_col, sent, first, count, pattern_hbm, own_hbm, nb_hbm, out, *rest):
    pattern_ref, sems = rest[-2:]
    tiles = half_tiles(lax.axis_index("row"), lax.axis_index("col"), n_col, own_hbm.shape[1], sent)
    pattern_copy = pltpu.make_async_copy(pattern_hbm, pattern_ref, sems.at[count])
    pattern_copy.start()
    copies = []
    for i in range(count):
        direction, row, at, _ = tiles[first + i]
        source = own_hbm.at[row, at] if direction is None else nb_hbm.at[direction, row, at]
        copies.append(pltpu.make_async_copy(source, out.at[i], sems.at[i]))
    for copy in copies:
        copy.start()
    pattern_copy.wait()
    for i in range(count):
        direction, row, at, weight = tiles[first + i]
        copies[i].wait()
        if direction is not None:
            scale = pattern_ref[row, at, direction].astype(jnp.float32)
            out[i] = out[i] * (scale if weight is None else scale * weight)
    if not sent:
        for h in range(ROWS):
            rest[0][h] = out[SIDE_B + h * HALF]


def block_of(refs, sizes, slot):
    for ref, size in zip(refs, sizes):
        if slot < size:
            return lambda g, n: ref[slot, g:g + n, :]
        slot -= size


def half_block(halves, i, slot):
    return block_of(halves[i], SPLIT[i], slot)


def tile_terms(halves, j, b):
    i, h = ORIGIN[j]
    terms = [(OWN + h * HALF + b, (j, b))]
    if h == 0:
        terms.append((OUT_IN + b, ((1, 2)[i], b)))
    else:
        terms.append((IN_OUT + b, ((0, 3)[i], b)))
        terms.append((IN_IN + b, ((2, 1)[i], b)))
    terms.append(((SIDE_A if b == 0 else SIDE_B) + h * HALF + b, (j, 1 - b)))
    return [(half_block(halves, i, slot), at) for slot, at in terms]


def halo_block(halves, j, b):
    i, h = ORIGIN[j]
    return half_block(halves, i, (SIDE_B if b == 0 else SIDE_A) + h * HALF + b)


def facing_block(halves, beyond_0, first_a, first_b, j, b):
    i, h = ORIGIN[j]
    if i == 0:
        return half_block(halves, i, FACING + h) if b == 1 else lambda g, n: beyond_0[h, g:g + n, :]
    first = first_a if b == 1 else first_b
    start = 2 * N + h * first.shape[1]
    return lambda g, n: first[start + g:start + g + n, :]


def matvec(terms, chunk=64):
    width = terms[0][1].shape[1]
    lane = lax.broadcasted_iota(jnp.int32, (chunk, width), 1)
    sub = lax.broadcasted_iota(jnp.int32, (chunk, width), 0)
    spread = jnp.zeros((chunk, width), jnp.float32)
    for g in range(0, width, chunk):
        acc = None
        for block, vec in terms:
            part = block(g, chunk) * vec
            acc = part if acc is None else acc + part
        total = jnp.sum(acc, axis=1, keepdims=True)
        spread = jnp.where(lane == sub + g, total, spread)
    return jnp.sum(spread, axis=0, keepdims=True)


def rows_of(ref, start=0, count=N * HALF):
    return [ref[start + i:start + i + 1, :] for i in range(count)]


def put(ref, rows, start=0):
    for i, row in enumerate(rows):
        ref[start + i:start + i + 1, :] = row


def each(body, *fields):
    return [body(*rows) for rows in zip(*fields)]


def tile(j, b):
    return j * HALF + b


def products(terms, f):
    return [(block, f[tile(*at)]) for block, at in terms]


def inner_product(f, halves):
    return [matvec(products(tile_terms(halves, j, b), f)) for j, b in TILES]


def message(f, g, b):
    order = range(N)[::-1] if b == 1 else range(N)
    return [x[tile(j, b)] for x in (f, g) for j in order]


def ahead(first, sweep, f, q, residue, capacity, injected):
    if first:
        return each(lambda source, a: source - a, injected, q)
    return each(
        lambda v, a, r, c: r - STRIDES[sweep] * (a + c * v) + MOMENTA[sweep + 1] * v, f, q, residue, capacity
    )


def small_part(small, index):
    return rows_of(small, index * N * HALF)


def join_kernel(keep, recv, small):
    n = ROWS * HALF
    for i in range(0, keep.shape[0], n):
        small[2 * i:2 * i + n, :] = keep[i:i + n, :]
        small[2 * i + n:2 * i + n + HALF, :] = recv[i + HALF:i + n, :]
        small[2 * i + n + HALF:2 * i + 2 * n, :] = recv[i:i + HALF, :]


def start_kernel(keep, recv_0, recv_1, small, msg_a, msg_b, q_out):
    halves = ((keep,), (recv_0, recv_1))
    f = small_part(small, INITIAL)
    q = inner_product(f, halves)
    put(q_out, q)
    g = ahead(True, 0, f, q, None, None, small_part(small, 0))
    put(msg_a, message(f, g, 1))
    put(msg_b, message(f, g, 0))
    width = small.shape[1]
    for h in range(ROWS):
        start = 2 * N + h * width
        msg_a[start:start + width, :] = keep[SIDE_A + h * HALF + 1]
        msg_b[start:start + width, :] = recv_0[SIDE_B + h * HALF]


def by_target_kernel(currents, slot_tile, out):
    targets, slots, frames = currents.shape
    width = out.shape[2] - slots * frames
    names = slot_tile[...].astype(jnp.float32)
    names = jnp.concatenate([names, jnp.zeros((targets, width - slots), jnp.float32)], axis=1)
    for d in range(targets):
        for k in range(slots):
            out[d, :, k * frames:(k + 1) * frames] = currents[d, k:k + 1, :]
        out[d, :, slots * frames:] = names[d:d + 1, :]


def small_kernel(place_ref, arrived, capacity, initial, keep, send, injected):
    y, col = place_ref[0], place_ref[1]
    tiles, frames = injected.shape
    _, cols, width = capacity.shape
    slots = (arrived.shape[1] - width) // frames
    for t in range(tiles):
        total = jnp.zeros((arrived.shape[0], frames), jnp.float32)
        for k in range(slots):
            feeds = arrived[:, slots * frames + k:slots * frames + k + 1] == float(t)
            total = total + jnp.where(feeds, 1.0, 0.0) * arrived[:, k * frames:(k + 1) * frames]
        injected[t:t + 1, :] = jnp.sum(total, axis=0, keepdims=True)
    for sent, out in ((0, keep), (1, send)):
        parity = (y + col + sent) % 2
        for h in range(ROWS):
            row = y if h == 0 else 1 - y
            for b in range(HALF):
                at = b + parity * (cols - 1 - 2 * b)
                currents = injected[pl.ds(row * cols + at, 1), :]
                parts = [currents[:, n * width:(n + 1) * width] for n in range(STEPS)]
                parts += [x[row, pl.ds(at, 1), :] for x in (capacity, initial)]
                for n, part in enumerate(parts):
                    i = n * ROWS * HALF + h * HALF + b
                    out[i:i + 1, :] = part


def advance(instant, pair, small, product, f, residue):
    if pair == 0:
        residue = each(lambda source, a: source - a, small_part(small, instant), product)
        return residue, residue, 1.0
    sweep = 2 * pair - 1
    residue = each(lambda r, a, c, v: r - STRIDES[sweep] * (a + c * v), residue, product, small_part(small, CAPACITY), f)
    return residue, each(lambda r, v: r + MOMENTA[sweep + 1] * v, residue, f), STRIDES[sweep]


def beside_kernel(instant, pair, keep, recv_0, recv_1, beyond_0, first_a, first_b, small, got_a, q_ref, *refs):
    halves = ((keep,), (recv_0, recv_1))
    response_out, product_out, part_out = refs[-3:]
    f = small_part(small, INITIAL) if instant == pair == 0 else rows_of(refs[0])
    residue = None if pair == 0 else rows_of(refs[1])
    product = rows_of(q_ref)
    for j in range(N):
        product[tile(j, 1)] += matvec([(halo_block(halves, j, 1), got_a[j:j + 1, :])])
    put(product_out, product)
    response = [
        matvec([(facing_block(halves, beyond_0, first_a, first_b, j, b), f[tile(j, b)])]) for j, b in TILES
    ]
    put(response_out, response)
    _, f2, scale = advance(instant, pair, small, product, f, residue)
    part = []
    for j, b in TILES:
        terms = products(tile_terms(halves, j, b), f2)
        if b == 1:
            beside = got_a[N + j:N + j + 1, :] - scale * response[tile(j, b)]
            part.append(matvec(terms[:-1] + [(halo_block(halves, j, b), beside)]))
        else:
            part.append(matvec(terms[-1:]))
    put(part_out, part)


def pair_kernel(instant, pair, last, keep, recv_0, recv_1, small, got_b, response, product_ref, part_ref, *refs):
    halves = ((keep,), (recv_0, recv_1))
    first = pair == 0
    capacity = small_part(small, CAPACITY)
    if first and instant == 0:
        f = small_part(small, INITIAL)
    else:
        f, refs = rows_of(refs[0]), refs[1:]
    residue = estimate = None
    if not first:
        residue, estimate, refs = rows_of(refs[0]), rows_of(refs[1]), refs[2:]

    product = rows_of(product_ref)
    for j in range(N):
        product[tile(j, 0)] += matvec([(halo_block(halves, j, 0), got_b[j:j + 1, :])])
    residue, f2, scale = advance(instant, pair, small, product, f, residue)
    if first:
        estimate = each(lambda v, p: v + STRIDES[0] * p, f, f2)
    else:
        estimate = each(lambda e, p: e + STRIDES[2 * pair] * p, estimate, f2)

    total = rows_of(part_ref)
    for j, b in TILES:
        i = tile(j, b)
        terms = products(tile_terms(halves, j, b), f2)
        if b == 0:
            beside = got_b[N + j:N + j + 1, :] - scale * response[i:i + 1, :]
            total[i] += matvec(terms[:-1] + [(halo_block(halves, j, b), beside)])
        else:
            total[i] += matvec(terms[-1:])
    sweep = 2 * pair
    residue = each(lambda r, a, c, v: r - STRIDES[sweep] * (a + c * v), residue, total, capacity, f2)
    f3 = each(lambda r, v: r + MOMENTA[sweep + 1] * v, residue, f2)
    estimate = each(lambda e, p: e + STRIDES[sweep + 1] * p, estimate, f3)
    closing = sweep + 2 == ITERS
    if closing:
        f3 = estimate
    f_out, refs = refs[0], refs[1:]
    put(f_out, f3)
    if last:
        return
    q = inner_product(f3, halves)
    upcoming = small_part(small, instant + 1) if closing else None
    g = ahead(closing, sweep + 1, f3, q, residue, capacity, upcoming)
    q_out, msg_a, msg_b = refs[:3]
    put(msg_a, message(f3, g, 1))
    put(msg_b, message(f3, g, 0))
    put(q_out, q)
    if not closing:
        put(refs[3], residue)
        put(refs[4], estimate)


def shards_chain(own_block, neighbor_block, pattern, capacity, initial, currents, slot_tile):
    tile_rows, tile_cols, width = initial.shape
    n_col = lax.axis_size("col")
    row, col = lax.axis_index("row"), lax.axis_index("col")
    both = ("row", "col")
    swap = [(0, 1), (1, 0)]
    b_pairs = []
    for unit in range(1, 2 * n_col - 1, 2):
        ends = [r * n_col + c for r, c in (unit_device(unit, n_col), unit_device(unit + 1, n_col))]
        b_pairs += [tuple(ends), tuple(ends[::-1])]
    parity = (row + col) % 2

    vmem = pl.BlockSpec(memory_space=pltpu.VMEM)
    smem = pl.BlockSpec(memory_space=pltpu.SMEM)
    hbm = pl.BlockSpec(memory_space=pltpu.HBM)
    limit = pltpu.CompilerParams(vmem_limit_bytes=16 * 2**20)
    place = jnp.stack([row, col]).astype(jnp.int32)
    blocks = [pltpu.with_memory_space_constraint(x, pltpu.HBM) for x in (pattern, own_block, neighbor_block)]

    def pack(sent, first, count, extra=()):
        return pl.pallas_call(
            functools.partial(pack_kernel, n_col, sent, first, count),
            out_shape=[jax.ShapeDtypeStruct((n, width, width), jnp.float32) for n in (count, *extra)],
            in_specs=[hbm, hbm, hbm],
            out_specs=[vmem] * (1 + len(extra)),
            scratch_shapes=[pltpu.SMEM(pattern.shape, jnp.int32), pltpu.SemaphoreType.DMA((count + 1,))],
            compiler_params=limit,
            name="pack",
        )(*blocks)

    recv = []
    for first, count in ((0, SPLIT[1][0]), SPLIT[1]):
        (send,) = pack(1, first, count)
        recv.append(lax.ppermute(send, "row", swap))
    keep, facing_0 = pack(0, 0, PACKED, (ROWS,))

    unit_small = jax.ShapeDtypeStruct(((STEPS + 2) * N * HALF, width), jnp.float32)

    def beside(currents, slot_tile, capacity, initial, facing_0):
        beyond_0 = lax.ppermute(facing_0, both, b_pairs)
        slots, frames = currents.shape[3:]
        by_target = pl.pallas_call(
            by_target_kernel,
            out_shape=jax.ShapeDtypeStruct((n_col, 1, slots * frames + width), jnp.float32),
            in_specs=[vmem, vmem],
            out_specs=vmem,
            compiler_params=limit,
            name="by_target",
        )(currents.reshape(n_col, slots, frames), slot_tile.reshape(n_col, slots))
        arrived = lax.all_to_all(by_target, "col", split_axis=0, concat_axis=0, tiled=True)
        half = jax.ShapeDtypeStruct(((STEPS + 2) * ROWS * HALF, width), jnp.float32)
        small, send = pl.pallas_call(
            small_kernel,
            out_shape=(half, half),
            in_specs=[smem, vmem, vmem, vmem],
            out_specs=(vmem, vmem),
            scratch_shapes=[pltpu.VMEM((tile_rows * tile_cols, frames), jnp.float32)],
            compiler_params=limit,
            name="small",
        )(place, arrived.reshape(n_col, slots * frames + width), capacity, initial)
        small = pl.pallas_call(
            join_kernel,
            out_shape=unit_small,
            in_specs=[vmem, vmem],
            out_specs=vmem,
            compiler_params=limit,
            name="join",
        )(small, lax.ppermute(send, "row", swap))
        return small, beyond_0

    small, beyond_0 = lax.cond(
        row < lax.axis_size("row"),
        beside,
        lambda currents, slot_tile, capacity, initial, facing_0: (
            jnp.zeros(unit_small.shape, jnp.float32), facing_0
        ),
        currents, slot_tile, capacity, initial, facing_0,
    )

    shape = jax.ShapeDtypeStruct((N * HALF, width), jnp.float32)
    halves = (keep, *recv)

    def call(body, outs, blocks, *ins):
        return pl.pallas_call(
            body,
            out_shape=outs,
            in_specs=[vmem] * len(ins),
            out_specs=(vmem,) * len(outs),
            compiler_params=limit,
            cost_estimate=pl.CostEstimate(flops=2 * blocks * width * width, bytes_accessed=blocks * width * width * 4,
                                          transcendentals=0),
            name="pair",
        )(*ins)

    first_shape = jax.ShapeDtypeStruct((2 * N + ROWS * width, width), jnp.float32)
    msg_a, msg_b, q = call(start_kernel, (first_shape, first_shape, shape), 28, *halves, small)
    field, state, frames, first = (), (), [], None
    for instant in range(STEPS):
        for pair in range(ITERS // 2):
            closing = pair + 1 == ITERS // 2
            last = closing and instant + 1 == STEPS
            got_b = lax.ppermute(msg_b, both, b_pairs)
            got_a = lax.ppermute(msg_a, "row", swap)
            first = first or (got_a, got_b)
            response, product, part = call(functools.partial(beside_kernel, instant, pair), (shape,) * 3, 30,
                                           *halves, beyond_0, *first, small, got_a, q, *field, *state[:1])
            out = call(functools.partial(pair_kernel, instant, pair, last), (shape,) * (1 if last else 4 if closing else 6),
                       50, *halves, small, got_b, response, product, part, *field, *state)
            field = out[:1]
            if not last:
                q, msg_a, msg_b = out[1:4]
                state = out[4:]
        frames.append(field[0])

    done = jnp.stack(frames).reshape(STEPS, N, HALF, width)
    got = lax.ppermute(jnp.flip(done[:, ROWS:], 1), "row", swap)
    mine = done[:, :ROWS]
    unit_0, unit_1 = jnp.where(parity == 1, got, mine), jnp.where(parity == 1, mine, got)
    done = jnp.concatenate([unit_0, jnp.flip(unit_1, 2)], axis=2)
    return jnp.where(row == 1, jnp.flip(done, 1), done)


def solution(mesh):
    rows, cols = mesh.shape["row"], mesh.shape["col"]
    return jax.shard_map(
        shards_chain if rows == 2 else shards_general,
        mesh=mesh,
        in_specs=(
            P("row", "col", None, None),
            P(None, "row", "col", None, None),
            P("row", "col", None),
            P("row", "col", None),
            P("row", "col", None),
            P("row", "col", None, None, None),
            P("row", "col", None, None),
        ),
        out_specs=P(None, "row", "col", None),
        check_vma=False,
    )
```

```python
import functools

import jax
import jax.numpy as jnp
from jax import lax
from jax.experimental import pallas as pl
from jax.experimental.pallas import tpu as pltpu
from jax.sharding import PartitionSpec as P

STEPS = 4
ITERS = 8

spec_center = 6.4
spec_radius = 5.6


def schedule():
    strides, momenta = [], []
    stride = 1.0 / spec_center
    for sweep in range(ITERS):
        if sweep == 0:
            momentum = 0.0
        else:
            if sweep == 1:
                momentum = 0.5 * (spec_radius * stride) ** 2
            else:
                momentum = (spec_radius * stride / 2.0) ** 2
            stride = 1.0 / (spec_center - momentum / stride)
        strides.append(stride)
        momenta.append(momentum)
    return strides, momenta


STRIDES, MOMENTA = schedule()


def swap_pairs(count, first):
    pairs = []
    for i in range(first, count - 1, 2):
        pairs += [(i, i + 1), (i + 1, i)]
    return pairs


def exchange(field):
    arrived = []
    for axis in ("row", "col"):
        count = lax.axis_size(axis)
        for first in (0, 1):
            pairs = swap_pairs(count, first)
            arrived.append(lax.ppermute(field, axis, pairs) if pairs else None)
    return arrived


def beside(field, halos, odd_row, odd_col, cols):
    tiles = field.shape[0]
    row_a, row_b, col_a, col_b = halos
    zero = jnp.zeros_like(field)
    row_a, row_b, col_a, col_b = [zero if h is None else h for h in (row_a, row_b, col_a, col_b)]
    above = jnp.where(odd_row, row_a, row_b)
    below = jnp.where(odd_row, row_b, row_a)
    west = jnp.where(odd_col, col_a, col_b)
    east = jnp.where(odd_col, col_b, col_a)
    up = jnp.concatenate([above[tiles - cols:], field[: tiles - cols]], axis=0)
    down = jnp.concatenate([field[cols:], below[:cols]], axis=0)
    column = lax.broadcasted_iota(jnp.int32, field.shape, 0) % cols
    rolled = jnp.concatenate([field[tiles - 1:], field[: tiles - 1]], axis=0)
    west_edge = jnp.concatenate([west[cols - 1:], west[: cols - 1]], axis=0)
    left = jnp.where(column == 0, west_edge, rolled)
    rolled = jnp.concatenate([field[1:], field[:1]], axis=0)
    east_edge = jnp.concatenate([east[tiles - cols + 1:], east[: tiles - cols + 1]], axis=0)
    right = jnp.where(column == cols - 1, east_edge, rolled)
    return up, down, left, right


def blocks_times(field, around, own_ref, nb_ref):
    tiles, width = field.shape
    chunk = 32
    lane = lax.broadcasted_iota(jnp.int32, (chunk, width), 1)
    sub = lax.broadcasted_iota(jnp.int32, (chunk, width), 0)
    outs = []
    for t in range(tiles):
        vecs = [f[t:t + 1] for f in around]
        mine = field[t:t + 1]
        spread = jnp.zeros((chunk, width), jnp.float32)
        for g in range(0, width, chunk):
            acc = own_ref[t, g:g + chunk, :] * mine
            for n, vec in enumerate(vecs):
                acc = acc + nb_ref[n, t, g:g + chunk, :] * vec
            total = jnp.sum(acc, axis=1, keepdims=True)
            spread = jnp.where(lane == sub + g, total, spread)
        outs.append(jnp.sum(spread, axis=0, keepdims=True))
    return jnp.concatenate(outs, axis=0)


def kernel(sweep, cols, present, flags, own_ref, nb_ref, weights, *refs):
    n_halo = sum(present)
    halo_refs, refs = refs[:n_halo], refs[n_halo:]
    halo_iter = iter(halo_refs)
    halos = [next(halo_iter)[...] if p else None for p in present]
    odd_row, odd_col = flags[0] == 1, flags[1] == 1
    field_ref, refs = refs[0], refs[1:]
    field = field_ref[...]
    around = beside(field, halos, odd_row, odd_col, cols)
    around = [f * weights[n] for n, f in enumerate(around)]
    product = blocks_times(field, around, own_ref, nb_ref)
    if sweep < 0:
        injected, search_out, residue_out, estimate_out = refs
        residue = injected[...] - product
        search_out[...] = residue
        residue_out[...] = residue
        estimate_out[...] = field + STRIDES[0] * residue
    else:
        capacity, residue_in, estimate_in = refs[:3]
        outs = refs[3:]
        residue = residue_in[...] - STRIDES[sweep] * (product + capacity[...] * field)
        search = residue + MOMENTA[sweep + 1] * field
        estimate = estimate_in[...] + STRIDES[sweep + 1] * search
        if sweep + 2 < ITERS:
            outs[0][...] = search
            outs[1][...] = residue
            outs[2][...] = estimate
        else:
            outs[0][...] = estimate


def collect(currents, slot_tile, tiles, width):
    slots, frames = currents.shape[3:]
    names = jnp.pad(slot_tile.astype(jnp.float32)[..., None, :],
                    ((0, 0), (0, 0), (0, 0), (0, 0), (0, frames - slots)))
    packed = jnp.concatenate([currents, names], axis=3)
    arrived = lax.all_to_all(packed, "col", split_axis=2, concat_axis=1, tiled=True)[0, :, 0]
    targets = arrived[:, slots, :slots]
    chooser = (targets[..., None] == jnp.arange(tiles, dtype=jnp.float32)).astype(jnp.float32)
    injected = jnp.einsum("skt,skf->tf", chooser, arrived[:, :slots], precision=lax.Precision.HIGHEST)
    return injected.reshape(tiles, STEPS, width)


def shards_general(own_block, neighbor_block, pattern, capacity, initial, currents, slot_tile):
    tile_rows, tile_cols, width = initial.shape
    tiles = tile_rows * tile_cols
    flags = jnp.stack([lax.axis_index("row") % 2, lax.axis_index("col") % 2]).astype(jnp.int32)

    voltage = initial.reshape(tiles, width)
    halos = exchange(voltage)

    injected = collect(currents, slot_tile, tiles, width)

    own = own_block.reshape(tiles, width, width)
    nb = neighbor_block.reshape(4, tiles, width, width)
    weights = jnp.broadcast_to(
        jnp.moveaxis(pattern.reshape(tiles, 4), 1, 0).astype(jnp.float32)[..., None], (4, tiles, width)
    )
    cap = capacity.reshape(tiles, width)
    shape = jax.ShapeDtypeStruct((tiles, width), jnp.float32)
    vmem = pl.BlockSpec(memory_space=pltpu.VMEM)
    smem = pl.BlockSpec(memory_space=pltpu.SMEM)

    def call(sweep, halos, *state):
        present = tuple(h is not None for h in halos)
        ins = (flags, own, nb, weights) + tuple(h for h in halos if h is not None) + state
        n_out = 1 if sweep + 2 == ITERS else 3
        out = pl.pallas_call(
            functools.partial(kernel, sweep, tile_cols, present),
            out_shape=(shape,) * n_out,
            in_specs=[smem] + [vmem] * (len(ins) - 1),
            out_specs=(vmem,) * n_out,
            compiler_params=pltpu.CompilerParams(vmem_limit_bytes=8 * 2**20),
            cost_estimate=pl.CostEstimate(flops=2 * 5 * tiles * width * width, bytes_accessed=5 * tiles * width * width * 4,
                                          transcendentals=0),
            name="couple",
        )(*ins)
        return out

    frames_out = []
    for instant in range(STEPS):
        if instant:
            halos = exchange(voltage)
        search, residue, estimate = call(-1, halos, voltage, injected[:, instant])
        for sweep in range(ITERS - 1):
            halos = exchange(search)
            out = call(sweep, halos, search, cap, residue, estimate)
            if sweep + 2 < ITERS:
                search, residue, estimate = out
            else:
                (voltage,) = out
        frames_out.append(voltage)
    return jnp.stack(frames_out).reshape(STEPS, tile_rows, tile_cols, width)


ROWS, HALF = 2, 2
N = 2 * ROWS
OWN, SIDE_B, ACROSS, OUT_IN, IN_OUT, IN_IN, EDGE_A, FACING, PACKED = 0, 4, 8, 10, 12, 14, 16, 18, 20
TILES = [(j, b) for j in range(N) for b in range(HALF)]
ORIGIN = [(0, 0), (0, 1), (1, 1), (1, 0)]
CAPACITY, INITIAL = STEPS, STEPS + 1
SPLIT = ((PACKED,), (OUT_IN, EDGE_A - OUT_IN))


def unit_device(unit, n_col):
    col = unit // 2
    return (unit + col) % 2, col


def half_tiles(y, col, n_col, cols, sent):
    k = (y + col + sent) % 2
    rows = (y, 1 - y)
    inward, outward = 1 - y, y
    at = [b + k * (cols - 1 - 2 * b) for b in range(HALF)]
    inside = jnp.where(col == k * (n_col - 1), 0.0, 1.0)
    tiles = [None] * PACKED
    for h in range(ROWS):
        for b in range(HALF):
            tiles[OWN + h * HALF + b] = (None, rows[h], at[b], None)
            tiles[(EDGE_A if b == 1 else ACROSS) + h] = (3 - k, rows[h], at[b], None)
            tiles[SIDE_B + h * HALF + b] = (2 + k, rows[h], at[b], inside if b == 0 else None)
        tiles[FACING + h] = (2 + k, rows[h], HALF - k, None)
    for b in range(HALF):
        tiles[OUT_IN + b] = (inward, rows[0], at[b], None)
        tiles[IN_OUT + b] = (outward, rows[1], at[b], None)
        tiles[IN_IN + b] = (inward, rows[1], at[b], None)
    return tiles


def pack_kernel(n_col, sent, first, count, pattern_hbm, own_hbm, nb_hbm, out, *rest):
    pattern_ref, sems = rest[-2:]
    tiles = half_tiles(lax.axis_index("row"), lax.axis_index("col"), n_col, own_hbm.shape[1], sent)
    pattern_copy = pltpu.make_async_copy(pattern_hbm, pattern_ref, sems.at[count])
    pattern_copy.start()
    copies = []
    for i in range(count):
        direction, row, at, _ = tiles[first + i]
        source = own_hbm.at[row, at] if direction is None else nb_hbm.at[direction, row, at]
        copies.append(pltpu.make_async_copy(source, out.at[i], sems.at[i]))
    for copy in copies:
        copy.start()
    pattern_copy.wait()
    for i in range(count):
        direction, row, at, weight = tiles[first + i]
        copies[i].wait()
        if direction is not None:
            scale = pattern_ref[row, at, direction].astype(jnp.float32)
            out[i] = out[i] * (scale if weight is None else scale * weight)
    if not sent:
        for h in range(ROWS):
            rest[0][h] = out[SIDE_B + h * HALF]


def block_of(refs, sizes, slot):
    for ref, size in zip(refs, sizes):
        if slot < size:
            return lambda g, n: ref[slot, g:g + n, :]
        slot -= size


def half_block(halves, i, slot):
    return block_of(halves[i], SPLIT[i], slot)


def tile_terms(halves, j, b):
    i, h = ORIGIN[j]
    terms = [(OWN + h * HALF + b, (j, b))]
    if h == 0:
        terms.append((OUT_IN + b, ((1, 2)[i], b)))
    else:
        terms.append((IN_OUT + b, ((0, 3)[i], b)))
        terms.append((IN_IN + b, ((2, 1)[i], b)))
    terms.append((ACROSS + h if b == 0 else SIDE_B + h * HALF + b, (j, 1 - b)))
    return [(half_block(halves, i, slot), at) for slot, at in terms]


def halo_block(halves, first_a, j, b):
    i, h = ORIGIN[j]
    if b == 0:
        return half_block(halves, i, SIDE_B + h * HALF)
    if i == 0:
        return half_block(halves, i, EDGE_A + h)
    start = 2 * N + (ROWS + h) * first_a.shape[1]
    return lambda g, n: first_a[start + g:start + g + n, :]


def facing_block(halves, beyond_0, first_a, first_b, j, b):
    i, h = ORIGIN[j]
    if i == 0:
        return half_block(halves, i, FACING + h) if b == 1 else lambda g, n: beyond_0[h, g:g + n, :]
    first = first_a if b == 1 else first_b
    start = 2 * N + h * first.shape[1]
    return lambda g, n: first[start + g:start + g + n, :]


def matvec(terms, chunk=64):
    width = terms[0][1].shape[1]
    lane = lax.broadcasted_iota(jnp.int32, (chunk, width), 1)
    sub = lax.broadcasted_iota(jnp.int32, (chunk, width), 0)
    spread = jnp.zeros((chunk, width), jnp.float32)
    for g in range(0, width, chunk):
        acc = None
        for block, vec in terms:
            part = block(g, chunk) * vec
            acc = part if acc is None else acc + part
        total = jnp.sum(acc, axis=1, keepdims=True)
        spread = jnp.where(lane == sub + g, total, spread)
    return jnp.sum(spread, axis=0, keepdims=True)


def rows_of(ref, start=0, count=N * HALF):
    return [ref[start + i:start + i + 1, :] for i in range(count)]


def put(ref, rows, start=0):
    for i, row in enumerate(rows):
        ref[start + i:start + i + 1, :] = row


def each(body, *fields):
    return [body(*rows) for rows in zip(*fields)]


def tile(j, b):
    return j * HALF + b


def products(terms, f):
    return [(block, f[tile(*at)]) for block, at in terms]


def inner_product(f, halves):
    return [matvec(products(tile_terms(halves, j, b), f)) for j, b in TILES]


def message(f, g, b):
    order = range(N)[::-1] if b == 1 else range(N)
    return [x[tile(j, b)] for x in (f, g) for j in order]


def ahead(first, sweep, f, q, residue, capacity, injected):
    if first:
        return each(lambda source, a: source - a, injected, q)
    return each(
        lambda v, a, r, c: r - STRIDES[sweep] * (a + c * v) + MOMENTA[sweep + 1] * v, f, q, residue, capacity
    )


def small_part(small, index):
    return rows_of(small, index * N * HALF)


def join_kernel(keep, recv, small):
    n = ROWS * HALF
    for i in range(0, keep.shape[0], n):
        small[2 * i:2 * i + n, :] = keep[i:i + n, :]
        small[2 * i + n:2 * i + n + HALF, :] = recv[i + HALF:i + n, :]
        small[2 * i + n + HALF:2 * i + 2 * n, :] = recv[i:i + HALF, :]


def start_kernel(keep, recv_0, recv_1, small, edge, msg_a, msg_b, q_out):
    halves = ((keep,), (recv_0, recv_1))
    f = small_part(small, INITIAL)
    q = inner_product(f, halves)
    put(q_out, q)
    g = ahead(True, 0, f, q, None, None, small_part(small, 0))
    put(msg_a, message(f, g, 1))
    put(msg_b, message(f, g, 0))
    width = small.shape[1]
    for h in range(ROWS):
        start = 2 * N + h * width
        msg_a[start:start + width, :] = keep[EDGE_A + h]
        msg_a[start + ROWS * width:start + (ROWS + 1) * width, :] = edge[h]
        msg_b[start:start + width, :] = recv_0[SIDE_B + h * HALF]


def by_target_kernel(currents, slot_tile, out):
    targets, slots, frames = currents.shape
    width = out.shape[2] - slots * frames
    names = slot_tile[...].astype(jnp.float32)
    names = jnp.concatenate([names, jnp.zeros((targets, width - slots), jnp.float32)], axis=1)
    for d in range(targets):
        for k in range(slots):
            out[d, :, k * frames:(k + 1) * frames] = currents[d, k:k + 1, :]
        out[d, :, slots * frames:] = names[d:d + 1, :]


def small_kernel(arrived, capacity, initial, keep, send, injected):
    y, col = lax.axis_index("row"), lax.axis_index("col")
    tiles, frames = injected.shape
    _, cols, width = capacity.shape
    slots = (arrived.shape[1] - width) // frames
    for t in range(tiles):
        total = jnp.zeros((arrived.shape[0], frames), jnp.float32)
        for k in range(slots):
            feeds = arrived[:, slots * frames + k:slots * frames + k + 1] == float(t)
            total = total + jnp.where(feeds, 1.0, 0.0) * arrived[:, k * frames:(k + 1) * frames]
        injected[t:t + 1, :] = jnp.sum(total, axis=0, keepdims=True)
    for sent, out in ((0, keep), (1, send)):
        parity = (y + col + sent) % 2
        for h in range(ROWS):
            row = y if h == 0 else 1 - y
            for b in range(HALF):
                at = b + parity * (cols - 1 - 2 * b)
                currents = injected[pl.ds(row * cols + at, 1), :]
                parts = [currents[:, n * width:(n + 1) * width] for n in range(STEPS)]
                parts += [x[row, pl.ds(at, 1), :] for x in (capacity, initial)]
                for n, part in enumerate(parts):
                    i = n * ROWS * HALF + h * HALF + b
                    out[i:i + 1, :] = part


def advance(instant, pair, small, product, f, residue):
    if pair == 0:
        residue = each(lambda source, a: source - a, small_part(small, instant), product)
        return residue, residue, 1.0
    sweep = 2 * pair - 1
    residue = each(lambda r, a, c, v: r - STRIDES[sweep] * (a + c * v), residue, product, small_part(small, CAPACITY), f)
    return residue, each(lambda r, v: r + MOMENTA[sweep + 1] * v, residue, f), STRIDES[sweep]


def beside_kernel(instant, pair, keep, recv_0, recv_1, beyond_0, first_a, first_b, small, got_a, q_ref, *refs):
    halves = ((keep,), (recv_0, recv_1))
    response_out, product_out, part_out = refs[-3:]
    f = small_part(small, INITIAL) if instant == pair == 0 else rows_of(refs[0])
    residue = None if pair == 0 else rows_of(refs[1])
    product = rows_of(q_ref)
    for j in range(N):
        product[tile(j, 1)] += matvec([(halo_block(halves, first_a, j, 1), got_a[j:j + 1, :])])
    put(product_out, product)
    response = [
        matvec([(facing_block(halves, beyond_0, first_a, first_b, j, b), f[tile(j, b)])]) for j, b in TILES
    ]
    put(response_out, response)
    _, f2, scale = advance(instant, pair, small, product, f, residue)
    part = []
    for j, b in TILES:
        terms = products(tile_terms(halves, j, b), f2)
        if b == 1:
            beside = got_a[N + j:N + j + 1, :] - scale * response[tile(j, b)]
            part.append(matvec(terms[:-1] + [(halo_block(halves, first_a, j, b), beside)]))
        else:
            part.append(matvec(terms[-1:]))
    put(part_out, part)


def pair_kernel(instant, pair, last, keep, recv_0, recv_1, small, got_b, response, product_ref, part_ref, *refs):
    halves = ((keep,), (recv_0, recv_1))
    first = pair == 0
    capacity = small_part(small, CAPACITY)
    if first and instant == 0:
        f = small_part(small, INITIAL)
    else:
        f, refs = rows_of(refs[0]), refs[1:]
    residue = estimate = None
    if not first:
        residue, estimate, refs = rows_of(refs[0]), rows_of(refs[1]), refs[2:]

    product = rows_of(product_ref)
    for j in range(N):
        product[tile(j, 0)] += matvec([(halo_block(halves, None, j, 0), got_b[j:j + 1, :])])
    residue, f2, scale = advance(instant, pair, small, product, f, residue)
    if first:
        estimate = each(lambda v, p: v + STRIDES[0] * p, f, f2)
    else:
        estimate = each(lambda e, p: e + STRIDES[2 * pair] * p, estimate, f2)

    total = rows_of(part_ref)
    for j, b in TILES:
        i = tile(j, b)
        terms = products(tile_terms(halves, j, b), f2)
        if b == 0:
            beside = got_b[N + j:N + j + 1, :] - scale * response[i:i + 1, :]
            total[i] += matvec(terms[:-1] + [(halo_block(halves, None, j, b), beside)])
        else:
            total[i] += matvec(terms[-1:])
    sweep = 2 * pair
    residue = each(lambda r, a, c, v: r - STRIDES[sweep] * (a + c * v), residue, total, capacity, f2)
    f3 = each(lambda r, v: r + MOMENTA[sweep + 1] * v, residue, f2)
    estimate = each(lambda e, p: e + STRIDES[sweep + 1] * p, estimate, f3)
    closing = sweep + 2 == ITERS
    if closing:
        f3 = estimate
    f_out, refs = refs[0], refs[1:]
    put(f_out, f3)
    if last:
        return
    q = inner_product(f3, halves)
    upcoming = small_part(small, instant + 1) if closing else None
    g = ahead(closing, sweep + 1, f3, q, residue, capacity, upcoming)
    q_out, msg_a, msg_b = refs[:3]
    put(msg_a, message(f3, g, 1))
    put(msg_b, message(f3, g, 0))
    put(q_out, q)
    if not closing:
        put(refs[3], residue)
        put(refs[4], estimate)


def shards_chain(own_block, neighbor_block, pattern, capacity, initial, currents, slot_tile):
    tile_rows, tile_cols, width = initial.shape
    n_col = lax.axis_size("col")
    row, col = lax.axis_index("row"), lax.axis_index("col")
    both = ("row", "col")
    swap = [(0, 1), (1, 0)]
    b_pairs = []
    for unit in range(1, 2 * n_col - 1, 2):
        ends = [r * n_col + c for r, c in (unit_device(unit, n_col), unit_device(unit + 1, n_col))]
        b_pairs += [tuple(ends), tuple(ends[::-1])]
    parity = (row + col) % 2

    vmem = pl.BlockSpec(memory_space=pltpu.VMEM)
    hbm = pl.BlockSpec(memory_space=pltpu.HBM)
    limit = pltpu.CompilerParams(vmem_limit_bytes=16 * 2**20)
    blocks = [pltpu.with_memory_space_constraint(x, pltpu.HBM) for x in (pattern, own_block, neighbor_block)]

    def pack(sent, first, count, extra=()):
        return pl.pallas_call(
            functools.partial(pack_kernel, n_col, sent, first, count),
            out_shape=[jax.ShapeDtypeStruct((n, width, width), jnp.float32) for n in (count, *extra)],
            in_specs=[hbm, hbm, hbm],
            out_specs=[vmem] * (1 + len(extra)),
            scratch_shapes=[pltpu.SMEM(pattern.shape, jnp.int32), pltpu.SemaphoreType.DMA((count + 1,))],
            compiler_params=limit,
            name="pack",
        )(*blocks)

    recv = []
    for first, count in ((0, SPLIT[1][0]), SPLIT[1]):
        (send,) = pack(1, first, count)
        recv.append(lax.ppermute(send, "row", swap))
    keep, facing_0 = pack(0, 0, PACKED, (ROWS,))
    (edge,) = pack(1, EDGE_A, ROWS)

    unit_small = jax.ShapeDtypeStruct(((STEPS + 2) * N * HALF, width), jnp.float32)

    def beside(currents, slot_tile, capacity, initial, facing_0):
        beyond_0 = lax.ppermute(facing_0, both, b_pairs)
        slots, frames = currents.shape[3:]
        by_target = pl.pallas_call(
            by_target_kernel,
            out_shape=jax.ShapeDtypeStruct((n_col, 1, slots * frames + width), jnp.float32),
            in_specs=[vmem, vmem],
            out_specs=vmem,
            compiler_params=limit,
            name="by_target",
        )(currents.reshape(n_col, slots, frames), slot_tile.reshape(n_col, slots))
        arrived = lax.all_to_all(by_target, "col", split_axis=0, concat_axis=0, tiled=True)
        half = jax.ShapeDtypeStruct(((STEPS + 2) * ROWS * HALF, width), jnp.float32)
        small, send = pl.pallas_call(
            small_kernel,
            out_shape=(half, half),
            in_specs=[vmem] * 3,
            out_specs=(vmem, vmem),
            scratch_shapes=[pltpu.VMEM((tile_rows * tile_cols, frames), jnp.float32)],
            compiler_params=limit,
            name="small",
        )(arrived.reshape(n_col, slots * frames + width), capacity, initial)
        small = pl.pallas_call(
            join_kernel,
            out_shape=unit_small,
            in_specs=[vmem, vmem],
            out_specs=vmem,
            compiler_params=limit,
            name="join",
        )(small, lax.ppermute(send, "row", swap))
        return small, beyond_0

    small, beyond_0 = lax.cond(
        row < lax.axis_size("row"),
        beside,
        lambda currents, slot_tile, capacity, initial, facing_0: (
            jnp.zeros(unit_small.shape, jnp.float32), facing_0
        ),
        currents, slot_tile, capacity, initial, facing_0,
    )

    shape = jax.ShapeDtypeStruct((N * HALF, width), jnp.float32)
    halves = (keep, *recv)

    def call(body, outs, blocks, *ins):
        return pl.pallas_call(
            body,
            out_shape=outs,
            in_specs=[vmem] * len(ins),
            out_specs=(vmem,) * len(outs),
            compiler_params=limit,
            cost_estimate=pl.CostEstimate(flops=2 * blocks * width * width, bytes_accessed=blocks * width * width * 4,
                                          transcendentals=0),
            name="pair",
        )(*ins)

    first_shape = jax.ShapeDtypeStruct((2 * N + ROWS * width, width), jnp.float32)
    first_a_shape = jax.ShapeDtypeStruct((2 * N + 2 * ROWS * width, width), jnp.float32)
    msg_a, msg_b, q = call(start_kernel, (first_a_shape, first_shape, shape), 28, *halves, small, edge)
    field, state, frames, first = (), (), [], None
    for instant in range(STEPS):
        for pair in range(ITERS // 2):
            closing = pair + 1 == ITERS // 2
            last = closing and instant + 1 == STEPS
            got_b = lax.ppermute(msg_b, both, b_pairs)
            got_a = lax.ppermute(msg_a, "row", swap)
            first = first or (got_a, got_b)
            response, product, part = call(functools.partial(beside_kernel, instant, pair), (shape,) * 3, 30,
                                           *halves, beyond_0, *first, small, got_a, q, *field, *state[:1])
            out = call(functools.partial(pair_kernel, instant, pair, last), (shape,) * (1 if last else 4 if closing else 6),
                       50, *halves, small, got_b, response, product, part, *field, *state)
            field = out[:1]
            if not last:
                q, msg_a, msg_b = out[1:4]
                state = out[4:]
        frames.append(field[0])

    done = jnp.stack(frames).reshape(STEPS, N, HALF, width)
    got = lax.ppermute(jnp.flip(done[:, ROWS:], 1), "row", swap)
    mine = done[:, :ROWS]
    unit_0, unit_1 = jnp.where(parity == 1, got, mine), jnp.where(parity == 1, mine, got)
    done = jnp.concatenate([unit_0, jnp.flip(unit_1, 2)], axis=2)
    return jnp.where(row == 1, jnp.flip(done, 1), done)


def solution(mesh):
    rows, cols = mesh.shape["row"], mesh.shape["col"]
    return jax.shard_map(
        shards_chain if rows == 2 else shards_general,
        mesh=mesh,
        in_specs=(
            P("row", "col", None, None),
            P(None, "row", "col", None, None),
            P("row", "col", None),
            P("row", "col", None),
            P("row", "col", None),
            P("row", "col", None, None, None),
            P("row", "col", None, None),
        ),
        out_specs=P(None, "row", "col", None),
        check_vma=False,
    )
```

```python
import functools

import jax
import jax.numpy as jnp
from jax import lax
from jax.experimental import pallas as pl
from jax.experimental.pallas import tpu as pltpu
from jax.sharding import PartitionSpec as P

STEPS = 4
ITERS = 8

spec_center = 6.4
spec_radius = 5.6


def schedule():
    strides, momenta = [], []
    stride = 1.0 / spec_center
    for sweep in range(ITERS):
        if sweep == 0:
            momentum = 0.0
        else:
            if sweep == 1:
                momentum = 0.5 * (spec_radius * stride) ** 2
            else:
                momentum = (spec_radius * stride / 2.0) ** 2
            stride = 1.0 / (spec_center - momentum / stride)
        strides.append(stride)
        momenta.append(momentum)
    return strides, momenta


STRIDES, MOMENTA = schedule()


def swap_pairs(count, first):
    pairs = []
    for i in range(first, count - 1, 2):
        pairs += [(i, i + 1), (i + 1, i)]
    return pairs


def exchange(field):
    arrived = []
    for axis in ("row", "col"):
        count = lax.axis_size(axis)
        for first in (0, 1):
            pairs = swap_pairs(count, first)
            arrived.append(lax.ppermute(field, axis, pairs) if pairs else None)
    return arrived


def beside(field, halos, odd_row, odd_col, cols):
    tiles = field.shape[0]
    row_a, row_b, col_a, col_b = halos
    zero = jnp.zeros_like(field)
    row_a, row_b, col_a, col_b = [zero if h is None else h for h in (row_a, row_b, col_a, col_b)]
    above = jnp.where(odd_row, row_a, row_b)
    below = jnp.where(odd_row, row_b, row_a)
    west = jnp.where(odd_col, col_a, col_b)
    east = jnp.where(odd_col, col_b, col_a)
    up = jnp.concatenate([above[tiles - cols:], field[: tiles - cols]], axis=0)
    down = jnp.concatenate([field[cols:], below[:cols]], axis=0)
    column = lax.broadcasted_iota(jnp.int32, field.shape, 0) % cols
    rolled = jnp.concatenate([field[tiles - 1:], field[: tiles - 1]], axis=0)
    west_edge = jnp.concatenate([west[cols - 1:], west[: cols - 1]], axis=0)
    left = jnp.where(column == 0, west_edge, rolled)
    rolled = jnp.concatenate([field[1:], field[:1]], axis=0)
    east_edge = jnp.concatenate([east[tiles - cols + 1:], east[: tiles - cols + 1]], axis=0)
    right = jnp.where(column == cols - 1, east_edge, rolled)
    return up, down, left, right


def blocks_times(field, around, own_ref, nb_ref):
    tiles, width = field.shape
    chunk = 32
    lane = lax.broadcasted_iota(jnp.int32, (chunk, width), 1)
    sub = lax.broadcasted_iota(jnp.int32, (chunk, width), 0)
    outs = []
    for t in range(tiles):
        vecs = [f[t:t + 1] for f in around]
        mine = field[t:t + 1]
        spread = jnp.zeros((chunk, width), jnp.float32)
        for g in range(0, width, chunk):
            acc = own_ref[t, g:g + chunk, :] * mine
            for n, vec in enumerate(vecs):
                acc = acc + nb_ref[n, t, g:g + chunk, :] * vec
            total = jnp.sum(acc, axis=1, keepdims=True)
            spread = jnp.where(lane == sub + g, total, spread)
        outs.append(jnp.sum(spread, axis=0, keepdims=True))
    return jnp.concatenate(outs, axis=0)


def kernel(sweep, cols, present, flags, own_ref, nb_ref, weights, *refs):
    n_halo = sum(present)
    halo_refs, refs = refs[:n_halo], refs[n_halo:]
    halo_iter = iter(halo_refs)
    halos = [next(halo_iter)[...] if p else None for p in present]
    odd_row, odd_col = flags[0] == 1, flags[1] == 1
    field_ref, refs = refs[0], refs[1:]
    field = field_ref[...]
    around = beside(field, halos, odd_row, odd_col, cols)
    around = [f * weights[n] for n, f in enumerate(around)]
    product = blocks_times(field, around, own_ref, nb_ref)
    if sweep < 0:
        injected, search_out, residue_out, estimate_out = refs
        residue = injected[...] - product
        search_out[...] = residue
        residue_out[...] = residue
        estimate_out[...] = field + STRIDES[0] * residue
    else:
        capacity, residue_in, estimate_in = refs[:3]
        outs = refs[3:]
        residue = residue_in[...] - STRIDES[sweep] * (product + capacity[...] * field)
        search = residue + MOMENTA[sweep + 1] * field
        estimate = estimate_in[...] + STRIDES[sweep + 1] * search
        if sweep + 2 < ITERS:
            outs[0][...] = search
            outs[1][...] = residue
            outs[2][...] = estimate
        else:
            outs[0][...] = estimate


def collect(currents, slot_tile, tiles, width):
    slots, frames = currents.shape[3:]
    names = jnp.pad(slot_tile.astype(jnp.float32)[..., None, :],
                    ((0, 0), (0, 0), (0, 0), (0, 0), (0, frames - slots)))
    packed = jnp.concatenate([currents, names], axis=3)
    arrived = lax.all_to_all(packed, "col", split_axis=2, concat_axis=1, tiled=True)[0, :, 0]
    targets = arrived[:, slots, :slots]
    chooser = (targets[..., None] == jnp.arange(tiles, dtype=jnp.float32)).astype(jnp.float32)
    injected = jnp.einsum("skt,skf->tf", chooser, arrived[:, :slots], precision=lax.Precision.HIGHEST)
    return injected.reshape(tiles, STEPS, width)


def shards_general(own_block, neighbor_block, pattern, capacity, initial, currents, slot_tile):
    tile_rows, tile_cols, width = initial.shape
    tiles = tile_rows * tile_cols
    flags = jnp.stack([lax.axis_index("row") % 2, lax.axis_index("col") % 2]).astype(jnp.int32)

    voltage = initial.reshape(tiles, width)
    halos = exchange(voltage)

    injected = collect(currents, slot_tile, tiles, width)

    own = own_block.reshape(tiles, width, width)
    nb = neighbor_block.reshape(4, tiles, width, width)
    weights = jnp.broadcast_to(
        jnp.moveaxis(pattern.reshape(tiles, 4), 1, 0).astype(jnp.float32)[..., None], (4, tiles, width)
    )
    cap = capacity.reshape(tiles, width)
    shape = jax.ShapeDtypeStruct((tiles, width), jnp.float32)
    vmem = pl.BlockSpec(memory_space=pltpu.VMEM)
    smem = pl.BlockSpec(memory_space=pltpu.SMEM)

    def call(sweep, halos, *state):
        present = tuple(h is not None for h in halos)
        ins = (flags, own, nb, weights) + tuple(h for h in halos if h is not None) + state
        n_out = 1 if sweep + 2 == ITERS else 3
        out = pl.pallas_call(
            functools.partial(kernel, sweep, tile_cols, present),
            out_shape=(shape,) * n_out,
            in_specs=[smem] + [vmem] * (len(ins) - 1),
            out_specs=(vmem,) * n_out,
            compiler_params=pltpu.CompilerParams(vmem_limit_bytes=8 * 2**20),
            cost_estimate=pl.CostEstimate(flops=2 * 5 * tiles * width * width, bytes_accessed=5 * tiles * width * width * 4,
                                          transcendentals=0),
            name="couple",
        )(*ins)
        return out

    frames_out = []
    for instant in range(STEPS):
        if instant:
            halos = exchange(voltage)
        search, residue, estimate = call(-1, halos, voltage, injected[:, instant])
        for sweep in range(ITERS - 1):
            halos = exchange(search)
            out = call(sweep, halos, search, cap, residue, estimate)
            if sweep + 2 < ITERS:
                search, residue, estimate = out
            else:
                (voltage,) = out
        frames_out.append(voltage)
    return jnp.stack(frames_out).reshape(STEPS, tile_rows, tile_cols, width)


ROWS, HALF = 2, 2
N = 2 * ROWS
OWN, SIDE_B, ACROSS, OUT_IN, IN_OUT, IN_IN, EDGE_A, FACING, PACKED = 0, 4, 8, 10, 12, 14, 16, 18, 20
TILES = [(j, b) for j in range(N) for b in range(HALF)]
ORIGIN = [(0, 0), (0, 1), (1, 1), (1, 0)]
CAPACITY, INITIAL = STEPS, STEPS + 1
SPLIT = ((PACKED,), (OUT_IN, EDGE_A - OUT_IN))


def unit_device(unit, n_col):
    col = unit // 2
    return (unit + col) % 2, col


def half_tiles(y, col, n_col, cols, sent):
    k = (y + col + sent) % 2
    rows = (y, 1 - y)
    inward, outward = 1 - y, y
    at = [b + k * (cols - 1 - 2 * b) for b in range(HALF)]
    inside = jnp.where(col == k * (n_col - 1), 0.0, 1.0)
    tiles = [None] * PACKED
    for h in range(ROWS):
        for b in range(HALF):
            tiles[OWN + h * HALF + b] = (None, rows[h], at[b], None)
            tiles[(EDGE_A if b == 1 else ACROSS) + h] = (3 - k, rows[h], at[b], None)
            tiles[SIDE_B + h * HALF + b] = (2 + k, rows[h], at[b], inside if b == 0 else None)
        tiles[FACING + h] = (2 + k, rows[h], HALF - k, None)
    for b in range(HALF):
        tiles[OUT_IN + b] = (inward, rows[0], at[b], None)
        tiles[IN_OUT + b] = (outward, rows[1], at[b], None)
        tiles[IN_IN + b] = (inward, rows[1], at[b], None)
    return tiles


def pack_kernel(n_col, sent, first, count, pattern_hbm, own_hbm, nb_hbm, out, *rest):
    pattern_ref, sems = rest[-2:]
    tiles = half_tiles(lax.axis_index("row"), lax.axis_index("col"), n_col, own_hbm.shape[1], sent)
    pattern_copy = pltpu.make_async_copy(pattern_hbm, pattern_ref, sems.at[count])
    pattern_copy.start()
    copies = []
    for i in range(count):
        direction, row, at, _ = tiles[first + i]
        source = own_hbm.at[row, at] if direction is None else nb_hbm.at[direction, row, at]
        copies.append(pltpu.make_async_copy(source, out.at[i], sems.at[i]))
    for copy in copies:
        copy.start()
    pattern_copy.wait()
    for i in range(count):
        direction, row, at, weight = tiles[first + i]
        copies[i].wait()
        if direction is not None:
            scale = pattern_ref[row, at, direction].astype(jnp.float32)
            out[i] = out[i] * (scale if weight is None else scale * weight)
    if not sent:
        for h in range(ROWS):
            rest[0][h] = out[SIDE_B + h * HALF]


def block_of(refs, sizes, slot):
    for ref, size in zip(refs, sizes):
        if slot < size:
            return lambda g, n: ref[slot, g:g + n, :]
        slot -= size


def half_block(halves, i, slot):
    return block_of(halves[i], SPLIT[i], slot)


def tile_terms(halves, j, b):
    i, h = ORIGIN[j]
    terms = [(OWN + h * HALF + b, (j, b))]
    if h == 0:
        terms.append((OUT_IN + b, ((1, 2)[i], b)))
    else:
        terms.append((IN_OUT + b, ((0, 3)[i], b)))
        terms.append((IN_IN + b, ((2, 1)[i], b)))
    terms.append((ACROSS + h if b == 0 else SIDE_B + h * HALF + b, (j, 1 - b)))
    return [(half_block(halves, i, slot), at) for slot, at in terms]


def halo_block(halves, first_a, j, b):
    i, h = ORIGIN[j]
    if b == 0:
        return half_block(halves, i, SIDE_B + h * HALF)
    if i == 0:
        return half_block(halves, i, EDGE_A + h)
    start = 2 * N + (ROWS + h) * first_a.shape[1]
    return lambda g, n: first_a[start + g:start + g + n, :]


def facing_block(halves, beyond_0, first_a, first_b, j, b):
    i, h = ORIGIN[j]
    if i == 0:
        return half_block(halves, i, FACING + h) if b == 1 else lambda g, n: beyond_0[h, g:g + n, :]
    first = first_a if b == 1 else first_b
    start = 2 * N + h * first.shape[1]
    return lambda g, n: first[start + g:start + g + n, :]


def matvec(terms, chunk=64):
    width = terms[0][1].shape[1]
    lane = lax.broadcasted_iota(jnp.int32, (chunk, width), 1)
    sub = lax.broadcasted_iota(jnp.int32, (chunk, width), 0)
    spread = jnp.zeros((chunk, width), jnp.float32)
    for g in range(0, width, chunk):
        acc = None
        for block, vec in terms:
            part = block(g, chunk) * vec
            acc = part if acc is None else acc + part
        total = jnp.sum(acc, axis=1, keepdims=True)
        spread = jnp.where(lane == sub + g, total, spread)
    return jnp.sum(spread, axis=0, keepdims=True)


def rows_of(ref, start=0, count=N * HALF):
    return [ref[start + i:start + i + 1, :] for i in range(count)]


def put(ref, rows, start=0):
    for i, row in enumerate(rows):
        ref[start + i:start + i + 1, :] = row


def each(body, *fields):
    return [body(*rows) for rows in zip(*fields)]


def tile(j, b):
    return j * HALF + b


def products(terms, f):
    return [(block, f[tile(*at)]) for block, at in terms]


def inner_product(f, halves):
    return [matvec(products(tile_terms(halves, j, b), f)) for j, b in TILES]


def message(f, g, b):
    order = range(N)[::-1] if b == 1 else range(N)
    return [x[tile(j, b)] for x in (f, g) for j in order]


def ahead(first, sweep, f, q, residue, capacity, injected):
    if first:
        return each(lambda source, a: source - a, injected, q)
    return each(
        lambda v, a, r, c: r - STRIDES[sweep] * (a + c * v) + MOMENTA[sweep + 1] * v, f, q, residue, capacity
    )


def small_part(small, index):
    return rows_of(small, index * N * HALF)


def start_kernel(keep, recv_0, recv_1, small_keep, small_recv, edge, msg_a, msg_b, q_out, small):
    n = ROWS * HALF
    for i in range(0, small_keep.shape[0], n):
        small[2 * i:2 * i + n, :] = small_keep[i:i + n, :]
        small[2 * i + n:2 * i + n + HALF, :] = small_recv[i + HALF:i + n, :]
        small[2 * i + n + HALF:2 * i + 2 * n, :] = small_recv[i:i + HALF, :]
    halves = ((keep,), (recv_0, recv_1))
    f = small_part(small, INITIAL)
    q = inner_product(f, halves)
    put(q_out, q)
    g = ahead(True, 0, f, q, None, None, small_part(small, 0))
    put(msg_a, message(f, g, 1))
    put(msg_b, message(f, g, 0))
    width = small.shape[1]
    for h in range(ROWS):
        start = 2 * N + h * width
        msg_a[start:start + width, :] = keep[EDGE_A + h]
        msg_a[start + ROWS * width:start + (ROWS + 1) * width, :] = edge[h]
        msg_b[start:start + width, :] = recv_0[SIDE_B + h * HALF]


def by_target_kernel(currents, slot_tile, out):
    targets, slots, frames = currents.shape
    width = out.shape[2] - slots * frames
    names = slot_tile[...].astype(jnp.float32)
    names = jnp.concatenate([names, jnp.zeros((targets, width - slots), jnp.float32)], axis=1)
    for d in range(targets):
        for k in range(slots):
            out[d, :, k * frames:(k + 1) * frames] = currents[d, k:k + 1, :]
        out[d, :, slots * frames:] = names[d:d + 1, :]


def small_kernel(arrived, capacity, initial, keep, send, injected):
    y, col = lax.axis_index("row"), lax.axis_index("col")
    tiles, frames = injected.shape
    _, cols, width = capacity.shape
    slots = (arrived.shape[1] - width) // frames
    for t in range(tiles):
        total = jnp.zeros((arrived.shape[0], frames), jnp.float32)
        for k in range(slots):
            feeds = arrived[:, slots * frames + k:slots * frames + k + 1] == float(t)
            total = total + jnp.where(feeds, 1.0, 0.0) * arrived[:, k * frames:(k + 1) * frames]
        injected[t:t + 1, :] = jnp.sum(total, axis=0, keepdims=True)
    for sent, out in ((0, keep), (1, send)):
        parity = (y + col + sent) % 2
        for h in range(ROWS):
            row = y if h == 0 else 1 - y
            for b in range(HALF):
                at = b + parity * (cols - 1 - 2 * b)
                currents = injected[pl.ds(row * cols + at, 1), :]
                parts = [currents[:, n * width:(n + 1) * width] for n in range(STEPS)]
                parts += [x[row, pl.ds(at, 1), :] for x in (capacity, initial)]
                for n, part in enumerate(parts):
                    i = n * ROWS * HALF + h * HALF + b
                    out[i:i + 1, :] = part


def advance(instant, pair, small, product, f, residue):
    if pair == 0:
        residue = each(lambda source, a: source - a, small_part(small, instant), product)
        return residue, residue, 1.0
    sweep = 2 * pair - 1
    residue = each(lambda r, a, c, v: r - STRIDES[sweep] * (a + c * v), residue, product, small_part(small, CAPACITY), f)
    return residue, each(lambda r, v: r + MOMENTA[sweep + 1] * v, residue, f), STRIDES[sweep]


def beside_kernel(instant, pair, keep, recv_0, recv_1, beyond_0, first_a, first_b, small, got_a, q_ref, *refs):
    halves = ((keep,), (recv_0, recv_1))
    response_out, product_out, part_out = refs[-3:]
    f = small_part(small, INITIAL) if instant == pair == 0 else rows_of(refs[0])
    residue = None if pair == 0 else rows_of(refs[1])
    product = rows_of(q_ref)
    for j in range(N):
        product[tile(j, 1)] += matvec([(halo_block(halves, first_a, j, 1), got_a[j:j + 1, :])])
    put(product_out, product)
    response = [
        matvec([(facing_block(halves, beyond_0, first_a, first_b, j, b), f[tile(j, b)])]) for j, b in TILES
    ]
    put(response_out, response)
    _, f2, scale = advance(instant, pair, small, product, f, residue)
    part = []
    for j, b in TILES:
        terms = products(tile_terms(halves, j, b), f2)
        if b == 1:
            beside = got_a[N + j:N + j + 1, :] - scale * response[tile(j, b)]
            part.append(matvec(terms[:-1] + [(halo_block(halves, first_a, j, b), beside)]))
        else:
            part.append(matvec(terms[-1:]))
    put(part_out, part)


def pair_kernel(instant, pair, last, keep, recv_0, recv_1, small, got_b, response, product_ref, part_ref, *refs):
    halves = ((keep,), (recv_0, recv_1))
    first = pair == 0
    capacity = small_part(small, CAPACITY)
    if first and instant == 0:
        f = small_part(small, INITIAL)
    else:
        f, refs = rows_of(refs[0]), refs[1:]
    residue = estimate = None
    if not first:
        residue, estimate, refs = rows_of(refs[0]), rows_of(refs[1]), refs[2:]

    product = rows_of(product_ref)
    for j in range(N):
        product[tile(j, 0)] += matvec([(halo_block(halves, None, j, 0), got_b[j:j + 1, :])])
    residue, f2, scale = advance(instant, pair, small, product, f, residue)
    if first:
        estimate = each(lambda v, p: v + STRIDES[0] * p, f, f2)
    else:
        estimate = each(lambda e, p: e + STRIDES[2 * pair] * p, estimate, f2)

    total = rows_of(part_ref)
    for j, b in TILES:
        i = tile(j, b)
        terms = products(tile_terms(halves, j, b), f2)
        if b == 0:
            beside = got_b[N + j:N + j + 1, :] - scale * response[i:i + 1, :]
            total[i] += matvec(terms[:-1] + [(halo_block(halves, None, j, b), beside)])
        else:
            total[i] += matvec(terms[-1:])
    sweep = 2 * pair
    residue = each(lambda r, a, c, v: r - STRIDES[sweep] * (a + c * v), residue, total, capacity, f2)
    f3 = each(lambda r, v: r + MOMENTA[sweep + 1] * v, residue, f2)
    estimate = each(lambda e, p: e + STRIDES[sweep + 1] * p, estimate, f3)
    closing = sweep + 2 == ITERS
    if closing:
        f3 = estimate
    f_out, refs = refs[0], refs[1:]
    put(f_out, f3)
    if last:
        return
    q = inner_product(f3, halves)
    upcoming = small_part(small, instant + 1) if closing else None
    g = ahead(closing, sweep + 1, f3, q, residue, capacity, upcoming)
    q_out, msg_a, msg_b = refs[:3]
    put(msg_a, message(f3, g, 1))
    put(msg_b, message(f3, g, 0))
    put(q_out, q)
    if not closing:
        put(refs[3], residue)
        put(refs[4], estimate)


def shards_chain(own_block, neighbor_block, pattern, capacity, initial, currents, slot_tile):
    tile_rows, tile_cols, width = initial.shape
    n_col = lax.axis_size("col")
    row, col = lax.axis_index("row"), lax.axis_index("col")
    both = ("row", "col")
    swap = [(0, 1), (1, 0)]
    b_pairs = []
    for unit in range(1, 2 * n_col - 1, 2):
        ends = [r * n_col + c for r, c in (unit_device(unit, n_col), unit_device(unit + 1, n_col))]
        b_pairs += [tuple(ends), tuple(ends[::-1])]
    parity = (row + col) % 2

    vmem = pl.BlockSpec(memory_space=pltpu.VMEM)
    hbm = pl.BlockSpec(memory_space=pltpu.HBM)
    limit = pltpu.CompilerParams(vmem_limit_bytes=16 * 2**20)
    blocks = [pltpu.with_memory_space_constraint(x, pltpu.HBM) for x in (pattern, own_block, neighbor_block)]

    def pack(sent, first, count, extra=()):
        return pl.pallas_call(
            functools.partial(pack_kernel, n_col, sent, first, count),
            out_shape=[jax.ShapeDtypeStruct((n, width, width), jnp.float32) for n in (count, *extra)],
            in_specs=[hbm, hbm, hbm],
            out_specs=[vmem] * (1 + len(extra)),
            scratch_shapes=[pltpu.SMEM(pattern.shape, jnp.int32), pltpu.SemaphoreType.DMA((count + 1,))],
            compiler_params=limit,
            name="pack",
        )(*blocks)

    recv = []
    for first, count in ((0, SPLIT[1][0]), SPLIT[1]):
        (send,) = pack(1, first, count)
        recv.append(lax.ppermute(send, "row", swap))
    keep, facing_0 = pack(0, 0, PACKED, (ROWS,))
    (edge,) = pack(1, EDGE_A, ROWS)

    unit_small = jax.ShapeDtypeStruct(((STEPS + 2) * N * HALF, width), jnp.float32)

    def beside(currents, slot_tile, capacity, initial, facing_0):
        beyond_0 = lax.ppermute(facing_0, both, b_pairs)
        slots, frames = currents.shape[3:]
        by_target = pl.pallas_call(
            by_target_kernel,
            out_shape=jax.ShapeDtypeStruct((n_col, 1, slots * frames + width), jnp.float32),
            in_specs=[vmem, vmem],
            out_specs=vmem,
            compiler_params=limit,
            name="by_target",
        )(currents.reshape(n_col, slots, frames), slot_tile.reshape(n_col, slots))
        arrived = lax.all_to_all(by_target, "col", split_axis=0, concat_axis=0, tiled=True)
        half = jax.ShapeDtypeStruct(((STEPS + 2) * ROWS * HALF, width), jnp.float32)
        small, send = pl.pallas_call(
            small_kernel,
            out_shape=(half, half),
            in_specs=[vmem] * 3,
            out_specs=(vmem, vmem),
            scratch_shapes=[pltpu.VMEM((tile_rows * tile_cols, frames), jnp.float32)],
            compiler_params=limit,
            name="small",
        )(arrived.reshape(n_col, slots * frames + width), capacity, initial)
        return small, lax.ppermute(send, "row", swap), beyond_0

    *small, beyond_0 = lax.cond(
        row < lax.axis_size("row"),
        beside,
        lambda currents, slot_tile, capacity, initial, facing_0: (
            *jnp.zeros((2, (STEPS + 2) * ROWS * HALF, width), jnp.float32), facing_0
        ),
        currents, slot_tile, capacity, initial, facing_0,
    )

    shape = jax.ShapeDtypeStruct((N * HALF, width), jnp.float32)
    halves = (keep, *recv)

    def call(body, outs, blocks, *ins):
        return pl.pallas_call(
            body,
            out_shape=outs,
            in_specs=[vmem] * len(ins),
            out_specs=(vmem,) * len(outs),
            compiler_params=limit,
            cost_estimate=pl.CostEstimate(flops=2 * blocks * width * width, bytes_accessed=blocks * width * width * 4,
                                          transcendentals=0),
            name="pair",
        )(*ins)

    first_shape = jax.ShapeDtypeStruct((2 * N + ROWS * width, width), jnp.float32)
    first_a_shape = jax.ShapeDtypeStruct((2 * N + 2 * ROWS * width, width), jnp.float32)
    msg_a, msg_b, q, small = call(start_kernel, (first_a_shape, first_shape, shape, unit_small), 28, *halves, *small, edge)
    field, state, frames, first = (), (), [], None
    for instant in range(STEPS):
        for pair in range(ITERS // 2):
            closing = pair + 1 == ITERS // 2
            last = closing and instant + 1 == STEPS
            got_b = lax.ppermute(msg_b, both, b_pairs)
            got_a = lax.ppermute(msg_a, "row", swap)
            first = first or (got_a, got_b)
            response, product, part = call(functools.partial(beside_kernel, instant, pair), (shape,) * 3, 30,
                                           *halves, beyond_0, *first, small, got_a, q, *field, *state[:1])
            out = call(functools.partial(pair_kernel, instant, pair, last), (shape,) * (1 if last else 4 if closing else 6),
                       50, *halves, small, got_b, response, product, part, *field, *state)
            field = out[:1]
            if not last:
                q, msg_a, msg_b = out[1:4]
                state = out[4:]
        frames.append(field[0])

    done = jnp.stack(frames).reshape(STEPS, N, HALF, width)
    got = lax.ppermute(jnp.flip(done[:, ROWS:], 1), "row", swap)
    mine = done[:, :ROWS]
    unit_0, unit_1 = jnp.where(parity == 1, got, mine), jnp.where(parity == 1, mine, got)
    done = jnp.concatenate([unit_0, jnp.flip(unit_1, 2)], axis=2)
    return jnp.where(row == 1, jnp.flip(done, 1), done)


def solution(mesh):
    rows, cols = mesh.shape["row"], mesh.shape["col"]
    return jax.shard_map(
        shards_chain if rows == 2 else shards_general,
        mesh=mesh,
        in_specs=(
            P("row", "col", None, None),
            P(None, "row", "col", None, None),
            P("row", "col", None),
            P("row", "col", None),
            P("row", "col", None),
            P("row", "col", None, None, None),
            P("row", "col", None, None),
        ),
        out_specs=P(None, "row", "col", None),
        check_vma=False,
    )
```

```python
import functools

import jax
import jax.numpy as jnp
from jax import lax
from jax.experimental import pallas as pl
from jax.experimental.pallas import tpu as pltpu
from jax.sharding import PartitionSpec as P

STEPS = 4
ITERS = 8

spec_center = 6.4
spec_radius = 5.6


def schedule():
    strides, momenta = [], []
    stride = 1.0 / spec_center
    for sweep in range(ITERS):
        if sweep == 0:
            momentum = 0.0
        else:
            if sweep == 1:
                momentum = 0.5 * (spec_radius * stride) ** 2
            else:
                momentum = (spec_radius * stride / 2.0) ** 2
            stride = 1.0 / (spec_center - momentum / stride)
        strides.append(stride)
        momenta.append(momentum)
    return strides, momenta


STRIDES, MOMENTA = schedule()


def swap_pairs(count, first):
    pairs = []
    for i in range(first, count - 1, 2):
        pairs += [(i, i + 1), (i + 1, i)]
    return pairs


def exchange(field):
    arrived = []
    for axis in ("row", "col"):
        count = lax.axis_size(axis)
        for first in (0, 1):
            pairs = swap_pairs(count, first)
            arrived.append(lax.ppermute(field, axis, pairs) if pairs else None)
    return arrived


def beside(field, halos, odd_row, odd_col, cols):
    tiles = field.shape[0]
    row_a, row_b, col_a, col_b = halos
    zero = jnp.zeros_like(field)
    row_a, row_b, col_a, col_b = [zero if h is None else h for h in (row_a, row_b, col_a, col_b)]
    above = jnp.where(odd_row, row_a, row_b)
    below = jnp.where(odd_row, row_b, row_a)
    west = jnp.where(odd_col, col_a, col_b)
    east = jnp.where(odd_col, col_b, col_a)
    up = jnp.concatenate([above[tiles - cols:], field[: tiles - cols]], axis=0)
    down = jnp.concatenate([field[cols:], below[:cols]], axis=0)
    column = lax.broadcasted_iota(jnp.int32, field.shape, 0) % cols
    rolled = jnp.concatenate([field[tiles - 1:], field[: tiles - 1]], axis=0)
    west_edge = jnp.concatenate([west[cols - 1:], west[: cols - 1]], axis=0)
    left = jnp.where(column == 0, west_edge, rolled)
    rolled = jnp.concatenate([field[1:], field[:1]], axis=0)
    east_edge = jnp.concatenate([east[tiles - cols + 1:], east[: tiles - cols + 1]], axis=0)
    right = jnp.where(column == cols - 1, east_edge, rolled)
    return up, down, left, right


def blocks_times(field, around, own_ref, nb_ref):
    tiles, width = field.shape
    chunk = 32
    lane = lax.broadcasted_iota(jnp.int32, (chunk, width), 1)
    sub = lax.broadcasted_iota(jnp.int32, (chunk, width), 0)
    outs = []
    for t in range(tiles):
        vecs = [f[t:t + 1] for f in around]
        mine = field[t:t + 1]
        spread = jnp.zeros((chunk, width), jnp.float32)
        for g in range(0, width, chunk):
            acc = own_ref[t, g:g + chunk, :] * mine
            for n, vec in enumerate(vecs):
                acc = acc + nb_ref[n, t, g:g + chunk, :] * vec
            total = jnp.sum(acc, axis=1, keepdims=True)
            spread = jnp.where(lane == sub + g, total, spread)
        outs.append(jnp.sum(spread, axis=0, keepdims=True))
    return jnp.concatenate(outs, axis=0)


def kernel(sweep, cols, present, flags, own_ref, nb_ref, weights, *refs):
    n_halo = sum(present)
    halo_refs, refs = refs[:n_halo], refs[n_halo:]
    halo_iter = iter(halo_refs)
    halos = [next(halo_iter)[...] if p else None for p in present]
    odd_row, odd_col = flags[0] == 1, flags[1] == 1
    field_ref, refs = refs[0], refs[1:]
    field = field_ref[...]
    around = beside(field, halos, odd_row, odd_col, cols)
    around = [f * weights[n] for n, f in enumerate(around)]
    product = blocks_times(field, around, own_ref, nb_ref)
    if sweep < 0:
        injected, search_out, residue_out, estimate_out = refs
        residue = injected[...] - product
        search_out[...] = residue
        residue_out[...] = residue
        estimate_out[...] = field + STRIDES[0] * residue
    else:
        capacity, residue_in, estimate_in = refs[:3]
        outs = refs[3:]
        residue = residue_in[...] - STRIDES[sweep] * (product + capacity[...] * field)
        search = residue + MOMENTA[sweep + 1] * field
        estimate = estimate_in[...] + STRIDES[sweep + 1] * search
        if sweep + 2 < ITERS:
            outs[0][...] = search
            outs[1][...] = residue
            outs[2][...] = estimate
        else:
            outs[0][...] = estimate


def collect(currents, slot_tile, tiles, width):
    slots, frames = currents.shape[3:]
    names = jnp.pad(slot_tile.astype(jnp.float32)[..., None, :],
                    ((0, 0), (0, 0), (0, 0), (0, 0), (0, frames - slots)))
    packed = jnp.concatenate([currents, names], axis=3)
    arrived = lax.all_to_all(packed, "col", split_axis=2, concat_axis=1, tiled=True)[0, :, 0]
    targets = arrived[:, slots, :slots]
    chooser = (targets[..., None] == jnp.arange(tiles, dtype=jnp.float32)).astype(jnp.float32)
    injected = jnp.einsum("skt,skf->tf", chooser, arrived[:, :slots], precision=lax.Precision.HIGHEST)
    return injected.reshape(tiles, STEPS, width)


def shards_general(own_block, neighbor_block, pattern, capacity, initial, currents, slot_tile):
    tile_rows, tile_cols, width = initial.shape
    tiles = tile_rows * tile_cols
    flags = jnp.stack([lax.axis_index("row") % 2, lax.axis_index("col") % 2]).astype(jnp.int32)

    voltage = initial.reshape(tiles, width)
    halos = exchange(voltage)

    injected = collect(currents, slot_tile, tiles, width)

    own = own_block.reshape(tiles, width, width)
    nb = neighbor_block.reshape(4, tiles, width, width)
    weights = jnp.broadcast_to(
        jnp.moveaxis(pattern.reshape(tiles, 4), 1, 0).astype(jnp.float32)[..., None], (4, tiles, width)
    )
    cap = capacity.reshape(tiles, width)
    shape = jax.ShapeDtypeStruct((tiles, width), jnp.float32)
    vmem = pl.BlockSpec(memory_space=pltpu.VMEM)
    smem = pl.BlockSpec(memory_space=pltpu.SMEM)

    def call(sweep, halos, *state):
        present = tuple(h is not None for h in halos)
        ins = (flags, own, nb, weights) + tuple(h for h in halos if h is not None) + state
        n_out = 1 if sweep + 2 == ITERS else 3
        out = pl.pallas_call(
            functools.partial(kernel, sweep, tile_cols, present),
            out_shape=(shape,) * n_out,
            in_specs=[smem] + [vmem] * (len(ins) - 1),
            out_specs=(vmem,) * n_out,
            compiler_params=pltpu.CompilerParams(vmem_limit_bytes=8 * 2**20),
            cost_estimate=pl.CostEstimate(flops=2 * 5 * tiles * width * width, bytes_accessed=5 * tiles * width * width * 4,
                                          transcendentals=0),
            name="couple",
        )(*ins)
        return out

    frames_out = []
    for instant in range(STEPS):
        if instant:
            halos = exchange(voltage)
        search, residue, estimate = call(-1, halos, voltage, injected[:, instant])
        for sweep in range(ITERS - 1):
            halos = exchange(search)
            out = call(sweep, halos, search, cap, residue, estimate)
            if sweep + 2 < ITERS:
                search, residue, estimate = out
            else:
                (voltage,) = out
        frames_out.append(voltage)
    return jnp.stack(frames_out).reshape(STEPS, tile_rows, tile_cols, width)


ROWS, HALF = 2, 2
N = 2 * ROWS
OWN, SIDE_B, ACROSS, OUT_IN, IN_OUT, IN_IN, EDGE_A, FACING, PACKED = 0, 4, 8, 10, 12, 14, 16, 18, 20
TILES = [(j, b) for j in range(N) for b in range(HALF)]
ORIGIN = [(0, 0), (0, 1), (1, 1), (1, 0)]
CAPACITY, INITIAL = STEPS, STEPS + 1
SPLIT = ((PACKED,), (OUT_IN, EDGE_A - OUT_IN))


def unit_device(unit, n_col):
    col = unit // 2
    return (unit + col) % 2, col


def half_tiles(y, col, n_col, cols, sent):
    k = (y + col + sent) % 2
    rows = (y, 1 - y)
    inward, outward = 1 - y, y
    at = [b + k * (cols - 1 - 2 * b) for b in range(HALF)]
    inside = jnp.where(col == k * (n_col - 1), 0.0, 1.0)
    tiles = [None] * PACKED
    for h in range(ROWS):
        for b in range(HALF):
            tiles[OWN + h * HALF + b] = (None, rows[h], at[b], None)
            tiles[(EDGE_A if b == 1 else ACROSS) + h] = (3 - k, rows[h], at[b], None)
            tiles[SIDE_B + h * HALF + b] = (2 + k, rows[h], at[b], inside if b == 0 else None)
        tiles[FACING + h] = (2 + k, rows[h], HALF - k, None)
    for b in range(HALF):
        tiles[OUT_IN + b] = (inward, rows[0], at[b], None)
        tiles[IN_OUT + b] = (outward, rows[1], at[b], None)
        tiles[IN_IN + b] = (inward, rows[1], at[b], None)
    return tiles


def pack_kernel(n_col, segments, pattern_hbm, own_hbm, nb_hbm, *refs):
    *outs, pattern_ref, sems = refs
    work = []
    for out, (sent, first, count) in zip(outs, segments):
        tiles = half_tiles(lax.axis_index("row"), lax.axis_index("col"), n_col, own_hbm.shape[1], sent)
        work += [(out, i, *tiles[first + i]) for i in range(count)]
    pattern_copy = pltpu.make_async_copy(pattern_hbm, pattern_ref, sems.at[len(work)])
    pattern_copy.start()
    copies = []
    for out, i, direction, row, at, _ in work:
        source = own_hbm.at[row, at] if direction is None else nb_hbm.at[direction, row, at]
        copies.append(pltpu.make_async_copy(source, out.at[i], sems.at[len(copies)]))
    for copy in copies:
        copy.start()
    pattern_copy.wait()
    for copy, (out, i, direction, row, at, weight) in zip(copies, work):
        copy.wait()
        if direction is not None:
            scale = pattern_ref[row, at, direction].astype(jnp.float32)
            out[i] = out[i] * (scale if weight is None else scale * weight)
    if len(outs) > len(segments):
        for h in range(ROWS):
            outs[-1][h] = outs[0][SIDE_B + h * HALF]


def block_of(refs, sizes, slot):
    for ref, size in zip(refs, sizes):
        if slot < size:
            return lambda g, n: ref[slot, g:g + n, :]
        slot -= size


def half_block(halves, i, slot):
    return block_of(halves[i], SPLIT[i], slot)


def tile_terms(halves, j, b):
    i, h = ORIGIN[j]
    terms = [(OWN + h * HALF + b, (j, b))]
    if h == 0:
        terms.append((OUT_IN + b, ((1, 2)[i], b)))
    else:
        terms.append((IN_OUT + b, ((0, 3)[i], b)))
        terms.append((IN_IN + b, ((2, 1)[i], b)))
    terms.append((ACROSS + h if b == 0 else SIDE_B + h * HALF + b, (j, 1 - b)))
    return [(half_block(halves, i, slot), at) for slot, at in terms]


def halo_block(halves, first_a, j, b):
    i, h = ORIGIN[j]
    if b == 0:
        return half_block(halves, i, SIDE_B + h * HALF)
    if i == 0:
        return half_block(halves, i, EDGE_A + h)
    start = 2 * N + (ROWS + h) * first_a.shape[1]
    return lambda g, n: first_a[start + g:start + g + n, :]


def facing_block(halves, beyond_0, first_a, first_b, j, b):
    i, h = ORIGIN[j]
    if i == 0:
        return half_block(halves, i, FACING + h) if b == 1 else lambda g, n: beyond_0[h, g:g + n, :]
    first = first_a if b == 1 else first_b
    start = 2 * N + h * first.shape[1]
    return lambda g, n: first[start + g:start + g + n, :]


def matvec(terms, chunk=64):
    width = terms[0][1].shape[1]
    lane = lax.broadcasted_iota(jnp.int32, (chunk, width), 1)
    sub = lax.broadcasted_iota(jnp.int32, (chunk, width), 0)
    spread = jnp.zeros((chunk, width), jnp.float32)
    for g in range(0, width, chunk):
        acc = None
        for block, vec in terms:
            part = block(g, chunk) * vec
            acc = part if acc is None else acc + part
        total = jnp.sum(acc, axis=1, keepdims=True)
        spread = jnp.where(lane == sub + g, total, spread)
    return jnp.sum(spread, axis=0, keepdims=True)


def rows_of(ref, start=0, count=N * HALF):
    return [ref[start + i:start + i + 1, :] for i in range(count)]


def put(ref, rows, start=0):
    for i, row in enumerate(rows):
        ref[start + i:start + i + 1, :] = row


def each(body, *fields):
    return [body(*rows) for rows in zip(*fields)]


def tile(j, b):
    return j * HALF + b


def products(terms, f):
    return [(block, f[tile(*at)]) for block, at in terms]


def inner_product(f, halves):
    return [matvec(products(tile_terms(halves, j, b), f)) for j, b in TILES]


def message(f, g, b):
    order = range(N)[::-1] if b == 1 else range(N)
    return [x[tile(j, b)] for x in (f, g) for j in order]


def ahead(first, sweep, f, q, residue, capacity, injected):
    if first:
        return each(lambda source, a: source - a, injected, q)
    return each(
        lambda v, a, r, c: r - STRIDES[sweep] * (a + c * v) + MOMENTA[sweep + 1] * v, f, q, residue, capacity
    )


def small_part(small, index):
    return rows_of(small, index * N * HALF)


def start_kernel(keep, recv_0, recv_1, small_keep, small_recv, edge, msg_a, msg_b, q_out, small):
    n = ROWS * HALF
    for i in range(0, small_keep.shape[0], n):
        small[2 * i:2 * i + n, :] = small_keep[i:i + n, :]
        small[2 * i + n:2 * i + n + HALF, :] = small_recv[i + HALF:i + n, :]
        small[2 * i + n + HALF:2 * i + 2 * n, :] = small_recv[i:i + HALF, :]
    halves = ((keep,), (recv_0, recv_1))
    f = small_part(small, INITIAL)
    q = inner_product(f, halves)
    put(q_out, q)
    g = ahead(True, 0, f, q, None, None, small_part(small, 0))
    put(msg_a, message(f, g, 1))
    put(msg_b, message(f, g, 0))
    width = small.shape[1]
    for h in range(ROWS):
        start = 2 * N + h * width
        msg_a[start:start + width, :] = keep[EDGE_A + h]
        msg_a[start + ROWS * width:start + (ROWS + 1) * width, :] = edge[h]
        msg_b[start:start + width, :] = recv_0[SIDE_B + h * HALF]


def by_target_kernel(currents, slot_tile, out):
    targets, slots, frames = currents.shape
    width = out.shape[2] - slots * frames
    names = slot_tile[...].astype(jnp.float32)
    names = jnp.concatenate([names, jnp.zeros((targets, width - slots), jnp.float32)], axis=1)
    for d in range(targets):
        for k in range(slots):
            out[d, :, k * frames:(k + 1) * frames] = currents[d, k:k + 1, :]
        out[d, :, slots * frames:] = names[d:d + 1, :]


def small_kernel(arrived, capacity, initial, keep, send, injected):
    y, col = lax.axis_index("row"), lax.axis_index("col")
    tiles, frames = injected.shape
    _, cols, width = capacity.shape
    slots = (arrived.shape[1] - width) // frames
    for t in range(tiles):
        total = jnp.zeros((arrived.shape[0], frames), jnp.float32)
        for k in range(slots):
            feeds = arrived[:, slots * frames + k:slots * frames + k + 1] == float(t)
            total = total + jnp.where(feeds, 1.0, 0.0) * arrived[:, k * frames:(k + 1) * frames]
        injected[t:t + 1, :] = jnp.sum(total, axis=0, keepdims=True)
    for sent, out in ((0, keep), (1, send)):
        parity = (y + col + sent) % 2
        for h in range(ROWS):
            row = y if h == 0 else 1 - y
            for b in range(HALF):
                at = b + parity * (cols - 1 - 2 * b)
                currents = injected[pl.ds(row * cols + at, 1), :]
                parts = [currents[:, n * width:(n + 1) * width] for n in range(STEPS)]
                parts += [x[row, pl.ds(at, 1), :] for x in (capacity, initial)]
                for n, part in enumerate(parts):
                    i = n * ROWS * HALF + h * HALF + b
                    out[i:i + 1, :] = part


def advance(instant, pair, small, product, f, residue):
    if pair == 0:
        residue = each(lambda source, a: source - a, small_part(small, instant), product)
        return residue, residue, 1.0
    sweep = 2 * pair - 1
    residue = each(lambda r, a, c, v: r - STRIDES[sweep] * (a + c * v), residue, product, small_part(small, CAPACITY), f)
    return residue, each(lambda r, v: r + MOMENTA[sweep + 1] * v, residue, f), STRIDES[sweep]


def beside_kernel(instant, pair, keep, recv_0, recv_1, beyond_0, first_a, first_b, small, got_a, q_ref, *refs):
    halves = ((keep,), (recv_0, recv_1))
    response_out, product_out, part_out = refs[-3:]
    f = small_part(small, INITIAL) if instant == pair == 0 else rows_of(refs[0])
    residue = None if pair == 0 else rows_of(refs[1])
    product = rows_of(q_ref)
    for j in range(N):
        product[tile(j, 1)] += matvec([(halo_block(halves, first_a, j, 1), got_a[j:j + 1, :])])
    put(product_out, product)
    response = [
        matvec([(facing_block(halves, beyond_0, first_a, first_b, j, b), f[tile(j, b)])]) for j, b in TILES
    ]
    put(response_out, response)
    _, f2, scale = advance(instant, pair, small, product, f, residue)
    part = []
    for j, b in TILES:
        terms = products(tile_terms(halves, j, b), f2)
        if b == 1:
            beside = got_a[N + j:N + j + 1, :] - scale * response[tile(j, b)]
            part.append(matvec(terms[:-1] + [(halo_block(halves, first_a, j, b), beside)]))
        else:
            part.append(matvec(terms[-1:]))
    put(part_out, part)


def pair_kernel(instant, pair, last, keep, recv_0, recv_1, small, got_b, response, product_ref, part_ref, *refs):
    halves = ((keep,), (recv_0, recv_1))
    first = pair == 0
    capacity = small_part(small, CAPACITY)
    if first and instant == 0:
        f = small_part(small, INITIAL)
    else:
        f, refs = rows_of(refs[0]), refs[1:]
    residue = estimate = None
    if not first:
        residue, estimate, refs = rows_of(refs[0]), rows_of(refs[1]), refs[2:]

    product = rows_of(product_ref)
    for j in range(N):
        product[tile(j, 0)] += matvec([(halo_block(halves, None, j, 0), got_b[j:j + 1, :])])
    residue, f2, scale = advance(instant, pair, small, product, f, residue)
    if first:
        estimate = each(lambda v, p: v + STRIDES[0] * p, f, f2)
    else:
        estimate = each(lambda e, p: e + STRIDES[2 * pair] * p, estimate, f2)

    total = rows_of(part_ref)
    for j, b in TILES:
        i = tile(j, b)
        terms = products(tile_terms(halves, j, b), f2)
        if b == 0:
            beside = got_b[N + j:N + j + 1, :] - scale * response[i:i + 1, :]
            total[i] += matvec(terms[:-1] + [(halo_block(halves, None, j, b), beside)])
        else:
            total[i] += matvec(terms[-1:])
    sweep = 2 * pair
    residue = each(lambda r, a, c, v: r - STRIDES[sweep] * (a + c * v), residue, total, capacity, f2)
    f3 = each(lambda r, v: r + MOMENTA[sweep + 1] * v, residue, f2)
    estimate = each(lambda e, p: e + STRIDES[sweep + 1] * p, estimate, f3)
    closing = sweep + 2 == ITERS
    if closing:
        f3 = estimate
    f_out, refs = refs[0], refs[1:]
    put(f_out, f3)
    if last:
        return
    q = inner_product(f3, halves)
    upcoming = small_part(small, instant + 1) if closing else None
    g = ahead(closing, sweep + 1, f3, q, residue, capacity, upcoming)
    q_out, msg_a, msg_b = refs[:3]
    put(msg_a, message(f3, g, 1))
    put(msg_b, message(f3, g, 0))
    put(q_out, q)
    if not closing:
        put(refs[3], residue)
        put(refs[4], estimate)


def shards_chain(own_block, neighbor_block, pattern, capacity, initial, currents, slot_tile):
    tile_rows, tile_cols, width = initial.shape
    n_col = lax.axis_size("col")
    row, col = lax.axis_index("row"), lax.axis_index("col")
    both = ("row", "col")
    swap = [(0, 1), (1, 0)]
    b_pairs = []
    for unit in range(1, 2 * n_col - 1, 2):
        ends = [r * n_col + c for r, c in (unit_device(unit, n_col), unit_device(unit + 1, n_col))]
        b_pairs += [tuple(ends), tuple(ends[::-1])]
    parity = (row + col) % 2

    vmem = pl.BlockSpec(memory_space=pltpu.VMEM)
    hbm = pl.BlockSpec(memory_space=pltpu.HBM)
    limit = pltpu.CompilerParams(vmem_limit_bytes=16 * 2**20)
    blocks = [pltpu.with_memory_space_constraint(x, pltpu.HBM) for x in (pattern, own_block, neighbor_block)]

    def pack(segments, extra=()):
        counts = [count for _, _, count in segments]
        return pl.pallas_call(
            functools.partial(pack_kernel, n_col, segments),
            out_shape=[jax.ShapeDtypeStruct((n, width, width), jnp.float32) for n in (*counts, *extra)],
            in_specs=[hbm, hbm, hbm],
            out_specs=[vmem] * (len(counts) + len(extra)),
            scratch_shapes=[pltpu.SMEM(pattern.shape, jnp.int32), pltpu.SemaphoreType.DMA((sum(counts) + 1,))],
            compiler_params=limit,
            name="pack",
        )(*blocks)

    recv = []
    for first, count in ((0, SPLIT[1][0]), SPLIT[1]):
        (send,) = pack(((1, first, count),))
        recv.append(lax.ppermute(send, "row", swap))
    keep, edge, facing_0 = pack(((0, 0, PACKED), (1, EDGE_A, ROWS)), (ROWS,))

    unit_small = jax.ShapeDtypeStruct(((STEPS + 2) * N * HALF, width), jnp.float32)

    def beside(currents, slot_tile, capacity, initial, facing_0):
        beyond_0 = lax.ppermute(facing_0, both, b_pairs)
        slots, frames = currents.shape[3:]
        by_target = pl.pallas_call(
            by_target_kernel,
            out_shape=jax.ShapeDtypeStruct((n_col, 1, slots * frames + width), jnp.float32),
            in_specs=[vmem, vmem],
            out_specs=vmem,
            compiler_params=limit,
            name="by_target",
        )(currents.reshape(n_col, slots, frames), slot_tile.reshape(n_col, slots))
        arrived = lax.all_to_all(by_target, "col", split_axis=0, concat_axis=0, tiled=True)
        half = jax.ShapeDtypeStruct(((STEPS + 2) * ROWS * HALF, width), jnp.float32)
        small, send = pl.pallas_call(
            small_kernel,
            out_shape=(half, half),
            in_specs=[vmem] * 3,
            out_specs=(vmem, vmem),
            scratch_shapes=[pltpu.VMEM((tile_rows * tile_cols, frames), jnp.float32)],
            compiler_params=limit,
            name="small",
        )(arrived.reshape(n_col, slots * frames + width), capacity, initial)
        return small, lax.ppermute(send, "row", swap), beyond_0

    *small, beyond_0 = lax.cond(
        row < lax.axis_size("row"),
        beside,
        lambda currents, slot_tile, capacity, initial, facing_0: (
            *jnp.zeros((2, (STEPS + 2) * ROWS * HALF, width), jnp.float32), facing_0
        ),
        currents, slot_tile, capacity, initial, facing_0,
    )

    shape = jax.ShapeDtypeStruct((N * HALF, width), jnp.float32)
    halves = (keep, *recv)

    def call(body, outs, blocks, *ins):
        return pl.pallas_call(
            body,
            out_shape=outs,
            in_specs=[vmem] * len(ins),
            out_specs=(vmem,) * len(outs),
            compiler_params=limit,
            cost_estimate=pl.CostEstimate(flops=2 * blocks * width * width, bytes_accessed=blocks * width * width * 4,
                                          transcendentals=0),
            name="pair",
        )(*ins)

    first_shape = jax.ShapeDtypeStruct((2 * N + ROWS * width, width), jnp.float32)
    first_a_shape = jax.ShapeDtypeStruct((2 * N + 2 * ROWS * width, width), jnp.float32)
    msg_a, msg_b, q, small = call(start_kernel, (first_a_shape, first_shape, shape, unit_small), 28, *halves, *small, edge)
    field, state, frames, first = (), (), [], None
    for instant in range(STEPS):
        for pair in range(ITERS // 2):
            closing = pair + 1 == ITERS // 2
            last = closing and instant + 1 == STEPS
            got_b = lax.ppermute(msg_b, both, b_pairs)
            got_a = lax.ppermute(msg_a, "row", swap)
            first = first or (got_a, got_b)
            response, product, part = call(functools.partial(beside_kernel, instant, pair), (shape,) * 3, 30,
                                           *halves, beyond_0, *first, small, got_a, q, *field, *state[:1])
            out = call(functools.partial(pair_kernel, instant, pair, last), (shape,) * (1 if last else 4 if closing else 6),
                       50, *halves, small, got_b, response, product, part, *field, *state)
            field = out[:1]
            if not last:
                q, msg_a, msg_b = out[1:4]
                state = out[4:]
        frames.append(field[0])

    done = jnp.stack(frames).reshape(STEPS, N, HALF, width)
    got = lax.ppermute(jnp.flip(done[:, ROWS:], 1), "row", swap)
    mine = done[:, :ROWS]
    unit_0, unit_1 = jnp.where(parity == 1, got, mine), jnp.where(parity == 1, mine, got)
    done = jnp.concatenate([unit_0, jnp.flip(unit_1, 2)], axis=2)
    return jnp.where(row == 1, jnp.flip(done, 1), done)


def solution(mesh):
    rows, cols = mesh.shape["row"], mesh.shape["col"]
    return jax.shard_map(
        shards_chain if rows == 2 else shards_general,
        mesh=mesh,
        in_specs=(
            P("row", "col", None, None),
            P(None, "row", "col", None, None),
            P("row", "col", None),
            P("row", "col", None),
            P("row", "col", None),
            P("row", "col", None, None, None),
            P("row", "col", None, None),
        ),
        out_specs=P(None, "row", "col", None),
        check_vma=False,
    )
```

```python
import functools

import jax
import jax.numpy as jnp
from jax import lax
from jax.experimental import pallas as pl
from jax.experimental.pallas import tpu as pltpu
from jax.sharding import PartitionSpec as P

STEPS = 4
ITERS = 8

spec_center = 6.4
spec_radius = 5.6


def schedule():
    strides, momenta = [], []
    stride = 1.0 / spec_center
    for sweep in range(ITERS):
        if sweep == 0:
            momentum = 0.0
        else:
            if sweep == 1:
                momentum = 0.5 * (spec_radius * stride) ** 2
            else:
                momentum = (spec_radius * stride / 2.0) ** 2
            stride = 1.0 / (spec_center - momentum / stride)
        strides.append(stride)
        momenta.append(momentum)
    return strides, momenta


STRIDES, MOMENTA = schedule()


def swap_pairs(count, first):
    pairs = []
    for i in range(first, count - 1, 2):
        pairs += [(i, i + 1), (i + 1, i)]
    return pairs


def exchange(field):
    arrived = []
    for axis in ("row", "col"):
        count = lax.axis_size(axis)
        for first in (0, 1):
            pairs = swap_pairs(count, first)
            arrived.append(lax.ppermute(field, axis, pairs) if pairs else None)
    return arrived


def beside(field, halos, odd_row, odd_col, cols):
    tiles = field.shape[0]
    row_a, row_b, col_a, col_b = halos
    zero = jnp.zeros_like(field)
    row_a, row_b, col_a, col_b = [zero if h is None else h for h in (row_a, row_b, col_a, col_b)]
    above = jnp.where(odd_row, row_a, row_b)
    below = jnp.where(odd_row, row_b, row_a)
    west = jnp.where(odd_col, col_a, col_b)
    east = jnp.where(odd_col, col_b, col_a)
    up = jnp.concatenate([above[tiles - cols:], field[: tiles - cols]], axis=0)
    down = jnp.concatenate([field[cols:], below[:cols]], axis=0)
    column = lax.broadcasted_iota(jnp.int32, field.shape, 0) % cols
    rolled = jnp.concatenate([field[tiles - 1:], field[: tiles - 1]], axis=0)
    west_edge = jnp.concatenate([west[cols - 1:], west[: cols - 1]], axis=0)
    left = jnp.where(column == 0, west_edge, rolled)
    rolled = jnp.concatenate([field[1:], field[:1]], axis=0)
    east_edge = jnp.concatenate([east[tiles - cols + 1:], east[: tiles - cols + 1]], axis=0)
    right = jnp.where(column == cols - 1, east_edge, rolled)
    return up, down, left, right


def blocks_times(field, around, own_ref, nb_ref):
    tiles, width = field.shape
    chunk = 32
    lane = lax.broadcasted_iota(jnp.int32, (chunk, width), 1)
    sub = lax.broadcasted_iota(jnp.int32, (chunk, width), 0)
    outs = []
    for t in range(tiles):
        vecs = [f[t:t + 1] for f in around]
        mine = field[t:t + 1]
        spread = jnp.zeros((chunk, width), jnp.float32)
        for g in range(0, width, chunk):
            acc = own_ref[t, g:g + chunk, :] * mine
            for n, vec in enumerate(vecs):
                acc = acc + nb_ref[n, t, g:g + chunk, :] * vec
            total = jnp.sum(acc, axis=1, keepdims=True)
            spread = jnp.where(lane == sub + g, total, spread)
        outs.append(jnp.sum(spread, axis=0, keepdims=True))
    return jnp.concatenate(outs, axis=0)


def kernel(sweep, cols, present, flags, own_ref, nb_ref, weights, *refs):
    n_halo = sum(present)
    halo_refs, refs = refs[:n_halo], refs[n_halo:]
    halo_iter = iter(halo_refs)
    halos = [next(halo_iter)[...] if p else None for p in present]
    odd_row, odd_col = flags[0] == 1, flags[1] == 1
    field_ref, refs = refs[0], refs[1:]
    field = field_ref[...]
    around = beside(field, halos, odd_row, odd_col, cols)
    around = [f * weights[n] for n, f in enumerate(around)]
    product = blocks_times(field, around, own_ref, nb_ref)
    if sweep < 0:
        injected, search_out, residue_out, estimate_out = refs
        residue = injected[...] - product
        search_out[...] = residue
        residue_out[...] = residue
        estimate_out[...] = field + STRIDES[0] * residue
    else:
        capacity, residue_in, estimate_in = refs[:3]
        outs = refs[3:]
        residue = residue_in[...] - STRIDES[sweep] * (product + capacity[...] * field)
        search = residue + MOMENTA[sweep + 1] * field
        estimate = estimate_in[...] + STRIDES[sweep + 1] * search
        if sweep + 2 < ITERS:
            outs[0][...] = search
            outs[1][...] = residue
            outs[2][...] = estimate
        else:
            outs[0][...] = estimate


def collect(currents, slot_tile, tiles, width):
    slots, frames = currents.shape[3:]
    names = jnp.pad(slot_tile.astype(jnp.float32)[..., None, :],
                    ((0, 0), (0, 0), (0, 0), (0, 0), (0, frames - slots)))
    packed = jnp.concatenate([currents, names], axis=3)
    arrived = lax.all_to_all(packed, "col", split_axis=2, concat_axis=1, tiled=True)[0, :, 0]
    targets = arrived[:, slots, :slots]
    chooser = (targets[..., None] == jnp.arange(tiles, dtype=jnp.float32)).astype(jnp.float32)
    injected = jnp.einsum("skt,skf->tf", chooser, arrived[:, :slots], precision=lax.Precision.HIGHEST)
    return injected.reshape(tiles, STEPS, width)


def shards_general(own_block, neighbor_block, pattern, capacity, initial, currents, slot_tile):
    tile_rows, tile_cols, width = initial.shape
    tiles = tile_rows * tile_cols
    flags = jnp.stack([lax.axis_index("row") % 2, lax.axis_index("col") % 2]).astype(jnp.int32)

    voltage = initial.reshape(tiles, width)
    halos = exchange(voltage)

    injected = collect(currents, slot_tile, tiles, width)

    own = own_block.reshape(tiles, width, width)
    nb = neighbor_block.reshape(4, tiles, width, width)
    weights = jnp.broadcast_to(
        jnp.moveaxis(pattern.reshape(tiles, 4), 1, 0).astype(jnp.float32)[..., None], (4, tiles, width)
    )
    cap = capacity.reshape(tiles, width)
    shape = jax.ShapeDtypeStruct((tiles, width), jnp.float32)
    vmem = pl.BlockSpec(memory_space=pltpu.VMEM)
    smem = pl.BlockSpec(memory_space=pltpu.SMEM)

    def call(sweep, halos, *state):
        present = tuple(h is not None for h in halos)
        ins = (flags, own, nb, weights) + tuple(h for h in halos if h is not None) + state
        n_out = 1 if sweep + 2 == ITERS else 3
        out = pl.pallas_call(
            functools.partial(kernel, sweep, tile_cols, present),
            out_shape=(shape,) * n_out,
            in_specs=[smem] + [vmem] * (len(ins) - 1),
            out_specs=(vmem,) * n_out,
            compiler_params=pltpu.CompilerParams(vmem_limit_bytes=8 * 2**20),
            cost_estimate=pl.CostEstimate(flops=2 * 5 * tiles * width * width, bytes_accessed=5 * tiles * width * width * 4,
                                          transcendentals=0),
            name="couple",
        )(*ins)
        return out

    frames_out = []
    for instant in range(STEPS):
        if instant:
            halos = exchange(voltage)
        search, residue, estimate = call(-1, halos, voltage, injected[:, instant])
        for sweep in range(ITERS - 1):
            halos = exchange(search)
            out = call(sweep, halos, search, cap, residue, estimate)
            if sweep + 2 < ITERS:
                search, residue, estimate = out
            else:
                (voltage,) = out
        frames_out.append(voltage)
    return jnp.stack(frames_out).reshape(STEPS, tile_rows, tile_cols, width)


ROWS, HALF = 2, 2
N = 2 * ROWS
OWN, SIDE_B, ACROSS, OUT_IN, IN_OUT, IN_IN, EDGE_A, FACING, PACKED = 0, 4, 8, 10, 12, 14, 16, 18, 20
TILES = [(j, b) for j in range(N) for b in range(HALF)]
ORIGIN = [(0, 0), (0, 1), (1, 1), (1, 0)]
CAPACITY, INITIAL = STEPS, STEPS + 1
SPLIT = ((PACKED,), (OUT_IN, EDGE_A - OUT_IN))


def unit_device(unit, n_col):
    col = unit // 2
    return (unit + col) % 2, col


def half_tiles(y, col, n_col, cols, sent):
    k = (y + col + sent) % 2
    rows = (y, 1 - y)
    inward, outward = 1 - y, y
    at = [b + k * (cols - 1 - 2 * b) for b in range(HALF)]
    inside = jnp.where(col == k * (n_col - 1), 0.0, 1.0)
    tiles = [None] * PACKED
    for h in range(ROWS):
        for b in range(HALF):
            tiles[OWN + h * HALF + b] = (None, rows[h], at[b], None)
            tiles[(EDGE_A if b == 1 else ACROSS) + h] = (3 - k, rows[h], at[b], None)
            tiles[SIDE_B + h * HALF + b] = (2 + k, rows[h], at[b], inside if b == 0 else None)
        tiles[FACING + h] = (2 + k, rows[h], HALF - k, None)
    for b in range(HALF):
        tiles[OUT_IN + b] = (inward, rows[0], at[b], None)
        tiles[IN_OUT + b] = (outward, rows[1], at[b], None)
        tiles[IN_IN + b] = (inward, rows[1], at[b], None)
    return tiles


def pack_kernel(n_col, segments, pattern_hbm, own_hbm, nb_hbm, *refs):
    *outs, pattern_ref, sems = refs
    work = []
    for out, (sent, first, count) in zip(outs, segments):
        tiles = half_tiles(lax.axis_index("row"), lax.axis_index("col"), n_col, own_hbm.shape[1], sent)
        work += [(out, i, *tiles[first + i]) for i in range(count)]
    pattern_copy = pltpu.make_async_copy(pattern_hbm, pattern_ref, sems.at[len(work)])
    pattern_copy.start()
    copies = []
    for out, i, direction, row, at, _ in work:
        source = own_hbm.at[row, at] if direction is None else nb_hbm.at[direction, row, at]
        copies.append(pltpu.make_async_copy(source, out.at[i], sems.at[len(copies)]))
    for copy in copies:
        copy.start()
    pattern_copy.wait()
    for copy, (out, i, direction, row, at, weight) in zip(copies, work):
        copy.wait()
        if direction is not None:
            scale = pattern_ref[row, at, direction].astype(jnp.float32)
            out[i] = out[i] * (scale if weight is None else scale * weight)
    if len(outs) > len(segments):
        for h in range(ROWS):
            outs[-1][h] = outs[0][SIDE_B + h * HALF]


def block_of(refs, sizes, slot):
    for ref, size in zip(refs, sizes):
        if slot < size:
            return lambda g, n: ref[slot, g:g + n, :]
        slot -= size


def half_block(halves, i, slot):
    return block_of(halves[i], SPLIT[i], slot)


def tile_terms(halves, j, b):
    i, h = ORIGIN[j]
    terms = [(OWN + h * HALF + b, (j, b))]
    if h == 0:
        terms.append((OUT_IN + b, ((1, 2)[i], b)))
    else:
        terms.append((IN_OUT + b, ((0, 3)[i], b)))
        terms.append((IN_IN + b, ((2, 1)[i], b)))
    terms.append((ACROSS + h if b == 0 else SIDE_B + h * HALF + b, (j, 1 - b)))
    return [(half_block(halves, i, slot), at) for slot, at in terms]


def halo_block(halves, first_a, j, b):
    i, h = ORIGIN[j]
    if b == 0:
        return half_block(halves, i, SIDE_B + h * HALF)
    if i == 0:
        return half_block(halves, i, EDGE_A + h)
    start = 2 * N + (ROWS + h) * first_a.shape[1]
    return lambda g, n: first_a[start + g:start + g + n, :]


def facing_block(halves, beyond_0, first_a, first_b, j, b):
    i, h = ORIGIN[j]
    if i == 0:
        return half_block(halves, i, FACING + h) if b == 1 else lambda g, n: beyond_0[h, g:g + n, :]
    first = first_a if b == 1 else first_b
    start = 2 * N + h * first.shape[1]
    return lambda g, n: first[start + g:start + g + n, :]


def matvec(terms, chunk=128):
    width = terms[0][1].shape[1]
    lane = lax.broadcasted_iota(jnp.int32, (chunk, width), 1)
    sub = lax.broadcasted_iota(jnp.int32, (chunk, width), 0)
    spread = jnp.zeros((chunk, width), jnp.float32)
    for g in range(0, width, chunk):
        acc = None
        for block, vec in terms:
            part = block(g, chunk) * vec
            acc = part if acc is None else acc + part
        total = jnp.sum(acc, axis=1, keepdims=True)
        spread = jnp.where(lane == sub + g, total, spread)
    return jnp.sum(spread, axis=0, keepdims=True)


def rows_of(ref, start=0, count=N * HALF):
    return [ref[start + i:start + i + 1, :] for i in range(count)]


def put(ref, rows, start=0):
    for i, row in enumerate(rows):
        ref[start + i:start + i + 1, :] = row


def each(body, *fields):
    return [body(*rows) for rows in zip(*fields)]


def tile(j, b):
    return j * HALF + b


def products(terms, f):
    return [(block, f[tile(*at)]) for block, at in terms]


def inner_product(f, halves):
    return [matvec(products(tile_terms(halves, j, b), f)) for j, b in TILES]


def message(f, g, b):
    order = range(N)[::-1] if b == 1 else range(N)
    return [x[tile(j, b)] for x in (f, g) for j in order]


def ahead(first, sweep, f, q, residue, capacity, injected):
    if first:
        return each(lambda source, a: source - a, injected, q)
    return each(
        lambda v, a, r, c: r - STRIDES[sweep] * (a + c * v) + MOMENTA[sweep + 1] * v, f, q, residue, capacity
    )


def small_part(small, index):
    return rows_of(small, index * N * HALF)


def start_kernel(keep, recv_0, recv_1, small_keep, small_recv, edge, msg_a, msg_b, q_out, small):
    n = ROWS * HALF
    for i in range(0, small_keep.shape[0], n):
        small[2 * i:2 * i + n, :] = small_keep[i:i + n, :]
        small[2 * i + n:2 * i + n + HALF, :] = small_recv[i + HALF:i + n, :]
        small[2 * i + n + HALF:2 * i + 2 * n, :] = small_recv[i:i + HALF, :]
    halves = ((keep,), (recv_0, recv_1))
    f = small_part(small, INITIAL)
    q = inner_product(f, halves)
    put(q_out, q)
    g = ahead(True, 0, f, q, None, None, small_part(small, 0))
    put(msg_a, message(f, g, 1))
    put(msg_b, message(f, g, 0))
    width = small.shape[1]
    for h in range(ROWS):
        start = 2 * N + h * width
        msg_a[start:start + width, :] = keep[EDGE_A + h]
        msg_a[start + ROWS * width:start + (ROWS + 1) * width, :] = edge[h]
        msg_b[start:start + width, :] = recv_0[SIDE_B + h * HALF]


def by_target_kernel(currents, slot_tile, out):
    targets, slots, frames = currents.shape
    width = out.shape[2] - slots * frames
    names = slot_tile[...].astype(jnp.float32)
    names = jnp.concatenate([names, jnp.zeros((targets, width - slots), jnp.float32)], axis=1)
    for d in range(targets):
        for k in range(slots):
            out[d, :, k * frames:(k + 1) * frames] = currents[d, k:k + 1, :]
        out[d, :, slots * frames:] = names[d:d + 1, :]


def small_kernel(arrived, capacity, initial, keep, send, injected):
    y, col = lax.axis_index("row"), lax.axis_index("col")
    tiles, frames = injected.shape
    _, cols, width = capacity.shape
    slots = (arrived.shape[1] - width) // frames
    for t in range(tiles):
        total = jnp.zeros((arrived.shape[0], frames), jnp.float32)
        for k in range(slots):
            feeds = arrived[:, slots * frames + k:slots * frames + k + 1] == float(t)
            total = total + jnp.where(feeds, 1.0, 0.0) * arrived[:, k * frames:(k + 1) * frames]
        injected[t:t + 1, :] = jnp.sum(total, axis=0, keepdims=True)
    for sent, out in ((0, keep), (1, send)):
        parity = (y + col + sent) % 2
        for h in range(ROWS):
            row = y if h == 0 else 1 - y
            for b in range(HALF):
                at = b + parity * (cols - 1 - 2 * b)
                currents = injected[pl.ds(row * cols + at, 1), :]
                parts = [currents[:, n * width:(n + 1) * width] for n in range(STEPS)]
                parts += [x[row, pl.ds(at, 1), :] for x in (capacity, initial)]
                for n, part in enumerate(parts):
                    i = n * ROWS * HALF + h * HALF + b
                    out[i:i + 1, :] = part


def advance(instant, pair, small, product, f, residue):
    if pair == 0:
        residue = each(lambda source, a: source - a, small_part(small, instant), product)
        return residue, residue, 1.0
    sweep = 2 * pair - 1
    residue = each(lambda r, a, c, v: r - STRIDES[sweep] * (a + c * v), residue, product, small_part(small, CAPACITY), f)
    return residue, each(lambda r, v: r + MOMENTA[sweep + 1] * v, residue, f), STRIDES[sweep]


def beside_kernel(instant, pair, keep, recv_0, recv_1, beyond_0, first_a, first_b, small, got_a, q_ref, *refs):
    halves = ((keep,), (recv_0, recv_1))
    response_out, product_out, part_out = refs[-3:]
    f = small_part(small, INITIAL) if instant == pair == 0 else rows_of(refs[0])
    residue = None if pair == 0 else rows_of(refs[1])
    product = rows_of(q_ref)
    for j in range(N):
        product[tile(j, 1)] += matvec([(halo_block(halves, first_a, j, 1), got_a[j:j + 1, :])])
    put(product_out, product)
    response = [
        matvec([(facing_block(halves, beyond_0, first_a, first_b, j, b), f[tile(j, b)])]) for j, b in TILES
    ]
    put(response_out, response)
    _, f2, scale = advance(instant, pair, small, product, f, residue)
    part = []
    for j, b in TILES:
        terms = products(tile_terms(halves, j, b), f2)
        if b == 1:
            beside = got_a[N + j:N + j + 1, :] - scale * response[tile(j, b)]
            part.append(matvec(terms[:-1] + [(halo_block(halves, first_a, j, b), beside)]))
        else:
            part.append(matvec(terms[-1:]))
    put(part_out, part)


def pair_kernel(instant, pair, last, keep, recv_0, recv_1, small, got_b, response, product_ref, part_ref, *refs):
    halves = ((keep,), (recv_0, recv_1))
    first = pair == 0
    capacity = small_part(small, CAPACITY)
    if first and instant == 0:
        f = small_part(small, INITIAL)
    else:
        f, refs = rows_of(refs[0]), refs[1:]
    residue = estimate = None
    if not first:
        residue, estimate, refs = rows_of(refs[0]), rows_of(refs[1]), refs[2:]

    product = rows_of(product_ref)
    for j in range(N):
        product[tile(j, 0)] += matvec([(halo_block(halves, None, j, 0), got_b[j:j + 1, :])])
    residue, f2, scale = advance(instant, pair, small, product, f, residue)
    if first:
        estimate = each(lambda v, p: v + STRIDES[0] * p, f, f2)
    else:
        estimate = each(lambda e, p: e + STRIDES[2 * pair] * p, estimate, f2)

    total = rows_of(part_ref)
    for j, b in TILES:
        i = tile(j, b)
        terms = products(tile_terms(halves, j, b), f2)
        if b == 0:
            beside = got_b[N + j:N + j + 1, :] - scale * response[i:i + 1, :]
            total[i] += matvec(terms[:-1] + [(halo_block(halves, None, j, b), beside)])
        else:
            total[i] += matvec(terms[-1:])
    sweep = 2 * pair
    residue = each(lambda r, a, c, v: r - STRIDES[sweep] * (a + c * v), residue, total, capacity, f2)
    f3 = each(lambda r, v: r + MOMENTA[sweep + 1] * v, residue, f2)
    estimate = each(lambda e, p: e + STRIDES[sweep + 1] * p, estimate, f3)
    closing = sweep + 2 == ITERS
    if closing:
        f3 = estimate
    f_out, refs = refs[0], refs[1:]
    put(f_out, f3)
    if last:
        return
    q = inner_product(f3, halves)
    upcoming = small_part(small, instant + 1) if closing else None
    g = ahead(closing, sweep + 1, f3, q, residue, capacity, upcoming)
    q_out, msg_a, msg_b = refs[:3]
    put(msg_a, message(f3, g, 1))
    put(msg_b, message(f3, g, 0))
    put(q_out, q)
    if not closing:
        put(refs[3], residue)
        put(refs[4], estimate)


def shards_chain(own_block, neighbor_block, pattern, capacity, initial, currents, slot_tile):
    tile_rows, tile_cols, width = initial.shape
    n_col = lax.axis_size("col")
    row, col = lax.axis_index("row"), lax.axis_index("col")
    both = ("row", "col")
    swap = [(0, 1), (1, 0)]
    b_pairs = []
    for unit in range(1, 2 * n_col - 1, 2):
        ends = [r * n_col + c for r, c in (unit_device(unit, n_col), unit_device(unit + 1, n_col))]
        b_pairs += [tuple(ends), tuple(ends[::-1])]
    parity = (row + col) % 2

    vmem = pl.BlockSpec(memory_space=pltpu.VMEM)
    hbm = pl.BlockSpec(memory_space=pltpu.HBM)
    limit = pltpu.CompilerParams(vmem_limit_bytes=16 * 2**20)
    blocks = [pltpu.with_memory_space_constraint(x, pltpu.HBM) for x in (pattern, own_block, neighbor_block)]

    def pack(segments, extra=()):
        counts = [count for _, _, count in segments]
        return pl.pallas_call(
            functools.partial(pack_kernel, n_col, segments),
            out_shape=[jax.ShapeDtypeStruct((n, width, width), jnp.float32) for n in (*counts, *extra)],
            in_specs=[hbm, hbm, hbm],
            out_specs=[vmem] * (len(counts) + len(extra)),
            scratch_shapes=[pltpu.SMEM(pattern.shape, jnp.int32), pltpu.SemaphoreType.DMA((sum(counts) + 1,))],
            compiler_params=limit,
            name="pack",
        )(*blocks)

    recv = []
    for first, count in ((0, SPLIT[1][0]), SPLIT[1]):
        (send,) = pack(((1, first, count),))
        recv.append(lax.ppermute(send, "row", swap))
    keep, edge, facing_0 = pack(((0, 0, PACKED), (1, EDGE_A, ROWS)), (ROWS,))

    unit_small = jax.ShapeDtypeStruct(((STEPS + 2) * N * HALF, width), jnp.float32)

    def beside(currents, slot_tile, capacity, initial, facing_0):
        beyond_0 = lax.ppermute(facing_0, both, b_pairs)
        slots, frames = currents.shape[3:]
        by_target = pl.pallas_call(
            by_target_kernel,
            out_shape=jax.ShapeDtypeStruct((n_col, 1, slots * frames + width), jnp.float32),
            in_specs=[vmem, vmem],
            out_specs=vmem,
            compiler_params=limit,
            name="by_target",
        )(currents.reshape(n_col, slots, frames), slot_tile.reshape(n_col, slots))
        arrived = lax.all_to_all(by_target, "col", split_axis=0, concat_axis=0, tiled=True)
        half = jax.ShapeDtypeStruct(((STEPS + 2) * ROWS * HALF, width), jnp.float32)
        small, send = pl.pallas_call(
            small_kernel,
            out_shape=(half, half),
            in_specs=[vmem] * 3,
            out_specs=(vmem, vmem),
            scratch_shapes=[pltpu.VMEM((tile_rows * tile_cols, frames), jnp.float32)],
            compiler_params=limit,
            name="small",
        )(arrived.reshape(n_col, slots * frames + width), capacity, initial)
        return small, lax.ppermute(send, "row", swap), beyond_0

    *small, beyond_0 = lax.cond(
        row < lax.axis_size("row"),
        beside,
        lambda currents, slot_tile, capacity, initial, facing_0: (
            *jnp.zeros((2, (STEPS + 2) * ROWS * HALF, width), jnp.float32), facing_0
        ),
        currents, slot_tile, capacity, initial, facing_0,
    )

    shape = jax.ShapeDtypeStruct((N * HALF, width), jnp.float32)
    halves = (keep, *recv)

    def call(body, outs, blocks, *ins):
        return pl.pallas_call(
            body,
            out_shape=outs,
            in_specs=[vmem] * len(ins),
            out_specs=(vmem,) * len(outs),
            compiler_params=limit,
            cost_estimate=pl.CostEstimate(flops=2 * blocks * width * width, bytes_accessed=blocks * width * width * 4,
                                          transcendentals=0),
            name="pair",
        )(*ins)

    first_shape = jax.ShapeDtypeStruct((2 * N + ROWS * width, width), jnp.float32)
    first_a_shape = jax.ShapeDtypeStruct((2 * N + 2 * ROWS * width, width), jnp.float32)
    msg_a, msg_b, q, small = call(start_kernel, (first_a_shape, first_shape, shape, unit_small), 28, *halves, *small, edge)
    field, state, frames, first = (), (), [], None
    for instant in range(STEPS):
        for pair in range(ITERS // 2):
            closing = pair + 1 == ITERS // 2
            last = closing and instant + 1 == STEPS
            got_b = lax.ppermute(msg_b, both, b_pairs)
            got_a = lax.ppermute(msg_a, "row", swap)
            first = first or (got_a, got_b)
            response, product, part = call(functools.partial(beside_kernel, instant, pair), (shape,) * 3, 30,
                                           *halves, beyond_0, *first, small, got_a, q, *field, *state[:1])
            out = call(functools.partial(pair_kernel, instant, pair, last), (shape,) * (1 if last else 4 if closing else 6),
                       50, *halves, small, got_b, response, product, part, *field, *state)
            field = out[:1]
            if not last:
                q, msg_a, msg_b = out[1:4]
                state = out[4:]
        frames.append(field[0])

    done = jnp.stack(frames).reshape(STEPS, N, HALF, width)
    got = lax.ppermute(jnp.flip(done[:, ROWS:], 1), "row", swap)
    mine = done[:, :ROWS]
    unit_0, unit_1 = jnp.where(parity == 1, got, mine), jnp.where(parity == 1, mine, got)
    done = jnp.concatenate([unit_0, jnp.flip(unit_1, 2)], axis=2)
    return jnp.where(row == 1, jnp.flip(done, 1), done)


def solution(mesh):
    rows, cols = mesh.shape["row"], mesh.shape["col"]
    return jax.shard_map(
        shards_chain if rows == 2 else shards_general,
        mesh=mesh,
        in_specs=(
            P("row", "col", None, None),
            P(None, "row", "col", None, None),
            P("row", "col", None),
            P("row", "col", None),
            P("row", "col", None),
            P("row", "col", None, None, None),
            P("row", "col", None, None),
        ),
        out_specs=P(None, "row", "col", None),
        check_vma=False,
    )
```
